32 devices in a mesh: dp: 16 (over z, y, x), tensor: 2 (over core).
Axes of the slice: x: 2, y: 2, z: 4, core: 2. Of those that a mesh axis runs over, the one named last changes fastest.
Arguments:
- question_tokens: bfloat16 [32, 64, 768], P('dp'), may hold values from -6 to 6
- passage_tokens: bfloat16 [32, 256, 768], P('dp'), may hold values from -6 to 6
- question_cotangent: bfloat16 [32, 64, 768], P('dp'), may hold values from -6 to 6
- passage_cotangent: bfloat16 [32, 256, 768], P('dp'), may hold values from -6 to 6
- question_lengths: int32 [32], P('dp'), may hold values from 16 to 64, as said below
- passage_lengths: int32 [32], P('dp'), may hold values from 64 to 256, as said below
- dataset_ids: int32 [32], replicated, may hold values from 0 to 3
- positives: int32 [32], replicated, may hold values from 0 to 31, as said below
- attn_in: bfloat16 [2, 768, 3, 768], P(None, None, None, 'tensor'), may hold values from -0.21875 to 0.21875
- attn_in_bias: bfloat16 [2, 2, 768], P(None, None, 'tensor'), may hold values from -3 to 3
- attn_out: bfloat16 [2, 768, 768], P(None, 'tensor'), may hold values from -0.875 to 0.875
- ffn_in: bfloat16 [2, 768, 3072], P(None, None, 'tensor'), may hold values from -0.21875 to 0.21875
- ffn_in_bias: bfloat16 [2, 3072], P(None, 'tensor'), may hold values from -3 to 3
- ffn_out: bfloat16 [2, 3072, 768], P(None, 'tensor'), may hold values from -0.109375 to 0.109375
- out_biases: bfloat16 [2, 2, 768], replicated, may hold values from -2 to 2
- norm_gains: bfloat16 [2, 2, 768], replicated, may hold values from 0.25 to 1.75
- norm_shifts: bfloat16 [2, 2, 768], replicated, may hold values from -2 to 2
Outputs:
- question_out: bfloat16 [32, 64, 768], P('dp')
- passage_out: bfloat16 [32, 256, 768], P('dp')
- contrastive_loss: float32 [], replicated
- question_grad: bfloat16 [32, 64, 768], P('dp')
- passage_grad: bfloat16 [32, 256, 768], P('dp')
- grad_attn_in: float32 [2, 768, 3, 768], P(None, 'dp', None, 'tensor')
- grad_attn_in_bias: float32 [2, 2, 768], P(None, None, ('tensor', 'dp'))
- grad_attn_out: float32 [2, 768, 768], P(None, 'tensor', 'dp')
- grad_ffn_in: float32 [2, 768, 3072], P(None, 'dp', 'tensor')
- grad_ffn_in_bias: float32 [2, 3072], P(None, ('tensor', 'dp'))
- grad_ffn_out: float32 [2, 3072, 768], P(None, 'tensor', 'dp')
- grad_out_biases: float32 [2, 2, 768], P(None, None, 'dp')
- grad_norm_gains: float32 [2, 2, 768], P(None, None, 'dp')
- grad_norm_shifts: float32 [2, 2, 768], P(None, None, 'dp')
The draws below stay inside these ranges and needn't reach their ends.
Inputs may be any that keep to these rules, and one draw needn't show every extreme that they name: `question_lengths`: some question has 64 real tokens and some has 16. `passage_lengths`: some passage has 256 real tokens and some has 64. `positives`: a permutation of the groups.
All inputs are finite; a program needn't handle non-finite values.
Results may differ from the reference program's by a relative error of at most 0.019.
Values may be sent and summed in bfloat16 or wider, within the bound.
A program may use at most 192 MiB of HBM per device.

```python
from functools import partial
import jax
import jax.numpy as jnp
from jax import lax

D = 768
HD = 64
FF = 3072
QLEN = 64
PLEN = 256
DATASETS = 4
GRP_DEV = 2
GROUPS = 32


def ragged_lengths(key, stream, most):
    folded = jax.random.fold_in(key, stream)
    draw_key, place_key = jax.random.split(folded)
    drawn = jax.random.randint(draw_key, (GROUPS,), most // 4, most + 1)
    peak_at = jax.random.randint(place_key, (), 0, GROUPS)
    drawn = drawn.at[peak_at].set(most)
    drawn = drawn.at[(peak_at + GROUPS // 2) % GROUPS].set(most // 4)
    return drawn.astype(jnp.int32)


def draw_question_lengths(key, part):
    return ragged_lengths(key, 17, QLEN)


def draw_passage_lengths(key, part):
    return ragged_lengths(key, 29, PLEN)


def place_target(order, row, target):
    holder = jnp.argmax(order == target).astype(jnp.int32)
    previous = order[row]
    order = order.at[holder].set(previous)
    return order.at[row].set(target)


def draw_positives(key, part):
    key = jax.random.fold_in(key, 41)
    order_key, row_key = jax.random.split(key)
    order = jax.random.permutation(order_key, GROUPS).astype(jnp.int32)
    first_row = jax.random.randint(row_key, (), 0, GROUPS).astype(jnp.int32)
    second_row = (first_row + 1) % GROUPS
    order = place_target(order, first_row, (first_row + GROUPS // 2) % GROUPS)
    order = place_target(order, second_row, (second_row - GRP_DEV + GROUPS) % GROUPS)
    return order.astype(jnp.int32)


def with_ends(values, stream_key, smallest, high):
    extent = values.shape
    spot = [jax.random.randint(jax.random.fold_in(stream_key, axis), (), 0, extent[axis]) for axis in range(len(extent))]
    values = values.at[tuple(spot)].set(smallest)
    longest = extent.index(max(extent))
    spot[longest] = (spot[longest] + 1) % extent[longest]
    return values.at[tuple(spot)].set(high)


def block_scale(stream_key, dims, cuts, smallest, largest):
    gain, own = 1.0, jax.random.fold_in(stream_key, 6)
    for axis_at, blocks in cuts:
        heights = jnp.exp(jax.random.uniform(jax.random.fold_in(own, axis_at), (blocks,), jnp.float32, smallest / len(cuts), largest / len(cuts)))
        gain = gain * jnp.repeat(heights, dims[axis_at] // blocks).reshape([-1 if axis == axis_at else 1 for axis in range(len(dims))])
    return gain


def bell_draw(stream_key, dims, spread, most, cuts=(), held_as=jnp.bfloat16):
    loudness = block_scale(stream_key, dims, cuts, -0.22, 0.18) if cuts else 1.0
    result = jax.random.normal(stream_key, dims, jnp.float32) * spread * loudness
    return jnp.minimum(jnp.maximum(result, -most), most).astype(held_as)


def setup_inputs(seed: int = 0) -> dict:
    arg_keys = jax.random.split(jax.random.key(seed), 18)
    return {
        "question_tokens": bell_draw(arg_keys[0], (GROUPS, QLEN, D), 1.0, 6.0, ((0, 16),)),
        "passage_tokens": bell_draw(arg_keys[1], (GROUPS, PLEN, D), 1.0, 6.0, ((0, 16),)),
        "question_cotangent": bell_draw(arg_keys[2], (GROUPS, QLEN, D), 1.0, 6.0, ((0, 16),)),
        "passage_cotangent": bell_draw(arg_keys[3], (GROUPS, PLEN, D), 1.0, 6.0, ((0, 16),)),
        "question_lengths": draw_question_lengths(jax.random.fold_in(arg_keys[17], 71), 0),
        "passage_lengths": draw_passage_lengths(jax.random.fold_in(arg_keys[17], 71), 0),
        "dataset_ids": with_ends(jax.random.randint(arg_keys[6], (GROUPS,), 0, DATASETS), jax.random.fold_in(arg_keys[6], 1), 0, DATASETS - 1).astype(jnp.int32),
        "positives": draw_positives(jax.random.fold_in(arg_keys[17], 71), 0),
        "attn_in": bell_draw(arg_keys[8], (2, D, 3, D), D ** -0.5, 0.21875, ((3, 2),)),
        "attn_in_bias": bell_draw(arg_keys[9], (2, 2, D), 0.5, 3.0, ((2, 2),)),
        "attn_out": bell_draw(arg_keys[10], (2, D, D), (D // 16) ** -0.5, 0.875, ((1, 2),)),
        "ffn_in": bell_draw(arg_keys[11], (2, D, FF), D ** -0.5, 0.21875, ((2, 2),)),
        "ffn_in_bias": bell_draw(arg_keys[12], (2, FF), 0.5, 3.0, ((1, 2),)),
        "ffn_out": bell_draw(arg_keys[13], (2, FF, D), FF ** -0.5, 0.109375, ((1, 2),)),
        "out_biases": bell_draw(arg_keys[14], (2, 2, D), 0.3, 2.0),
        "norm_gains": jnp.clip(1.0 + 0.15 * jax.random.normal(arg_keys[15], (2, 2, D), jnp.float32), 0.25, 1.75).astype(jnp.bfloat16),
        "norm_shifts": bell_draw(arg_keys[16], (2, 2, D), 0.3, 2.0),
    }


EPSILON = 1e-06
NEGATIVE = -1e+30
HIGHEST = lax.Precision.HIGHEST
score_gain = 3.0

@jax.custom_vjp
def low(v):
    return lax.optimization_barrier(v.astype(jnp.bfloat16)).astype(jnp.float32)

@jax.custom_vjp
def low_back(v):
    return v

def low_keep(v):
    return (low(v), None)

def low_pass(kept, grad):
    return (grad,)

def back_keep(v):
    return (v, None)

def back_low(kept, grad):
    return (low(grad),)
low.defvjp(low_keep, low_pass)
low_back.defvjp(back_keep, back_low)

def layer_norm(summed, scale_row, shift_row):
    row_mean = lax.optimization_barrier(jnp.mean(summed, axis=-1, keepdims=True))
    centred = summed - row_mean
    variance = lax.optimization_barrier(jnp.mean(centred * centred, axis=-1, keepdims=True))
    return centred * lax.rsqrt(variance + EPSILON) * scale_row + shift_row

def encode_block(params, tokens, lengths):
    attn_in, attn_in_bias, attn_out, ffn_in, ffn_in_bias, ffn_out, out_biases, norm_gains, norm_shifts = params
    groups_here, length, model_width = tokens.shape
    head_count = model_width // HD
    projected = jnp.einsum('bld,dce->blce', tokens, attn_in, precision=HIGHEST)
    queries = low_back(low(projected[:, :, 0] + attn_in_bias[0]))
    key_rows = low_back(low(projected[:, :, 1]))
    values = low_back(low(projected[:, :, 2] + attn_in_bias[1]))
    queries = queries.reshape(groups_here, length, head_count, HD)
    key_rows = key_rows.reshape(groups_here, length, head_count, HD)
    values = values.reshape(groups_here, length, head_count, HD)
    scores = low_back(jnp.einsum('bqhe,bkhe->bhqk', queries, key_rows, precision=HIGHEST) * HD ** (-0.5))
    positions = jnp.arange(length, dtype=jnp.int32)
    visible = (positions[None, :] < lengths[:, None])[:, None, None, :]
    scores = jnp.where(visible, scores, NEGATIVE)
    attn_probs = low(jax.nn.softmax(scores, axis=-1))
    context = jnp.einsum('bhqk,bkhe->bqhe', attn_probs, values, precision=HIGHEST)
    context = low_back(low(context.reshape(groups_here, length, model_width)))
    attn = low_back(jnp.einsum('ble,ed->bld', context, attn_out, precision=HIGHEST) + out_biases[0])
    hidden = low(layer_norm(tokens + attn, norm_gains[0], norm_shifts[0]))
    up_pre = low_back(jnp.einsum('bld,df->blf', hidden, ffn_in, precision=HIGHEST) + ffn_in_bias)
    activated = low(jax.nn.gelu(up_pre, approximate=False))
    down = low_back(jnp.einsum('blf,fd->bld', activated, ffn_out, precision=HIGHEST) + out_biases[1])
    return layer_norm(hidden + down, norm_gains[1], norm_shifts[1])

def encode(params, tokens, lengths):
    groups_all, length, model_width = tokens.shape
    block_count = groups_all // GRP_DEV
    block_tokens = tokens.reshape(block_count, GRP_DEV, length, model_width)
    block_lengths = lengths.reshape(block_count, GRP_DEV)
    block_step = jax.checkpoint(partial(encode_block, params))

    def run_block(block_pair):
        return block_step(block_pair[0], block_pair[1])
    encoded = lax.map(run_block, (block_tokens, block_lengths))
    return encoded.reshape(groups_all, length, model_width)

def reference(question_tokens, passage_tokens, question_cotangent, passage_cotangent, question_lengths, passage_lengths, dataset_ids, positives, attn_in, attn_in_bias, attn_out, ffn_in, ffn_in_bias, ffn_out, out_biases, norm_gains, norm_shifts):
    weights = tuple((weight_arr.astype(jnp.float32) for weight_arr in (attn_in, attn_in_bias, attn_out, ffn_in, ffn_in_bias, ffn_out, out_biases, norm_gains, norm_shifts)))

    def objective(weight_set, question_float, passage_float):
        question_params = tuple((weight_arr[0] for weight_arr in weight_set))
        passage_params = tuple((weight_arr[1] for weight_arr in weight_set))
        question_outputs = encode(question_params, question_float, question_lengths)
        passage_outputs = encode(passage_params, passage_float, passage_lengths)
        question_heads = low(question_outputs[:, 0])
        passage_heads = low(passage_outputs[:, 0])
        class_scores = jnp.einsum('gd,jd->gj', question_heads, passage_heads, precision=HIGHEST) * (score_gain * D ** (-0.5))
        columns = jnp.arange(class_scores.shape[1], dtype=jnp.int32)
        chosen = positives[:, None] == columns[None, :]
        own_set = lax.optimization_barrier(jnp.sum(jnp.where(chosen, dataset_ids[None, :], 0), axis=1))
        allowed = dataset_ids[None, :] == own_set[:, None]
        logits = jnp.where(allowed, class_scores, NEGATIVE)
        cross = jax.nn.logsumexp(logits, axis=1) - lax.optimization_barrier(jnp.sum(jnp.where(chosen, class_scores, 0.0), axis=1))
        return (question_outputs, passage_outputs, jnp.sum(cross))
    primal, pull = jax.vjp(objective, weights, question_tokens.astype(jnp.float32), passage_tokens.astype(jnp.float32))
    question_outputs, passage_outputs, total = primal
    weight_grads, question_grad, passage_grad = pull((question_cotangent.astype(jnp.float32), passage_cotangent.astype(jnp.float32), jnp.ones((), total.dtype)))
    contrastive_loss = total / GROUPS
    return (question_outputs.astype(jnp.bfloat16), passage_outputs.astype(jnp.bfloat16), contrastive_loss, question_grad.astype(jnp.bfloat16), passage_grad.astype(jnp.bfloat16), weight_grads[0], weight_grads[1], weight_grads[2], weight_grads[3], weight_grads[4], weight_grads[5], weight_grads[6], weight_grads[7], weight_grads[8])
```

```python
from functools import partial

import jax
import jax.numpy as jnp
from jax import lax
from jax.experimental import pallas as pl
from jax.experimental.pallas import tpu as pltpu
from jax.sharding import PartitionSpec as P

D = 768
HD = 64


EPSILON = 1e-06
NEGATIVE = -1e30
HIGHEST = lax.Precision.HIGHEST
score_gain = 3.0


def norm_forward(summed, scale_row, shift_row):
    row_mean = jnp.mean(summed, axis=-1, keepdims=True)
    centred = summed - row_mean
    inv_std = lax.rsqrt(jnp.mean(centred * centred, axis=-1, keepdims=True) + EPSILON)
    normed = centred * inv_std
    return (normed * scale_row + shift_row, normed, inv_std)


def norm_backward(incoming, normed, inv_std, scale_row):
    scaled = incoming * scale_row
    outgoing = inv_std * (
        scaled
        - jnp.mean(scaled, axis=-1, keepdims=True)
        - normed * jnp.mean(scaled * normed, axis=-1, keepdims=True)
    )
    return (outgoing, jnp.sum(incoming * normed, axis=(0, 1)), jnp.sum(incoming, axis=(0, 1)))


def key_visible(lengths, length):
    positions = jnp.arange(length, dtype=jnp.int32)
    return (positions[None, :] < lengths[:, None])[:, None, None, :]


def head_scores(queries, key_rows, visible):
    raw_scores = jnp.einsum(
        "bqhe,bkhe->bhqk", queries, key_rows, preferred_element_type=jnp.float32
    ) * HD ** (-0.5)
    return jnp.where(visible, raw_scores, NEGATIVE)


def split_heads(matrix):
    return matrix.reshape(matrix.shape[0], matrix.shape[1], matrix.shape[2] // HD, HD)


def join_heads(per_head):
    return per_head.reshape(
        per_head.shape[0], per_head.shape[1], per_head.shape[2] * per_head.shape[3]
    )


def encoder_forward(tokens, lengths, params):
    (
        attn_in,
        attn_in_bias,
        attn_out,
        ffn_in,
        ffn_in_bias,
        ffn_out,
        out_biases,
        norm_gains,
        norm_shifts,
    ) = params
    projected = jnp.einsum("bld,dce->blce", tokens, attn_in, preferred_element_type=jnp.float32)
    in_bias = attn_in_bias.astype(jnp.float32)
    queries = split_heads((projected[:, :, 0] + in_bias[0]).astype(jnp.bfloat16))
    key_rows = split_heads(projected[:, :, 1].astype(jnp.bfloat16))
    values = split_heads((projected[:, :, 2] + in_bias[1]).astype(jnp.bfloat16))
    visible = key_visible(lengths, tokens.shape[1])
    scores = head_scores(queries, key_rows, visible)
    row_top = jnp.max(scores, axis=-1, keepdims=True)
    log_total = row_top + jnp.log(jnp.sum(jnp.exp(scores - row_top), axis=-1, keepdims=True))
    attn_probs = jnp.exp(scores - log_total).astype(jnp.bfloat16)
    context = join_heads(
        jnp.einsum(
            "bhqk,bkhe->bqhe", attn_probs, values, preferred_element_type=jnp.float32
        ).astype(jnp.bfloat16)
    )
    attn_part = jnp.einsum("ble,ed->bld", context, attn_out, preferred_element_type=jnp.float32)
    attn_sum = lax.psum(attn_part.astype(jnp.bfloat16), "tensor").astype(jnp.float32)
    bias_rows = out_biases.astype(jnp.float32)
    gain_rows = norm_gains.astype(jnp.float32)
    shift_rows = norm_shifts.astype(jnp.float32)
    hidden_float, normed_first, inv_first = norm_forward(
        tokens.astype(jnp.float32) + attn_sum + bias_rows[0], gain_rows[0], shift_rows[0]
    )
    hidden = hidden_float.astype(jnp.bfloat16)
    up_pre = jnp.einsum(
        "bld,df->blf", hidden, ffn_in, preferred_element_type=jnp.float32
    ) + ffn_in_bias.astype(jnp.float32)
    activated = jax.nn.gelu(up_pre, approximate=False).astype(jnp.bfloat16)
    down_part = jnp.einsum("blf,fd->bld", activated, ffn_out, preferred_element_type=jnp.float32)
    down_sum = lax.psum(down_part.astype(jnp.bfloat16), "tensor").astype(jnp.float32)
    outputs, normed_second, inv_second = norm_forward(
        hidden.astype(jnp.float32) + down_sum + bias_rows[1], gain_rows[1], shift_rows[1]
    )
    saved = (
        tokens,
        queries,
        key_rows,
        values,
        log_total,
        context,
        normed_first,
        inv_first,
        hidden,
        up_pre,
        activated,
        normed_second,
        inv_second,
    )
    return (outputs, saved)


def encoder_backward(incoming, saved, lengths, params):
    (
        attn_in,
        attn_in_bias,
        attn_out,
        ffn_in,
        ffn_in_bias,
        ffn_out,
        out_biases,
        norm_gains,
        norm_shifts,
    ) = params
    (
        tokens,
        queries,
        key_rows,
        values,
        log_total,
        context,
        normed_first,
        inv_first,
        hidden,
        up_pre,
        activated,
        normed_second,
        inv_second,
    ) = saved
    groups_here, length, model_width = tokens.shape
    gain_rows = norm_gains.astype(jnp.float32)
    d_second, gain_second, shift_second = norm_backward(
        incoming, normed_second, inv_second, gain_rows[1]
    )
    d_down = d_second.astype(jnp.bfloat16)
    grad_ffn_out = jnp.einsum("blf,bld->fd", activated, d_down, preferred_element_type=jnp.float32)
    d_activated = jnp.einsum("bld,fd->blf", d_down, ffn_out, preferred_element_type=jnp.float32)
    gelu_pull = jax.vjp(partial(jax.nn.gelu, approximate=False), up_pre)[1]
    d_up = gelu_pull(d_activated)[0].astype(jnp.bfloat16)
    grad_ffn_in = jnp.einsum("bld,blf->df", hidden, d_up, preferred_element_type=jnp.float32)
    hidden_part = jnp.einsum("blf,df->bld", d_up, ffn_in, preferred_element_type=jnp.float32)
    d_hidden = d_second + lax.psum(hidden_part.astype(jnp.bfloat16), "tensor").astype(jnp.float32)
    d_first, gain_first, shift_first = norm_backward(
        d_hidden, normed_first, inv_first, gain_rows[0]
    )
    d_attn = d_first.astype(jnp.bfloat16)
    grad_attn_out = jnp.einsum("ble,bld->ed", context, d_attn, preferred_element_type=jnp.float32)
    d_context = split_heads(
        jnp.einsum("bld,ed->ble", d_attn, attn_out, preferred_element_type=jnp.float32).astype(
            jnp.bfloat16
        )
    )
    visible = key_visible(lengths, length)
    scores = head_scores(queries, key_rows, visible)
    probs_float = jnp.exp(scores - log_total)
    d_probs = jnp.einsum("bqhe,bkhe->bhqk", d_context, values, preferred_element_type=jnp.float32)
    d_values = jnp.einsum(
        "bhqk,bqhe->bkhe",
        probs_float.astype(jnp.bfloat16),
        d_context,
        preferred_element_type=jnp.float32,
    ).astype(jnp.bfloat16)
    d_scores = (
        probs_float * (d_probs - jnp.sum(probs_float * d_probs, axis=-1, keepdims=True))
    ).astype(jnp.bfloat16)
    d_queries = (
        jnp.einsum("bhqk,bkhe->bqhe", d_scores, key_rows, preferred_element_type=jnp.float32)
        * HD ** (-0.5)
    ).astype(jnp.bfloat16)
    d_keys = (
        jnp.einsum("bhqk,bqhe->bkhe", d_scores, queries, preferred_element_type=jnp.float32)
        * HD ** (-0.5)
    ).astype(jnp.bfloat16)
    query_grad = join_heads(d_queries)
    value_grad = join_heads(d_values)
    d_projected = jnp.stack([query_grad, join_heads(d_keys), value_grad], axis=2)
    grad_attn_in = jnp.einsum(
        "bld,blce->dce", tokens, d_projected, preferred_element_type=jnp.float32
    )
    token_part = jnp.einsum(
        "blce,dce->bld", d_projected, attn_in, preferred_element_type=jnp.float32
    )
    d_tokens = (
        d_first + lax.psum(token_part.astype(jnp.bfloat16), "tensor").astype(jnp.float32)
    ).astype(jnp.bfloat16)
    grad_in_bias = jnp.stack(
        [
            jnp.sum(query_grad.astype(jnp.float32), axis=(0, 1)),
            jnp.sum(value_grad.astype(jnp.float32), axis=(0, 1)),
        ]
    )
    grad_ffn_bias = jnp.sum(d_up.astype(jnp.float32), axis=(0, 1))
    grad_out_biases = jnp.stack(
        [
            jnp.sum(d_attn.astype(jnp.float32), axis=(0, 1)),
            jnp.sum(d_down.astype(jnp.float32), axis=(0, 1)),
        ]
    )
    grad_gains = jnp.stack([gain_first, gain_second])
    grad_shifts = jnp.stack([shift_first, shift_second])
    return (
        d_tokens,
        (
            grad_attn_in,
            grad_in_bias,
            grad_attn_out,
            grad_ffn_in,
            grad_ffn_bias,
            grad_ffn_out,
            grad_out_biases,
            grad_gains,
            grad_shifts,
        ),
    )


def contrastive(question_rows, passage_rows, own_positive, dataset_ids):
    class_scores = jnp.einsum(
        "gd,jd->gj", question_rows, passage_rows, preferred_element_type=jnp.float32
    ) * (score_gain * D ** (-0.5))
    columns = jnp.arange(passage_rows.shape[0], dtype=jnp.int32)
    chosen = own_positive[:, None] == columns[None, :]
    own_set = jnp.sum(jnp.where(chosen, dataset_ids[None, :], 0), axis=1)
    logits = jnp.where(dataset_ids[None, :] == own_set[:, None], class_scores, NEGATIVE)
    row_top = jnp.max(logits, axis=1, keepdims=True)
    log_total = row_top + jnp.log(jnp.sum(jnp.exp(logits - row_top), axis=1, keepdims=True))
    target = jnp.sum(jnp.where(chosen, class_scores, 0.0), axis=1)
    d_class = (jnp.exp(logits - log_total) - chosen.astype(jnp.float32)) * (
        score_gain * D ** (-0.5)
    )
    return (log_total[:, 0] - target, d_class)


def per_device(
    question_tokens,
    passage_tokens,
    question_cotangent,
    passage_cotangent,
    question_lengths,
    passage_lengths,
    dataset_ids,
    positives,
    attn_in,
    attn_in_bias,
    attn_out,
    ffn_in,
    ffn_in_bias,
    ffn_out,
    out_biases,
    norm_gains,
    norm_shifts,
):

    def encoder_params(encoder):
        return (
            attn_in[encoder],
            attn_in_bias[encoder],
            attn_out[encoder],
            ffn_in[encoder],
            ffn_in_bias[encoder],
            ffn_out[encoder],
            out_biases[encoder],
            norm_gains[encoder],
            norm_shifts[encoder],
        )

    question_params = encoder_params(0)
    passage_params = encoder_params(1)
    question_float, question_saved = encoder_forward(
        question_tokens, question_lengths, question_params
    )
    passage_float, passage_saved = encoder_forward(passage_tokens, passage_lengths, passage_params)
    question_heads = question_float[:, 0].astype(jnp.bfloat16)
    passage_heads = passage_float[:, 0].astype(jnp.bfloat16)
    local_groups = question_heads.shape[0]
    own_start = lax.axis_index("dp") * local_groups
    all_passages = lax.all_gather(passage_heads, "dp", axis=0, tiled=True)
    own_positive = lax.dynamic_slice_in_dim(positives, own_start, local_groups)
    cross, d_class = contrastive(question_heads, all_passages, own_positive, dataset_ids)
    total = lax.psum(jnp.sum(cross), "dp")
    contrastive_loss = total / all_passages.shape[0]
    d_question_heads = jnp.einsum(
        "gj,jd->gd", d_class, all_passages.astype(jnp.float32), precision=HIGHEST
    )
    question_heads_float = question_heads.astype(jnp.float32)
    d_passage_heads = lax.psum_scatter(
        jnp.einsum("gj,gd->jd", d_class, question_heads_float, precision=HIGHEST),
        "dp",
        scatter_dimension=0,
        tiled=True,
    )
    d_question_out = question_cotangent.astype(jnp.float32).at[:, 0].add(d_question_heads)
    d_passage_out = passage_cotangent.astype(jnp.float32).at[:, 0].add(d_passage_heads)
    passage_grad, passage_weights = encoder_backward(
        d_passage_out, passage_saved, passage_lengths, passage_params
    )
    question_grad, question_weights = encoder_backward(
        d_question_out, question_saved, question_lengths, question_params
    )
    joined = (
        lax.psum_scatter(question_weights[0], "dp", scatter_dimension=0, tiled=True),
        lax.psum_scatter(question_weights[1], "dp", scatter_dimension=1, tiled=True),
        lax.psum_scatter(question_weights[2], "dp", scatter_dimension=1, tiled=True),
        lax.psum_scatter(question_weights[3], "dp", scatter_dimension=0, tiled=True),
        lax.psum_scatter(question_weights[4], "dp", scatter_dimension=0, tiled=True),
        lax.psum_scatter(question_weights[5], "dp", scatter_dimension=1, tiled=True),
        lax.psum_scatter(question_weights[6], "dp", scatter_dimension=1, tiled=True),
        lax.psum_scatter(question_weights[7], "dp", scatter_dimension=1, tiled=True),
        lax.psum_scatter(question_weights[8], "dp", scatter_dimension=1, tiled=True),
        lax.psum_scatter(passage_weights[0], "dp", scatter_dimension=0, tiled=True),
        lax.psum_scatter(passage_weights[1], "dp", scatter_dimension=1, tiled=True),
        lax.psum_scatter(passage_weights[2], "dp", scatter_dimension=1, tiled=True),
        lax.psum_scatter(passage_weights[3], "dp", scatter_dimension=0, tiled=True),
        lax.psum_scatter(passage_weights[4], "dp", scatter_dimension=0, tiled=True),
        lax.psum_scatter(passage_weights[5], "dp", scatter_dimension=1, tiled=True),
        lax.psum_scatter(passage_weights[6], "dp", scatter_dimension=1, tiled=True),
        lax.psum_scatter(passage_weights[7], "dp", scatter_dimension=1, tiled=True),
        lax.psum_scatter(passage_weights[8], "dp", scatter_dimension=1, tiled=True),
    )
    question_parts = joined[:9]
    passage_parts = joined[9:]
    stacked = [
        jnp.stack([question_piece, passage_piece])
        for question_piece, passage_piece in zip(question_parts, passage_parts)
    ]
    return (
        question_float.astype(jnp.bfloat16),
        passage_float.astype(jnp.bfloat16),
        contrastive_loss,
        question_grad,
        passage_grad,
        stacked[0],
        stacked[1],
        stacked[2],
        stacked[3],
        stacked[4],
        stacked[5],
        stacked[6],
        stacked[7],
        stacked[8],
    )


MESH_ID = pl.DeviceIdType.MESH
F32 = jnp.float32
BF16 = jnp.bfloat16
ZN = 4
ROWS_OUT = 48
JOBS = 12
COLS = 384
D1, DZ, D3, DS = 8, 4, 2, 2
TOKS = (128, 512)
BLK = (128, 256)
SMALL = 24


def dot(a, b):
    return jnp.dot(a, b, preferred_element_type=F32)


def dot_t(a, b):
    return lax.dot_general(a, b, (((1,), (1,)), ((), ())), preferred_element_type=F32)


def t_dot(a, b):
    return lax.dot_general(a, b, (((0,), (0,)), ((), ())), preferred_element_type=F32)


def gelu_and_slope(u):
    size = jnp.abs(u)
    bell = jnp.exp(-0.5 * u * u)
    t = 1.0 / (1.0 + (0.3275911 * 0.7071067811865476) * size)
    poly = t * (
        0.127414796
        + t * (-0.142248368 + t * (0.7107068705 + t * (-0.7265760135 + t * 0.5307027145)))
    )
    tail = poly * bell
    phi = jnp.where(u >= 0.0, 1.0 - tail, tail)
    return u * phi, phi + u * bell * 0.3989422804014327


def row_mean(v):
    return jnp.sum(v, axis=-1, keepdims=True) * (1.0 / D)


def fold8(v):
    return jnp.sum(v.reshape(v.shape[0] // 8, 8, v.shape[1]), axis=0)


def rows_at(start, size, step=16):
    return pl.ds(pl.multiple_of(start, step), size)


def fused_kernel(
    xq_in, xp_in, cq_in, cp_in, qlen, plen, dsid, posi,
    win_in, bin_in, wo_in, wf_in, bfi_in, wd_in, bo_in, gain_in, shift_in,
    oq_out, op_out, loss_out, gq_out, gp_out, g_in, g_out, g_fi, g_fo, sm_out,
    win, wo, wf, wd, xq, xp, cq, cp, qkvq, qkvp, prq, prp, hq, hp, n1q, n1p, n2q, n2p,
    i1q, i1p, i2q, i2p, sq, sp, obq, obp, ddq, ddp, dcq, dcp, ballq, ballp, atq, atp,
    exsq, exsp, exrq, exrp, par, pin, pfi, masks, hg, hf, dh, acc_s, acc_b, acc_f, smb, smr,
    p1s, p1r, zr, zl, p3r,
    in_sem, out_sem, exs_sem, exr_sem, hgs_sem, hgr_sem, sms_sem, smr_sem,
    p1s_sem, p1r_sem, zrs_sem, zrr_sem, zls_sem, zlr_sem, p3s_sem, p3r_sem,
    *, last,
):
    me = lax.axis_index("dp")
    core = lax.axis_index("tensor")
    z, y, x = me // 4, (me // 2) % 2, me % 2
    partner = {"dp": me, "tensor": 1 - core}
    at_x = {"dp": me + 1 - 2 * x, "tensor": core}
    at_y = {"dp": me + 2 - 4 * y, "tensor": core}

    def at_dp(index):
        return {"dp": index, "tensor": core}

    X, COT, QKV, PR, HID = (xq, xp), (cq, cp), (qkvq, qkvp), (prq, prp), (hq, hp)
    N1, N2, I1, I2, SLOPE = (n1q, n1p), (n2q, n2p), (i1q, i1p), (i2q, i2p), (sq, sp)
    OB, DD, DC, BALL, AT = (obq, obp), (ddq, ddp), (dcq, dcp), (ballq, ballp), (atq, atp)
    EXS, EXR = (exsq, exsp), (exrq, exrp)

    loads = [
        (xq_in, xq),
        *[(win_in.at[0, j], win.at[0, :, pl.ds(j * COLS, COLS)]) for j in range(3)],
        (xp_in, xp),
        *[(win_in.at[1, j], win.at[1, :, pl.ds(j * COLS, COLS)]) for j in range(3)],
        (wo_in.at[0], wo.at[0]),
        (wo_in.at[1], wo.at[1]),
        (wf_in.at[0], wf.at[0]),
        (wf_in.at[1], wf.at[1]),
        (wd_in.at[0], wd.at[0]),
        (wd_in.at[1], wd.at[1]),
        (cq_in, cq),
        (cp_in, cp),
    ]
    loads = [pltpu.make_async_copy(s, d, in_sem.at[i]) for i, (s, d) in enumerate(loads)]
    for copy in loads:
        copy.start()
    ready = set()

    def need(*which):
        for i in which:
            if i not in ready:
                loads[i].wait()
                ready.add(i)

    barrier = pltpu.get_barrier_semaphore()
    pl.semaphore_signal(barrier, inc=1, device_id=partner, device_id_type=MESH_ID)
    for k in range(1, 16):
        pl.semaphore_signal(barrier, inc=1, device_id=at_dp(me ^ k), device_id_type=MESH_ID)

    for e in range(2):
        for i in range(2):
            par[e * 8 + i : e * 8 + i + 1, :] = bo_in[e].astype(F32)[i : i + 1]
            par[e * 8 + 2 + i : e * 8 + 3 + i, :] = gain_in[e].astype(F32)[i : i + 1]
            par[e * 8 + 4 + i : e * 8 + 5 + i, :] = shift_in[e].astype(F32)[i : i + 1]
            pin[e * 2 + i : e * 2 + i + 1, :] = bin_in[e].astype(F32)[i : i + 1]
        pfi[e : e + 1, :] = bfi_in[...].astype(F32)[e : e + 1]
    acc_s[...] = jnp.zeros_like(acc_s)
    acc_b[...] = jnp.zeros_like(acc_b)
    acc_f[...] = jnp.zeros_like(acc_f)

    r32 = lax.broadcasted_iota(jnp.int32, (32, 32), 0)
    c32 = lax.broadcasted_iota(jnp.int32, (32, 32), 1)
    own_pos = jnp.zeros((32, 32), F32)
    set_col = jnp.zeros((32, 32), F32)
    for g in range(32):
        at = (g % 2) * 16 + g // 2
        own_pos = jnp.where(r32 == at, posi[g].astype(F32), own_pos)
        set_col = jnp.where(c32 == at, dsid[g].astype(F32), set_col)
    col_group = ((c32 % 16) * 2 + c32 // 16).astype(F32)
    chosen = jnp.where(own_pos == col_group, 1.0, 0.0)
    own_set = jnp.sum(chosen * set_col, axis=1, keepdims=True)
    masks[0:32, :] = chosen
    masks[32:64, :] = jnp.where(set_col == own_set, 1.0, 0.0)

    lane_lo = lax.broadcasted_iota(jnp.int32, (1, 128), 1) < HD

    def side(v, hh):
        return jnp.where(lane_lo if hh == 0 else jnp.logical_not(lane_lo), v, jnp.zeros_like(v))

    def exchange(e, b, parity):
        slot = 0 if e == 0 else 1 + b
        rows = rows_at(b * BLK[e], BLK[e]) if not isinstance(b, int) else pl.ds(b * BLK[e], BLK[e])
        return pltpu.make_async_remote_copy(
            src_ref=EXS[e].at[rows],
            dst_ref=EXR[e].at[parity, rows],
            send_sem=exs_sem.at[slot],
            recv_sem=exr_sem.at[parity, slot],
            device_id=partner,
            device_id_type=MESH_ID,
        )

    def block_rows(e, b):
        if e == 0:
            return pl.ds(0, BLK[0])
        return rows_at(b * BLK[1], BLK[1], BLK[1])

    def blocks(e, body):
        if e == 0:
            body(0)
        else:
            pl.loop(0, 2)(body)

    def attend(e, b):
        size = BLK[e]
        rows = block_rows(e, b)
        xb = X[e][rows, :]
        for j in range(3):
            cols = pl.ds(j * COLS, COLS)
            got = dot(xb, win[e, :, cols])
            if j == 0:
                got = (got + pin[e * 2 : e * 2 + 1, :]).astype(BF16) * jnp.asarray(HD**-0.5, BF16)
            elif j == 2:
                got = got + pin[e * 2 + 1 : e * 2 + 2, :]
            QKV[e][rows, cols] = got.astype(BF16)

        col = lax.broadcasted_iota(jnp.int32, (size, size), 1)
        if e == 0:
            row = lax.broadcasted_iota(jnp.int32, (size, size), 0)
            first = jnp.logical_and(row < 64, col < qlen[0])
            second = jnp.logical_and(
                row >= 64, jnp.logical_and(col >= 64, col < 64 + qlen[1])
            )
            seen = jnp.logical_or(first, second)
        else:
            seen = col < plen[b]

        @pl.loop(0, 3)
        def _(pair):
            q2 = QKV[e][rows, rows_at(pair * 128, 128, 128)]
            k2 = QKV[e][rows, rows_at(COLS + pair * 128, 128, 128)]
            v2 = QKV[e][rows, rows_at(2 * COLS + pair * 128, 128, 128)]
            total = jnp.zeros((size, 128), F32)
            for hh in range(2):
                s = dot_t(side(q2, hh), k2)
                s = jnp.where(seen, s, NEGATIVE)
                p = jnp.exp(s - jnp.max(s, axis=-1, keepdims=True))
                p = (p * (1.0 / jnp.sum(p, axis=-1, keepdims=True))).astype(BF16)
                PR[e][b, pair * 2 + hh] = p
                total = total + dot(p, side(v2, hh))
            BALL[e][rows, rows_at(8 * COLS + pair * 128, 128, 128)] = total.astype(BF16)

        ctx = BALL[e][rows, pl.ds(8 * COLS, COLS)]
        EXS[e][rows, :] = dot(ctx, wo[e]).astype(BF16)
        exchange(e, b, 0).start()

    CH = 32

    def first_norm(e, b):
        exchange(e, b, 0).wait()

        @pl.loop(0, BLK[e] // CH)
        def _(c):
            rows = rows_at(b * BLK[e] + c * CH, CH, CH)
            v = (
                X[e][rows, :].astype(F32)
                + (EXS[e][rows, :].astype(F32) + EXR[e][0, rows, :].astype(F32))
                + par[e * 8 : e * 8 + 1, :]
            )
            v = v - row_mean(v)
            inv = lax.rsqrt(row_mean(v * v) + EPSILON)
            n = v * inv
            N1[e][rows, :] = n
            I1[e][rows, :] = inv
            HID[e][rows, :] = (
                n * par[e * 8 + 2 : e * 8 + 3, :] + par[e * 8 + 4 : e * 8 + 5, :]
            ).astype(BF16)

    def feed(e, b):
        rows = block_rows(e, b)

        @pl.loop(0, 6)
        def _(n):
            cols = rows_at(n * 256, 256, 256)
            u = dot(HID[e][rows, :], wf[e, :, cols]) + pfi[e : e + 1, cols]
            a, slope = gelu_and_slope(u)
            BALL[e][rows, cols] = a.astype(BF16)
            SLOPE[e][rows, cols] = slope.astype(BF16)

        @pl.loop(0, 3)
        def _(n):
            cols = rows_at(n * 256, 256, 256)
            EXS[e][rows, cols] = dot(BALL[e][rows, pl.ds(0, FF_HERE)], wd[e, :, cols]).astype(BF16)

        exchange(e, b, 1).start()

    def second_norm(e, b):
        exchange(e, b, 1).wait()

        @pl.loop(0, BLK[e] // CH)
        def _(c):
            rows = rows_at(b * BLK[e] + c * CH, CH, CH)
            v = (
                HID[e][rows, :].astype(F32)
                + (EXS[e][rows, :].astype(F32) + EXR[e][1, rows, :].astype(F32))
                + par[e * 8 + 1 : e * 8 + 2, :]
            )
            v = v - row_mean(v)
            inv = lax.rsqrt(row_mean(v * v) + EPSILON)
            n = v * inv
            N2[e][rows, :] = n
            I2[e][rows, :] = inv
            OB[e][rows, :] = (
                n * par[e * 8 + 3 : e * 8 + 4, :] + par[e * 8 + 5 : e * 8 + 6, :]
            ).astype(BF16)

    need(0, 1, 2, 3, 8)
    pl.semaphore_wait(barrier, 16)
    attend(0, 0)
    need(4, 5, 6, 7, 9)
    blocks(1, lambda b: attend(1, b))
    first_norm(0, 0)
    need(10, 12)
    feed(0, 0)
    need(11, 13)

    def passage_mid(b):
        first_norm(1, b)
        feed(1, b)

    blocks(1, passage_mid)
    second_norm(0, 0)
    blocks(1, lambda b: second_norm(1, b))
    out_q = pltpu.make_async_copy(obq, oq_out, out_sem.at[0])
    out_p = pltpu.make_async_copy(obp, op_out, out_sem.at[1])
    out_q.start()
    out_p.start()

    pieces = []
    for ref, at in ((obq, 0), (obq, 64), (obp, 0), (obp, 256)):
        head = ref[at : at + 16, :].astype(F32)[0:1]
        pieces += [head[:, k * 256 : (k + 1) * 256] for k in range(3)]
    pieces.append(jnp.zeros((4, 256), F32))
    hg[me] = jnp.concatenate(pieces, axis=0).astype(BF16)

    def heads(k):
        return pltpu.make_async_remote_copy(
            src_ref=hg.at[me],
            dst_ref=hg.at[me],
            send_sem=hgs_sem.at[k],
            recv_sem=hgr_sem.at[k],
            device_id=at_dp(me ^ k),
            device_id_type=MESH_ID,
        )

    for k in range(1, 16):
        heads(k).start()
    need(14, 15)
    for k in range(1, 16):
        copy = pltpu.make_async_remote_copy(
            src_ref=hg.at[me],
            dst_ref=hg.at[me ^ k],
            send_sem=hgs_sem.at[k],
            recv_sem=hgr_sem.at[k],
            device_id=at_dp(me ^ k),
            device_id_type=MESH_ID,
        )
        copy.wait()
    gathered = hg[...].astype(F32).reshape(256, 256)
    hf[0] = gathered[:, 0:128]
    hf[1] = gathered[:, 128:256]

    def all_heads(first):
        groups = []
        for i in range(2):
            parts = [
                hf[c, pl.ds(first + i * 3 + k, 16, stride=16), :] for k in range(3) for c in range(2)
            ]
            groups.append(jnp.concatenate(parts, axis=1))
        return jnp.concatenate(groups, axis=0)

    heads_q, heads_p = all_heads(0), all_heads(6)
    gain = score_gain * D ** (-0.5)
    class_scores = dot_t(heads_q.astype(BF16), heads_p.astype(BF16)) * gain
    chosen = masks[0:32, :]
    logits = jnp.where(masks[32:64, :] > 0.5, class_scores, NEGATIVE)
    top = jnp.max(logits, axis=1, keepdims=True)
    log_total = top + jnp.log(jnp.sum(jnp.exp(logits - top), axis=1, keepdims=True))
    target = jnp.sum(chosen * class_scores, axis=1, keepdims=True)
    loss = jnp.sum(log_total - target, axis=0, keepdims=True) * (1.0 / 32)
    loss_out[...] = jnp.broadcast_to(loss, loss_out.shape)
    d_class = (jnp.exp(logits - log_total) - chosen) * gain
    dh[0:32, :] = lax.dot_general(
        d_class, heads_p, (((1,), (0,)), ((), ())), precision=HIGHEST, preferred_element_type=F32
    )
    dh[32:64, :] = lax.dot_general(
        d_class, heads_q, (((0,), (0,)), ((), ())), precision=HIGHEST, preferred_element_type=F32
    )

    def norm_back(incoming, n, inv, scale):
        scaled = incoming * scale
        return inv * (scaled - row_mean(scaled) - n * row_mean(scaled * n))

    def transpose_into(e, k, src, b, width=D):
        rows = block_rows(e, b)

        @pl.loop(0, width // 256)
        def _(c):
            tile = src[rows, rows_at(c * 256, 256, 256)]
            AT[e][rows_at(k * D + c * 256, 256, 256), rows] = tile.T

    def second_back(e, b):
        row0 = lax.broadcasted_iota(jnp.int32, (CH, 1), 0)
        seqs = 2 if e == 0 else 1
        length = 64 if e == 0 else 256
        for i in range(seqs):
            group = i if e == 0 else b
            extra = dh[pl.ds(e * 32 + group * 16 + me, 1), :]

            @pl.loop(0, length // CH)
            def _(c):
                rows = rows_at(group * length + c * CH, CH, CH)
                add = jnp.where(row0 + c * CH == 0, extra, 0.0)
                d = COT[e][rows, :].astype(F32) + add
                n = N2[e][rows, :]
                out = norm_back(d, n, I2[e][rows, :], par[e * 8 + 3 : e * 8 + 4, :])
                N2[e][rows, :] = out
                low = out.astype(BF16)
                DD[e][rows, :] = low
                acc_s[e * 6 + 1] += fold8(d * n)
                acc_s[e * 6 + 3] += fold8(d)
                acc_s[e * 6 + 5] += fold8(low.astype(F32))

        transpose_into(e, 0, DD[e], b)

    def feed_back(e, b):
        rows = block_rows(e, b)

        @pl.loop(0, 6)
        def _(n):
            cols = rows_at(n * 256, 256, 256)
            d = dot_t(DD[e][rows, :], wd[e, cols, :]) * SLOPE[e][rows, cols].astype(F32)
            d = d.astype(BF16)
            BALL[e][rows, rows_at(4 * COLS + n * 256, 256, 256)] = d
            acc_f[e, :, cols] += fold8(d.astype(F32))

        @pl.loop(0, 3)
        def _(n):
            cols = rows_at(n * 256, 256, 256)
            EXS[e][rows, cols] = dot_t(BALL[e][rows, pl.ds(4 * COLS, FF_HERE)], wf[e, cols, :]).astype(BF16)

        exchange(e, b, 0).start()
        transpose_into(e, 1, HID[e], b)

    def first_back(e, b):
        exchange(e, b, 0).wait()

        @pl.loop(0, BLK[e] // CH)
        def _(c):
            rows = rows_at(b * BLK[e] + c * CH, CH, CH)
            d = N2[e][rows, :] + (EXS[e][rows, :].astype(F32) + EXR[e][0, rows, :].astype(F32))
            n = N1[e][rows, :]
            out = norm_back(d, n, I1[e][rows, :], par[e * 8 + 2 : e * 8 + 3, :])
            N1[e][rows, :] = out
            low = out.astype(BF16)
            DD[e][rows, :] = low
            acc_s[e * 6 + 0] += fold8(d * n)
            acc_s[e * 6 + 2] += fold8(d)
            acc_s[e * 6 + 4] += fold8(low.astype(F32))

        transpose_into(e, 2, DD[e], b)

    def attend_back(e, b):
        rows = block_rows(e, b)
        size = BLK[e]
        DC[e][rows, :] = dot_t(DD[e][rows, :], wo[e]).astype(BF16)

        @pl.loop(0, 3)
        def _(pair):
            q2 = QKV[e][rows, rows_at(pair * 128, 128, 128)]
            k2 = QKV[e][rows, rows_at(COLS + pair * 128, 128, 128)]
            v2 = QKV[e][rows, rows_at(2 * COLS + pair * 128, 128, 128)]
            dc2 = DC[e][rows, rows_at(pair * 128, 128, 128)]
            dq = jnp.zeros((size, 128), F32)
            dk = jnp.zeros((size, 128), F32)
            dv = jnp.zeros((size, 128), F32)
            for hh in range(2):
                low = PR[e][b, pair * 2 + hh]
                p = low.astype(F32)
                dch = side(dc2, hh)
                dp = dot_t(dch, v2)
                ds = (p * (dp - jnp.sum(p * dp, axis=-1, keepdims=True))).astype(BF16)
                dv = dv + t_dot(low, dch)
                dq = dq + dot(ds, side(k2, hh))
                dk = dk + t_dot(ds, side(q2, hh))
            dq = (dq * HD**-0.5).astype(BF16)
            dv = dv.astype(BF16)
            cols = rows_at(pair * 128, 128, 128)
            BALL[e][rows, rows_at(9 * COLS + pair * 128, 128, 128)] = dq
            BALL[e][rows, rows_at(10 * COLS + pair * 128, 128, 128)] = dk.astype(BF16)
            BALL[e][rows, rows_at(11 * COLS + pair * 128, 128, 128)] = dv
            acc_b[e, :, cols] += fold8(dq.astype(F32))
            acc_b[e, :, rows_at(COLS + pair * 128, 128, 128)] += fold8(dv.astype(F32))

        transpose_into(e, 3, X[e], b)

    def token_back(e, b):
        rows = block_rows(e, b)

        @pl.loop(0, 3)
        def _(n):
            cols = rows_at(n * 256, 256, 256)
            EXS[e][rows, cols] = dot_t(BALL[e][rows, pl.ds(9 * COLS, 3 * COLS)], win[e, cols, :]).astype(BF16)

        exchange(e, b, 1).start()

    def token_end(e, b):
        exchange(e, b, 1).wait()

        @pl.loop(0, BLK[e] // CH)
        def _(c):
            rows = rows_at(b * BLK[e] + c * CH, CH, CH)
            OB[e][rows, :] = (
                N1[e][rows, :] + (EXS[e][rows, :].astype(F32) + EXR[e][1, rows, :].astype(F32))
            ).astype(BF16)

    def job_of(j):
        return (j // 2) % 2, (j // 4) * 2 + j % 2

    def product(e, half, blk, sel):
        a = jnp.where(blk < 8, blk // 4, jnp.where(blk == 8, 2, 3)) * D
        if half == 0:
            rows = [AT[e][rows_at(a + i * 96 + sel * 48, 48), :] for i in range(8)]
        else:
            rows = [AT[e][rows_at(a + i * 192 + sel * 96, 96), :] for i in range(4)]
        return dot(jnp.concatenate(rows, axis=0), BALL[e][:, rows_at(blk * COLS, COLS, 128)])

    first_dev, other_dev = (at_x, at_y), (at_y, at_x)
    first_at, other_at = (x, y), (y, x)

    def p1(j, half):
        return pltpu.make_async_remote_copy(
            src_ref=p1s.at[j % DS, half],
            dst_ref=p1r.at[j % D1, half],
            send_sem=p1s_sem.at[j % DS, half],
            recv_sem=p1r_sem.at[j % D1, half],
            device_id=first_dev[half],
            device_id_type=MESH_ID,
        )

    def along(j, half, d, right, relay):
        buf, send, recv = (zr, zrs_sem, zrr_sem) if right else (zl, zls_sem, zlr_sem)
        src = buf.at[j % DZ, half, d] if relay else p1r.at[j % D1, half, pl.ds(d * 96, 96)]
        return pltpu.make_async_remote_copy(
            src_ref=src,
            dst_ref=buf.at[j % DZ, half, d],
            send_sem=send.at[j % DZ, half, d],
            recv_sem=recv.at[j % DZ, half, d],
            device_id=at_dp(me + 4 if right else me - 4),
            device_id_type=MESH_ID,
        )

    def p3(j, half):
        return pltpu.make_async_remote_copy(
            src_ref=p1r.at[j % D1, half, rows_at(z * 96 + (1 - other_at[half]) * 48, 48)],
            dst_ref=p3r.at[j % D3, half],
            send_sem=p3s_sem.at[j % D3, half],
            recv_sem=p3r_sem.at[j % D3, half],
            device_id=other_dev[half],
            device_id_type=MESH_ID,
        )

    def add_into(dst, rows, other):
        dst[rows, :] = (dst[rows, :].astype(F32) + other.astype(F32)).astype(BF16)

    def step0(j):
        e_of, pair = job_of(j)
        for e in range(2):

            @pl.when(e_of == e)
            def _():
                for half in range(2):
                    p1s[j % DS, half] = product(e, half, pair * 2 + half, 1 - first_at[half]).astype(BF16)
                    p1(j, half).start()

    def step1(j):
        e_of, pair = job_of(j)
        for half in range(2):
            p1(j, half).wait()
        for e in range(2):

            @pl.when(e_of == e)
            def _():
                for half in range(2):
                    own = product(e, half, pair * 2 + half, first_at[half])
                    p1r[j % D1, half] = (own + p1r[j % D1, half].astype(F32)).astype(BF16)

        @pl.when(z == 0)
        def _():
            for half in range(2):
                for d in (3, 2, 1):
                    along(j, half, d, True, False).start()

        @pl.when(z == 3)
        def _():
            for half in range(2):
                for d in (0, 1, 2):
                    along(j, half, d, False, False).start()

    def relay(j, half, d, right):
        buf = zr if right else zl
        along(j, half, d, right, True).wait_recv()
        add_into(buf.at[j % DZ, half, d], slice(None), p1r[j % D1, half, pl.ds(d * 96, 96), :])
        along(j, half, d, right, True).start()

    def step2(j):
        @pl.when(z == 1)
        def _():
            for half in range(2):
                for d in (3, 2):
                    relay(j, half, d, True)

        @pl.when(z == 2)
        def _():
            for half in range(2):
                for d in (0, 1):
                    relay(j, half, d, False)

    def step3(j):
        @pl.when(z == 2)
        def _():
            for half in range(2):
                relay(j, half, 3, True)

        @pl.when(z == 1)
        def _():
            for half in range(2):
                relay(j, half, 0, False)

    def step4(j):
        for half in range(2):
            mine = p1r.at[j % D1, half]
            rows = rows_at(z * 96, 96)

            @pl.when(z > 0)
            def _():
                along(j, half, z, True, True).wait_recv()
                add_into(mine, rows, zr[j % DZ, half, z])

            @pl.when(z < 3)
            def _():
                along(j, half, z, False, True).wait_recv()
                add_into(mine, rows, zl[j % DZ, half, z])

            p3(j, half).start()
            for d in range(4):

                @pl.when(d > z)
                def _():
                    along(j, half, d, True, True).wait_send()

                @pl.when(d < z)
                def _():
                    along(j, half, d, False, True).wait_send()

    def step5(j):
        e_of, pair = job_of(j)
        for half in range(2):
            p3(j, half).wait()
            rows = rows_at(z * 96 + other_at[half] * 48, 48)
            total = p1r[j % D1, half, rows, :].astype(F32) + p3r[j % D3, half].astype(F32)
            for e in range(2):
                for p in range(6):

                    @pl.when(jnp.logical_and(e_of == e, pair == p))
                    def _():
                        blk = p * 2 + half
                        if blk < 4:
                            g_fo[e, :, blk * COLS : (blk + 1) * COLS] = total
                        elif blk < 8:
                            g_fi[e, :, (blk - 4) * COLS : (blk - 3) * COLS] = total
                        elif blk == 8:
                            g_out[e] = total
                        else:
                            g_in[e, blk - 9] = total

    small_to = (at_x, at_y, at_dp(me ^ 4), at_dp(me ^ 8))

    def small(k):
        return pltpu.make_async_remote_copy(
            src_ref=smb.at[k],
            dst_ref=smr.at[k],
            send_sem=sms_sem.at[k],
            recv_sem=smr_sem.at[k],
            device_id=small_to[k],
            device_id_type=MESH_ID,
        )

    def small_first():
        smb[0] = jnp.zeros_like(smb[0])
        for e in range(2):
            for i in range(6):
                smb[0, e * 9 + i : e * 9 + i + 1, :] = jnp.sum(acc_s[e * 6 + i], axis=0, keepdims=True)
            smb[0, e * 9 + 6 : e * 9 + 7, :] = jnp.sum(acc_b[e], axis=0, keepdims=True)
            for i in range(2):
                smb[0, e * 9 + 7 + i : e * 9 + 8 + i, :] = jnp.sum(
                    acc_f[e, :, i * D : (i + 1) * D], axis=0, keepdims=True
                )
        small(0).start()

    def small_next(k):
        small(k).wait()
        if k < 3:
            smb[k + 1] = smb[k] + smr[k]
            small(k + 1).start()
        else:
            sm_out[...] = smb[k] + smr[k]

    def both(body):
        body(0, 0)
        blocks(1, lambda b: body(1, b))

    def all_token_end():
        both(token_end)
        pltpu.make_async_copy(obq, gq_out, out_sem.at[0]).start()
        pltpu.make_async_copy(obp, gp_out, out_sem.at[1]).start()

    def wait_out():
        pltpu.make_async_copy(obq, oq_out, out_sem.at[0]).wait()
        pltpu.make_async_copy(obp, op_out, out_sem.at[1]).wait()

    work = {
        0: [lambda: second_back(0, 0)],
        1: [lambda: blocks(1, lambda b: second_back(1, b))],
        2: [lambda: feed_back(0, 0)],
        3: [lambda: blocks(1, lambda b: feed_back(1, b)), wait_out],
        4: [lambda: first_back(0, 0)],
        5: [lambda: blocks(1, lambda b: first_back(1, b))],
        6: [lambda: attend_back(0, 0)],
        7: [lambda: blocks(1, lambda b: attend_back(1, b))],
        8: [lambda: both(token_back)],
        9: [all_token_end],
        10: [small_first],
        11: [lambda: small_next(0)],
        12: [lambda: small_next(1)],
        13: [lambda: small_next(2)],
        14: [lambda: small_next(3)],
    }
    steps = (step1, step2, step3, step4, step5)

    @pl.loop(0, JOBS + 5)
    def _(tick):
        for at, things in work.items():

            @pl.when(tick == at)
            def _():
                for thing in things:
                    thing()

        @pl.when(tick < JOBS)
        def _():
            step0(tick)

        for late in (5, 4, 3, 2, 1):

            @pl.when(jnp.logical_and(tick >= late, tick < JOBS + late))
            def _():
                steps[late - 1](tick - late)

    pltpu.make_async_copy(obq, gq_out, out_sem.at[0]).wait()
    pltpu.make_async_copy(obp, gp_out, out_sem.at[1]).wait()


FF_HERE = 1536


def fused(
    question_tokens, passage_tokens, question_cotangent, passage_cotangent,
    question_lengths, passage_lengths, dataset_ids, positives,
    attn_in, attn_in_bias, attn_out, ffn_in, ffn_in_bias, ffn_out, out_biases, norm_gains, norm_shifts,
):
    any_spec = pl.BlockSpec(memory_space=pl.ANY)
    vmem = pl.BlockSpec(memory_space=pltpu.VMEM)
    smem = pl.BlockSpec(memory_space=pltpu.SMEM)

    def both(shape, dtype):
        return [pltpu.VMEM(shape(m), dtype) for m in TOKS]

    shape = jax.ShapeDtypeStruct
    dma = pltpu.SemaphoreType.DMA
    outs = pl.pallas_call(
        partial(fused_kernel, last=0),
        name="fused",
        in_specs=[any_spec] * 4 + [smem] * 4 + [any_spec, vmem, any_spec, any_spec, vmem, any_spec] + [vmem] * 3,
        out_specs=[any_spec, any_spec, vmem, any_spec, any_spec] + [vmem] * 5,
        out_shape=[
            shape((128, D), BF16),
            shape((512, D), BF16),
            shape((8, 128), F32),
            shape((128, D), BF16),
            shape((512, D), BF16),
            shape((2, 3, ROWS_OUT, COLS), F32),
            shape((2, ROWS_OUT, COLS), F32),
            shape((2, ROWS_OUT, FF_HERE), F32),
            shape((2, ROWS_OUT, FF_HERE), F32),
            shape((SMALL, D), F32),
        ],
        scratch_shapes=[
            pltpu.VMEM((2, D, 3 * COLS), BF16),
            pltpu.VMEM((2, COLS, D), BF16),
            pltpu.VMEM((2, D, FF_HERE), BF16),
            pltpu.VMEM((2, FF_HERE, D), BF16),
            *both(lambda m: (m, D), BF16),
            *both(lambda m: (m, D), BF16),
            *both(lambda m: (m, 3 * COLS), BF16),
            pltpu.VMEM((1, 6, 128, 128), BF16),
            pltpu.VMEM((2, 6, 256, 256), BF16),
            *both(lambda m: (m, D), BF16),
            *both(lambda m: (m, D), F32),
            *both(lambda m: (m, D), F32),
            *both(lambda m: (m, 1), F32),
            *both(lambda m: (m, 1), F32),
            *both(lambda m: (m, FF_HERE), BF16),
            *both(lambda m: (m, D), BF16),
            *both(lambda m: (m, D), BF16),
            *both(lambda m: (m, COLS), BF16),
            *both(lambda m: (m, 12 * COLS), BF16),
            *both(lambda m: (4 * D, m), BF16),
            *both(lambda m: (m, D), BF16),
            *both(lambda m: (2, m, D), BF16),
            pltpu.VMEM((16, D), F32),
            pltpu.VMEM((8, COLS), F32),
            pltpu.VMEM((8, FF_HERE), F32),
            pltpu.VMEM((64, 32), F32),
            pltpu.VMEM((16, 16, 256), BF16),
            pltpu.VMEM((2, 256, 128), F32),
            pltpu.VMEM((64, D), F32),
            pltpu.VMEM((12, 8, D), F32),
            pltpu.VMEM((2, 8, 2 * COLS), F32),
            pltpu.VMEM((2, 8, FF_HERE), F32),
            pltpu.VMEM((4, SMALL, D), F32),
            pltpu.VMEM((4, SMALL, D), F32),
            pltpu.VMEM((DS, 2, COLS, COLS), BF16),
            pltpu.VMEM((D1, 2, COLS, COLS), BF16),
            pltpu.VMEM((DZ, 2, ZN, 96, COLS), BF16),
            pltpu.VMEM((DZ, 2, ZN, 96, COLS), BF16),
            pltpu.VMEM((D3, 2, ROWS_OUT, COLS), BF16),
            dma((16,)),
            dma((2,)),
            dma((3,)),
            dma((2, 3)),
            dma((16,)),
            dma((16,)),
            dma((4,)),
            dma((4,)),
            dma((DS, 2)),
            dma((D1, 2)),
            dma((DZ, 2, ZN)),
            dma((DZ, 2, ZN)),
            dma((DZ, 2, ZN)),
            dma((DZ, 2, ZN)),
            dma((D3, 2)),
            dma((D3, 2)),
        ],
        compiler_params=pltpu.CompilerParams(
            collective_id=0, has_side_effects=True, vmem_limit_bytes=VMEM_BYTES
        ),
    )(
        question_tokens.reshape(128, D),
        passage_tokens.reshape(512, D),
        question_cotangent.reshape(128, D),
        passage_cotangent.reshape(512, D),
        question_lengths, passage_lengths, dataset_ids, positives,
        attn_in.transpose(0, 2, 1, 3), attn_in_bias, attn_out, ffn_in, ffn_in_bias, ffn_out,
        out_biases, norm_gains, norm_shifts,
    )
    oq, op, loss, gq, gp, g_in, g_out, g_fi, g_fo, sums = outs
    me = lax.axis_index("dp")
    sums = sums[:18].reshape(2, 9, D)
    wide = lax.dynamic_slice_in_dim(sums[:, 0:6], me * ROWS_OUT, ROWS_OUT, axis=2)
    in_bias = lax.dynamic_slice_in_dim(sums[:, 6].reshape(2, 2, COLS), me * 24, 24, axis=2)
    fi_bias = lax.dynamic_slice_in_dim(sums[:, 7:9].reshape(2, FF_HERE), me * 96, 96, axis=1)
    return (
        oq.reshape(2, 64, D),
        op.reshape(2, 256, D),
        loss[0, 0],
        gq.reshape(2, 64, D),
        gp.reshape(2, 256, D),
        g_in.transpose(0, 2, 1, 3),
        in_bias,
        g_out.transpose(0, 2, 1),
        g_fi,
        fi_bias,
        g_fo.transpose(0, 2, 1),
        wide[:, 4:6],
        wide[:, 0:2],
        wide[:, 2:4],
    )


VMEM_BYTES = 62 * 1024 * 1024


def solution(mesh):
    in_specs = (
        P("dp", None, None),
        P("dp", None, None),
        P("dp", None, None),
        P("dp", None, None),
        P("dp"),
        P("dp"),
        P(),
        P(),
        P(None, None, None, "tensor"),
        P(None, None, "tensor"),
        P(None, "tensor", None),
        P(None, None, "tensor"),
        P(None, "tensor"),
        P(None, "tensor", None),
        P(),
        P(),
        P(),
    )
    out_specs = (
        P("dp", None, None),
        P("dp", None, None),
        P(),
        P("dp", None, None),
        P("dp", None, None),
        P(None, "dp", None, "tensor"),
        P(None, None, ("tensor", "dp")),
        P(None, "tensor", "dp"),
        P(None, "dp", "tensor"),
        P(None, ("tensor", "dp")),
        P(None, "tensor", "dp"),
        P(None, None, "dp"),
        P(None, None, "dp"),
        P(None, None, "dp"),
    )
    step = fused if mesh.shape["dp"] == 4 * ZN and mesh.shape["tensor"] == 2 else per_device
    return jax.shard_map(
        step, mesh=mesh, in_specs=in_specs, out_specs=out_specs, check_vma=False
    )
```

```python
from functools import partial

import jax
import jax.numpy as jnp
from jax import lax
from jax.experimental import pallas as pl
from jax.experimental.pallas import tpu as pltpu
from jax.sharding import PartitionSpec as P

D = 768
HD = 64


EPSILON = 1e-06
NEGATIVE = -1e30
HIGHEST = lax.Precision.HIGHEST
score_gain = 3.0


def norm_forward(summed, scale_row, shift_row):
    row_mean = jnp.mean(summed, axis=-1, keepdims=True)
    centred = summed - row_mean
    inv_std = lax.rsqrt(jnp.mean(centred * centred, axis=-1, keepdims=True) + EPSILON)
    normed = centred * inv_std
    return (normed * scale_row + shift_row, normed, inv_std)


def norm_backward(incoming, normed, inv_std, scale_row):
    scaled = incoming * scale_row
    outgoing = inv_std * (
        scaled
        - jnp.mean(scaled, axis=-1, keepdims=True)
        - normed * jnp.mean(scaled * normed, axis=-1, keepdims=True)
    )
    return (outgoing, jnp.sum(incoming * normed, axis=(0, 1)), jnp.sum(incoming, axis=(0, 1)))


def key_visible(lengths, length):
    positions = jnp.arange(length, dtype=jnp.int32)
    return (positions[None, :] < lengths[:, None])[:, None, None, :]


def head_scores(queries, key_rows, visible):
    raw_scores = jnp.einsum(
        "bqhe,bkhe->bhqk", queries, key_rows, preferred_element_type=jnp.float32
    ) * HD ** (-0.5)
    return jnp.where(visible, raw_scores, NEGATIVE)


def split_heads(matrix):
    return matrix.reshape(matrix.shape[0], matrix.shape[1], matrix.shape[2] // HD, HD)


def join_heads(per_head):
    return per_head.reshape(
        per_head.shape[0], per_head.shape[1], per_head.shape[2] * per_head.shape[3]
    )


def encoder_forward(tokens, lengths, params):
    (
        attn_in,
        attn_in_bias,
        attn_out,
        ffn_in,
        ffn_in_bias,
        ffn_out,
        out_biases,
        norm_gains,
        norm_shifts,
    ) = params
    projected = jnp.einsum("bld,dce->blce", tokens, attn_in, preferred_element_type=jnp.float32)
    in_bias = attn_in_bias.astype(jnp.float32)
    queries = split_heads((projected[:, :, 0] + in_bias[0]).astype(jnp.bfloat16))
    key_rows = split_heads(projected[:, :, 1].astype(jnp.bfloat16))
    values = split_heads((projected[:, :, 2] + in_bias[1]).astype(jnp.bfloat16))
    visible = key_visible(lengths, tokens.shape[1])
    scores = head_scores(queries, key_rows, visible)
    row_top = jnp.max(scores, axis=-1, keepdims=True)
    log_total = row_top + jnp.log(jnp.sum(jnp.exp(scores - row_top), axis=-1, keepdims=True))
    attn_probs = jnp.exp(scores - log_total).astype(jnp.bfloat16)
    context = join_heads(
        jnp.einsum(
            "bhqk,bkhe->bqhe", attn_probs, values, preferred_element_type=jnp.float32
        ).astype(jnp.bfloat16)
    )
    attn_part = jnp.einsum("ble,ed->bld", context, attn_out, preferred_element_type=jnp.float32)
    attn_sum = lax.psum(attn_part.astype(jnp.bfloat16), "tensor").astype(jnp.float32)
    bias_rows = out_biases.astype(jnp.float32)
    gain_rows = norm_gains.astype(jnp.float32)
    shift_rows = norm_shifts.astype(jnp.float32)
    hidden_float, normed_first, inv_first = norm_forward(
        tokens.astype(jnp.float32) + attn_sum + bias_rows[0], gain_rows[0], shift_rows[0]
    )
    hidden = hidden_float.astype(jnp.bfloat16)
    up_pre = jnp.einsum(
        "bld,df->blf", hidden, ffn_in, preferred_element_type=jnp.float32
    ) + ffn_in_bias.astype(jnp.float32)
    activated = jax.nn.gelu(up_pre, approximate=False).astype(jnp.bfloat16)
    down_part = jnp.einsum("blf,fd->bld", activated, ffn_out, preferred_element_type=jnp.float32)
    down_sum = lax.psum(down_part.astype(jnp.bfloat16), "tensor").astype(jnp.float32)
    outputs, normed_second, inv_second = norm_forward(
        hidden.astype(jnp.float32) + down_sum + bias_rows[1], gain_rows[1], shift_rows[1]
    )
    saved = (
        tokens,
        queries,
        key_rows,
        values,
        log_total,
        context,
        normed_first,
        inv_first,
        hidden,
        up_pre,
        activated,
        normed_second,
        inv_second,
    )
    return (outputs, saved)


def encoder_backward(incoming, saved, lengths, params):
    (
        attn_in,
        attn_in_bias,
        attn_out,
        ffn_in,
        ffn_in_bias,
        ffn_out,
        out_biases,
        norm_gains,
        norm_shifts,
    ) = params
    (
        tokens,
        queries,
        key_rows,
        values,
        log_total,
        context,
        normed_first,
        inv_first,
        hidden,
        up_pre,
        activated,
        normed_second,
        inv_second,
    ) = saved
    groups_here, length, model_width = tokens.shape
    gain_rows = norm_gains.astype(jnp.float32)
    d_second, gain_second, shift_second = norm_backward(
        incoming, normed_second, inv_second, gain_rows[1]
    )
    d_down = d_second.astype(jnp.bfloat16)
    grad_ffn_out = jnp.einsum("blf,bld->fd", activated, d_down, preferred_element_type=jnp.float32)
    d_activated = jnp.einsum("bld,fd->blf", d_down, ffn_out, preferred_element_type=jnp.float32)
    gelu_pull = jax.vjp(partial(jax.nn.gelu, approximate=False), up_pre)[1]
    d_up = gelu_pull(d_activated)[0].astype(jnp.bfloat16)
    grad_ffn_in = jnp.einsum("bld,blf->df", hidden, d_up, preferred_element_type=jnp.float32)
    hidden_part = jnp.einsum("blf,df->bld", d_up, ffn_in, preferred_element_type=jnp.float32)
    d_hidden = d_second + lax.psum(hidden_part.astype(jnp.bfloat16), "tensor").astype(jnp.float32)
    d_first, gain_first, shift_first = norm_backward(
        d_hidden, normed_first, inv_first, gain_rows[0]
    )
    d_attn = d_first.astype(jnp.bfloat16)
    grad_attn_out = jnp.einsum("ble,bld->ed", context, d_attn, preferred_element_type=jnp.float32)
    d_context = split_heads(
        jnp.einsum("bld,ed->ble", d_attn, attn_out, preferred_element_type=jnp.float32).astype(
            jnp.bfloat16
        )
    )
    visible = key_visible(lengths, length)
    scores = head_scores(queries, key_rows, visible)
    probs_float = jnp.exp(scores - log_total)
    d_probs = jnp.einsum("bqhe,bkhe->bhqk", d_context, values, preferred_element_type=jnp.float32)
    d_values = jnp.einsum(
        "bhqk,bqhe->bkhe",
        probs_float.astype(jnp.bfloat16),
        d_context,
        preferred_element_type=jnp.float32,
    ).astype(jnp.bfloat16)
    d_scores = (
        probs_float * (d_probs - jnp.sum(probs_float * d_probs, axis=-1, keepdims=True))
    ).astype(jnp.bfloat16)
    d_queries = (
        jnp.einsum("bhqk,bkhe->bqhe", d_scores, key_rows, preferred_element_type=jnp.float32)
        * HD ** (-0.5)
    ).astype(jnp.bfloat16)
    d_keys = (
        jnp.einsum("bhqk,bqhe->bkhe", d_scores, queries, preferred_element_type=jnp.float32)
        * HD ** (-0.5)
    ).astype(jnp.bfloat16)
    query_grad = join_heads(d_queries)
    value_grad = join_heads(d_values)
    d_projected = jnp.stack([query_grad, join_heads(d_keys), value_grad], axis=2)
    grad_attn_in = jnp.einsum(
        "bld,blce->dce", tokens, d_projected, preferred_element_type=jnp.float32
    )
    token_part = jnp.einsum(
        "blce,dce->bld", d_projected, attn_in, preferred_element_type=jnp.float32
    )
    d_tokens = (
        d_first + lax.psum(token_part.astype(jnp.bfloat16), "tensor").astype(jnp.float32)
    ).astype(jnp.bfloat16)
    grad_in_bias = jnp.stack(
        [
            jnp.sum(query_grad.astype(jnp.float32), axis=(0, 1)),
            jnp.sum(value_grad.astype(jnp.float32), axis=(0, 1)),
        ]
    )
    grad_ffn_bias = jnp.sum(d_up.astype(jnp.float32), axis=(0, 1))
    grad_out_biases = jnp.stack(
        [
            jnp.sum(d_attn.astype(jnp.float32), axis=(0, 1)),
            jnp.sum(d_down.astype(jnp.float32), axis=(0, 1)),
        ]
    )
    grad_gains = jnp.stack([gain_first, gain_second])
    grad_shifts = jnp.stack([shift_first, shift_second])
    return (
        d_tokens,
        (
            grad_attn_in,
            grad_in_bias,
            grad_attn_out,
            grad_ffn_in,
            grad_ffn_bias,
            grad_ffn_out,
            grad_out_biases,
            grad_gains,
            grad_shifts,
        ),
    )


def contrastive(question_rows, passage_rows, own_positive, dataset_ids):
    class_scores = jnp.einsum(
        "gd,jd->gj", question_rows, passage_rows, preferred_element_type=jnp.float32
    ) * (score_gain * D ** (-0.5))
    columns = jnp.arange(passage_rows.shape[0], dtype=jnp.int32)
    chosen = own_positive[:, None] == columns[None, :]
    own_set = jnp.sum(jnp.where(chosen, dataset_ids[None, :], 0), axis=1)
    logits = jnp.where(dataset_ids[None, :] == own_set[:, None], class_scores, NEGATIVE)
    row_top = jnp.max(logits, axis=1, keepdims=True)
    log_total = row_top + jnp.log(jnp.sum(jnp.exp(logits - row_top), axis=1, keepdims=True))
    target = jnp.sum(jnp.where(chosen, class_scores, 0.0), axis=1)
    d_class = (jnp.exp(logits - log_total) - chosen.astype(jnp.float32)) * (
        score_gain * D ** (-0.5)
    )
    return (log_total[:, 0] - target, d_class)


def per_device(
    question_tokens,
    passage_tokens,
    question_cotangent,
    passage_cotangent,
    question_lengths,
    passage_lengths,
    dataset_ids,
    positives,
    attn_in,
    attn_in_bias,
    attn_out,
    ffn_in,
    ffn_in_bias,
    ffn_out,
    out_biases,
    norm_gains,
    norm_shifts,
):

    def encoder_params(encoder):
        return (
            attn_in[encoder],
            attn_in_bias[encoder],
            attn_out[encoder],
            ffn_in[encoder],
            ffn_in_bias[encoder],
            ffn_out[encoder],
            out_biases[encoder],
            norm_gains[encoder],
            norm_shifts[encoder],
        )

    question_params = encoder_params(0)
    passage_params = encoder_params(1)
    question_float, question_saved = encoder_forward(
        question_tokens, question_lengths, question_params
    )
    passage_float, passage_saved = encoder_forward(passage_tokens, passage_lengths, passage_params)
    question_heads = question_float[:, 0].astype(jnp.bfloat16)
    passage_heads = passage_float[:, 0].astype(jnp.bfloat16)
    local_groups = question_heads.shape[0]
    own_start = lax.axis_index("dp") * local_groups
    all_passages = lax.all_gather(passage_heads, "dp", axis=0, tiled=True)
    own_positive = lax.dynamic_slice_in_dim(positives, own_start, local_groups)
    cross, d_class = contrastive(question_heads, all_passages, own_positive, dataset_ids)
    total = lax.psum(jnp.sum(cross), "dp")
    contrastive_loss = total / all_passages.shape[0]
    d_question_heads = jnp.einsum(
        "gj,jd->gd", d_class, all_passages.astype(jnp.float32), precision=HIGHEST
    )
    question_heads_float = question_heads.astype(jnp.float32)
    d_passage_heads = lax.psum_scatter(
        jnp.einsum("gj,gd->jd", d_class, question_heads_float, precision=HIGHEST),
        "dp",
        scatter_dimension=0,
        tiled=True,
    )
    d_question_out = question_cotangent.astype(jnp.float32).at[:, 0].add(d_question_heads)
    d_passage_out = passage_cotangent.astype(jnp.float32).at[:, 0].add(d_passage_heads)
    passage_grad, passage_weights = encoder_backward(
        d_passage_out, passage_saved, passage_lengths, passage_params
    )
    question_grad, question_weights = encoder_backward(
        d_question_out, question_saved, question_lengths, question_params
    )
    joined = (
        lax.psum_scatter(question_weights[0], "dp", scatter_dimension=0, tiled=True),
        lax.psum_scatter(question_weights[1], "dp", scatter_dimension=1, tiled=True),
        lax.psum_scatter(question_weights[2], "dp", scatter_dimension=1, tiled=True),
        lax.psum_scatter(question_weights[3], "dp", scatter_dimension=0, tiled=True),
        lax.psum_scatter(question_weights[4], "dp", scatter_dimension=0, tiled=True),
        lax.psum_scatter(question_weights[5], "dp", scatter_dimension=1, tiled=True),
        lax.psum_scatter(question_weights[6], "dp", scatter_dimension=1, tiled=True),
        lax.psum_scatter(question_weights[7], "dp", scatter_dimension=1, tiled=True),
        lax.psum_scatter(question_weights[8], "dp", scatter_dimension=1, tiled=True),
        lax.psum_scatter(passage_weights[0], "dp", scatter_dimension=0, tiled=True),
        lax.psum_scatter(passage_weights[1], "dp", scatter_dimension=1, tiled=True),
        lax.psum_scatter(passage_weights[2], "dp", scatter_dimension=1, tiled=True),
        lax.psum_scatter(passage_weights[3], "dp", scatter_dimension=0, tiled=True),
        lax.psum_scatter(passage_weights[4], "dp", scatter_dimension=0, tiled=True),
        lax.psum_scatter(passage_weights[5], "dp", scatter_dimension=1, tiled=True),
        lax.psum_scatter(passage_weights[6], "dp", scatter_dimension=1, tiled=True),
        lax.psum_scatter(passage_weights[7], "dp", scatter_dimension=1, tiled=True),
        lax.psum_scatter(passage_weights[8], "dp", scatter_dimension=1, tiled=True),
    )
    question_parts = joined[:9]
    passage_parts = joined[9:]
    stacked = [
        jnp.stack([question_piece, passage_piece])
        for question_piece, passage_piece in zip(question_parts, passage_parts)
    ]
    return (
        question_float.astype(jnp.bfloat16),
        passage_float.astype(jnp.bfloat16),
        contrastive_loss,
        question_grad,
        passage_grad,
        stacked[0],
        stacked[1],
        stacked[2],
        stacked[3],
        stacked[4],
        stacked[5],
        stacked[6],
        stacked[7],
        stacked[8],
    )


MESH_ID = pl.DeviceIdType.MESH
F32 = jnp.float32
BF16 = jnp.bfloat16
ZN = 4
ROWS_OUT = 48
JOBS = 12
COLS = 384
D1, DZ, D3, DS = 8, 4, 2, 2
TOKS = (128, 512)
BLK = (128, 256)
SMALL = 24


def dot(a, b):
    return jnp.dot(a, b, preferred_element_type=F32)


def dot_t(a, b):
    return lax.dot_general(a, b, (((1,), (1,)), ((), ())), preferred_element_type=F32)


def t_dot(a, b):
    return lax.dot_general(a, b, (((0,), (0,)), ((), ())), preferred_element_type=F32)


def gelu_and_slope(u):
    size = jnp.abs(u)
    bell = jnp.exp(-0.5 * u * u)
    t = 1.0 / (1.0 + (0.3275911 * 0.7071067811865476) * size)
    poly = t * (
        0.127414796
        + t * (-0.142248368 + t * (0.7107068705 + t * (-0.7265760135 + t * 0.5307027145)))
    )
    tail = poly * bell
    phi = jnp.where(u >= 0.0, 1.0 - tail, tail)
    return u * phi, phi + u * bell * 0.3989422804014327


def row_mean(v):
    return jnp.sum(v, axis=-1, keepdims=True) * (1.0 / D)


def fold8(v):
    return jnp.sum(v.reshape(v.shape[0] // 8, 8, v.shape[1]), axis=0)


def rows_at(start, size, step=16):
    return pl.ds(pl.multiple_of(start, step), size)


def fused_kernel(
    xq_in, xp_in, cq_in, cp_in, qlen, plen, dsid, posi,
    win_in, bin_in, wo_in, wf_in, bfi_in, wd_in, bo_in, gain_in, shift_in,
    oq_out, op_out, loss_out, gq_out, gp_out, g_in, g_out, g_fi, g_fo, sm_out,
    win, wo, wf, wd, xq, xp, cq, cp, qkvq, qkvp, prq, prp, hq, hp, n1q, n1p, n2q, n2p,
    i1q, i1p, i2q, i2p, sq, sp, obq, obp, ddq, ddp, dcq, dcp, ballq, ballp, atq, atp,
    exsq, exsp, exrq, exrp, par, pin, pfi, masks, hg, hf, dh, acc_s, acc_b, acc_f, smb, smr,
    p1s, p1r, zr, zl, p3r, fin,
    fin_sem, in_sem, out_sem, exs_sem, exr_sem, hgs_sem, hgr_sem, sms_sem, smr_sem,
    p1s_sem, p1r_sem, zrs_sem, zrr_sem, zls_sem, zlr_sem, p3s_sem, p3r_sem,
    *, last,
):
    me = lax.axis_index("dp")
    core = lax.axis_index("tensor")
    z, y, x = me // 4, (me // 2) % 2, me % 2
    partner = {"dp": me, "tensor": 1 - core}
    at_x = {"dp": me + 1 - 2 * x, "tensor": core}
    at_y = {"dp": me + 2 - 4 * y, "tensor": core}

    def at_dp(index):
        return {"dp": index, "tensor": core}

    X, COT, QKV, PR, HID = (xq, xp), (cq, cp), (qkvq, qkvp), (prq, prp), (hq, hp)
    N1, N2, I1, I2, SLOPE = (n1q, n1p), (n2q, n2p), (i1q, i1p), (i2q, i2p), (sq, sp)
    OB, DD, DC, BALL, AT = (obq, obp), (ddq, ddp), (dcq, dcp), (ballq, ballp), (atq, atp)
    EXS, EXR = (exsq, exsp), (exrq, exrp)

    loads = [
        (xq_in, xq),
        *[(win_in.at[0, j], win.at[0, :, pl.ds(j * COLS, COLS)]) for j in range(3)],
        (xp_in, xp),
        *[(win_in.at[1, j], win.at[1, :, pl.ds(j * COLS, COLS)]) for j in range(3)],
        (wo_in.at[0], wo.at[0]),
        (wo_in.at[1], wo.at[1]),
        (wf_in.at[0], wf.at[0]),
        (wf_in.at[1], wf.at[1]),
        (wd_in.at[0], wd.at[0]),
        (wd_in.at[1], wd.at[1]),
        (cq_in, cq),
        (cp_in, cp),
    ]
    loads = [pltpu.make_async_copy(s, d, in_sem.at[i]) for i, (s, d) in enumerate(loads)]
    for copy in loads:
        copy.start()
    ready = set()

    def need(*which):
        for i in which:
            if i not in ready:
                loads[i].wait()
                ready.add(i)

    barrier = pltpu.get_barrier_semaphore()
    pl.semaphore_signal(barrier, inc=1, device_id=partner, device_id_type=MESH_ID)
    for k in range(1, 16):
        pl.semaphore_signal(barrier, inc=1, device_id=at_dp(me ^ k), device_id_type=MESH_ID)

    for e in range(2):
        for i in range(2):
            par[e * 8 + i : e * 8 + i + 1, :] = bo_in[e].astype(F32)[i : i + 1]
            par[e * 8 + 2 + i : e * 8 + 3 + i, :] = gain_in[e].astype(F32)[i : i + 1]
            par[e * 8 + 4 + i : e * 8 + 5 + i, :] = shift_in[e].astype(F32)[i : i + 1]
            pin[e * 2 + i : e * 2 + i + 1, :] = bin_in[e].astype(F32)[i : i + 1]
        pfi[e : e + 1, :] = bfi_in[...].astype(F32)[e : e + 1]
    acc_s[...] = jnp.zeros_like(acc_s)
    acc_b[...] = jnp.zeros_like(acc_b)
    acc_f[...] = jnp.zeros_like(acc_f)

    r32 = lax.broadcasted_iota(jnp.int32, (32, 32), 0)
    c32 = lax.broadcasted_iota(jnp.int32, (32, 32), 1)
    own_pos = jnp.zeros((32, 32), F32)
    set_col = jnp.zeros((32, 32), F32)
    for g in range(32):
        at = (g % 2) * 16 + g // 2
        own_pos = jnp.where(r32 == at, posi[g].astype(F32), own_pos)
        set_col = jnp.where(c32 == at, dsid[g].astype(F32), set_col)
    col_group = ((c32 % 16) * 2 + c32 // 16).astype(F32)
    chosen = jnp.where(own_pos == col_group, 1.0, 0.0)
    own_set = jnp.sum(chosen * set_col, axis=1, keepdims=True)
    masks[0:32, :] = chosen
    masks[32:64, :] = jnp.where(set_col == own_set, 1.0, 0.0)

    lane_lo = lax.broadcasted_iota(jnp.int32, (1, 128), 1) < HD

    def side(v, hh):
        return jnp.where(lane_lo if hh == 0 else jnp.logical_not(lane_lo), v, jnp.zeros_like(v))

    def exchange(e, b, parity):
        slot = 0 if e == 0 else 1 + b
        rows = rows_at(b * BLK[e], BLK[e]) if not isinstance(b, int) else pl.ds(b * BLK[e], BLK[e])
        return pltpu.make_async_remote_copy(
            src_ref=EXS[e].at[rows],
            dst_ref=EXR[e].at[parity, rows],
            send_sem=exs_sem.at[slot],
            recv_sem=exr_sem.at[parity, slot],
            device_id=partner,
            device_id_type=MESH_ID,
        )

    def block_rows(e, b):
        if e == 0:
            return pl.ds(0, BLK[0])
        return rows_at(b * BLK[1], BLK[1], BLK[1])

    def blocks(e, body):
        if e == 0:
            body(0)
        else:
            pl.loop(0, 2)(body)

    def attend(e, b):
        size = BLK[e]
        rows = block_rows(e, b)
        xb = X[e][rows, :]
        for j in range(3):
            cols = pl.ds(j * COLS, COLS)
            got = dot(xb, win[e, :, cols])
            if j == 0:
                got = (got + pin[e * 2 : e * 2 + 1, :]).astype(BF16) * jnp.asarray(HD**-0.5, BF16)
            elif j == 2:
                got = got + pin[e * 2 + 1 : e * 2 + 2, :]
            QKV[e][rows, cols] = got.astype(BF16)

        col = lax.broadcasted_iota(jnp.int32, (size, size), 1)
        if e == 0:
            row = lax.broadcasted_iota(jnp.int32, (size, size), 0)
            first = jnp.logical_and(row < 64, col < qlen[0])
            second = jnp.logical_and(
                row >= 64, jnp.logical_and(col >= 64, col < 64 + qlen[1])
            )
            seen = jnp.logical_or(first, second)
        else:
            seen = col < plen[b]

        @pl.loop(0, 3)
        def _(pair):
            q2 = QKV[e][rows, rows_at(pair * 128, 128, 128)]
            k2 = QKV[e][rows, rows_at(COLS + pair * 128, 128, 128)]
            v2 = QKV[e][rows, rows_at(2 * COLS + pair * 128, 128, 128)]
            total = jnp.zeros((size, 128), F32)
            for hh in range(2):
                s = dot_t(side(q2, hh), k2)
                s = jnp.where(seen, s, NEGATIVE)
                p = jnp.exp(s - jnp.max(s, axis=-1, keepdims=True))
                p = (p * (1.0 / jnp.sum(p, axis=-1, keepdims=True))).astype(BF16)
                PR[e][b, pair * 2 + hh] = p
                total = total + dot(p, side(v2, hh))
            BALL[e][rows, rows_at(8 * COLS + pair * 128, 128, 128)] = total.astype(BF16)

        ctx = BALL[e][rows, pl.ds(8 * COLS, COLS)]
        EXS[e][rows, :] = dot(ctx, wo[e]).astype(BF16)
        exchange(e, b, 0).start()

    CH = 32

    def first_norm(e, b):
        exchange(e, b, 0).wait()

        @pl.loop(0, BLK[e] // CH)
        def _(c):
            rows = rows_at(b * BLK[e] + c * CH, CH, CH)
            v = (
                X[e][rows, :].astype(F32)
                + (EXS[e][rows, :].astype(F32) + EXR[e][0, rows, :].astype(F32))
                + par[e * 8 : e * 8 + 1, :]
            )
            v = v - row_mean(v)
            inv = lax.rsqrt(row_mean(v * v) + EPSILON)
            n = v * inv
            N1[e][rows, :] = n
            I1[e][rows, :] = inv
            HID[e][rows, :] = (
                n * par[e * 8 + 2 : e * 8 + 3, :] + par[e * 8 + 4 : e * 8 + 5, :]
            ).astype(BF16)

    def feed(e, b):
        rows = block_rows(e, b)

        @pl.loop(0, 6)
        def _(n):
            cols = rows_at(n * 256, 256, 256)
            u = dot(HID[e][rows, :], wf[e, :, cols]) + pfi[e : e + 1, cols]
            a, slope = gelu_and_slope(u)
            BALL[e][rows, cols] = a.astype(BF16)
            SLOPE[e][rows, cols] = slope.astype(BF16)

        @pl.loop(0, 3)
        def _(n):
            cols = rows_at(n * 256, 256, 256)
            EXS[e][rows, cols] = dot(BALL[e][rows, pl.ds(0, FF_HERE)], wd[e, :, cols]).astype(BF16)

        exchange(e, b, 1).start()

    def second_norm(e, b):
        exchange(e, b, 1).wait()

        @pl.loop(0, BLK[e] // CH)
        def _(c):
            rows = rows_at(b * BLK[e] + c * CH, CH, CH)
            v = (
                HID[e][rows, :].astype(F32)
                + (EXS[e][rows, :].astype(F32) + EXR[e][1, rows, :].astype(F32))
                + par[e * 8 + 1 : e * 8 + 2, :]
            )
            v = v - row_mean(v)
            inv = lax.rsqrt(row_mean(v * v) + EPSILON)
            n = v * inv
            N2[e][rows, :] = n
            I2[e][rows, :] = inv
            OB[e][rows, :] = (
                n * par[e * 8 + 3 : e * 8 + 4, :] + par[e * 8 + 5 : e * 8 + 6, :]
            ).astype(BF16)

    need(0, 1, 2, 3, 8)
    pl.semaphore_wait(barrier, 16)
    attend(0, 0)
    need(4, 5, 6, 7, 9)
    blocks(1, lambda b: attend(1, b))
    first_norm(0, 0)
    need(10, 12)
    feed(0, 0)
    need(11, 13)

    def passage_mid(b):
        first_norm(1, b)
        feed(1, b)

    blocks(1, passage_mid)
    second_norm(0, 0)
    blocks(1, lambda b: second_norm(1, b))
    out_q = pltpu.make_async_copy(obq, oq_out, out_sem.at[0])
    out_p = pltpu.make_async_copy(obp, op_out, out_sem.at[1])
    out_q.start()
    out_p.start()

    pieces = []
    for ref, at in ((obq, 0), (obq, 64), (obp, 0), (obp, 256)):
        head = ref[at : at + 16, :].astype(F32)[0:1]
        pieces += [head[:, k * 256 : (k + 1) * 256] for k in range(3)]
    pieces.append(jnp.zeros((4, 256), F32))
    hg[me] = jnp.concatenate(pieces, axis=0).astype(BF16)

    def heads(k):
        return pltpu.make_async_remote_copy(
            src_ref=hg.at[me],
            dst_ref=hg.at[me],
            send_sem=hgs_sem.at[k],
            recv_sem=hgr_sem.at[k],
            device_id=at_dp(me ^ k),
            device_id_type=MESH_ID,
        )

    for k in range(1, 16):
        heads(k).start()
    need(14, 15)
    for k in range(1, 16):
        copy = pltpu.make_async_remote_copy(
            src_ref=hg.at[me],
            dst_ref=hg.at[me ^ k],
            send_sem=hgs_sem.at[k],
            recv_sem=hgr_sem.at[k],
            device_id=at_dp(me ^ k),
            device_id_type=MESH_ID,
        )
        copy.wait()
    gathered = hg[...].astype(F32).reshape(256, 256)
    hf[0] = gathered[:, 0:128]
    hf[1] = gathered[:, 128:256]

    def all_heads(first):
        groups = []
        for i in range(2):
            parts = [
                hf[c, pl.ds(first + i * 3 + k, 16, stride=16), :] for k in range(3) for c in range(2)
            ]
            groups.append(jnp.concatenate(parts, axis=1))
        return jnp.concatenate(groups, axis=0)

    heads_q, heads_p = all_heads(0), all_heads(6)
    gain = score_gain * D ** (-0.5)
    class_scores = dot_t(heads_q.astype(BF16), heads_p.astype(BF16)) * gain
    chosen = masks[0:32, :]
    logits = jnp.where(masks[32:64, :] > 0.5, class_scores, NEGATIVE)
    top = jnp.max(logits, axis=1, keepdims=True)
    log_total = top + jnp.log(jnp.sum(jnp.exp(logits - top), axis=1, keepdims=True))
    target = jnp.sum(chosen * class_scores, axis=1, keepdims=True)
    loss = jnp.sum(log_total - target, axis=0, keepdims=True) * (1.0 / 32)
    loss_out[...] = jnp.broadcast_to(loss, loss_out.shape)
    d_class = (jnp.exp(logits - log_total) - chosen) * gain
    dh[0:32, :] = lax.dot_general(
        d_class, heads_p, (((1,), (0,)), ((), ())), precision=HIGHEST, preferred_element_type=F32
    )
    dh[32:64, :] = lax.dot_general(
        d_class, heads_q, (((0,), (0,)), ((), ())), precision=HIGHEST, preferred_element_type=F32
    )

    def norm_back(incoming, n, inv, scale):
        scaled = incoming * scale
        return inv * (scaled - row_mean(scaled) - n * row_mean(scaled * n))

    def transpose_into(e, k, src, b, width=D):
        rows = block_rows(e, b)

        @pl.loop(0, width // 256)
        def _(c):
            tile = src[rows, rows_at(c * 256, 256, 256)]
            AT[e][rows_at(k * D + c * 256, 256, 256), rows] = tile.T

    def second_back(e, b):
        row0 = lax.broadcasted_iota(jnp.int32, (CH, 1), 0)
        seqs = 2 if e == 0 else 1
        length = 64 if e == 0 else 256
        for i in range(seqs):
            group = i if e == 0 else b
            extra = dh[pl.ds(e * 32 + group * 16 + me, 1), :]

            @pl.loop(0, length // CH)
            def _(c):
                rows = rows_at(group * length + c * CH, CH, CH)
                add = jnp.where(row0 + c * CH == 0, extra, 0.0)
                d = COT[e][rows, :].astype(F32) + add
                n = N2[e][rows, :]
                out = norm_back(d, n, I2[e][rows, :], par[e * 8 + 3 : e * 8 + 4, :])
                N2[e][rows, :] = out
                low = out.astype(BF16)
                DD[e][rows, :] = low
                acc_s[e * 6 + 1] += fold8(d * n)
                acc_s[e * 6 + 3] += fold8(d)
                acc_s[e * 6 + 5] += fold8(low.astype(F32))

        transpose_into(e, 0, DD[e], b)

    def feed_back(e, b):
        rows = block_rows(e, b)

        @pl.loop(0, 6)
        def _(n):
            cols = rows_at(n * 256, 256, 256)
            d = dot_t(DD[e][rows, :], wd[e, cols, :]) * SLOPE[e][rows, cols].astype(F32)
            d = d.astype(BF16)
            BALL[e][rows, rows_at(4 * COLS + n * 256, 256, 256)] = d
            acc_f[e, :, cols] += fold8(d.astype(F32))

        @pl.loop(0, 3)
        def _(n):
            cols = rows_at(n * 256, 256, 256)
            EXS[e][rows, cols] = dot_t(BALL[e][rows, pl.ds(4 * COLS, FF_HERE)], wf[e, cols, :]).astype(BF16)

        exchange(e, b, 0).start()
        transpose_into(e, 1, HID[e], b)

    def first_back(e, b):
        exchange(e, b, 0).wait()

        @pl.loop(0, BLK[e] // CH)
        def _(c):
            rows = rows_at(b * BLK[e] + c * CH, CH, CH)
            d = N2[e][rows, :] + (EXS[e][rows, :].astype(F32) + EXR[e][0, rows, :].astype(F32))
            n = N1[e][rows, :]
            out = norm_back(d, n, I1[e][rows, :], par[e * 8 + 2 : e * 8 + 3, :])
            N1[e][rows, :] = out
            low = out.astype(BF16)
            DD[e][rows, :] = low
            acc_s[e * 6 + 0] += fold8(d * n)
            acc_s[e * 6 + 2] += fold8(d)
            acc_s[e * 6 + 4] += fold8(low.astype(F32))

        transpose_into(e, 2, DD[e], b)

    def attend_back(e, b):
        rows = block_rows(e, b)
        size = BLK[e]
        DC[e][rows, :] = dot_t(DD[e][rows, :], wo[e]).astype(BF16)

        @pl.loop(0, 3)
        def _(pair):
            q2 = QKV[e][rows, rows_at(pair * 128, 128, 128)]
            k2 = QKV[e][rows, rows_at(COLS + pair * 128, 128, 128)]
            v2 = QKV[e][rows, rows_at(2 * COLS + pair * 128, 128, 128)]
            dc2 = DC[e][rows, rows_at(pair * 128, 128, 128)]
            dq = jnp.zeros((size, 128), F32)
            dk = jnp.zeros((size, 128), F32)
            dv = jnp.zeros((size, 128), F32)
            for hh in range(2):
                low = PR[e][b, pair * 2 + hh]
                p = low.astype(F32)
                dch = side(dc2, hh)
                dp = dot_t(dch, v2)
                ds = (p * (dp - jnp.sum(p * dp, axis=-1, keepdims=True))).astype(BF16)
                dv = dv + t_dot(low, dch)
                dq = dq + dot(ds, side(k2, hh))
                dk = dk + t_dot(ds, side(q2, hh))
            dq = (dq * HD**-0.5).astype(BF16)
            dv = dv.astype(BF16)
            cols = rows_at(pair * 128, 128, 128)
            BALL[e][rows, rows_at(9 * COLS + pair * 128, 128, 128)] = dq
            BALL[e][rows, rows_at(10 * COLS + pair * 128, 128, 128)] = dk.astype(BF16)
            BALL[e][rows, rows_at(11 * COLS + pair * 128, 128, 128)] = dv
            acc_b[e, :, cols] += fold8(dq.astype(F32))
            acc_b[e, :, rows_at(COLS + pair * 128, 128, 128)] += fold8(dv.astype(F32))

        transpose_into(e, 3, X[e], b)

    def token_back(e, b):
        rows = block_rows(e, b)

        @pl.loop(0, 3)
        def _(n):
            cols = rows_at(n * 256, 256, 256)
            EXS[e][rows, cols] = dot_t(BALL[e][rows, pl.ds(9 * COLS, 3 * COLS)], win[e, cols, :]).astype(BF16)

        exchange(e, b, 1).start()

    def token_end(e, b):
        exchange(e, b, 1).wait()

        @pl.loop(0, BLK[e] // CH)
        def _(c):
            rows = rows_at(b * BLK[e] + c * CH, CH, CH)
            OB[e][rows, :] = (
                N1[e][rows, :] + (EXS[e][rows, :].astype(F32) + EXR[e][1, rows, :].astype(F32))
            ).astype(BF16)

    def job_of(j):
        return (j // 2) % 2, (j // 4) * 2 + j % 2

    def product(e, half, blk, sel):
        a = jnp.where(blk < 8, blk // 4, jnp.where(blk == 8, 2, 3)) * D
        if half == 0:
            rows = [AT[e][rows_at(a + i * 96 + sel * 48, 48), :] for i in range(8)]
        else:
            rows = [AT[e][rows_at(a + i * 192 + sel * 96, 96), :] for i in range(4)]
        return dot(jnp.concatenate(rows, axis=0), BALL[e][:, rows_at(blk * COLS, COLS, 128)])

    first_dev, other_dev = (at_x, at_y), (at_y, at_x)
    first_at, other_at = (x, y), (y, x)

    def p1(j, half):
        return pltpu.make_async_remote_copy(
            src_ref=p1s.at[j % DS, half],
            dst_ref=p1r.at[j % D1, half],
            send_sem=p1s_sem.at[j % DS, half],
            recv_sem=p1r_sem.at[j % D1, half],
            device_id=first_dev[half],
            device_id_type=MESH_ID,
        )

    def along(j, half, d, right, relay):
        buf, send, recv = (zr, zrs_sem, zrr_sem) if right else (zl, zls_sem, zlr_sem)
        src = buf.at[j % DZ, half, d] if relay else p1r.at[j % D1, half, pl.ds(d * 96, 96)]
        return pltpu.make_async_remote_copy(
            src_ref=src,
            dst_ref=buf.at[j % DZ, half, d],
            send_sem=send.at[j % DZ, half, d],
            recv_sem=recv.at[j % DZ, half, d],
            device_id=at_dp(me + 4 if right else me - 4),
            device_id_type=MESH_ID,
        )

    def p3(j, half):
        return pltpu.make_async_remote_copy(
            src_ref=p1r.at[j % D1, half, rows_at(z * 96 + (1 - other_at[half]) * 48, 48)],
            dst_ref=p3r.at[j % D3, half],
            send_sem=p3s_sem.at[j % D3, half],
            recv_sem=p3r_sem.at[j % D3, half],
            device_id=other_dev[half],
            device_id_type=MESH_ID,
        )

    def add_into(dst, rows, other):
        dst[rows, :] = (dst[rows, :].astype(F32) + other.astype(F32)).astype(BF16)

    def step0(j):
        e_of, pair = job_of(j)
        for e in range(2):

            @pl.when(e_of == e)
            def _():
                for half in range(2):
                    p1s[j % DS, half] = product(e, half, pair * 2 + half, 1 - first_at[half]).astype(BF16)
                    p1(j, half).start()

    def step1(j):
        e_of, pair = job_of(j)
        for half in range(2):
            p1(j, half).wait()
        for e in range(2):

            @pl.when(e_of == e)
            def _():
                for half in range(2):
                    own = product(e, half, pair * 2 + half, first_at[half])
                    p1r[j % D1, half] = (own + p1r[j % D1, half].astype(F32)).astype(BF16)

        @pl.when(z == 0)
        def _():
            for half in range(2):
                for d in (3, 2, 1):
                    along(j, half, d, True, False).start()

        @pl.when(z == 3)
        def _():
            for half in range(2):
                for d in (0, 1, 2):
                    along(j, half, d, False, False).start()

    def relay(j, half, d, right):
        buf = zr if right else zl
        along(j, half, d, right, True).wait_recv()
        add_into(buf.at[j % DZ, half, d], slice(None), p1r[j % D1, half, pl.ds(d * 96, 96), :])
        along(j, half, d, right, True).start()

    def step2(j):
        @pl.when(z == 1)
        def _():
            for half in range(2):
                for d in (3, 2):
                    relay(j, half, d, True)

        @pl.when(z == 2)
        def _():
            for half in range(2):
                for d in (0, 1):
                    relay(j, half, d, False)

    def step3(j):
        @pl.when(z == 2)
        def _():
            for half in range(2):
                relay(j, half, 3, True)

        @pl.when(z == 1)
        def _():
            for half in range(2):
                relay(j, half, 0, False)

    def step4(j):
        for half in range(2):
            mine = p1r.at[j % D1, half]
            rows = rows_at(z * 96, 96)

            @pl.when(z > 0)
            def _():
                along(j, half, z, True, True).wait_recv()
                add_into(mine, rows, zr[j % DZ, half, z])

            @pl.when(z < 3)
            def _():
                along(j, half, z, False, True).wait_recv()
                add_into(mine, rows, zl[j % DZ, half, z])

            p3(j, half).start()
            for d in range(4):

                @pl.when(d > z)
                def _():
                    along(j, half, d, True, True).wait_send()

                @pl.when(d < z)
                def _():
                    along(j, half, d, False, True).wait_send()

    def result(slot, half, to):
        return pltpu.make_async_copy(fin.at[slot, half], to, fin_sem.at[slot, half])

    def step5(j):
        e_of, pair = job_of(j)
        for half in range(2):
            p3(j, half).wait()
            rows = rows_at(z * 96 + other_at[half] * 48, 48)
            total = p1r[j % D1, half, rows, :].astype(F32) + p3r[j % D3, half].astype(F32)

            @pl.when(j >= 2)
            def _():
                result(j % 2, half, g_out.at[0]).wait()

            fin[j % 2, half] = total
            for e in range(2):
                for p in range(6):

                    @pl.when(jnp.logical_and(e_of == e, pair == p))
                    def _():
                        blk = p * 2 + half
                        if blk < 4:
                            to = g_fo.at[e, :, pl.ds(blk * COLS, COLS)]
                        elif blk < 8:
                            to = g_fi.at[e, :, pl.ds((blk - 4) * COLS, COLS)]
                        elif blk == 8:
                            to = g_out.at[e]
                        else:
                            to = g_in.at[e, blk - 9]
                        result(j % 2, half, to).start()

    small_to = (at_x, at_y, at_dp(me ^ 4), at_dp(me ^ 8))

    def small(k):
        return pltpu.make_async_remote_copy(
            src_ref=smb.at[k],
            dst_ref=smr.at[k],
            send_sem=sms_sem.at[k],
            recv_sem=smr_sem.at[k],
            device_id=small_to[k],
            device_id_type=MESH_ID,
        )

    def small_first():
        smb[0] = jnp.zeros_like(smb[0])
        for e in range(2):
            for i in range(6):
                smb[0, e * 9 + i : e * 9 + i + 1, :] = jnp.sum(acc_s[e * 6 + i], axis=0, keepdims=True)
            smb[0, e * 9 + 6 : e * 9 + 7, :] = jnp.sum(acc_b[e], axis=0, keepdims=True)
            for i in range(2):
                smb[0, e * 9 + 7 + i : e * 9 + 8 + i, :] = jnp.sum(
                    acc_f[e, :, i * D : (i + 1) * D], axis=0, keepdims=True
                )
        small(0).start()

    def small_next(k):
        small(k).wait()
        if k < 3:
            smb[k + 1] = smb[k] + smr[k]
            small(k + 1).start()
        else:
            total = smb[k] + smr[k]
            sm_out[...] = jnp.zeros_like(sm_out)
            wide = pltpu.roll(total, lax.rem(D - me * ROWS_OUT, D), 1)
            sm_out[:, 0:ROWS_OUT] = wide[:, 0:ROWS_OUT]
            heads_own = pltpu.roll(total, lax.rem(D - me * 24, D), 1)
            feed_own = pltpu.roll(total, lax.rem(D - (me % 8) * 96, D), 1)
            for e in range(2):
                at = e * 9 + 6
                for i in range(2):
                    sm_out[at + i : at + i + 1, 0:24] = heads_own[at : at + 1, i * COLS : i * COLS + 24]
                low, high = feed_own[at + 1 : at + 2, 0:96], feed_own[at + 2 : at + 3, 0:96]
                sm_out[at + 2 : at + 3, 0:96] = jnp.where(me < 8, low, high)

    def both(body):
        body(0, 0)
        blocks(1, lambda b: body(1, b))

    def all_token_end():
        both(token_end)
        pltpu.make_async_copy(obq, gq_out, out_sem.at[0]).start()
        pltpu.make_async_copy(obp, gp_out, out_sem.at[1]).start()

    def wait_out():
        pltpu.make_async_copy(obq, oq_out, out_sem.at[0]).wait()
        pltpu.make_async_copy(obp, op_out, out_sem.at[1]).wait()

    work = {
        0: [lambda: second_back(0, 0)],
        1: [lambda: blocks(1, lambda b: second_back(1, b))],
        2: [lambda: feed_back(0, 0)],
        3: [lambda: blocks(1, lambda b: feed_back(1, b)), wait_out],
        4: [lambda: first_back(0, 0)],
        5: [lambda: blocks(1, lambda b: first_back(1, b))],
        6: [lambda: attend_back(0, 0)],
        7: [lambda: blocks(1, lambda b: attend_back(1, b))],
        8: [lambda: both(token_back)],
        9: [all_token_end],
        10: [small_first],
        11: [lambda: small_next(0)],
        12: [lambda: small_next(1)],
        13: [lambda: small_next(2)],
        14: [lambda: small_next(3)],
    }
    steps = (step1, step2, step3, step4, step5)

    @pl.loop(0, JOBS + 5)
    def _(tick):
        for at, things in work.items():

            @pl.when(tick == at)
            def _():
                for thing in things:
                    thing()

        @pl.when(tick < JOBS)
        def _():
            step0(tick)

        for late in (5, 4, 3, 2, 1):

            @pl.when(jnp.logical_and(tick >= late, tick < JOBS + late))
            def _():
                steps[late - 1](tick - late)

    pltpu.make_async_copy(obq, gq_out, out_sem.at[0]).wait()
    pltpu.make_async_copy(obp, gp_out, out_sem.at[1]).wait()
    for slot in range(2):
        for half in range(2):
            result(slot, half, g_out.at[0]).wait()


def finish_kernel(*refs):
    oq, op, gq, gp, g_in, g_out, g_fi, g_fo, loss, sums = refs[:10]
    large, (loss_to, in_bias, fi_bias, bo, gain, shift) = refs[10:18], refs[18:24]
    held, in_sems, out_sems = refs[24:32], refs[32], refs[33]
    sources = (oq, op, gq, gp, g_in, g_out, g_fi, g_fo)
    loads = [pltpu.make_async_copy(sources[i], held[i], in_sems.at[i]) for i in range(8)]
    stores = [pltpu.make_async_copy(held[i], large[i], out_sems.at[i]) for i in range(8)]
    for load in loads:
        load.start()
    loss_to[...] = loss[0:1, 0:1]
    for e in range(2):
        at = e * 9
        gain[e] = sums[at : at + 2, 0:ROWS_OUT]
        shift[e] = sums[at + 2 : at + 4, 0:ROWS_OUT]
        bo[e] = sums[at + 4 : at + 6, 0:ROWS_OUT]
        in_bias[e] = sums[at + 6 : at + 8, 0:24]
        fi_bias[e : e + 1] = sums[at + 8 : at + 9, 0:96]
    for load, store in zip(loads, stores):
        load.wait()
        store.start()
    for store in stores:
        store.wait()


FF_HERE = 1536


def fused(
    question_tokens, passage_tokens, question_cotangent, passage_cotangent,
    question_lengths, passage_lengths, dataset_ids, positives,
    attn_in, attn_in_bias, attn_out, ffn_in, ffn_in_bias, ffn_out, out_biases, norm_gains, norm_shifts,
):
    any_spec = pl.BlockSpec(memory_space=pl.ANY)
    vmem = pl.BlockSpec(memory_space=pltpu.VMEM)
    smem = pl.BlockSpec(memory_space=pltpu.SMEM)

    def both(shape, dtype):
        return [pltpu.VMEM(shape(m), dtype) for m in TOKS]

    shape = jax.ShapeDtypeStruct
    dma = pltpu.SemaphoreType.DMA
    outs = pl.pallas_call(
        partial(fused_kernel, last=0),
        name="fused",
        in_specs=[any_spec] * 4 + [smem] * 4 + [any_spec, vmem, any_spec, any_spec, vmem, any_spec] + [vmem] * 3,
        out_specs=[any_spec, any_spec, vmem] + [any_spec] * 6 + [vmem],
        out_shape=[
            shape((128, D), BF16),
            shape((512, D), BF16),
            shape((8, 128), F32),
            shape((128, D), BF16),
            shape((512, D), BF16),
            shape((2, 3, ROWS_OUT, COLS), F32),
            shape((2, ROWS_OUT, COLS), F32),
            shape((2, ROWS_OUT, FF_HERE), F32),
            shape((2, ROWS_OUT, FF_HERE), F32),
            shape((SMALL, 128), F32),
        ],
        scratch_shapes=[
            pltpu.VMEM((2, D, 3 * COLS), BF16),
            pltpu.VMEM((2, COLS, D), BF16),
            pltpu.VMEM((2, D, FF_HERE), BF16),
            pltpu.VMEM((2, FF_HERE, D), BF16),
            *both(lambda m: (m, D), BF16),
            *both(lambda m: (m, D), BF16),
            *both(lambda m: (m, 3 * COLS), BF16),
            pltpu.VMEM((1, 6, 128, 128), BF16),
            pltpu.VMEM((2, 6, 256, 256), BF16),
            *both(lambda m: (m, D), BF16),
            *both(lambda m: (m, D), F32),
            *both(lambda m: (m, D), F32),
            *both(lambda m: (m, 1), F32),
            *both(lambda m: (m, 1), F32),
            *both(lambda m: (m, FF_HERE), BF16),
            *both(lambda m: (m, D), BF16),
            *both(lambda m: (m, D), BF16),
            *both(lambda m: (m, COLS), BF16),
            *both(lambda m: (m, 12 * COLS), BF16),
            *both(lambda m: (4 * D, m), BF16),
            *both(lambda m: (m, D), BF16),
            *both(lambda m: (2, m, D), BF16),
            pltpu.VMEM((16, D), F32),
            pltpu.VMEM((8, COLS), F32),
            pltpu.VMEM((8, FF_HERE), F32),
            pltpu.VMEM((64, 32), F32),
            pltpu.VMEM((16, 16, 256), BF16),
            pltpu.VMEM((2, 256, 128), F32),
            pltpu.VMEM((64, D), F32),
            pltpu.VMEM((12, 8, D), F32),
            pltpu.VMEM((2, 8, 2 * COLS), F32),
            pltpu.VMEM((2, 8, FF_HERE), F32),
            pltpu.VMEM((4, SMALL, D), F32),
            pltpu.VMEM((4, SMALL, D), F32),
            pltpu.VMEM((DS, 2, COLS, COLS), BF16),
            pltpu.VMEM((D1, 2, COLS, COLS), BF16),
            pltpu.VMEM((DZ, 2, ZN, 96, COLS), BF16),
            pltpu.VMEM((DZ, 2, ZN, 96, COLS), BF16),
            pltpu.VMEM((D3, 2, ROWS_OUT, COLS), BF16),
            pltpu.VMEM((2, 2, ROWS_OUT, COLS), F32),
            dma((2, 2)),
            dma((16,)),
            dma((2,)),
            dma((3,)),
            dma((2, 3)),
            dma((16,)),
            dma((16,)),
            dma((4,)),
            dma((4,)),
            dma((DS, 2)),
            dma((D1, 2)),
            dma((DZ, 2, ZN)),
            dma((DZ, 2, ZN)),
            dma((DZ, 2, ZN)),
            dma((DZ, 2, ZN)),
            dma((D3, 2)),
            dma((D3, 2)),
        ],
        compiler_params=pltpu.CompilerParams(
            collective_id=0, has_side_effects=True, vmem_limit_bytes=VMEM_BYTES
        ),
    )(
        question_tokens.reshape(128, D),
        passage_tokens.reshape(512, D),
        question_cotangent.reshape(128, D),
        passage_cotangent.reshape(512, D),
        question_lengths, passage_lengths, dataset_ids, positives,
        attn_in.transpose(0, 2, 1, 3), attn_in_bias, attn_out, ffn_in, ffn_in_bias, ffn_out,
        out_biases, norm_gains, norm_shifts,
    )
    oq, op, loss, gq, gp, g_in, g_out, g_fi, g_fo, sums = outs
    large = (oq, op, gq, gp, g_in, g_out, g_fi, g_fo)
    small = [(1, 1), (2, 2, 24), (2, 96), (2, 2, ROWS_OUT), (2, 2, ROWS_OUT), (2, 2, ROWS_OUT)]
    oq, op, gq, gp, g_in, g_out, g_fi, g_fo, loss, in_bias, fi_bias, bo, gain, shift = pl.pallas_call(
        finish_kernel,
        name="finish",
        in_specs=[any_spec] * 8 + [vmem] * 2,
        out_specs=[any_spec] * 8 + [vmem] * 6,
        out_shape=[shape(a.shape, a.dtype) for a in large] + [shape(dims, F32) for dims in small],
        scratch_shapes=[*[pltpu.VMEM(a.shape, a.dtype) for a in large], dma((8,)), dma((8,))],
        compiler_params=pltpu.CompilerParams(vmem_limit_bytes=VMEM_BYTES),
    )(*large, loss, sums)
    return (
        oq.reshape(2, 64, D),
        op.reshape(2, 256, D),
        loss.reshape(()),
        gq.reshape(2, 64, D),
        gp.reshape(2, 256, D),
        g_in.transpose(0, 2, 1, 3),
        in_bias,
        g_out.transpose(0, 2, 1),
        g_fi,
        fi_bias,
        g_fo.transpose(0, 2, 1),
        bo,
        gain,
        shift,
    )


VMEM_BYTES = 62 * 1024 * 1024


def solution(mesh):
    in_specs = (
        P("dp", None, None),
        P("dp", None, None),
        P("dp", None, None),
        P("dp", None, None),
        P("dp"),
        P("dp"),
        P(),
        P(),
        P(None, None, None, "tensor"),
        P(None, None, "tensor"),
        P(None, "tensor", None),
        P(None, None, "tensor"),
        P(None, "tensor"),
        P(None, "tensor", None),
        P(),
        P(),
        P(),
    )
    out_specs = (
        P("dp", None, None),
        P("dp", None, None),
        P(),
        P("dp", None, None),
        P("dp", None, None),
        P(None, "dp", None, "tensor"),
        P(None, None, ("tensor", "dp")),
        P(None, "tensor", "dp"),
        P(None, "dp", "tensor"),
        P(None, ("tensor", "dp")),
        P(None, "tensor", "dp"),
        P(None, None, "dp"),
        P(None, None, "dp"),
        P(None, None, "dp"),
    )
    step = fused if mesh.shape["dp"] == 4 * ZN and mesh.shape["tensor"] == 2 else per_device
    return jax.shard_map(
        step, mesh=mesh, in_specs=in_specs, out_specs=out_specs, check_vma=False
    )
```

```python
from functools import partial

import jax
import jax.numpy as jnp
from jax import lax
from jax.experimental import pallas as pl
from jax.experimental.pallas import tpu as pltpu
from jax.sharding import PartitionSpec as P

D = 768
HD = 64


EPSILON = 1e-06
NEGATIVE = -1e30
HIGHEST = lax.Precision.HIGHEST
score_gain = 3.0


def norm_forward(summed, scale_row, shift_row):
    row_mean = jnp.mean(summed, axis=-1, keepdims=True)
    centred = summed - row_mean
    inv_std = lax.rsqrt(jnp.mean(centred * centred, axis=-1, keepdims=True) + EPSILON)
    normed = centred * inv_std
    return (normed * scale_row + shift_row, normed, inv_std)


def norm_backward(incoming, normed, inv_std, scale_row):
    scaled = incoming * scale_row
    outgoing = inv_std * (
        scaled
        - jnp.mean(scaled, axis=-1, keepdims=True)
        - normed * jnp.mean(scaled * normed, axis=-1, keepdims=True)
    )
    return (outgoing, jnp.sum(incoming * normed, axis=(0, 1)), jnp.sum(incoming, axis=(0, 1)))


def key_visible(lengths, length):
    positions = jnp.arange(length, dtype=jnp.int32)
    return (positions[None, :] < lengths[:, None])[:, None, None, :]


def head_scores(queries, key_rows, visible):
    raw_scores = jnp.einsum(
        "bqhe,bkhe->bhqk", queries, key_rows, preferred_element_type=jnp.float32
    ) * HD ** (-0.5)
    return jnp.where(visible, raw_scores, NEGATIVE)


def split_heads(matrix):
    return matrix.reshape(matrix.shape[0], matrix.shape[1], matrix.shape[2] // HD, HD)


def join_heads(per_head):
    return per_head.reshape(
        per_head.shape[0], per_head.shape[1], per_head.shape[2] * per_head.shape[3]
    )


def encoder_forward(tokens, lengths, params):
    (
        attn_in,
        attn_in_bias,
        attn_out,
        ffn_in,
        ffn_in_bias,
        ffn_out,
        out_biases,
        norm_gains,
        norm_shifts,
    ) = params
    projected = jnp.einsum("bld,dce->blce", tokens, attn_in, preferred_element_type=jnp.float32)
    in_bias = attn_in_bias.astype(jnp.float32)
    queries = split_heads((projected[:, :, 0] + in_bias[0]).astype(jnp.bfloat16))
    key_rows = split_heads(projected[:, :, 1].astype(jnp.bfloat16))
    values = split_heads((projected[:, :, 2] + in_bias[1]).astype(jnp.bfloat16))
    visible = key_visible(lengths, tokens.shape[1])
    scores = head_scores(queries, key_rows, visible)
    row_top = jnp.max(scores, axis=-1, keepdims=True)
    log_total = row_top + jnp.log(jnp.sum(jnp.exp(scores - row_top), axis=-1, keepdims=True))
    attn_probs = jnp.exp(scores - log_total).astype(jnp.bfloat16)
    context = join_heads(
        jnp.einsum(
            "bhqk,bkhe->bqhe", attn_probs, values, preferred_element_type=jnp.float32
        ).astype(jnp.bfloat16)
    )
    attn_part = jnp.einsum("ble,ed->bld", context, attn_out, preferred_element_type=jnp.float32)
    attn_sum = lax.psum(attn_part.astype(jnp.bfloat16), "tensor").astype(jnp.float32)
    bias_rows = out_biases.astype(jnp.float32)
    gain_rows = norm_gains.astype(jnp.float32)
    shift_rows = norm_shifts.astype(jnp.float32)
    hidden_float, normed_first, inv_first = norm_forward(
        tokens.astype(jnp.float32) + attn_sum + bias_rows[0], gain_rows[0], shift_rows[0]
    )
    hidden = hidden_float.astype(jnp.bfloat16)
    up_pre = jnp.einsum(
        "bld,df->blf", hidden, ffn_in, preferred_element_type=jnp.float32
    ) + ffn_in_bias.astype(jnp.float32)
    activated = jax.nn.gelu(up_pre, approximate=False).astype(jnp.bfloat16)
    down_part = jnp.einsum("blf,fd->bld", activated, ffn_out, preferred_element_type=jnp.float32)
    down_sum = lax.psum(down_part.astype(jnp.bfloat16), "tensor").astype(jnp.float32)
    outputs, normed_second, inv_second = norm_forward(
        hidden.astype(jnp.float32) + down_sum + bias_rows[1], gain_rows[1], shift_rows[1]
    )
    saved = (
        tokens,
        queries,
        key_rows,
        values,
        log_total,
        context,
        normed_first,
        inv_first,
        hidden,
        up_pre,
        activated,
        normed_second,
        inv_second,
    )
    return (outputs, saved)


def encoder_backward(incoming, saved, lengths, params):
    (
        attn_in,
        attn_in_bias,
        attn_out,
        ffn_in,
        ffn_in_bias,
        ffn_out,
        out_biases,
        norm_gains,
        norm_shifts,
    ) = params
    (
        tokens,
        queries,
        key_rows,
        values,
        log_total,
        context,
        normed_first,
        inv_first,
        hidden,
        up_pre,
        activated,
        normed_second,
        inv_second,
    ) = saved
    groups_here, length, model_width = tokens.shape
    gain_rows = norm_gains.astype(jnp.float32)
    d_second, gain_second, shift_second = norm_backward(
        incoming, normed_second, inv_second, gain_rows[1]
    )
    d_down = d_second.astype(jnp.bfloat16)
    grad_ffn_out = jnp.einsum("blf,bld->fd", activated, d_down, preferred_element_type=jnp.float32)
    d_activated = jnp.einsum("bld,fd->blf", d_down, ffn_out, preferred_element_type=jnp.float32)
    gelu_pull = jax.vjp(partial(jax.nn.gelu, approximate=False), up_pre)[1]
    d_up = gelu_pull(d_activated)[0].astype(jnp.bfloat16)
    grad_ffn_in = jnp.einsum("bld,blf->df", hidden, d_up, preferred_element_type=jnp.float32)
    hidden_part = jnp.einsum("blf,df->bld", d_up, ffn_in, preferred_element_type=jnp.float32)
    d_hidden = d_second + lax.psum(hidden_part.astype(jnp.bfloat16), "tensor").astype(jnp.float32)
    d_first, gain_first, shift_first = norm_backward(
        d_hidden, normed_first, inv_first, gain_rows[0]
    )
    d_attn = d_first.astype(jnp.bfloat16)
    grad_attn_out = jnp.einsum("ble,bld->ed", context, d_attn, preferred_element_type=jnp.float32)
    d_context = split_heads(
        jnp.einsum("bld,ed->ble", d_attn, attn_out, preferred_element_type=jnp.float32).astype(
            jnp.bfloat16
        )
    )
    visible = key_visible(lengths, length)
    scores = head_scores(queries, key_rows, visible)
    probs_float = jnp.exp(scores - log_total)
    d_probs = jnp.einsum("bqhe,bkhe->bhqk", d_context, values, preferred_element_type=jnp.float32)
    d_values = jnp.einsum(
        "bhqk,bqhe->bkhe",
        probs_float.astype(jnp.bfloat16),
        d_context,
        preferred_element_type=jnp.float32,
    ).astype(jnp.bfloat16)
    d_scores = (
        probs_float * (d_probs - jnp.sum(probs_float * d_probs, axis=-1, keepdims=True))
    ).astype(jnp.bfloat16)
    d_queries = (
        jnp.einsum("bhqk,bkhe->bqhe", d_scores, key_rows, preferred_element_type=jnp.float32)
        * HD ** (-0.5)
    ).astype(jnp.bfloat16)
    d_keys = (
        jnp.einsum("bhqk,bqhe->bkhe", d_scores, queries, preferred_element_type=jnp.float32)
        * HD ** (-0.5)
    ).astype(jnp.bfloat16)
    query_grad = join_heads(d_queries)
    value_grad = join_heads(d_values)
    d_projected = jnp.stack([query_grad, join_heads(d_keys), value_grad], axis=2)
    grad_attn_in = jnp.einsum(
        "bld,blce->dce", tokens, d_projected, preferred_element_type=jnp.float32
    )
    token_part = jnp.einsum(
        "blce,dce->bld", d_projected, attn_in, preferred_element_type=jnp.float32
    )
    d_tokens = (
        d_first + lax.psum(token_part.astype(jnp.bfloat16), "tensor").astype(jnp.float32)
    ).astype(jnp.bfloat16)
    grad_in_bias = jnp.stack(
        [
            jnp.sum(query_grad.astype(jnp.float32), axis=(0, 1)),
            jnp.sum(value_grad.astype(jnp.float32), axis=(0, 1)),
        ]
    )
    grad_ffn_bias = jnp.sum(d_up.astype(jnp.float32), axis=(0, 1))
    grad_out_biases = jnp.stack(
        [
            jnp.sum(d_attn.astype(jnp.float32), axis=(0, 1)),
            jnp.sum(d_down.astype(jnp.float32), axis=(0, 1)),
        ]
    )
    grad_gains = jnp.stack([gain_first, gain_second])
    grad_shifts = jnp.stack([shift_first, shift_second])
    return (
        d_tokens,
        (
            grad_attn_in,
            grad_in_bias,
            grad_attn_out,
            grad_ffn_in,
            grad_ffn_bias,
            grad_ffn_out,
            grad_out_biases,
            grad_gains,
            grad_shifts,
        ),
    )


def contrastive(question_rows, passage_rows, own_positive, dataset_ids):
    class_scores = jnp.einsum(
        "gd,jd->gj", question_rows, passage_rows, preferred_element_type=jnp.float32
    ) * (score_gain * D ** (-0.5))
    columns = jnp.arange(passage_rows.shape[0], dtype=jnp.int32)
    chosen = own_positive[:, None] == columns[None, :]
    own_set = jnp.sum(jnp.where(chosen, dataset_ids[None, :], 0), axis=1)
    logits = jnp.where(dataset_ids[None, :] == own_set[:, None], class_scores, NEGATIVE)
    row_top = jnp.max(logits, axis=1, keepdims=True)
    log_total = row_top + jnp.log(jnp.sum(jnp.exp(logits - row_top), axis=1, keepdims=True))
    target = jnp.sum(jnp.where(chosen, class_scores, 0.0), axis=1)
    d_class = (jnp.exp(logits - log_total) - chosen.astype(jnp.float32)) * (
        score_gain * D ** (-0.5)
    )
    return (log_total[:, 0] - target, d_class)


def per_device(
    question_tokens,
    passage_tokens,
    question_cotangent,
    passage_cotangent,
    question_lengths,
    passage_lengths,
    dataset_ids,
    positives,
    attn_in,
    attn_in_bias,
    attn_out,
    ffn_in,
    ffn_in_bias,
    ffn_out,
    out_biases,
    norm_gains,
    norm_shifts,
):

    def encoder_params(encoder):
        return (
            attn_in[encoder],
            attn_in_bias[encoder],
            attn_out[encoder],
            ffn_in[encoder],
            ffn_in_bias[encoder],
            ffn_out[encoder],
            out_biases[encoder],
            norm_gains[encoder],
            norm_shifts[encoder],
        )

    question_params = encoder_params(0)
    passage_params = encoder_params(1)
    question_float, question_saved = encoder_forward(
        question_tokens, question_lengths, question_params
    )
    passage_float, passage_saved = encoder_forward(passage_tokens, passage_lengths, passage_params)
    question_heads = question_float[:, 0].astype(jnp.bfloat16)
    passage_heads = passage_float[:, 0].astype(jnp.bfloat16)
    local_groups = question_heads.shape[0]
    own_start = lax.axis_index("dp") * local_groups
    all_passages = lax.all_gather(passage_heads, "dp", axis=0, tiled=True)
    own_positive = lax.dynamic_slice_in_dim(positives, own_start, local_groups)
    cross, d_class = contrastive(question_heads, all_passages, own_positive, dataset_ids)
    total = lax.psum(jnp.sum(cross), "dp")
    contrastive_loss = total / all_passages.shape[0]
    d_question_heads = jnp.einsum(
        "gj,jd->gd", d_class, all_passages.astype(jnp.float32), precision=HIGHEST
    )
    question_heads_float = question_heads.astype(jnp.float32)
    d_passage_heads = lax.psum_scatter(
        jnp.einsum("gj,gd->jd", d_class, question_heads_float, precision=HIGHEST),
        "dp",
        scatter_dimension=0,
        tiled=True,
    )
    d_question_out = question_cotangent.astype(jnp.float32).at[:, 0].add(d_question_heads)
    d_passage_out = passage_cotangent.astype(jnp.float32).at[:, 0].add(d_passage_heads)
    passage_grad, passage_weights = encoder_backward(
        d_passage_out, passage_saved, passage_lengths, passage_params
    )
    question_grad, question_weights = encoder_backward(
        d_question_out, question_saved, question_lengths, question_params
    )
    joined = (
        lax.psum_scatter(question_weights[0], "dp", scatter_dimension=0, tiled=True),
        lax.psum_scatter(question_weights[1], "dp", scatter_dimension=1, tiled=True),
        lax.psum_scatter(question_weights[2], "dp", scatter_dimension=1, tiled=True),
        lax.psum_scatter(question_weights[3], "dp", scatter_dimension=0, tiled=True),
        lax.psum_scatter(question_weights[4], "dp", scatter_dimension=0, tiled=True),
        lax.psum_scatter(question_weights[5], "dp", scatter_dimension=1, tiled=True),
        lax.psum_scatter(question_weights[6], "dp", scatter_dimension=1, tiled=True),
        lax.psum_scatter(question_weights[7], "dp", scatter_dimension=1, tiled=True),
        lax.psum_scatter(question_weights[8], "dp", scatter_dimension=1, tiled=True),
        lax.psum_scatter(passage_weights[0], "dp", scatter_dimension=0, tiled=True),
        lax.psum_scatter(passage_weights[1], "dp", scatter_dimension=1, tiled=True),
        lax.psum_scatter(passage_weights[2], "dp", scatter_dimension=1, tiled=True),
        lax.psum_scatter(passage_weights[3], "dp", scatter_dimension=0, tiled=True),
        lax.psum_scatter(passage_weights[4], "dp", scatter_dimension=0, tiled=True),
        lax.psum_scatter(passage_weights[5], "dp", scatter_dimension=1, tiled=True),
        lax.psum_scatter(passage_weights[6], "dp", scatter_dimension=1, tiled=True),
        lax.psum_scatter(passage_weights[7], "dp", scatter_dimension=1, tiled=True),
        lax.psum_scatter(passage_weights[8], "dp", scatter_dimension=1, tiled=True),
    )
    question_parts = joined[:9]
    passage_parts = joined[9:]
    stacked = [
        jnp.stack([question_piece, passage_piece])
        for question_piece, passage_piece in zip(question_parts, passage_parts)
    ]
    return (
        question_float.astype(jnp.bfloat16),
        passage_float.astype(jnp.bfloat16),
        contrastive_loss,
        question_grad,
        passage_grad,
        stacked[0],
        stacked[1],
        stacked[2],
        stacked[3],
        stacked[4],
        stacked[5],
        stacked[6],
        stacked[7],
        stacked[8],
    )


MESH_ID = pl.DeviceIdType.MESH
F32 = jnp.float32
BF16 = jnp.bfloat16
ZN = 4
ROWS_OUT = 48
JOBS = 12
COLS = 384
D1, D2, DZ, DS = 8, 6, 5, 2
LINE_FIRST = (6, 8, 9, 11)
TOKS = (128, 512)
BLK = (128, 256)
SMALL = 24


def dot(a, b):
    return jnp.dot(a, b, preferred_element_type=F32)


def dot_t(a, b):
    return lax.dot_general(a, b, (((1,), (1,)), ((), ())), preferred_element_type=F32)


def t_dot(a, b):
    return lax.dot_general(a, b, (((0,), (0,)), ((), ())), preferred_element_type=F32)


def gelu_and_slope(u):
    size = jnp.abs(u)
    bell = jnp.exp(-0.5 * u * u)
    t = 1.0 / (1.0 + (0.3275911 * 0.7071067811865476) * size)
    poly = t * (
        0.127414796
        + t * (-0.142248368 + t * (0.7107068705 + t * (-0.7265760135 + t * 0.5307027145)))
    )
    tail = poly * bell
    phi = jnp.where(u >= 0.0, 1.0 - tail, tail)
    return u * phi, phi + u * bell * 0.3989422804014327


def row_mean(v):
    return jnp.sum(v, axis=-1, keepdims=True) * (1.0 / D)


def fold8(v):
    return jnp.sum(v.reshape(v.shape[0] // 8, 8, v.shape[1]), axis=0)


def rows_at(start, size, step=16):
    return pl.ds(pl.multiple_of(start, step), size)


def fused_kernel(
    xq_in, xp_in, cq_in, cp_in, qlen, plen, dsid, posi,
    win_in, bin_in, wo_in, wf_in, bfi_in, wd_in, bo_in, gain_in, shift_in,
    oq_out, op_out, loss_out, gq_out, gp_out, g_in, g_out, g_fi, g_fo, sm_out,
    win, wo, wf, wd, xq, xp, cq, cp, qkvq, qkvp, prq, prp, hq, hp, n1q, n1p, n2q, n2p,
    i1q, i1p, i2q, i2p, sq, sp, obq, obp, ddq, ddp, dcq, dcp, ballq, ballp, atq, atp,
    exsq, exsp, exrq, exrp, par, pin, pfi, masks, hg, hf, dh, acc_s, acc_b, acc_f, smb, smr,
    p1s, p1r, p2r, zr, zl, fin, fra, frb, xms, xmr, hm, am,
    fin_sem, in_sem, out_sem, exs_sem, exr_sem, hgs_sem, hgr_sem, sms_sem, smr_sem,
    p1s_sem, p1r_sem, p2s_sem, p2r_sem, zrs_sem, zrr_sem, zls_sem, zlr_sem,
    fas_sem, far_sem, fbs_sem, fbr_sem, xms_sem, xmr_sem,
    *, last,
):
    me = lax.axis_index("dp")
    core = lax.axis_index("tensor")
    z, y, x = me // 4, (me // 2) % 2, me % 2
    partner = {"dp": me, "tensor": 1 - core}
    at_x = {"dp": me + 1 - 2 * x, "tensor": core}
    at_y = {"dp": me + 2 - 4 * y, "tensor": core}

    def at_dp(index):
        return {"dp": index, "tensor": core}

    X, COT, QKV, PR, HID = (xq, xp), (cq, cp), (qkvq, qkvp), (prq, prp), (hq, hp)
    N1, N2, I1, I2, SLOPE = (n1q, n1p), (n2q, n2p), (i1q, i1p), (i2q, i2p), (sq, sp)
    OB, DD, DC, BALL, AT = (obq, obp), (ddq, ddp), (dcq, dcp), (ballq, ballp), (atq, atp)
    EXS, EXR = (exsq, exsp), (exrq, exrp)

    loads = [
        (xq_in, xq),
        *[(win_in.at[0, j], win.at[0, :, pl.ds(j * COLS, COLS)]) for j in range(3)],
        (xp_in, xp),
        *[(win_in.at[1, j], win.at[1, :, pl.ds(j * COLS, COLS)]) for j in range(3)],
        (wo_in.at[0], wo.at[0]),
        (wo_in.at[1], wo.at[1]),
        (wf_in.at[0], wf.at[0]),
        (wf_in.at[1], wf.at[1]),
        (wd_in.at[0], wd.at[0]),
        (wd_in.at[1], wd.at[1]),
        (cq_in, cq),
        (cp_in, cp),
    ]
    loads = [pltpu.make_async_copy(s, d, in_sem.at[i]) for i, (s, d) in enumerate(loads)]
    for copy in loads:
        copy.start()
    ready = set()

    def need(*which):
        for i in which:
            if i not in ready:
                loads[i].wait()
                ready.add(i)

    barrier = pltpu.get_barrier_semaphore()
    pl.semaphore_signal(barrier, inc=1, device_id=partner, device_id_type=MESH_ID)
    for k in range(1, 16):
        pl.semaphore_signal(barrier, inc=1, device_id=at_dp(me ^ k), device_id_type=MESH_ID)

    for e in range(2):
        for i in range(2):
            par[e * 8 + i : e * 8 + i + 1, :] = bo_in[e].astype(F32)[i : i + 1]
            par[e * 8 + 2 + i : e * 8 + 3 + i, :] = gain_in[e].astype(F32)[i : i + 1]
            par[e * 8 + 4 + i : e * 8 + 5 + i, :] = shift_in[e].astype(F32)[i : i + 1]
            pin[e * 2 + i : e * 2 + i + 1, :] = bin_in[e].astype(F32)[i : i + 1]
        pfi[e : e + 1, :] = bfi_in[...].astype(F32)[e : e + 1]
    acc_s[...] = jnp.zeros_like(acc_s)
    acc_b[...] = jnp.zeros_like(acc_b)
    acc_f[...] = jnp.zeros_like(acc_f)

    r32 = lax.broadcasted_iota(jnp.int32, (32, 32), 0)
    c32 = lax.broadcasted_iota(jnp.int32, (32, 32), 1)
    own_pos = jnp.zeros((32, 32), F32)
    set_col = jnp.zeros((32, 32), F32)
    for g in range(32):
        at = (g % 2) * 16 + g // 2
        own_pos = jnp.where(r32 == at, posi[g].astype(F32), own_pos)
        set_col = jnp.where(c32 == at, dsid[g].astype(F32), set_col)
    col_group = ((c32 % 16) * 2 + c32 // 16).astype(F32)
    chosen = jnp.where(own_pos == col_group, 1.0, 0.0)
    own_set = jnp.sum(chosen * set_col, axis=1, keepdims=True)
    masks[0:32, :] = chosen
    masks[32:64, :] = jnp.where(set_col == own_set, 1.0, 0.0)

    lane_lo = lax.broadcasted_iota(jnp.int32, (1, 128), 1) < HD

    def side(v, hh):
        return jnp.where(lane_lo if hh == 0 else jnp.logical_not(lane_lo), v, jnp.zeros_like(v))

    def exchange(e, b, parity):
        slot = 0 if e == 0 else 1 + b
        rows = rows_at(b * BLK[e], BLK[e]) if not isinstance(b, int) else pl.ds(b * BLK[e], BLK[e])
        return pltpu.make_async_remote_copy(
            src_ref=EXS[e].at[rows],
            dst_ref=EXR[e].at[parity, rows],
            send_sem=exs_sem.at[slot],
            recv_sem=exr_sem.at[parity, slot],
            device_id=partner,
            device_id_type=MESH_ID,
        )

    def block_rows(e, b):
        if e == 0:
            return pl.ds(0, BLK[0])
        return rows_at(b * BLK[1], BLK[1], BLK[1])

    def blocks(e, body):
        if e == 0:
            body(0)
        else:
            pl.loop(0, 2)(body)

    def project(e, b, which):
        rows = block_rows(e, b)
        xb = X[e][rows, :]
        for j in which:
            cols = pl.ds(j * COLS, COLS)
            got = dot(xb, win[e, :, cols])
            if j == 0:
                got = (got + pin[e * 2 : e * 2 + 1, :]).astype(BF16) * jnp.asarray(HD**-0.5, BF16)
            elif j == 2:
                got = got + pin[e * 2 + 1 : e * 2 + 2, :]
            QKV[e][rows, cols] = got.astype(BF16)

    def attend(e, b):
        size = BLK[e]
        rows = block_rows(e, b)
        col = lax.broadcasted_iota(jnp.int32, (size, size), 1)
        if e == 0:
            row = lax.broadcasted_iota(jnp.int32, (size, size), 0)
            first = jnp.logical_and(row < 64, col < qlen[0])
            second = jnp.logical_and(
                row >= 64, jnp.logical_and(col >= 64, col < 64 + qlen[1])
            )
            seen = jnp.logical_or(first, second)
        else:
            seen = col < plen[b]

        @pl.loop(0, 3)
        def _(pair):
            q2 = QKV[e][rows, rows_at(pair * 128, 128, 128)]
            k2 = QKV[e][rows, rows_at(COLS + pair * 128, 128, 128)]
            v2 = QKV[e][rows, rows_at(2 * COLS + pair * 128, 128, 128)]
            total = jnp.zeros((size, 128), F32)
            for hh in range(2):
                s = dot_t(side(q2, hh), k2)
                s = jnp.where(seen, s, NEGATIVE)
                p = jnp.exp(s - jnp.max(s, axis=-1, keepdims=True))
                p = (p * (1.0 / jnp.sum(p, axis=-1, keepdims=True))).astype(BF16)
                PR[e][b, pair * 2 + hh] = p
                total = total + dot(p, side(v2, hh))
            BALL[e][rows, rows_at(8 * COLS + pair * 128, 128, 128)] = total.astype(BF16)

        ctx = BALL[e][rows, pl.ds(8 * COLS, COLS)]
        EXS[e][rows, :] = dot(ctx, wo[e]).astype(BF16)
        exchange(e, b, 0).start()

    CH = 32

    def first_norm(e, b):
        exchange(e, b, 0).wait()

        @pl.loop(0, BLK[e] // CH)
        def _(c):
            rows = rows_at(b * BLK[e] + c * CH, CH, CH)
            v = (
                X[e][rows, :].astype(F32)
                + (EXS[e][rows, :].astype(F32) + EXR[e][0, rows, :].astype(F32))
                + par[e * 8 : e * 8 + 1, :]
            )
            v = v - row_mean(v)
            inv = lax.rsqrt(row_mean(v * v) + EPSILON)
            n = v * inv
            N1[e][rows, :] = n
            I1[e][rows, :] = inv
            HID[e][rows, :] = (
                n * par[e * 8 + 2 : e * 8 + 3, :] + par[e * 8 + 4 : e * 8 + 5, :]
            ).astype(BF16)

    def feed(e, b):
        rows = block_rows(e, b)

        @pl.loop(0, 6)
        def _(n):
            cols = rows_at(n * 256, 256, 256)
            u = dot(HID[e][rows, :], wf[e, :, cols]) + pfi[e : e + 1, cols]
            a, slope = gelu_and_slope(u)
            BALL[e][rows, cols] = a.astype(BF16)
            SLOPE[e][rows, cols] = slope.astype(BF16)

        @pl.loop(0, 3)
        def _(n):
            cols = rows_at(n * 256, 256, 256)
            EXS[e][rows, cols] = dot(BALL[e][rows, pl.ds(0, FF_HERE)], wd[e, :, cols]).astype(BF16)

        exchange(e, b, 1).start()

    def second_norm(e, b):
        exchange(e, b, 1).wait()

        @pl.loop(0, BLK[e] // CH)
        def _(c):
            rows = rows_at(b * BLK[e] + c * CH, CH, CH)
            v = (
                HID[e][rows, :].astype(F32)
                + (EXS[e][rows, :].astype(F32) + EXR[e][1, rows, :].astype(F32))
                + par[e * 8 + 1 : e * 8 + 2, :]
            )
            v = v - row_mean(v)
            inv = lax.rsqrt(row_mean(v * v) + EPSILON)
            n = v * inv
            N2[e][rows, :] = n
            I2[e][rows, :] = inv
            OB[e][rows, :] = (
                n * par[e * 8 + 3 : e * 8 + 4, :] + par[e * 8 + 5 : e * 8 + 6, :]
            ).astype(BF16)

    def mini_exchange(k):
        return pltpu.make_async_remote_copy(
            src_ref=xms.at[k],
            dst_ref=xmr.at[k],
            send_sem=xms_sem.at[k],
            recv_sem=xmr_sem.at[k],
            device_id=partner,
            device_id_type=MESH_ID,
        )

    def first_rows(ref):
        rows = [ref[b * 256 : b * 256 + 16, :].astype(F32)[0:1] for b in range(2)]
        return jnp.concatenate([*rows, jnp.zeros((14, rows[0].shape[1]), F32)], axis=0)

    def mini_attend():
        xm = first_rows(xp).astype(BF16)
        q = (dot(xm, win[1, :, pl.ds(0, COLS)]) + pin[2:3, :]).astype(BF16).astype(F32) * HD**-0.5
        of_head = lax.broadcasted_iota(jnp.int32, (16, COLS), 1) // HD == lax.broadcasted_iota(
            jnp.int32, (16, COLS), 0
        )
        col = lax.broadcasted_iota(jnp.int32, (16, 256), 1)
        rows = []
        for b in range(2):
            keys = qkvp[b * 256 : (b + 1) * 256, COLS : 2 * COLS]
            vals = qkvp[b * 256 : (b + 1) * 256, 2 * COLS : 3 * COLS]
            s = dot_t(jnp.where(of_head, q[b : b + 1], 0.0).astype(BF16), keys)
            s = jnp.where(col < plen[b], s, NEGATIVE)
            p = jnp.exp(s - jnp.max(s, axis=-1, keepdims=True))
            p = (p * (1.0 / jnp.sum(p, axis=-1, keepdims=True))).astype(BF16)
            rows.append(jnp.sum(jnp.where(of_head, dot(p, vals), 0.0), axis=0, keepdims=True))
        ctx = jnp.concatenate([*rows, jnp.zeros((14, COLS), F32)], axis=0)
        xms[0] = dot(ctx.astype(BF16), wo[1]).astype(BF16)
        mini_exchange(0).start()

    def mini_norm(k, v):
        mini_exchange(k).wait()
        v = v + (xms[k].astype(F32) + xmr[k].astype(F32)) + par[8 + k : 9 + k, :]
        v = v - row_mean(v)
        n = v * lax.rsqrt(row_mean(v * v) + EPSILON)
        return (n * par[10 + k : 11 + k, :] + par[12 + k : 13 + k, :]).astype(BF16)

    def mini_feed():
        hm[...] = mini_norm(0, first_rows(xp))

        @pl.loop(0, 6)
        def _(n):
            cols = rows_at(n * 256, 256, 256)
            u = dot(hm[...], wf[1, :, cols]) + pfi[1:2, cols]
            am[:, cols] = gelu_and_slope(u)[0].astype(BF16)

        @pl.loop(0, 3)
        def _(n):
            cols = rows_at(n * 256, 256, 256)
            xms[1, :, cols] = dot(am[...], wd[1, :, cols]).astype(BF16)

        mini_exchange(1).start()

    def transpose_into(e, k, src, b):
        rows = block_rows(e, b)

        @pl.loop(0, 2)
        def _(c):
            tile = src[rows, rows_at(c * COLS, COLS, 128)].T
            AT[e][k, pl.ds(c * 2, 2), :, :, :, rows] = tile.reshape(2, 2, 2, ROWS_OUT, BLK[e])

    def left_factor(axis, k):
        return pltpu.make_async_remote_copy(
            src_ref=atq.at[k, :, :, 1 - x] if axis == 0 else atq.at[k, :, 1 - y],
            dst_ref=fra.at[axis, k],
            send_sem=fas_sem.at[axis, k],
            recv_sem=far_sem.at[axis, k],
            device_id=first_dev[axis],
            device_id_type=MESH_ID,
        )

    def right_factor(axis, pair):
        return pltpu.make_async_remote_copy(
            src_ref=ballq.at[:, pl.ds((pair * 2 + axis) * COLS, COLS)],
            dst_ref=frb.at[axis, pair],
            send_sem=fbs_sem.at[axis, pair],
            recv_sem=fbr_sem.at[axis, pair],
            device_id=first_dev[axis],
            device_id_type=MESH_ID,
        )

    first_dev, other_dev = (at_x, at_y), (at_y, at_x)
    first_at, other_at = (x, y), (y, x)

    need(0, 1, 2, 3, 8)
    pl.semaphore_wait(barrier, 16)
    project(0, 0, (0, 1, 2))
    attend(0, 0)
    right_factor(0, 4).start()
    need(4, 5, 6, 7, 9)
    blocks(1, lambda b: project(1, b, (1, 2)))
    mini_attend()
    transpose_into(0, 3, xq, 0)
    left_factor(0, 3).start()
    left_factor(1, 3).start()
    first_norm(0, 0)
    need(10, 12)
    feed(0, 0)
    for axis in range(2):
        for pair in range(2):
            right_factor(axis, pair).start()
    need(11, 13)
    mini_feed()
    transpose_into(0, 1, hq, 0)
    left_factor(0, 1).start()
    left_factor(1, 1).start()
    second_norm(0, 0)
    out_q = pltpu.make_async_copy(obq, oq_out, out_sem.at[0])
    out_p = pltpu.make_async_copy(obp, op_out, out_sem.at[1])
    out_q.start()
    mini_out = mini_norm(1, hm[...].astype(F32)).astype(F32)

    pieces = []
    rows = [obq[at : at + 16, :].astype(F32)[0:1] for at in (0, 64)]
    for head in (*rows, mini_out[0:1], mini_out[1:2]):
        pieces += [head[:, k * 256 : (k + 1) * 256] for k in range(3)]
    pieces.append(jnp.zeros((4, 256), F32))
    hg[me] = jnp.concatenate(pieces, axis=0).astype(BF16)

    def heads(k):
        return pltpu.make_async_remote_copy(
            src_ref=hg.at[me],
            dst_ref=hg.at[me],
            send_sem=hgs_sem.at[k],
            recv_sem=hgr_sem.at[k],
            device_id=at_dp(me ^ k),
            device_id_type=MESH_ID,
        )

    for k in range(1, 16):
        heads(k).start()
    need(14, 15)
    blocks(1, lambda b: project(1, b, (0,)))
    attend(1, 0)
    for k in range(1, 16):
        copy = pltpu.make_async_remote_copy(
            src_ref=hg.at[me],
            dst_ref=hg.at[me ^ k],
            send_sem=hgs_sem.at[k],
            recv_sem=hgr_sem.at[k],
            device_id=at_dp(me ^ k),
            device_id_type=MESH_ID,
        )
        copy.wait()
    gathered = hg[...].astype(F32).reshape(256, 256)
    hf[0] = gathered[:, 0:128]
    hf[1] = gathered[:, 128:256]

    def all_heads(first):
        groups = []
        for i in range(2):
            parts = [
                hf[c, pl.ds(first + i * 3 + k, 16, stride=16), :] for k in range(3) for c in range(2)
            ]
            groups.append(jnp.concatenate(parts, axis=1))
        return jnp.concatenate(groups, axis=0)

    heads_q, heads_p = all_heads(0), all_heads(6)
    gain = score_gain * D ** (-0.5)
    class_scores = dot_t(heads_q.astype(BF16), heads_p.astype(BF16)) * gain
    chosen = masks[0:32, :]
    logits = jnp.where(masks[32:64, :] > 0.5, class_scores, NEGATIVE)
    top = jnp.max(logits, axis=1, keepdims=True)
    log_total = top + jnp.log(jnp.sum(jnp.exp(logits - top), axis=1, keepdims=True))
    target = jnp.sum(chosen * class_scores, axis=1, keepdims=True)
    loss = jnp.sum(log_total - target, axis=0, keepdims=True) * (1.0 / 32)
    loss_out[...] = jnp.broadcast_to(loss, loss_out.shape)
    d_class = (jnp.exp(logits - log_total) - chosen) * gain
    dh[0:32, :] = lax.dot_general(
        d_class, heads_p, (((1,), (0,)), ((), ())), precision=HIGHEST, preferred_element_type=F32
    )
    dh[32:64, :] = lax.dot_general(
        d_class, heads_q, (((0,), (0,)), ((), ())), precision=HIGHEST, preferred_element_type=F32
    )

    def norm_back(incoming, n, inv, scale):
        scaled = incoming * scale
        return inv * (scaled - row_mean(scaled) - n * row_mean(scaled * n))

    def second_back(e, b):
        row0 = lax.broadcasted_iota(jnp.int32, (CH, 1), 0)
        seqs = 2 if e == 0 else 1
        length = 64 if e == 0 else 256
        for i in range(seqs):
            group = i if e == 0 else b
            extra = dh[pl.ds(e * 32 + group * 16 + me, 1), :]

            @pl.loop(0, length // CH)
            def _(c):
                rows = rows_at(group * length + c * CH, CH, CH)
                add = jnp.where(row0 + c * CH == 0, extra, 0.0)
                d = COT[e][rows, :].astype(F32) + add
                n = N2[e][rows, :]
                out = norm_back(d, n, I2[e][rows, :], par[e * 8 + 3 : e * 8 + 4, :])
                N2[e][rows, :] = out
                low = out.astype(BF16)
                DD[e][rows, :] = low
                acc_s[e * 6 + 1] += fold8(d * n)
                acc_s[e * 6 + 3] += fold8(d)
                acc_s[e * 6 + 5] += fold8(low.astype(F32))

        transpose_into(e, 0, DD[e], b)

    def feed_back(e, b):
        rows = block_rows(e, b)

        @pl.loop(0, 6)
        def _(n):
            cols = rows_at(n * 256, 256, 256)
            d = dot_t(DD[e][rows, :], wd[e, cols, :]) * SLOPE[e][rows, cols].astype(F32)
            d = d.astype(BF16)
            BALL[e][rows, rows_at(4 * COLS + n * 256, 256, 256)] = d
            acc_f[e, :, cols] += fold8(d.astype(F32))

        @pl.loop(0, 3)
        def _(n):
            cols = rows_at(n * 256, 256, 256)
            EXS[e][rows, cols] = dot_t(BALL[e][rows, pl.ds(4 * COLS, FF_HERE)], wf[e, cols, :]).astype(BF16)

        exchange(e, b, 0).start()
        if e == 1:
            transpose_into(e, 1, HID[e], b)

    def first_back(e, b):
        exchange(e, b, 0).wait()

        @pl.loop(0, BLK[e] // CH)
        def _(c):
            rows = rows_at(b * BLK[e] + c * CH, CH, CH)
            d = N2[e][rows, :] + (EXS[e][rows, :].astype(F32) + EXR[e][0, rows, :].astype(F32))
            n = N1[e][rows, :]
            out = norm_back(d, n, I1[e][rows, :], par[e * 8 + 2 : e * 8 + 3, :])
            N1[e][rows, :] = out
            low = out.astype(BF16)
            DD[e][rows, :] = low
            acc_s[e * 6 + 0] += fold8(d * n)
            acc_s[e * 6 + 2] += fold8(d)
            acc_s[e * 6 + 4] += fold8(low.astype(F32))

        transpose_into(e, 2, DD[e], b)

    def attend_back(e, b):
        rows = block_rows(e, b)
        size = BLK[e]
        DC[e][rows, :] = dot_t(DD[e][rows, :], wo[e]).astype(BF16)

        @pl.loop(0, 3)
        def _(pair):
            q2 = QKV[e][rows, rows_at(pair * 128, 128, 128)]
            k2 = QKV[e][rows, rows_at(COLS + pair * 128, 128, 128)]
            v2 = QKV[e][rows, rows_at(2 * COLS + pair * 128, 128, 128)]
            dc2 = DC[e][rows, rows_at(pair * 128, 128, 128)]
            dq = jnp.zeros((size, 128), F32)
            dk = jnp.zeros((size, 128), F32)
            dv = jnp.zeros((size, 128), F32)
            for hh in range(2):
                low = PR[e][b, pair * 2 + hh]
                p = low.astype(F32)
                dch = side(dc2, hh)
                dp = dot_t(dch, v2)
                ds = (p * (dp - jnp.sum(p * dp, axis=-1, keepdims=True))).astype(BF16)
                dv = dv + t_dot(low, dch)
                dq = dq + dot(ds, side(k2, hh))
                dk = dk + t_dot(ds, side(q2, hh))
            dq = (dq * HD**-0.5).astype(BF16)
            dv = dv.astype(BF16)
            cols = rows_at(pair * 128, 128, 128)
            BALL[e][rows, rows_at(9 * COLS + pair * 128, 128, 128)] = dq
            BALL[e][rows, rows_at(10 * COLS + pair * 128, 128, 128)] = dk.astype(BF16)
            BALL[e][rows, rows_at(11 * COLS + pair * 128, 128, 128)] = dv
            acc_b[e, :, cols] += fold8(dq.astype(F32))
            acc_b[e, :, rows_at(COLS + pair * 128, 128, 128)] += fold8(dv.astype(F32))

        if e == 1:
            transpose_into(e, 3, X[e], b)

    def token_back(e, b):
        rows = block_rows(e, b)

        @pl.loop(0, 3)
        def _(n):
            cols = rows_at(n * 256, 256, 256)
            EXS[e][rows, cols] = dot_t(BALL[e][rows, pl.ds(9 * COLS, 3 * COLS)], win[e, cols, :]).astype(BF16)

        exchange(e, b, 1).start()

    def token_end(e, b):
        exchange(e, b, 1).wait()

        @pl.loop(0, BLK[e] // CH)
        def _(c):
            rows = rows_at(b * BLK[e] + c * CH, CH, CH)
            OB[e][rows, :] = (
                N1[e][rows, :] + (EXS[e][rows, :].astype(F32) + EXR[e][1, rows, :].astype(F32))
            ).astype(BF16)

    def job_of(j):
        return j // 6, j % 6

    def product(half, blk, sel):
        k = jnp.where(blk < 8, blk // 4, jnp.where(blk == 8, 2, 3))
        rows = atp[k, :, :, sel] if half == 0 else atp[k, :, sel]
        out = dot(rows.reshape(COLS, TOKS[1]), ballp[:, rows_at(blk * COLS, COLS, 128)])
        return out.reshape(ZN, 2, ROWS_OUT, COLS)

    def pair_product(half, pair):
        blk = pair * 2 + half
        k = blk // 4 if blk < 8 else 2 if blk == 8 else 3
        rows = atq[k, :, :, x] if half == 0 else atq[k, :, y]
        rows = jnp.concatenate([rows.reshape(COLS, TOKS[0]), fra[half, k].reshape(COLS, TOKS[0])], axis=1)
        cols = jnp.concatenate([ballq[:, blk * COLS : (blk + 1) * COLS], frb[half, pair]], axis=0)
        return dot(rows, cols).reshape(ZN, 2, ROWS_OUT, COLS)

    def p1(j, half):
        return pltpu.make_async_remote_copy(
            src_ref=p1s.at[j % DS, half],
            dst_ref=p1r.at[j % D1, half],
            send_sem=p1s_sem.at[j % DS, half],
            recv_sem=p1r_sem.at[j % D1, half],
            device_id=first_dev[half],
            device_id_type=MESH_ID,
        )

    def other(j, half, line_first):
        mine, to = p1r.at[j % D1, half], p2r.at[j % D2, half]
        return pltpu.make_async_remote_copy(
            src_ref=mine.at[z, 1 - other_at[half]] if line_first else mine.at[:, 1 - other_at[half]],
            dst_ref=to.at[0] if line_first else to,
            send_sem=p2s_sem.at[j % D2, half],
            recv_sem=p2r_sem.at[j % D2, half],
            device_id=other_dev[half],
            device_id_type=MESH_ID,
        )

    def block(ref, j, half, d, line_first):
        return ref.at[j % DZ, half, d] if line_first else ref.at[j % DZ, half, d, 0]

    def own_block(j, half, d, line_first):
        return p1r.at[j % D1, half, d] if line_first else p2r.at[j % D2, half, d]

    def along(j, half, d, right, relayed, line_first):
        buf, send, recv = (zr, zrs_sem, zrr_sem) if right else (zl, zls_sem, zlr_sem)
        there = block(buf, j, half, d, line_first)
        return pltpu.make_async_remote_copy(
            src_ref=there if relayed else own_block(j, half, d, line_first),
            dst_ref=there,
            send_sem=send.at[j % DZ, half, d],
            recv_sem=recv.at[j % DZ, half, d],
            device_id=at_dp(me + 4 if right else me - 4),
            device_id_type=MESH_ID,
        )

    def total_of(a, b):
        return (a[...].astype(F32) + b[...].astype(F32)).astype(BF16)

    def step0(j):
        _, pair = job_of(j)
        for half in range(2):
            p1s[j % DS, half] = product(half, pair * 2 + half, 1 - first_at[half]).astype(BF16)
            p1(j, half).start()

    def step1(j):
        e_of, pair = job_of(j)

        @pl.when(e_of == 1)
        def _():
            for half in range(2):
                p1(j, half).wait()
            for half in range(2):
                own = product(half, pair * 2 + half, first_at[half])
                p1r[j % D1, half] = (own + p1r[j % D1, half].astype(F32)).astype(BF16)

        for p in range(6):

            @pl.when(jnp.logical_and(e_of == 0, pair == p))
            def _():
                for half in range(2):
                    if p in (0, 2):
                        left_factor(half, p // 2).wait()
                    elif p == 4:
                        left_factor(half, 2 + half).wait()
                    elif p == 5 and half == 0:
                        left_factor(0, 3).wait()
                    right_factor(half, p).wait()
                    p1r[j % D1, half] = pair_product(half, p).astype(BF16)

    def turn(j):
        for half in range(2):
            other(j, half, False).start()

    def turned(j):
        for half in range(2):
            other(j, half, False).wait()
            mine = p2r.at[j % D2, half]
            mine[...] = total_of(mine, p1r.at[j % D1, half, :, other_at[half]])

    def ends(j, line_first):
        @pl.when(z == 0)
        def _():
            for half in range(2):
                for d in (3, 2, 1):
                    along(j, half, d, True, False, line_first).start()

        @pl.when(z == 3)
        def _():
            for half in range(2):
                for d in (0, 1, 2):
                    along(j, half, d, False, False, line_first).start()

    def relay(j, half, d, right, line_first):
        held = block(zr if right else zl, j, half, d, line_first)
        along(j, half, d, right, True, line_first).wait_recv()
        held[...] = total_of(held, own_block(j, half, d, line_first))
        along(j, half, d, right, True, line_first).start()

    def middle1(j, line_first):
        @pl.when(z == 1)
        def _():
            for half in range(2):
                for d in (3, 2):
                    relay(j, half, d, True, line_first)

        @pl.when(z == 2)
        def _():
            for half in range(2):
                for d in (0, 1):
                    relay(j, half, d, False, line_first)

    def middle2(j, line_first):
        @pl.when(z == 2)
        def _():
            for half in range(2):
                relay(j, half, 3, True, line_first)

        @pl.when(z == 1)
        def _():
            for half in range(2):
                relay(j, half, 0, False, line_first)

    def line_end(j, line_first):
        for half in range(2):
            mine = own_block(j, half, z, line_first)

            @pl.when(z > 0)
            def _():
                along(j, half, z, True, True, line_first).wait_recv()
                mine[...] = total_of(mine, block(zr, j, half, z, line_first))

            @pl.when(z < 3)
            def _():
                along(j, half, z, False, True, line_first).wait_recv()
                mine[...] = total_of(mine, block(zl, j, half, z, line_first))

            for d in range(4):

                @pl.when(d > z)
                def _():
                    along(j, half, d, True, True, line_first).wait_send()

                @pl.when(d < z)
                def _():
                    along(j, half, d, False, True, line_first).wait_send()

    def pass_on(j):
        for half in range(2):
            other(j, half, True).start()

    def passed(j):
        for half in range(2):
            other(j, half, True).wait()

    def result(slot, half, to):
        return pltpu.make_async_copy(fin.at[slot, half], to, fin_sem.at[slot, half])

    def output(j, line_first):
        e_of, pair = job_of(j)
        for half in range(2):

            @pl.when(j >= 2)
            def _():
                result(j % 2, half, g_out.at[0]).wait()

            if line_first:
                total = p1r[j % D1, half, z, other_at[half]].astype(F32) + p2r[j % D2, half, 0].astype(F32)
            else:
                total = p2r[j % D2, half, z].astype(F32)
            fin[j % 2, half] = total
            for e in range(2):
                for p in range(6):

                    @pl.when(jnp.logical_and(e_of == e, pair == p))
                    def _():
                        blk = p * 2 + half
                        if blk < 4:
                            to = g_fo.at[e, :, pl.ds(blk * COLS, COLS)]
                        elif blk < 8:
                            to = g_fi.at[e, :, pl.ds((blk - 4) * COLS, COLS)]
                        elif blk == 8:
                            to = g_out.at[e]
                        else:
                            to = g_in.at[e, blk - 9]
                        result(j % 2, half, to).start()

    small_to = (at_x, at_y, at_dp(me ^ 4), at_dp(me ^ 8))

    def small(k):
        return pltpu.make_async_remote_copy(
            src_ref=smb.at[k],
            dst_ref=smr.at[k],
            send_sem=sms_sem.at[k],
            recv_sem=smr_sem.at[k],
            device_id=small_to[k],
            device_id_type=MESH_ID,
        )

    def small_first():
        smb[0] = jnp.zeros_like(smb[0])
        for e in range(2):
            for i in range(6):
                smb[0, e * 9 + i : e * 9 + i + 1, :] = jnp.sum(acc_s[e * 6 + i], axis=0, keepdims=True)
            smb[0, e * 9 + 6 : e * 9 + 7, :] = jnp.sum(acc_b[e], axis=0, keepdims=True)
            for i in range(2):
                smb[0, e * 9 + 7 + i : e * 9 + 8 + i, :] = jnp.sum(
                    acc_f[e, :, i * D : (i + 1) * D], axis=0, keepdims=True
                )
        small(0).start()

    def small_next(k):
        small(k).wait()
        if k < 3:
            smb[k + 1] = smb[k] + smr[k]
            small(k + 1).start()
        else:
            total = smb[k] + smr[k]
            sm_out[...] = jnp.zeros_like(sm_out)
            wide = pltpu.roll(total, lax.rem(D - me * ROWS_OUT, D), 1)
            sm_out[:, 0:ROWS_OUT] = wide[:, 0:ROWS_OUT]
            heads_own = pltpu.roll(total, lax.rem(D - me * 24, D), 1)
            feed_own = pltpu.roll(total, lax.rem(D - (me % 8) * 96, D), 1)
            for e in range(2):
                at = e * 9 + 6
                for i in range(2):
                    sm_out[at + i : at + i + 1, 0:24] = heads_own[at : at + 1, i * COLS : i * COLS + 24]
                low, high = feed_own[at + 1 : at + 2, 0:96], feed_own[at + 2 : at + 3, 0:96]
                sm_out[at + 2 : at + 3, 0:96] = jnp.where(me < 8, low, high)

    def q_second_back():
        second_back(0, 0)
        left_factor(0, 0).start()
        left_factor(1, 0).start()

    def q_feed_back():
        feed_back(0, 0)
        for axis in range(2):
            for pair in (2, 3):
                right_factor(axis, pair).start()

    def q_first_back():
        first_back(0, 0)
        left_factor(0, 2).start()

    def q_attend_back():
        attend_back(0, 0)
        right_factor(1, 4).start()
        right_factor(0, 5).start()
        right_factor(1, 5).start()

    def q_token_end():
        token_end(0, 0)
        pltpu.make_async_copy(obq, gq_out, out_sem.at[0]).start()

    def p_token_end():
        blocks(1, lambda b: token_end(1, b))
        pltpu.make_async_copy(obp, gp_out, out_sem.at[1]).start()

    def p_mid(b):
        first_norm(1, b)
        feed(1, b)

    def p_second():
        blocks(1, lambda b: second_norm(1, b))
        out_p.start()

    def passages(piece):
        return lambda: blocks(1, lambda b: piece(1, b))

    work = {
        0: [q_feed_back, lambda: attend(1, 1)],
        1: [q_first_back, lambda: p_mid(0)],
        2: [q_attend_back, lambda: p_mid(1)],
        3: [lambda: token_back(0, 0), p_second, out_q.wait],
        4: [q_token_end, passages(second_back)],
        5: [passages(feed_back)],
        6: [passages(first_back)],
        7: [passages(attend_back)],
        8: [passages(token_back)],
        9: [out_p.wait, p_token_end],
        10: [small_first],
        11: [lambda: small_next(0)],
        12: [lambda: small_next(1)],
        13: [lambda: small_next(2)],
        14: [lambda: small_next(3)],
    }

    def is_line_first(j):
        found = j == LINE_FIRST[0]
        for k in LINE_FIRST[1:]:
            found = jnp.logical_or(found, j == k)
        return found

    def steps(late, j):
        line_first = is_line_first(j)
        if late == 1:
            step1(j)

        @pl.when(line_first)
        def _():
            if late == 1:
                ends(j, True)
            elif late == 2:
                middle1(j, True)
            elif late == 3:
                middle2(j, True)
            elif late == 4:
                line_end(j, True)
                pass_on(j)
            else:
                passed(j)
                output(j, True)

        @pl.when(jnp.logical_not(line_first))
        def _():
            if late == 1:
                turn(j)
            elif late == 2:
                turned(j)
                ends(j, False)
            elif late == 3:
                middle1(j, False)
            elif late == 4:
                middle2(j, False)
            else:
                line_end(j, False)
                output(j, False)

    q_second_back()

    @pl.loop(0, JOBS + 5)
    def _(tick):
        for at, things in work.items():

            @pl.when(tick == at)
            def _():
                for thing in things:
                    thing()

        @pl.when(jnp.logical_and(tick >= 6, tick < JOBS))
        def _():
            step0(tick)

        for late in (5, 4, 3, 2, 1):

            @pl.when(jnp.logical_and(tick >= late, tick < JOBS + late))
            def _():
                steps(late, tick - late)

    pltpu.make_async_copy(obq, gq_out, out_sem.at[0]).wait()
    pltpu.make_async_copy(obp, gp_out, out_sem.at[1]).wait()
    for slot in range(2):
        for half in range(2):
            result(slot, half, g_out.at[0]).wait()


def finish_kernel(*refs):
    oq, op, gq, gp, g_in, g_out, g_fi, g_fo, loss, sums = refs[:10]
    large, (loss_to, in_bias, fi_bias, bo, gain, shift) = refs[10:18], refs[18:24]
    held, in_sems, out_sems = refs[24:32], refs[32], refs[33]
    sources = (oq, op, gq, gp, g_in, g_out, g_fi, g_fo)
    loads = [pltpu.make_async_copy(sources[i], held[i], in_sems.at[i]) for i in range(8)]
    stores = [pltpu.make_async_copy(held[i], large[i], out_sems.at[i]) for i in range(8)]
    for load in loads:
        load.start()
    loss_to[...] = loss[0:1, 0:1]
    for e in range(2):
        at = e * 9
        gain[e] = sums[at : at + 2, 0:ROWS_OUT]
        shift[e] = sums[at + 2 : at + 4, 0:ROWS_OUT]
        bo[e] = sums[at + 4 : at + 6, 0:ROWS_OUT]
        in_bias[e] = sums[at + 6 : at + 8, 0:24]
        fi_bias[e : e + 1] = sums[at + 8 : at + 9, 0:96]
    for load, store in zip(loads, stores):
        load.wait()
        store.start()
    for store in stores:
        store.wait()


FF_HERE = 1536


def fused(
    question_tokens, passage_tokens, question_cotangent, passage_cotangent,
    question_lengths, passage_lengths, dataset_ids, positives,
    attn_in, attn_in_bias, attn_out, ffn_in, ffn_in_bias, ffn_out, out_biases, norm_gains, norm_shifts,
):
    any_spec = pl.BlockSpec(memory_space=pl.ANY)
    vmem = pl.BlockSpec(memory_space=pltpu.VMEM)
    smem = pl.BlockSpec(memory_space=pltpu.SMEM)

    def both(shape, dtype):
        return [pltpu.VMEM(shape(m), dtype) for m in TOKS]

    shape = jax.ShapeDtypeStruct
    dma = pltpu.SemaphoreType.DMA
    outs = pl.pallas_call(
        partial(fused_kernel, last=0),
        name="fused",
        in_specs=[any_spec] * 4 + [smem] * 4 + [any_spec, vmem, any_spec, any_spec, vmem, any_spec] + [vmem] * 3,
        out_specs=[any_spec, any_spec, vmem] + [any_spec] * 6 + [vmem],
        out_shape=[
            shape((128, D), BF16),
            shape((512, D), BF16),
            shape((8, 128), F32),
            shape((128, D), BF16),
            shape((512, D), BF16),
            shape((2, 3, ROWS_OUT, COLS), F32),
            shape((2, ROWS_OUT, COLS), F32),
            shape((2, ROWS_OUT, FF_HERE), F32),
            shape((2, ROWS_OUT, FF_HERE), F32),
            shape((SMALL, 128), F32),
        ],
        scratch_shapes=[
            pltpu.VMEM((2, D, 3 * COLS), BF16),
            pltpu.VMEM((2, COLS, D), BF16),
            pltpu.VMEM((2, D, FF_HERE), BF16),
            pltpu.VMEM((2, FF_HERE, D), BF16),
            *both(lambda m: (m, D), BF16),
            *both(lambda m: (m, D), BF16),
            *both(lambda m: (m, 3 * COLS), BF16),
            pltpu.VMEM((1, 6, 128, 128), BF16),
            pltpu.VMEM((2, 6, 256, 256), BF16),
            *both(lambda m: (m, D), BF16),
            *both(lambda m: (m, D), F32),
            *both(lambda m: (m, D), F32),
            *both(lambda m: (m, 1), F32),
            *both(lambda m: (m, 1), F32),
            *both(lambda m: (m, FF_HERE), BF16),
            *both(lambda m: (m, D), BF16),
            *both(lambda m: (m, D), BF16),
            *both(lambda m: (m, COLS), BF16),
            *both(lambda m: (m, 12 * COLS), BF16),
            *both(lambda m: (4, ZN, 2, 2, ROWS_OUT, m), BF16),
            *both(lambda m: (m, D), BF16),
            *both(lambda m: (2, m, D), BF16),
            pltpu.VMEM((16, D), F32),
            pltpu.VMEM((8, COLS), F32),
            pltpu.VMEM((8, FF_HERE), F32),
            pltpu.VMEM((64, 32), F32),
            pltpu.VMEM((16, 16, 256), BF16),
            pltpu.VMEM((2, 256, 128), F32),
            pltpu.VMEM((64, D), F32),
            pltpu.VMEM((12, 8, D), F32),
            pltpu.VMEM((2, 8, 2 * COLS), F32),
            pltpu.VMEM((2, 8, FF_HERE), F32),
            pltpu.VMEM((4, SMALL, D), F32),
            pltpu.VMEM((4, SMALL, D), F32),
            pltpu.VMEM((DS, 2, ZN, 2, ROWS_OUT, COLS), BF16),
            pltpu.VMEM((D1, 2, ZN, 2, ROWS_OUT, COLS), BF16),
            pltpu.VMEM((D2, 2, ZN, ROWS_OUT, COLS), BF16),
            pltpu.VMEM((DZ, 2, ZN, 2, ROWS_OUT, COLS), BF16),
            pltpu.VMEM((DZ, 2, ZN, 2, ROWS_OUT, COLS), BF16),
            pltpu.VMEM((2, 2, ROWS_OUT, COLS), F32),
            pltpu.VMEM((2, 4, ZN, 2, ROWS_OUT, TOKS[0]), BF16),
            pltpu.VMEM((2, 6, TOKS[0], COLS), BF16),
            pltpu.VMEM((2, 16, D), BF16),
            pltpu.VMEM((2, 16, D), BF16),
            pltpu.VMEM((16, D), BF16),
            pltpu.VMEM((16, FF_HERE), BF16),
            dma((2, 2)),
            dma((16,)),
            dma((2,)),
            dma((3,)),
            dma((2, 3)),
            dma((16,)),
            dma((16,)),
            dma((4,)),
            dma((4,)),
            dma((DS, 2)),
            dma((D1, 2)),
            dma((D2, 2)),
            dma((D2, 2)),
            dma((DZ, 2, ZN)),
            dma((DZ, 2, ZN)),
            dma((DZ, 2, ZN)),
            dma((DZ, 2, ZN)),
            dma((2, 4)),
            dma((2, 4)),
            dma((2, 6)),
            dma((2, 6)),
            dma((2,)),
            dma((2,)),
        ],
        compiler_params=pltpu.CompilerParams(
            collective_id=0, has_side_effects=True, vmem_limit_bytes=VMEM_BYTES
        ),
    )(
        question_tokens.reshape(128, D),
        passage_tokens.reshape(512, D),
        question_cotangent.reshape(128, D),
        passage_cotangent.reshape(512, D),
        question_lengths, passage_lengths, dataset_ids, positives,
        attn_in.transpose(0, 2, 1, 3), attn_in_bias, attn_out, ffn_in, ffn_in_bias, ffn_out,
        out_biases, norm_gains, norm_shifts,
    )
    oq, op, loss, gq, gp, g_in, g_out, g_fi, g_fo, sums = outs
    large = (oq, op, gq, gp, g_in, g_out, g_fi, g_fo)
    small = [(1, 1), (2, 2, 24), (2, 96), (2, 2, ROWS_OUT), (2, 2, ROWS_OUT), (2, 2, ROWS_OUT)]
    oq, op, gq, gp, g_in, g_out, g_fi, g_fo, loss, in_bias, fi_bias, bo, gain, shift = pl.pallas_call(
        finish_kernel,
        name="finish",
        in_specs=[any_spec] * 8 + [vmem] * 2,
        out_specs=[any_spec] * 8 + [vmem] * 6,
        out_shape=[shape(a.shape, a.dtype) for a in large] + [shape(dims, F32) for dims in small],
        scratch_shapes=[*[pltpu.VMEM(a.shape, a.dtype) for a in large], dma((8,)), dma((8,))],
        compiler_params=pltpu.CompilerParams(vmem_limit_bytes=VMEM_BYTES),
    )(*large, loss, sums)
    return (
        oq.reshape(2, 64, D),
        op.reshape(2, 256, D),
        loss.reshape(()),
        gq.reshape(2, 64, D),
        gp.reshape(2, 256, D),
        g_in.transpose(0, 2, 1, 3),
        in_bias,
        g_out.transpose(0, 2, 1),
        g_fi,
        fi_bias,
        g_fo.transpose(0, 2, 1),
        bo,
        gain,
        shift,
    )


VMEM_BYTES = 62 * 1024 * 1024


def solution(mesh):
    in_specs = (
        P("dp", None, None),
        P("dp", None, None),
        P("dp", None, None),
        P("dp", None, None),
        P("dp"),
        P("dp"),
        P(),
        P(),
        P(None, None, None, "tensor"),
        P(None, None, "tensor"),
        P(None, "tensor", None),
        P(None, None, "tensor"),
        P(None, "tensor"),
        P(None, "tensor", None),
        P(),
        P(),
        P(),
    )
    out_specs = (
        P("dp", None, None),
        P("dp", None, None),
        P(),
        P("dp", None, None),
        P("dp", None, None),
        P(None, "dp", None, "tensor"),
        P(None, None, ("tensor", "dp")),
        P(None, "tensor", "dp"),
        P(None, "dp", "tensor"),
        P(None, ("tensor", "dp")),
        P(None, "tensor", "dp"),
        P(None, None, "dp"),
        P(None, None, "dp"),
        P(None, None, "dp"),
    )
    step = fused if mesh.shape["dp"] == 4 * ZN and mesh.shape["tensor"] == 2 else per_device
    return jax.shard_map(
        step, mesh=mesh, in_specs=in_specs, out_specs=out_specs, check_vma=False
    )
```

```python
from functools import partial

import jax
import jax.numpy as jnp
from jax import lax
from jax.experimental import pallas as pl
from jax.experimental.pallas import tpu as pltpu
from jax.sharding import PartitionSpec as P

D = 768
HD = 64


EPSILON = 1e-06
NEGATIVE = -1e30
HIGHEST = lax.Precision.HIGHEST
score_gain = 3.0


def norm_forward(summed, scale_row, shift_row):
    row_mean = jnp.mean(summed, axis=-1, keepdims=True)
    centred = summed - row_mean
    inv_std = lax.rsqrt(jnp.mean(centred * centred, axis=-1, keepdims=True) + EPSILON)
    normed = centred * inv_std
    return (normed * scale_row + shift_row, normed, inv_std)


def norm_backward(incoming, normed, inv_std, scale_row):
    scaled = incoming * scale_row
    outgoing = inv_std * (
        scaled
        - jnp.mean(scaled, axis=-1, keepdims=True)
        - normed * jnp.mean(scaled * normed, axis=-1, keepdims=True)
    )
    return (outgoing, jnp.sum(incoming * normed, axis=(0, 1)), jnp.sum(incoming, axis=(0, 1)))


def key_visible(lengths, length):
    positions = jnp.arange(length, dtype=jnp.int32)
    return (positions[None, :] < lengths[:, None])[:, None, None, :]


def head_scores(queries, key_rows, visible):
    raw_scores = jnp.einsum(
        "bqhe,bkhe->bhqk", queries, key_rows, preferred_element_type=jnp.float32
    ) * HD ** (-0.5)
    return jnp.where(visible, raw_scores, NEGATIVE)


def split_heads(matrix):
    return matrix.reshape(matrix.shape[0], matrix.shape[1], matrix.shape[2] // HD, HD)


def join_heads(per_head):
    return per_head.reshape(
        per_head.shape[0], per_head.shape[1], per_head.shape[2] * per_head.shape[3]
    )


def encoder_forward(tokens, lengths, params):
    (
        attn_in,
        attn_in_bias,
        attn_out,
        ffn_in,
        ffn_in_bias,
        ffn_out,
        out_biases,
        norm_gains,
        norm_shifts,
    ) = params
    projected = jnp.einsum("bld,dce->blce", tokens, attn_in, preferred_element_type=jnp.float32)
    in_bias = attn_in_bias.astype(jnp.float32)
    queries = split_heads((projected[:, :, 0] + in_bias[0]).astype(jnp.bfloat16))
    key_rows = split_heads(projected[:, :, 1].astype(jnp.bfloat16))
    values = split_heads((projected[:, :, 2] + in_bias[1]).astype(jnp.bfloat16))
    visible = key_visible(lengths, tokens.shape[1])
    scores = head_scores(queries, key_rows, visible)
    row_top = jnp.max(scores, axis=-1, keepdims=True)
    log_total = row_top + jnp.log(jnp.sum(jnp.exp(scores - row_top), axis=-1, keepdims=True))
    attn_probs = jnp.exp(scores - log_total).astype(jnp.bfloat16)
    context = join_heads(
        jnp.einsum(
            "bhqk,bkhe->bqhe", attn_probs, values, preferred_element_type=jnp.float32
        ).astype(jnp.bfloat16)
    )
    attn_part = jnp.einsum("ble,ed->bld", context, attn_out, preferred_element_type=jnp.float32)
    attn_sum = lax.psum(attn_part.astype(jnp.bfloat16), "tensor").astype(jnp.float32)
    bias_rows = out_biases.astype(jnp.float32)
    gain_rows = norm_gains.astype(jnp.float32)
    shift_rows = norm_shifts.astype(jnp.float32)
    hidden_float, normed_first, inv_first = norm_forward(
        tokens.astype(jnp.float32) + attn_sum + bias_rows[0], gain_rows[0], shift_rows[0]
    )
    hidden = hidden_float.astype(jnp.bfloat16)
    up_pre = jnp.einsum(
        "bld,df->blf", hidden, ffn_in, preferred_element_type=jnp.float32
    ) + ffn_in_bias.astype(jnp.float32)
    activated = jax.nn.gelu(up_pre, approximate=False).astype(jnp.bfloat16)
    down_part = jnp.einsum("blf,fd->bld", activated, ffn_out, preferred_element_type=jnp.float32)
    down_sum = lax.psum(down_part.astype(jnp.bfloat16), "tensor").astype(jnp.float32)
    outputs, normed_second, inv_second = norm_forward(
        hidden.astype(jnp.float32) + down_sum + bias_rows[1], gain_rows[1], shift_rows[1]
    )
    saved = (
        tokens,
        queries,
        key_rows,
        values,
        log_total,
        context,
        normed_first,
        inv_first,
        hidden,
        up_pre,
        activated,
        normed_second,
        inv_second,
    )
    return (outputs, saved)


def encoder_backward(incoming, saved, lengths, params):
    (
        attn_in,
        attn_in_bias,
        attn_out,
        ffn_in,
        ffn_in_bias,
        ffn_out,
        out_biases,
        norm_gains,
        norm_shifts,
    ) = params
    (
        tokens,
        queries,
        key_rows,
        values,
        log_total,
        context,
        normed_first,
        inv_first,
        hidden,
        up_pre,
        activated,
        normed_second,
        inv_second,
    ) = saved
    groups_here, length, model_width = tokens.shape
    gain_rows = norm_gains.astype(jnp.float32)
    d_second, gain_second, shift_second = norm_backward(
        incoming, normed_second, inv_second, gain_rows[1]
    )
    d_down = d_second.astype(jnp.bfloat16)
    grad_ffn_out = jnp.einsum("blf,bld->fd", activated, d_down, preferred_element_type=jnp.float32)
    d_activated = jnp.einsum("bld,fd->blf", d_down, ffn_out, preferred_element_type=jnp.float32)
    gelu_pull = jax.vjp(partial(jax.nn.gelu, approximate=False), up_pre)[1]
    d_up = gelu_pull(d_activated)[0].astype(jnp.bfloat16)
    grad_ffn_in = jnp.einsum("bld,blf->df", hidden, d_up, preferred_element_type=jnp.float32)
    hidden_part = jnp.einsum("blf,df->bld", d_up, ffn_in, preferred_element_type=jnp.float32)
    d_hidden = d_second + lax.psum(hidden_part.astype(jnp.bfloat16), "tensor").astype(jnp.float32)
    d_first, gain_first, shift_first = norm_backward(
        d_hidden, normed_first, inv_first, gain_rows[0]
    )
    d_attn = d_first.astype(jnp.bfloat16)
    grad_attn_out = jnp.einsum("ble,bld->ed", context, d_attn, preferred_element_type=jnp.float32)
    d_context = split_heads(
        jnp.einsum("bld,ed->ble", d_attn, attn_out, preferred_element_type=jnp.float32).astype(
            jnp.bfloat16
        )
    )
    visible = key_visible(lengths, length)
    scores = head_scores(queries, key_rows, visible)
    probs_float = jnp.exp(scores - log_total)
    d_probs = jnp.einsum("bqhe,bkhe->bhqk", d_context, values, preferred_element_type=jnp.float32)
    d_values = jnp.einsum(
        "bhqk,bqhe->bkhe",
        probs_float.astype(jnp.bfloat16),
        d_context,
        preferred_element_type=jnp.float32,
    ).astype(jnp.bfloat16)
    d_scores = (
        probs_float * (d_probs - jnp.sum(probs_float * d_probs, axis=-1, keepdims=True))
    ).astype(jnp.bfloat16)
    d_queries = (
        jnp.einsum("bhqk,bkhe->bqhe", d_scores, key_rows, preferred_element_type=jnp.float32)
        * HD ** (-0.5)
    ).astype(jnp.bfloat16)
    d_keys = (
        jnp.einsum("bhqk,bqhe->bkhe", d_scores, queries, preferred_element_type=jnp.float32)
        * HD ** (-0.5)
    ).astype(jnp.bfloat16)
    query_grad = join_heads(d_queries)
    value_grad = join_heads(d_values)
    d_projected = jnp.stack([query_grad, join_heads(d_keys), value_grad], axis=2)
    grad_attn_in = jnp.einsum(
        "bld,blce->dce", tokens, d_projected, preferred_element_type=jnp.float32
    )
    token_part = jnp.einsum(
        "blce,dce->bld", d_projected, attn_in, preferred_element_type=jnp.float32
    )
    d_tokens = (
        d_first + lax.psum(token_part.astype(jnp.bfloat16), "tensor").astype(jnp.float32)
    ).astype(jnp.bfloat16)
    grad_in_bias = jnp.stack(
        [
            jnp.sum(query_grad.astype(jnp.float32), axis=(0, 1)),
            jnp.sum(value_grad.astype(jnp.float32), axis=(0, 1)),
        ]
    )
    grad_ffn_bias = jnp.sum(d_up.astype(jnp.float32), axis=(0, 1))
    grad_out_biases = jnp.stack(
        [
            jnp.sum(d_attn.astype(jnp.float32), axis=(0, 1)),
            jnp.sum(d_down.astype(jnp.float32), axis=(0, 1)),
        ]
    )
    grad_gains = jnp.stack([gain_first, gain_second])
    grad_shifts = jnp.stack([shift_first, shift_second])
    return (
        d_tokens,
        (
            grad_attn_in,
            grad_in_bias,
            grad_attn_out,
            grad_ffn_in,
            grad_ffn_bias,
            grad_ffn_out,
            grad_out_biases,
            grad_gains,
            grad_shifts,
        ),
    )


def contrastive(question_rows, passage_rows, own_positive, dataset_ids):
    class_scores = jnp.einsum(
        "gd,jd->gj", question_rows, passage_rows, preferred_element_type=jnp.float32
    ) * (score_gain * D ** (-0.5))
    columns = jnp.arange(passage_rows.shape[0], dtype=jnp.int32)
    chosen = own_positive[:, None] == columns[None, :]
    own_set = jnp.sum(jnp.where(chosen, dataset_ids[None, :], 0), axis=1)
    logits = jnp.where(dataset_ids[None, :] == own_set[:, None], class_scores, NEGATIVE)
    row_top = jnp.max(logits, axis=1, keepdims=True)
    log_total = row_top + jnp.log(jnp.sum(jnp.exp(logits - row_top), axis=1, keepdims=True))
    target = jnp.sum(jnp.where(chosen, class_scores, 0.0), axis=1)
    d_class = (jnp.exp(logits - log_total) - chosen.astype(jnp.float32)) * (
        score_gain * D ** (-0.5)
    )
    return (log_total[:, 0] - target, d_class)


def per_device(
    question_tokens,
    passage_tokens,
    question_cotangent,
    passage_cotangent,
    question_lengths,
    passage_lengths,
    dataset_ids,
    positives,
    attn_in,
    attn_in_bias,
    attn_out,
    ffn_in,
    ffn_in_bias,
    ffn_out,
    out_biases,
    norm_gains,
    norm_shifts,
):

    def encoder_params(encoder):
        return (
            attn_in[encoder],
            attn_in_bias[encoder],
            attn_out[encoder],
            ffn_in[encoder],
            ffn_in_bias[encoder],
            ffn_out[encoder],
            out_biases[encoder],
            norm_gains[encoder],
            norm_shifts[encoder],
        )

    question_params = encoder_params(0)
    passage_params = encoder_params(1)
    question_float, question_saved = encoder_forward(
        question_tokens, question_lengths, question_params
    )
    passage_float, passage_saved = encoder_forward(passage_tokens, passage_lengths, passage_params)
    question_heads = question_float[:, 0].astype(jnp.bfloat16)
    passage_heads = passage_float[:, 0].astype(jnp.bfloat16)
    local_groups = question_heads.shape[0]
    own_start = lax.axis_index("dp") * local_groups
    all_passages = lax.all_gather(passage_heads, "dp", axis=0, tiled=True)
    own_positive = lax.dynamic_slice_in_dim(positives, own_start, local_groups)
    cross, d_class = contrastive(question_heads, all_passages, own_positive, dataset_ids)
    total = lax.psum(jnp.sum(cross), "dp")
    contrastive_loss = total / all_passages.shape[0]
    d_question_heads = jnp.einsum(
        "gj,jd->gd", d_class, all_passages.astype(jnp.float32), precision=HIGHEST
    )
    question_heads_float = question_heads.astype(jnp.float32)
    d_passage_heads = lax.psum_scatter(
        jnp.einsum("gj,gd->jd", d_class, question_heads_float, precision=HIGHEST),
        "dp",
        scatter_dimension=0,
        tiled=True,
    )
    d_question_out = question_cotangent.astype(jnp.float32).at[:, 0].add(d_question_heads)
    d_passage_out = passage_cotangent.astype(jnp.float32).at[:, 0].add(d_passage_heads)
    passage_grad, passage_weights = encoder_backward(
        d_passage_out, passage_saved, passage_lengths, passage_params
    )
    question_grad, question_weights = encoder_backward(
        d_question_out, question_saved, question_lengths, question_params
    )
    joined = (
        lax.psum_scatter(question_weights[0], "dp", scatter_dimension=0, tiled=True),
        lax.psum_scatter(question_weights[1], "dp", scatter_dimension=1, tiled=True),
        lax.psum_scatter(question_weights[2], "dp", scatter_dimension=1, tiled=True),
        lax.psum_scatter(question_weights[3], "dp", scatter_dimension=0, tiled=True),
        lax.psum_scatter(question_weights[4], "dp", scatter_dimension=0, tiled=True),
        lax.psum_scatter(question_weights[5], "dp", scatter_dimension=1, tiled=True),
        lax.psum_scatter(question_weights[6], "dp", scatter_dimension=1, tiled=True),
        lax.psum_scatter(question_weights[7], "dp", scatter_dimension=1, tiled=True),
        lax.psum_scatter(question_weights[8], "dp", scatter_dimension=1, tiled=True),
        lax.psum_scatter(passage_weights[0], "dp", scatter_dimension=0, tiled=True),
        lax.psum_scatter(passage_weights[1], "dp", scatter_dimension=1, tiled=True),
        lax.psum_scatter(passage_weights[2], "dp", scatter_dimension=1, tiled=True),
        lax.psum_scatter(passage_weights[3], "dp", scatter_dimension=0, tiled=True),
        lax.psum_scatter(passage_weights[4], "dp", scatter_dimension=0, tiled=True),
        lax.psum_scatter(passage_weights[5], "dp", scatter_dimension=1, tiled=True),
        lax.psum_scatter(passage_weights[6], "dp", scatter_dimension=1, tiled=True),
        lax.psum_scatter(passage_weights[7], "dp", scatter_dimension=1, tiled=True),
        lax.psum_scatter(passage_weights[8], "dp", scatter_dimension=1, tiled=True),
    )
    question_parts = joined[:9]
    passage_parts = joined[9:]
    stacked = [
        jnp.stack([question_piece, passage_piece])
        for question_piece, passage_piece in zip(question_parts, passage_parts)
    ]
    return (
        question_float.astype(jnp.bfloat16),
        passage_float.astype(jnp.bfloat16),
        contrastive_loss,
        question_grad,
        passage_grad,
        stacked[0],
        stacked[1],
        stacked[2],
        stacked[3],
        stacked[4],
        stacked[5],
        stacked[6],
        stacked[7],
        stacked[8],
    )


MESH_ID = pl.DeviceIdType.MESH
F32 = jnp.float32
BF16 = jnp.bfloat16
ZN = 4
ROWS_OUT = 48
JOBS = 12
COLS = 384
D1, D2, DZ, DS = 8, 8, 8, 2
LINE_FIRST = (6, 8, 9)
TOKS = (128, 512)
BLK = (128, 256)
SMALL = 24
CHUNK = 64
NORM_UNROLL = (2, 4)
UP_UNROLL = (6, 6)
DOWN_UNROLL = (3, 3)
PAIR_UNROLL = (3, 3)


def dot(a, b):
    return jnp.dot(a, b, preferred_element_type=F32)


def dot_t(a, b):
    return lax.dot_general(a, b, (((1,), (1,)), ((), ())), preferred_element_type=F32)


def t_dot(a, b):
    return lax.dot_general(a, b, (((0,), (0,)), ((), ())), preferred_element_type=F32)


def gelu_and_slope(u):
    size = jnp.abs(u)
    bell = jnp.exp(-0.5 * u * u)
    t = 1.0 / (1.0 + (0.3275911 * 0.7071067811865476) * size)
    poly = t * (
        0.127414796
        + t * (-0.142248368 + t * (0.7107068705 + t * (-0.7265760135 + t * 0.5307027145)))
    )
    tail = poly * bell
    phi = jnp.where(u >= 0.0, 1.0 - tail, tail)
    return u * phi, phi + u * bell * 0.3989422804014327


def row_mean(v):
    return jnp.sum(v, axis=-1, keepdims=True) * (1.0 / D)


def fold8(v):
    return jnp.sum(v.reshape(v.shape[0] // 8, 8, v.shape[1]), axis=0)


def rows_at(start, size, step=16):
    return pl.ds(pl.multiple_of(start, step), size)


def fused_kernel(
    xq_in, xp_in, cq_in, cp_in, qlen, plen, dsid, posi,
    win_in, bin_in, wo_in, wf_in, bfi_in, wd_in, bo_in, gain_in, shift_in,
    oq_out, op_out, loss_out, gq_out, gp_out, g_in, g_out, g_fi, g_fo, sm_out,
    win, wo, wf, wd, xq, xp, cq, cp, qkvq, qkvp, prq, prp, hq, hp, n1q, n1p, n2q, n2p,
    i1q, i1p, i2q, i2p, sq, sp, obq, obp, ddq, ddp, dcq, dcp, ballq, ballp, atq, atp,
    exsq, exsp, exrq, exrp, par, pin, pfi, masks, hg, hf, dh, acc_s, acc_b, acc_f, smb, smr,
    p1s, p1r, p2r, zb, fin, fra, frb, xms, xmr, hm,
    fin_sem, in_sem, out_sem, exs_sem, exr_sem, hgs_sem, hgr_sem, sms_sem, smr_sem,
    p1s_sem, p1r_sem, p2s_sem, p2r_sem, zrs_sem, zrr_sem, zls_sem, zlr_sem,
    fas_sem, far_sem, fbs_sem, fbr_sem, xms_sem, xmr_sem,
    *, last,
):
    me = lax.axis_index("dp")
    core = lax.axis_index("tensor")
    z, y, x = me // 4, (me // 2) % 2, me % 2
    partner = {"dp": me, "tensor": 1 - core}
    at_x = {"dp": me + 1 - 2 * x, "tensor": core}
    at_y = {"dp": me + 2 - 4 * y, "tensor": core}

    def at_dp(index):
        return {"dp": index, "tensor": core}

    X, COT, QKV, PR, HID = (xq, xp), (cq, cp), (qkvq, qkvp), (prq, prp), (hq, hp)
    N1, N2, I1, I2, SLOPE = (n1q, n1p), (n2q, n2p), (i1q, i1p), (i2q, i2p), (sq, sp)
    OB, DD, DC, BALL, AT = (obq, obp), (ddq, ddp), (dcq, dcp), (ballq, ballp), (atq, atp)
    EXS, EXR = (exsq, exsp), (exrq, exrp)

    loads = [
        (xq_in, xq),
        *[(win_in.at[0, j], win.at[0, :, pl.ds(j * COLS, COLS)]) for j in range(3)],
        (xp_in, xp),
        *[(win_in.at[1, j], win.at[1, :, pl.ds(j * COLS, COLS)]) for j in range(3)],
        (wo_in.at[0], wo.at[0]),
        (wo_in.at[1], wo.at[1]),
        (wf_in.at[0], wf.at[0]),
        (wf_in.at[1], wf.at[1]),
        (wd_in.at[0], wd.at[0]),
        (wd_in.at[1], wd.at[1]),
        (cq_in, cq),
        (cp_in, cp),
    ]
    loads = [pltpu.make_async_copy(s, d, in_sem.at[i]) for i, (s, d) in enumerate(loads)]
    for copy in loads:
        copy.start()
    ready = set()

    def need(*which):
        for i in which:
            if i not in ready:
                loads[i].wait()
                ready.add(i)

    barrier = pltpu.get_barrier_semaphore()
    pl.semaphore_signal(barrier, inc=1, device_id=partner, device_id_type=MESH_ID)
    for k in range(1, 16):
        pl.semaphore_signal(barrier, inc=1, device_id=at_dp(me ^ k), device_id_type=MESH_ID)

    for e in range(2):
        for i in range(2):
            par[e * 8 + i : e * 8 + i + 1, :] = bo_in[e].astype(F32)[i : i + 1]
            par[e * 8 + 2 + i : e * 8 + 3 + i, :] = gain_in[e].astype(F32)[i : i + 1]
            par[e * 8 + 4 + i : e * 8 + 5 + i, :] = shift_in[e].astype(F32)[i : i + 1]
            pin[e * 2 + i : e * 2 + i + 1, :] = bin_in[e].astype(F32)[i : i + 1]
        pfi[e : e + 1, :] = bfi_in[...].astype(F32)[e : e + 1]
    acc_s[...] = jnp.zeros_like(acc_s)
    acc_b[...] = jnp.zeros_like(acc_b)
    acc_f[...] = jnp.zeros_like(acc_f)

    r32 = lax.broadcasted_iota(jnp.int32, (32, 32), 0)
    c32 = lax.broadcasted_iota(jnp.int32, (32, 32), 1)
    own_pos = jnp.zeros((32, 32), F32)
    set_col = jnp.zeros((32, 32), F32)
    for g in range(32):
        at = (g % 2) * 16 + g // 2
        own_pos = jnp.where(r32 == at, posi[g].astype(F32), own_pos)
        set_col = jnp.where(c32 == at, dsid[g].astype(F32), set_col)
    col_group = ((c32 % 16) * 2 + c32 // 16).astype(F32)
    chosen = jnp.where(own_pos == col_group, 1.0, 0.0)
    own_set = jnp.sum(chosen * set_col, axis=1, keepdims=True)
    masks[0:32, :] = chosen
    masks[32:64, :] = jnp.where(set_col == own_set, 1.0, 0.0)

    lane_lo = lax.broadcasted_iota(jnp.int32, (1, 128), 1) < HD

    def side(v, hh):
        return jnp.where(lane_lo if hh == 0 else jnp.logical_not(lane_lo), v, jnp.zeros_like(v))

    def exchange(e, b, parity):
        slot = 0 if e == 0 else 1 + b
        rows = rows_at(b * BLK[e], BLK[e]) if not isinstance(b, int) else pl.ds(b * BLK[e], BLK[e])
        return pltpu.make_async_remote_copy(
            src_ref=EXS[e].at[rows],
            dst_ref=EXR[e].at[parity, rows],
            send_sem=exs_sem.at[slot],
            recv_sem=exr_sem.at[parity, slot],
            device_id=partner,
            device_id_type=MESH_ID,
        )

    def block_rows(e, b):
        if e == 0:
            return pl.ds(0, BLK[0])
        return rows_at(b * BLK[1], BLK[1], BLK[1])

    def blocks(e, body):
        if e == 0:
            body(0)
        else:
            pl.loop(0, 2)(body)

    def project(e, b, which):
        rows = block_rows(e, b)
        xb = X[e][rows, :]
        for j in which:
            cols = pl.ds(j * COLS, COLS)
            got = dot(xb, win[e, :, cols])
            if j == 0:
                got = (got + pin[e * 2 : e * 2 + 1, :]).astype(BF16) * jnp.asarray(HD**-0.5, BF16)
            elif j == 2:
                got = got + pin[e * 2 + 1 : e * 2 + 2, :]
            QKV[e][rows, cols] = got.astype(BF16)

    def attend(e, b):
        size = BLK[e]
        rows = block_rows(e, b)
        col = lax.broadcasted_iota(jnp.int32, (size, size), 1)
        if e == 0:
            row = lax.broadcasted_iota(jnp.int32, (size, size), 0)
            first = jnp.logical_and(row < 64, col < qlen[0])
            second = jnp.logical_and(
                row >= 64, jnp.logical_and(col >= 64, col < 64 + qlen[1])
            )
            seen = jnp.logical_or(first, second)
        else:
            seen = col < plen[b]

        @pl.loop(0, 3, unroll=PAIR_UNROLL[e])
        def _(pair):
            q2 = QKV[e][rows, rows_at(pair * 128, 128, 128)]
            k2 = QKV[e][rows, rows_at(COLS + pair * 128, 128, 128)]
            v2 = QKV[e][rows, rows_at(2 * COLS + pair * 128, 128, 128)]
            total = jnp.zeros((size, 128), F32)
            for hh in range(2):
                s = dot_t(side(q2, hh), k2)
                s = jnp.where(seen, s, NEGATIVE)
                p = jnp.exp(s - jnp.max(s, axis=-1, keepdims=True))
                p = (p * (1.0 / jnp.sum(p, axis=-1, keepdims=True))).astype(BF16)
                PR[e][b, pair * 2 + hh] = p
                total = total + dot(p, side(v2, hh))
            BALL[e][rows, rows_at(8 * COLS + pair * 128, 128, 128)] = total.astype(BF16)

        ctx = BALL[e][rows, pl.ds(8 * COLS, COLS)]
        EXS[e][rows, :] = dot(ctx, wo[e]).astype(BF16)
        exchange(e, b, 0).start()

    CH = CHUNK

    def first_norm(e, b):
        exchange(e, b, 0).wait()

        @pl.loop(0, BLK[e] // CH, unroll=NORM_UNROLL[e])
        def _(c):
            rows = rows_at(b * BLK[e] + c * CH, CH, CH)
            v = (
                X[e][rows, :].astype(F32)
                + (EXS[e][rows, :].astype(F32) + EXR[e][0, rows, :].astype(F32))
                + par[e * 8 : e * 8 + 1, :]
            )
            v = v - row_mean(v)
            inv = lax.rsqrt(row_mean(v * v) + EPSILON)
            n = v * inv
            N1[e][rows, :] = n
            I1[e][rows, :] = inv
            HID[e][rows, :] = (
                n * par[e * 8 + 2 : e * 8 + 3, :] + par[e * 8 + 4 : e * 8 + 5, :]
            ).astype(BF16)

    def feed(e, b):
        rows = block_rows(e, b)

        @pl.loop(0, 6, unroll=UP_UNROLL[e])
        def _(n):
            cols = rows_at(n * 256, 256, 256)
            u = dot(HID[e][rows, :], wf[e, :, cols]) + pfi[e : e + 1, cols]
            a, slope = gelu_and_slope(u)
            BALL[e][rows, cols] = a.astype(BF16)
            SLOPE[e][rows, cols] = slope.astype(BF16)

        @pl.loop(0, 3, unroll=DOWN_UNROLL[e])
        def _(n):
            cols = rows_at(n * 256, 256, 256)
            EXS[e][rows, cols] = dot(BALL[e][rows, pl.ds(0, FF_HERE)], wd[e, :, cols]).astype(BF16)

        exchange(e, b, 1).start()

    def second_norm(e, b):
        exchange(e, b, 1).wait()

        @pl.loop(0, BLK[e] // CH, unroll=NORM_UNROLL[e])
        def _(c):
            rows = rows_at(b * BLK[e] + c * CH, CH, CH)
            v = (
                HID[e][rows, :].astype(F32)
                + (EXS[e][rows, :].astype(F32) + EXR[e][1, rows, :].astype(F32))
                + par[e * 8 + 1 : e * 8 + 2, :]
            )
            v = v - row_mean(v)
            inv = lax.rsqrt(row_mean(v * v) + EPSILON)
            n = v * inv
            N2[e][rows, :] = n
            I2[e][rows, :] = inv
            OB[e][rows, :] = (
                n * par[e * 8 + 3 : e * 8 + 4, :] + par[e * 8 + 5 : e * 8 + 6, :]
            ).astype(BF16)

    def mini_exchange(k):
        return pltpu.make_async_remote_copy(
            src_ref=xms.at[k],
            dst_ref=xmr.at[k],
            send_sem=xms_sem.at[k],
            recv_sem=xmr_sem.at[k],
            device_id=partner,
            device_id_type=MESH_ID,
        )

    def first_rows(ref):
        rows = [ref[b * 256 : b * 256 + 16, :].astype(F32)[0:1] for b in range(2)]
        return jnp.concatenate([*rows, jnp.zeros((14, rows[0].shape[1]), F32)], axis=0)

    def mini_attend():
        xm = first_rows(xp).astype(BF16)
        q = (dot(xm, win[1, :, pl.ds(0, COLS)]) + pin[2:3, :]).astype(BF16).astype(F32) * HD**-0.5
        of_head = lax.broadcasted_iota(jnp.int32, (16, COLS), 1) // HD == lax.broadcasted_iota(
            jnp.int32, (16, COLS), 0
        )
        col = lax.broadcasted_iota(jnp.int32, (16, 256), 1)
        rows = []
        for b in range(2):
            keys = qkvp[b * 256 : (b + 1) * 256, COLS : 2 * COLS]
            vals = qkvp[b * 256 : (b + 1) * 256, 2 * COLS : 3 * COLS]
            s = dot_t(jnp.where(of_head, q[b : b + 1], 0.0).astype(BF16), keys)
            s = jnp.where(col < plen[b], s, NEGATIVE)
            p = jnp.exp(s - jnp.max(s, axis=-1, keepdims=True))
            p = (p * (1.0 / jnp.sum(p, axis=-1, keepdims=True))).astype(BF16)
            rows.append(jnp.sum(jnp.where(of_head, dot(p, vals), 0.0), axis=0, keepdims=True))
        ctx = jnp.concatenate([*rows, jnp.zeros((14, COLS), F32)], axis=0)
        xms[0] = dot(ctx.astype(BF16), wo[1]).astype(BF16)
        mini_exchange(0).start()

    def mini_norm(k, v):
        mini_exchange(k).wait()
        v = v + (xms[k].astype(F32) + xmr[k].astype(F32)) + par[8 + k : 9 + k, :]
        v = v - row_mean(v)
        n = v * lax.rsqrt(row_mean(v * v) + EPSILON)
        return (n * par[10 + k : 11 + k, :] + par[12 + k : 13 + k, :]).astype(BF16)

    def mini_feed():
        hm[...] = mini_norm(0, first_rows(xp))

        u = dot(hm[...], wf[1]) + pfi[1:2, :]
        a = gelu_and_slope(u)[0].astype(BF16)
        xms[1] = dot(a, wd[1]).astype(BF16)

        mini_exchange(1).start()

    def transpose_into(e, k, src, b):
        rows = block_rows(e, b)

        @pl.loop(0, 2)
        def _(c):
            tile = src[rows, rows_at(c * COLS, COLS, 128)].T
            AT[e][k, pl.ds(c * 2, 2), :, :, :, rows] = tile.reshape(2, 2, 2, ROWS_OUT, BLK[e])

    def left_factor(axis, k):
        return pltpu.make_async_remote_copy(
            src_ref=atq.at[k, :, :, 1 - x] if axis == 0 else atq.at[k, :, 1 - y],
            dst_ref=fra.at[axis, k],
            send_sem=fas_sem.at[axis, k],
            recv_sem=far_sem.at[axis, k],
            device_id=first_dev[axis],
            device_id_type=MESH_ID,
        )

    def right_factor(axis, pair):
        return pltpu.make_async_remote_copy(
            src_ref=ballq.at[:, pl.ds((pair * 2 + axis) * COLS, COLS)],
            dst_ref=frb.at[axis, pair],
            send_sem=fbs_sem.at[axis, pair],
            recv_sem=fbr_sem.at[axis, pair],
            device_id=first_dev[axis],
            device_id_type=MESH_ID,
        )

    first_dev, other_dev = (at_x, at_y), (at_y, at_x)
    first_at, other_at = (x, y), (y, x)

    need(0, 1, 2, 3, 8)
    pl.semaphore_wait(barrier, 16)
    project(0, 0, (0, 1, 2))
    attend(0, 0)
    right_factor(0, 4).start()
    need(4, 5, 6, 7, 9)
    blocks(1, lambda b: project(1, b, (1, 2)))
    mini_attend()
    transpose_into(0, 3, xq, 0)
    left_factor(0, 3).start()
    left_factor(1, 3).start()
    first_norm(0, 0)
    need(10, 12)
    feed(0, 0)
    for axis in range(2):
        for pair in range(2):
            right_factor(axis, pair).start()
    need(11, 13)
    mini_feed()
    transpose_into(0, 1, hq, 0)
    left_factor(0, 1).start()
    left_factor(1, 1).start()
    second_norm(0, 0)
    out_q = pltpu.make_async_copy(obq, oq_out, out_sem.at[0])
    out_p = pltpu.make_async_copy(obp, op_out, out_sem.at[1])
    out_q.start()
    mini_out = mini_norm(1, hm[...].astype(F32)).astype(F32)

    pieces = []
    rows = [obq[at : at + 16, :].astype(F32)[0:1] for at in (0, 64)]
    for head in (*rows, mini_out[0:1], mini_out[1:2]):
        pieces += [head[:, k * 256 : (k + 1) * 256] for k in range(3)]
    pieces.append(jnp.zeros((4, 256), F32))
    hg[me] = jnp.concatenate(pieces, axis=0).astype(BF16)

    def heads(k):
        return pltpu.make_async_remote_copy(
            src_ref=hg.at[me],
            dst_ref=hg.at[me],
            send_sem=hgs_sem.at[k],
            recv_sem=hgr_sem.at[k],
            device_id=at_dp(me ^ k),
            device_id_type=MESH_ID,
        )

    for k in range(1, 16):
        heads(k).start()
    need(14, 15)
    blocks(1, lambda b: project(1, b, (0,)))
    attend(1, 0)
    for k in range(1, 16):
        copy = pltpu.make_async_remote_copy(
            src_ref=hg.at[me],
            dst_ref=hg.at[me ^ k],
            send_sem=hgs_sem.at[k],
            recv_sem=hgr_sem.at[k],
            device_id=at_dp(me ^ k),
            device_id_type=MESH_ID,
        )
        copy.wait()
    gathered = hg[...].astype(F32).reshape(256, 256)
    hf[0] = gathered[:, 0:128]
    hf[1] = gathered[:, 128:256]

    def all_heads(first):
        groups = []
        for i in range(2):
            parts = [
                hf[c, pl.ds(first + i * 3 + k, 16, stride=16), :] for k in range(3) for c in range(2)
            ]
            groups.append(jnp.concatenate(parts, axis=1))
        return jnp.concatenate(groups, axis=0)

    heads_q, heads_p = all_heads(0), all_heads(6)
    gain = score_gain * D ** (-0.5)
    class_scores = dot_t(heads_q.astype(BF16), heads_p.astype(BF16)) * gain
    chosen = masks[0:32, :]
    logits = jnp.where(masks[32:64, :] > 0.5, class_scores, NEGATIVE)
    top = jnp.max(logits, axis=1, keepdims=True)
    log_total = top + jnp.log(jnp.sum(jnp.exp(logits - top), axis=1, keepdims=True))
    target = jnp.sum(chosen * class_scores, axis=1, keepdims=True)
    loss = jnp.sum(log_total - target, axis=0, keepdims=True) * (1.0 / 32)
    loss_out[...] = jnp.broadcast_to(loss, loss_out.shape)
    d_class = (jnp.exp(logits - log_total) - chosen) * gain
    dh[0:32, :] = lax.dot_general(
        d_class, heads_p, (((1,), (0,)), ((), ())), precision=HIGHEST, preferred_element_type=F32
    )
    dh[32:64, :] = lax.dot_general(
        d_class, heads_q, (((0,), (0,)), ((), ())), precision=HIGHEST, preferred_element_type=F32
    )

    def norm_back(incoming, n, inv, scale):
        scaled = incoming * scale
        return inv * (scaled - row_mean(scaled) - n * row_mean(scaled * n))

    def second_back(e, b):
        row0 = lax.broadcasted_iota(jnp.int32, (CH, 1), 0)
        seqs = 2 if e == 0 else 1
        length = 64 if e == 0 else 256
        for i in range(seqs):
            group = i if e == 0 else b
            extra = dh[pl.ds(e * 32 + group * 16 + me, 1), :]

            @pl.loop(0, length // CH, unroll=NORM_UNROLL[e])
            def _(c):
                rows = rows_at(group * length + c * CH, CH, CH)
                add = jnp.where(row0 + c * CH == 0, extra, 0.0)
                d = COT[e][rows, :].astype(F32) + add
                n = N2[e][rows, :]
                out = norm_back(d, n, I2[e][rows, :], par[e * 8 + 3 : e * 8 + 4, :])
                N2[e][rows, :] = out
                low = out.astype(BF16)
                DD[e][rows, :] = low
                acc_s[e * 6 + 1] += fold8(d * n)
                acc_s[e * 6 + 3] += fold8(d)
                acc_s[e * 6 + 5] += fold8(low.astype(F32))

        transpose_into(e, 0, DD[e], b)

    def feed_back(e, b):
        rows = block_rows(e, b)

        @pl.loop(0, 6, unroll=UP_UNROLL[e])
        def _(n):
            cols = rows_at(n * 256, 256, 256)
            d = dot_t(DD[e][rows, :], wd[e, cols, :]) * SLOPE[e][rows, cols].astype(F32)
            d = d.astype(BF16)
            BALL[e][rows, rows_at(4 * COLS + n * 256, 256, 256)] = d
            acc_f[e, :, cols] += fold8(d.astype(F32))

        @pl.loop(0, 3, unroll=DOWN_UNROLL[e])
        def _(n):
            cols = rows_at(n * 256, 256, 256)
            EXS[e][rows, cols] = dot_t(BALL[e][rows, pl.ds(4 * COLS, FF_HERE)], wf[e, cols, :]).astype(BF16)

        exchange(e, b, 0).start()
        if e == 1:
            transpose_into(e, 1, HID[e], b)

    def first_back(e, b):
        exchange(e, b, 0).wait()

        @pl.loop(0, BLK[e] // CH, unroll=NORM_UNROLL[e])
        def _(c):
            rows = rows_at(b * BLK[e] + c * CH, CH, CH)
            d = N2[e][rows, :] + (EXS[e][rows, :].astype(F32) + EXR[e][0, rows, :].astype(F32))
            n = N1[e][rows, :]
            out = norm_back(d, n, I1[e][rows, :], par[e * 8 + 2 : e * 8 + 3, :])
            N1[e][rows, :] = out
            low = out.astype(BF16)
            DD[e][rows, :] = low
            acc_s[e * 6 + 0] += fold8(d * n)
            acc_s[e * 6 + 2] += fold8(d)
            acc_s[e * 6 + 4] += fold8(low.astype(F32))

        transpose_into(e, 2, DD[e], b)

    def attend_back(e, b):
        rows = block_rows(e, b)
        size = BLK[e]
        DC[e][rows, :] = dot_t(DD[e][rows, :], wo[e]).astype(BF16)

        @pl.loop(0, 3, unroll=PAIR_UNROLL[e])
        def _(pair):
            q2 = QKV[e][rows, rows_at(pair * 128, 128, 128)]
            k2 = QKV[e][rows, rows_at(COLS + pair * 128, 128, 128)]
            v2 = QKV[e][rows, rows_at(2 * COLS + pair * 128, 128, 128)]
            dc2 = DC[e][rows, rows_at(pair * 128, 128, 128)]
            dq = jnp.zeros((size, 128), F32)
            dk = jnp.zeros((size, 128), F32)
            dv = jnp.zeros((size, 128), F32)
            for hh in range(2):
                low = PR[e][b, pair * 2 + hh]
                p = low.astype(F32)
                dch = side(dc2, hh)
                dp = dot_t(dch, v2)
                ds = (p * (dp - jnp.sum(p * dp, axis=-1, keepdims=True))).astype(BF16)
                dv = dv + t_dot(low, dch)
                dq = dq + dot(ds, side(k2, hh))
                dk = dk + t_dot(ds, side(q2, hh))
            dq = (dq * HD**-0.5).astype(BF16)
            dv = dv.astype(BF16)
            cols = rows_at(pair * 128, 128, 128)
            BALL[e][rows, rows_at(9 * COLS + pair * 128, 128, 128)] = dq
            BALL[e][rows, rows_at(10 * COLS + pair * 128, 128, 128)] = dk.astype(BF16)
            BALL[e][rows, rows_at(11 * COLS + pair * 128, 128, 128)] = dv
            acc_b[e, :, cols] += fold8(dq.astype(F32))
            acc_b[e, :, rows_at(COLS + pair * 128, 128, 128)] += fold8(dv.astype(F32))

        if e == 1:
            transpose_into(e, 3, X[e], b)

    def token_back(e, b):
        rows = block_rows(e, b)

        @pl.loop(0, 3, unroll=DOWN_UNROLL[e])
        def _(n):
            cols = rows_at(n * 256, 256, 256)
            EXS[e][rows, cols] = dot_t(BALL[e][rows, pl.ds(9 * COLS, 3 * COLS)], win[e, cols, :]).astype(BF16)

        exchange(e, b, 1).start()

    def token_end(e, b):
        exchange(e, b, 1).wait()

        @pl.loop(0, BLK[e] // CH, unroll=NORM_UNROLL[e])
        def _(c):
            rows = rows_at(b * BLK[e] + c * CH, CH, CH)
            OB[e][rows, :] = (
                N1[e][rows, :] + (EXS[e][rows, :].astype(F32) + EXR[e][1, rows, :].astype(F32))
            ).astype(BF16)

    def job_of(j):
        return j // 6, j % 6

    def product(half, blk, sel):
        k = jnp.where(blk < 8, blk // 4, jnp.where(blk == 8, 2, 3))
        rows = atp[k, :, :, sel] if half == 0 else atp[k, :, sel]
        out = dot(rows.reshape(COLS, TOKS[1]), ballp[:, rows_at(blk * COLS, COLS, 128)])
        return out.reshape(ZN, 2, ROWS_OUT, COLS)

    def pair_product(half, pair):
        blk = pair * 2 + half
        k = blk // 4 if blk < 8 else 2 if blk == 8 else 3
        rows = atq[k, :, :, x] if half == 0 else atq[k, :, y]
        rows = jnp.concatenate([rows.reshape(COLS, TOKS[0]), fra[half, k].reshape(COLS, TOKS[0])], axis=1)
        cols = jnp.concatenate([ballq[:, blk * COLS : (blk + 1) * COLS], frb[half, pair]], axis=0)
        return dot(rows, cols).reshape(ZN, 2, ROWS_OUT, COLS)

    def p1(j, half):
        return pltpu.make_async_remote_copy(
            src_ref=p1s.at[j % DS, half],
            dst_ref=p1r.at[j % D1, half],
            send_sem=p1s_sem.at[j % DS, half],
            recv_sem=p1r_sem.at[j % D1, half],
            device_id=first_dev[half],
            device_id_type=MESH_ID,
        )

    def other(j, half, line_first):
        mine, to = p1r.at[j % D1, half], p2r.at[j % D2, half]
        return pltpu.make_async_remote_copy(
            src_ref=mine.at[z, 1 - other_at[half]] if line_first else mine.at[:, 1 - other_at[half]],
            dst_ref=to.at[0] if line_first else to,
            send_sem=p2s_sem.at[j % D2, half],
            recv_sem=p2r_sem.at[j % D2, half],
            device_id=other_dev[half],
            device_id_type=MESH_ID,
        )

    def block(j, half, d, right, line_first, at):
        slot = d if right else jnp.where(d == at, ZN, d)
        return zb.at[j % DZ, half, slot] if line_first else zb.at[j % DZ, half, slot, 0]

    def own_block(j, half, d, line_first):
        return p1r.at[j % D1, half, d] if line_first else p2r.at[j % D2, half, d]

    def along(j, half, d, right, relayed, line_first):
        send, recv = (zrs_sem, zrr_sem) if right else (zls_sem, zlr_sem)
        here = block(j, half, d, right, line_first, z)
        return pltpu.make_async_remote_copy(
            src_ref=here if relayed else own_block(j, half, d, line_first),
            dst_ref=block(j, half, d, right, line_first, z + 1 if right else z - 1),
            send_sem=send.at[j % DZ, half, d],
            recv_sem=recv.at[j % DZ, half, d],
            device_id=at_dp(me + 4 if right else me - 4),
            device_id_type=MESH_ID,
        )

    def total_of(a, b):
        return (a[...].astype(F32) + b[...].astype(F32)).astype(BF16)

    def step0(j):
        _, pair = job_of(j)
        for half in range(2):
            p1s[j % DS, half] = product(half, pair * 2 + half, 1 - first_at[half]).astype(BF16)
            p1(j, half).start()

    def step1(j):
        e_of, pair = job_of(j)

        @pl.when(e_of == 1)
        def _():
            for half in range(2):
                p1(j, half).wait()
            for half in range(2):
                own = product(half, pair * 2 + half, first_at[half])
                p1r[j % D1, half] = (own + p1r[j % D1, half].astype(F32)).astype(BF16)

        for p in range(6):

            @pl.when(jnp.logical_and(e_of == 0, pair == p))
            def _():
                for half in range(2):
                    if p in (0, 2):
                        left_factor(half, p // 2).wait()
                    elif p == 4:
                        left_factor(half, 2 + half).wait()
                    elif p == 5 and half == 0:
                        left_factor(0, 3).wait()
                    right_factor(half, p).wait()
                    p1r[j % D1, half] = pair_product(half, p).astype(BF16)

    def turn(j):
        for half in range(2):
            other(j, half, False).start()

    def turned(j):
        for half in range(2):
            other(j, half, False).wait()
            mine = p2r.at[j % D2, half]
            mine[...] = total_of(mine, p1r.at[j % D1, half, :, other_at[half]])

    def ends(j, line_first):
        @pl.when(z == 0)
        def _():
            for half in range(2):
                for d in (3, 2, 1):
                    along(j, half, d, True, False, line_first).start()

        @pl.when(z == 3)
        def _():
            for half in range(2):
                for d in (0, 1, 2):
                    along(j, half, d, False, False, line_first).start()

    def relay(j, half, d, right, line_first):
        held = block(j, half, d, right, line_first, z)
        along(j, half, d, right, True, line_first).wait_recv()
        held[...] = total_of(held, own_block(j, half, d, line_first))
        along(j, half, d, right, True, line_first).start()

    def middle1(j, line_first):
        @pl.when(z == 1)
        def _():
            for half in range(2):
                for d in (3, 2):
                    relay(j, half, d, True, line_first)

        @pl.when(z == 2)
        def _():
            for half in range(2):
                for d in (0, 1):
                    relay(j, half, d, False, line_first)

    def middle2(j, line_first):
        @pl.when(z == 2)
        def _():
            for half in range(2):
                relay(j, half, 3, True, line_first)

        @pl.when(z == 1)
        def _():
            for half in range(2):
                relay(j, half, 0, False, line_first)

    def line_end(j, line_first):
        for half in range(2):
            mine = own_block(j, half, z, line_first)

            @pl.when(z > 0)
            def _():
                along(j, half, z, True, True, line_first).wait_recv()
                mine[...] = total_of(mine, block(j, half, z, True, line_first, z))

            @pl.when(z < 3)
            def _():
                along(j, half, z, False, True, line_first).wait_recv()
                mine[...] = total_of(mine, block(j, half, z, False, line_first, z))

            for d in range(4):

                @pl.when(d > z)
                def _():
                    along(j, half, d, True, True, line_first).wait_send()

                @pl.when(d < z)
                def _():
                    along(j, half, d, False, True, line_first).wait_send()

    def pass_on(j):
        for half in range(2):
            other(j, half, True).start()

    def passed(j):
        for half in range(2):
            other(j, half, True).wait()

    def result(slot, half, to):
        return pltpu.make_async_copy(fin.at[slot, half], to, fin_sem.at[slot, half])

    def output(j, line_first):
        e_of, pair = job_of(j)
        for half in range(2):

            @pl.when(j >= 2)
            def _():
                result(j % 2, half, g_out.at[0]).wait()

            if line_first:
                total = p1r[j % D1, half, z, other_at[half]].astype(F32) + p2r[j % D2, half, 0].astype(F32)
            else:
                total = p2r[j % D2, half, z].astype(F32)
            fin[j % 2, half] = total
            for e in range(2):
                for p in range(6):

                    @pl.when(jnp.logical_and(e_of == e, pair == p))
                    def _():
                        blk = p * 2 + half
                        if blk < 4:
                            to = g_fo.at[e, :, pl.ds(blk * COLS, COLS)]
                        elif blk < 8:
                            to = g_fi.at[e, :, pl.ds((blk - 4) * COLS, COLS)]
                        elif blk == 8:
                            to = g_out.at[e]
                        else:
                            to = g_in.at[e, blk - 9]
                        result(j % 2, half, to).start()

    small_to = (at_x, at_y, at_dp(me ^ 4), at_dp(me ^ 8))

    def small(k):
        return pltpu.make_async_remote_copy(
            src_ref=smb.at[k],
            dst_ref=smr.at[k],
            send_sem=sms_sem.at[k],
            recv_sem=smr_sem.at[k],
            device_id=small_to[k],
            device_id_type=MESH_ID,
        )

    def small_first():
        smb[0] = jnp.zeros_like(smb[0])
        for e in range(2):
            for i in range(6):
                smb[0, e * 9 + i : e * 9 + i + 1, :] = jnp.sum(acc_s[e * 6 + i], axis=0, keepdims=True)
            smb[0, e * 9 + 6 : e * 9 + 7, :] = jnp.sum(acc_b[e], axis=0, keepdims=True)
            for i in range(2):
                smb[0, e * 9 + 7 + i : e * 9 + 8 + i, :] = jnp.sum(
                    acc_f[e, :, i * D : (i + 1) * D], axis=0, keepdims=True
                )
        small(0).start()

    def small_next(k):
        small(k).wait()
        if k < 3:
            smb[k + 1] = smb[k] + smr[k]
            small(k + 1).start()
        else:
            total = smb[k] + smr[k]
            sm_out[...] = jnp.zeros_like(sm_out)
            wide = pltpu.roll(total, lax.rem(D - me * ROWS_OUT, D), 1)
            sm_out[:, 0:ROWS_OUT] = wide[:, 0:ROWS_OUT]
            heads_own = pltpu.roll(total, lax.rem(D - me * 24, D), 1)
            feed_own = pltpu.roll(total, lax.rem(D - (me % 8) * 96, D), 1)
            for e in range(2):
                at = e * 9 + 6
                for i in range(2):
                    sm_out[at + i : at + i + 1, 0:24] = heads_own[at : at + 1, i * COLS : i * COLS + 24]
                low, high = feed_own[at + 1 : at + 2, 0:96], feed_own[at + 2 : at + 3, 0:96]
                sm_out[at + 2 : at + 3, 0:96] = jnp.where(me < 8, low, high)

    def q_second_back():
        second_back(0, 0)
        left_factor(0, 0).start()
        left_factor(1, 0).start()

    def q_feed_back():
        feed_back(0, 0)
        for axis in range(2):
            for pair in (2, 3):
                right_factor(axis, pair).start()

    def q_first_back():
        first_back(0, 0)
        left_factor(0, 2).start()

    def q_attend_back():
        attend_back(0, 0)
        right_factor(1, 4).start()
        right_factor(0, 5).start()
        right_factor(1, 5).start()

    def q_token_end():
        token_end(0, 0)
        pltpu.make_async_copy(obq, gq_out, out_sem.at[0]).start()

    def p_token_end():
        blocks(1, lambda b: token_end(1, b))
        pltpu.make_async_copy(obp, gp_out, out_sem.at[1]).start()

    def p_mid(b):
        first_norm(1, b)
        feed(1, b)

    def p_second():
        blocks(1, lambda b: second_norm(1, b))
        out_p.start()

    def passages(piece):
        return lambda: blocks(1, lambda b: piece(1, b))

    work = {
        1: [q_feed_back, lambda: attend(1, 1)],
        2: [q_first_back, lambda: p_mid(0), q_attend_back, lambda: p_mid(1)],
        3: [lambda: token_back(0, 0), p_second, out_q.wait, q_token_end, passages(second_back)],
        4: [passages(feed_back)],
        7: [passages(first_back), passages(attend_back)],
        9: [passages(token_back)],
        11: [small_first],
        12: [out_p.wait, p_token_end, lambda: small_next(0)],
        13: [lambda: small_next(1)],
        14: [lambda: small_next(2)],
        15: [lambda: small_next(3)],
    }

    def is_line_first(j):
        found = j == LINE_FIRST[0]
        for k in LINE_FIRST[1:]:
            found = jnp.logical_or(found, j == k)
        return found

    def steps(late, j):
        line_first = is_line_first(j)
        if late == 1:
            step1(j)

        @pl.when(line_first)
        def _():
            if late == 1:
                ends(j, True)
            elif late == 2:
                middle1(j, True)
            elif late == 3:
                middle2(j, True)
            elif late == 4:
                line_end(j, True)
                pass_on(j)
            else:
                passed(j)
                output(j, True)

        @pl.when(jnp.logical_not(line_first))
        def _():
            if late == 1:
                turn(j)
            elif late == 2:
                turned(j)
                ends(j, False)
            elif late == 3:
                middle1(j, False)
            elif late == 4:
                middle2(j, False)
            else:
                line_end(j, False)
                output(j, False)

    q_second_back()

    @pl.loop(0, JOBS + 5)
    def _(tick):
        for at, things in work.items():

            @pl.when(tick == at)
            def _():
                for thing in things:
                    thing()

        @pl.when(jnp.logical_and(tick >= 6, tick < JOBS))
        def _():
            step0(tick)

        for late in (1, 2, 3, 4, 5):

            @pl.when(jnp.logical_and(tick >= late, tick < JOBS + late))
            def _():
                steps(late, tick - late)

    pltpu.make_async_copy(obq, gq_out, out_sem.at[0]).wait()
    pltpu.make_async_copy(obp, gp_out, out_sem.at[1]).wait()
    for slot in range(2):
        for half in range(2):
            result(slot, half, g_out.at[0]).wait()


def finish_kernel(*refs):
    oq, op, gq, gp, g_in, g_out, g_fi, g_fo, loss, sums = refs[:10]
    large, (loss_to, in_bias, fi_bias, bo, gain, shift) = refs[10:18], refs[18:24]
    held, in_sems, out_sems = refs[24:32], refs[32], refs[33]
    sources = (oq, op, gq, gp, g_in, g_out, g_fi, g_fo)
    loads = [pltpu.make_async_copy(sources[i], held[i], in_sems.at[i]) for i in range(8)]
    stores = [pltpu.make_async_copy(held[i], large[i], out_sems.at[i]) for i in range(8)]
    for load in loads:
        load.start()
    loss_to[...] = loss[0:1, 0:1]
    for e in range(2):
        at = e * 9
        gain[e] = sums[at : at + 2, 0:ROWS_OUT]
        shift[e] = sums[at + 2 : at + 4, 0:ROWS_OUT]
        bo[e] = sums[at + 4 : at + 6, 0:ROWS_OUT]
        in_bias[e] = sums[at + 6 : at + 8, 0:24]
        fi_bias[e : e + 1] = sums[at + 8 : at + 9, 0:96]
    for load, store in zip(loads, stores):
        load.wait()
        store.start()
    for store in stores:
        store.wait()


FF_HERE = 1536


def fused(
    question_tokens, passage_tokens, question_cotangent, passage_cotangent,
    question_lengths, passage_lengths, dataset_ids, positives,
    attn_in, attn_in_bias, attn_out, ffn_in, ffn_in_bias, ffn_out, out_biases, norm_gains, norm_shifts,
):
    any_spec = pl.BlockSpec(memory_space=pl.ANY)
    vmem = pl.BlockSpec(memory_space=pltpu.VMEM)
    smem = pl.BlockSpec(memory_space=pltpu.SMEM)

    def both(shape, dtype):
        return [pltpu.VMEM(shape(m), dtype) for m in TOKS]

    shape = jax.ShapeDtypeStruct
    dma = pltpu.SemaphoreType.DMA
    outs = pl.pallas_call(
        partial(fused_kernel, last=0),
        name="fused",
        in_specs=[any_spec] * 4 + [smem] * 4 + [any_spec, vmem, any_spec, any_spec, vmem, any_spec] + [vmem] * 3,
        out_specs=[any_spec, any_spec, vmem] + [any_spec] * 6 + [vmem],
        out_shape=[
            shape((128, D), BF16),
            shape((512, D), BF16),
            shape((8, 128), F32),
            shape((128, D), BF16),
            shape((512, D), BF16),
            shape((2, 3, ROWS_OUT, COLS), F32),
            shape((2, ROWS_OUT, COLS), F32),
            shape((2, ROWS_OUT, FF_HERE), F32),
            shape((2, ROWS_OUT, FF_HERE), F32),
            shape((SMALL, 128), F32),
        ],
        scratch_shapes=[
            pltpu.VMEM((2, D, 3 * COLS), BF16),
            pltpu.VMEM((2, COLS, D), BF16),
            pltpu.VMEM((2, D, FF_HERE), BF16),
            pltpu.VMEM((2, FF_HERE, D), BF16),
            *both(lambda m: (m, D), BF16),
            *both(lambda m: (m, D), BF16),
            *both(lambda m: (m, 3 * COLS), BF16),
            pltpu.VMEM((1, 6, 128, 128), BF16),
            pltpu.VMEM((2, 6, 256, 256), BF16),
            *both(lambda m: (m, D), BF16),
            *both(lambda m: (m, D), F32),
            *both(lambda m: (m, D), F32),
            *both(lambda m: (m, 1), F32),
            *both(lambda m: (m, 1), F32),
            *both(lambda m: (m, FF_HERE), BF16),
            *both(lambda m: (m, D), BF16),
            *both(lambda m: (m, D), BF16),
            *both(lambda m: (m, COLS), BF16),
            *both(lambda m: (m, 12 * COLS), BF16),
            *both(lambda m: (4, ZN, 2, 2, ROWS_OUT, m), BF16),
            *both(lambda m: (m, D), BF16),
            *both(lambda m: (2, m, D), BF16),
            pltpu.VMEM((16, D), F32),
            pltpu.VMEM((8, COLS), F32),
            pltpu.VMEM((8, FF_HERE), F32),
            pltpu.VMEM((64, 32), F32),
            pltpu.VMEM((16, 16, 256), BF16),
            pltpu.VMEM((2, 256, 128), F32),
            pltpu.VMEM((64, D), F32),
            pltpu.VMEM((12, 8, D), F32),
            pltpu.VMEM((2, 8, 2 * COLS), F32),
            pltpu.VMEM((2, 8, FF_HERE), F32),
            pltpu.VMEM((4, SMALL, D), F32),
            pltpu.VMEM((4, SMALL, D), F32),
            pltpu.VMEM((DS, 2, ZN, 2, ROWS_OUT, COLS), BF16),
            pltpu.VMEM((D1, 2, ZN, 2, ROWS_OUT, COLS), BF16),
            pltpu.VMEM((D2, 2, ZN, ROWS_OUT, COLS), BF16),
            pltpu.VMEM((DZ, 2, ZN + 1, 2, ROWS_OUT, COLS), BF16),
            pltpu.VMEM((2, 2, ROWS_OUT, COLS), F32),
            pltpu.VMEM((2, 4, ZN, 2, ROWS_OUT, TOKS[0]), BF16),
            pltpu.VMEM((2, 6, TOKS[0], COLS), BF16),
            pltpu.VMEM((2, 16, D), BF16),
            pltpu.VMEM((2, 16, D), BF16),
            pltpu.VMEM((16, D), BF16),
            dma((2, 2)),
            dma((16,)),
            dma((2,)),
            dma((3,)),
            dma((2, 3)),
            dma((16,)),
            dma((16,)),
            dma((4,)),
            dma((4,)),
            dma((DS, 2)),
            dma((D1, 2)),
            dma((D2, 2)),
            dma((D2, 2)),
            dma((DZ, 2, ZN)),
            dma((DZ, 2, ZN)),
            dma((DZ, 2, ZN)),
            dma((DZ, 2, ZN)),
            dma((2, 4)),
            dma((2, 4)),
            dma((2, 6)),
            dma((2, 6)),
            dma((2,)),
            dma((2,)),
        ],
        compiler_params=pltpu.CompilerParams(
            collective_id=0, has_side_effects=True, vmem_limit_bytes=VMEM_BYTES
        ),
    )(
        question_tokens.reshape(128, D),
        passage_tokens.reshape(512, D),
        question_cotangent.reshape(128, D),
        passage_cotangent.reshape(512, D),
        question_lengths, passage_lengths, dataset_ids, positives,
        attn_in.transpose(0, 2, 1, 3), attn_in_bias, attn_out, ffn_in, ffn_in_bias, ffn_out,
        out_biases, norm_gains, norm_shifts,
    )
    oq, op, loss, gq, gp, g_in, g_out, g_fi, g_fo, sums = outs
    large = (oq, op, gq, gp, g_in, g_out, g_fi, g_fo)
    small = [(1, 1), (2, 2, 24), (2, 96), (2, 2, ROWS_OUT), (2, 2, ROWS_OUT), (2, 2, ROWS_OUT)]
    oq, op, gq, gp, g_in, g_out, g_fi, g_fo, loss, in_bias, fi_bias, bo, gain, shift = pl.pallas_call(
        finish_kernel,
        name="finish",
        in_specs=[any_spec] * 8 + [vmem] * 2,
        out_specs=[any_spec] * 8 + [vmem] * 6,
        out_shape=[shape(a.shape, a.dtype) for a in large] + [shape(dims, F32) for dims in small],
        scratch_shapes=[*[pltpu.VMEM(a.shape, a.dtype) for a in large], dma((8,)), dma((8,))],
        compiler_params=pltpu.CompilerParams(vmem_limit_bytes=VMEM_BYTES),
    )(*large, loss, sums)
    return (
        oq.reshape(2, 64, D),
        op.reshape(2, 256, D),
        loss.reshape(()),
        gq.reshape(2, 64, D),
        gp.reshape(2, 256, D),
        g_in.transpose(0, 2, 1, 3),
        in_bias,
        g_out.transpose(0, 2, 1),
        g_fi,
        fi_bias,
        g_fo.transpose(0, 2, 1),
        bo,
        gain,
        shift,
    )


VMEM_BYTES = 62 * 1024 * 1024


def solution(mesh):
    in_specs = (
        P("dp", None, None),
        P("dp", None, None),
        P("dp", None, None),
        P("dp", None, None),
        P("dp"),
        P("dp"),
        P(),
        P(),
        P(None, None, None, "tensor"),
        P(None, None, "tensor"),
        P(None, "tensor", None),
        P(None, None, "tensor"),
        P(None, "tensor"),
        P(None, "tensor", None),
        P(),
        P(),
        P(),
    )
    out_specs = (
        P("dp", None, None),
        P("dp", None, None),
        P(),
        P("dp", None, None),
        P("dp", None, None),
        P(None, "dp", None, "tensor"),
        P(None, None, ("tensor", "dp")),
        P(None, "tensor", "dp"),
        P(None, "dp", "tensor"),
        P(None, ("tensor", "dp")),
        P(None, "tensor", "dp"),
        P(None, None, "dp"),
        P(None, None, "dp"),
        P(None, None, "dp"),
    )
    step = fused if mesh.shape["dp"] == 4 * ZN and mesh.shape["tensor"] == 2 else per_device
    return jax.shard_map(
        step, mesh=mesh, in_specs=in_specs, out_specs=out_specs, check_vma=False
    )
```

```python
from functools import partial

import jax
import jax.numpy as jnp
from jax import lax
from jax.experimental import pallas as pl
from jax.experimental.pallas import tpu as pltpu
from jax.sharding import PartitionSpec as P

D = 768
HD = 64


EPSILON = 1e-06
NEGATIVE = -1e30
HIGHEST = lax.Precision.HIGHEST
score_gain = 3.0


def norm_forward(summed, scale_row, shift_row):
    row_mean = jnp.mean(summed, axis=-1, keepdims=True)
    centred = summed - row_mean
    inv_std = lax.rsqrt(jnp.mean(centred * centred, axis=-1, keepdims=True) + EPSILON)
    normed = centred * inv_std
    return (normed * scale_row + shift_row, normed, inv_std)


def norm_backward(incoming, normed, inv_std, scale_row):
    scaled = incoming * scale_row
    outgoing = inv_std * (
        scaled
        - jnp.mean(scaled, axis=-1, keepdims=True)
        - normed * jnp.mean(scaled * normed, axis=-1, keepdims=True)
    )
    return (outgoing, jnp.sum(incoming * normed, axis=(0, 1)), jnp.sum(incoming, axis=(0, 1)))


def key_visible(lengths, length):
    positions = jnp.arange(length, dtype=jnp.int32)
    return (positions[None, :] < lengths[:, None])[:, None, None, :]


def head_scores(queries, key_rows, visible):
    raw_scores = jnp.einsum(
        "bqhe,bkhe->bhqk", queries, key_rows, preferred_element_type=jnp.float32
    ) * HD ** (-0.5)
    return jnp.where(visible, raw_scores, NEGATIVE)


def split_heads(matrix):
    return matrix.reshape(matrix.shape[0], matrix.shape[1], matrix.shape[2] // HD, HD)


def join_heads(per_head):
    return per_head.reshape(
        per_head.shape[0], per_head.shape[1], per_head.shape[2] * per_head.shape[3]
    )


def encoder_forward(tokens, lengths, params):
    (
        attn_in,
        attn_in_bias,
        attn_out,
        ffn_in,
        ffn_in_bias,
        ffn_out,
        out_biases,
        norm_gains,
        norm_shifts,
    ) = params
    projected = jnp.einsum("bld,dce->blce", tokens, attn_in, preferred_element_type=jnp.float32)
    in_bias = attn_in_bias.astype(jnp.float32)
    queries = split_heads((projected[:, :, 0] + in_bias[0]).astype(jnp.bfloat16))
    key_rows = split_heads(projected[:, :, 1].astype(jnp.bfloat16))
    values = split_heads((projected[:, :, 2] + in_bias[1]).astype(jnp.bfloat16))
    visible = key_visible(lengths, tokens.shape[1])
    scores = head_scores(queries, key_rows, visible)
    row_top = jnp.max(scores, axis=-1, keepdims=True)
    log_total = row_top + jnp.log(jnp.sum(jnp.exp(scores - row_top), axis=-1, keepdims=True))
    attn_probs = jnp.exp(scores - log_total).astype(jnp.bfloat16)
    context = join_heads(
        jnp.einsum(
            "bhqk,bkhe->bqhe", attn_probs, values, preferred_element_type=jnp.float32
        ).astype(jnp.bfloat16)
    )
    attn_part = jnp.einsum("ble,ed->bld", context, attn_out, preferred_element_type=jnp.float32)
    attn_sum = lax.psum(attn_part.astype(jnp.bfloat16), "tensor").astype(jnp.float32)
    bias_rows = out_biases.astype(jnp.float32)
    gain_rows = norm_gains.astype(jnp.float32)
    shift_rows = norm_shifts.astype(jnp.float32)
    hidden_float, normed_first, inv_first = norm_forward(
        tokens.astype(jnp.float32) + attn_sum + bias_rows[0], gain_rows[0], shift_rows[0]
    )
    hidden = hidden_float.astype(jnp.bfloat16)
    up_pre = jnp.einsum(
        "bld,df->blf", hidden, ffn_in, preferred_element_type=jnp.float32
    ) + ffn_in_bias.astype(jnp.float32)
    activated = jax.nn.gelu(up_pre, approximate=False).astype(jnp.bfloat16)
    down_part = jnp.einsum("blf,fd->bld", activated, ffn_out, preferred_element_type=jnp.float32)
    down_sum = lax.psum(down_part.astype(jnp.bfloat16), "tensor").astype(jnp.float32)
    outputs, normed_second, inv_second = norm_forward(
        hidden.astype(jnp.float32) + down_sum + bias_rows[1], gain_rows[1], shift_rows[1]
    )
    saved = (
        tokens,
        queries,
        key_rows,
        values,
        log_total,
        context,
        normed_first,
        inv_first,
        hidden,
        up_pre,
        activated,
        normed_second,
        inv_second,
    )
    return (outputs, saved)


def encoder_backward(incoming, saved, lengths, params):
    (
        attn_in,
        attn_in_bias,
        attn_out,
        ffn_in,
        ffn_in_bias,
        ffn_out,
        out_biases,
        norm_gains,
        norm_shifts,
    ) = params
    (
        tokens,
        queries,
        key_rows,
        values,
        log_total,
        context,
        normed_first,
        inv_first,
        hidden,
        up_pre,
        activated,
        normed_second,
        inv_second,
    ) = saved
    groups_here, length, model_width = tokens.shape
    gain_rows = norm_gains.astype(jnp.float32)
    d_second, gain_second, shift_second = norm_backward(
        incoming, normed_second, inv_second, gain_rows[1]
    )
    d_down = d_second.astype(jnp.bfloat16)
    grad_ffn_out = jnp.einsum("blf,bld->fd", activated, d_down, preferred_element_type=jnp.float32)
    d_activated = jnp.einsum("bld,fd->blf", d_down, ffn_out, preferred_element_type=jnp.float32)
    gelu_pull = jax.vjp(partial(jax.nn.gelu, approximate=False), up_pre)[1]
    d_up = gelu_pull(d_activated)[0].astype(jnp.bfloat16)
    grad_ffn_in = jnp.einsum("bld,blf->df", hidden, d_up, preferred_element_type=jnp.float32)
    hidden_part = jnp.einsum("blf,df->bld", d_up, ffn_in, preferred_element_type=jnp.float32)
    d_hidden = d_second + lax.psum(hidden_part.astype(jnp.bfloat16), "tensor").astype(jnp.float32)
    d_first, gain_first, shift_first = norm_backward(
        d_hidden, normed_first, inv_first, gain_rows[0]
    )
    d_attn = d_first.astype(jnp.bfloat16)
    grad_attn_out = jnp.einsum("ble,bld->ed", context, d_attn, preferred_element_type=jnp.float32)
    d_context = split_heads(
        jnp.einsum("bld,ed->ble", d_attn, attn_out, preferred_element_type=jnp.float32).astype(
            jnp.bfloat16
        )
    )
    visible = key_visible(lengths, length)
    scores = head_scores(queries, key_rows, visible)
    probs_float = jnp.exp(scores - log_total)
    d_probs = jnp.einsum("bqhe,bkhe->bhqk", d_context, values, preferred_element_type=jnp.float32)
    d_values = jnp.einsum(
        "bhqk,bqhe->bkhe",
        probs_float.astype(jnp.bfloat16),
        d_context,
        preferred_element_type=jnp.float32,
    ).astype(jnp.bfloat16)
    d_scores = (
        probs_float * (d_probs - jnp.sum(probs_float * d_probs, axis=-1, keepdims=True))
    ).astype(jnp.bfloat16)
    d_queries = (
        jnp.einsum("bhqk,bkhe->bqhe", d_scores, key_rows, preferred_element_type=jnp.float32)
        * HD ** (-0.5)
    ).astype(jnp.bfloat16)
    d_keys = (
        jnp.einsum("bhqk,bqhe->bkhe", d_scores, queries, preferred_element_type=jnp.float32)
        * HD ** (-0.5)
    ).astype(jnp.bfloat16)
    query_grad = join_heads(d_queries)
    value_grad = join_heads(d_values)
    d_projected = jnp.stack([query_grad, join_heads(d_keys), value_grad], axis=2)
    grad_attn_in = jnp.einsum(
        "bld,blce->dce", tokens, d_projected, preferred_element_type=jnp.float32
    )
    token_part = jnp.einsum(
        "blce,dce->bld", d_projected, attn_in, preferred_element_type=jnp.float32
    )
    d_tokens = (
        d_first + lax.psum(token_part.astype(jnp.bfloat16), "tensor").astype(jnp.float32)
    ).astype(jnp.bfloat16)
    grad_in_bias = jnp.stack(
        [
            jnp.sum(query_grad.astype(jnp.float32), axis=(0, 1)),
            jnp.sum(value_grad.astype(jnp.float32), axis=(0, 1)),
        ]
    )
    grad_ffn_bias = jnp.sum(d_up.astype(jnp.float32), axis=(0, 1))
    grad_out_biases = jnp.stack(
        [
            jnp.sum(d_attn.astype(jnp.float32), axis=(0, 1)),
            jnp.sum(d_down.astype(jnp.float32), axis=(0, 1)),
        ]
    )
    grad_gains = jnp.stack([gain_first, gain_second])
    grad_shifts = jnp.stack([shift_first, shift_second])
    return (
        d_tokens,
        (
            grad_attn_in,
            grad_in_bias,
            grad_attn_out,
            grad_ffn_in,
            grad_ffn_bias,
            grad_ffn_out,
            grad_out_biases,
            grad_gains,
            grad_shifts,
        ),
    )


def contrastive(question_rows, passage_rows, own_positive, dataset_ids):
    class_scores = jnp.einsum(
        "gd,jd->gj", question_rows, passage_rows, preferred_element_type=jnp.float32
    ) * (score_gain * D ** (-0.5))
    columns = jnp.arange(passage_rows.shape[0], dtype=jnp.int32)
    chosen = own_positive[:, None] == columns[None, :]
    own_set = jnp.sum(jnp.where(chosen, dataset_ids[None, :], 0), axis=1)
    logits = jnp.where(dataset_ids[None, :] == own_set[:, None], class_scores, NEGATIVE)
    row_top = jnp.max(logits, axis=1, keepdims=True)
    log_total = row_top + jnp.log(jnp.sum(jnp.exp(logits - row_top), axis=1, keepdims=True))
    target = jnp.sum(jnp.where(chosen, class_scores, 0.0), axis=1)
    d_class = (jnp.exp(logits - log_total) - chosen.astype(jnp.float32)) * (
        score_gain * D ** (-0.5)
    )
    return (log_total[:, 0] - target, d_class)


def per_device(
    question_tokens,
    passage_tokens,
    question_cotangent,
    passage_cotangent,
    question_lengths,
    passage_lengths,
    dataset_ids,
    positives,
    attn_in,
    attn_in_bias,
    attn_out,
    ffn_in,
    ffn_in_bias,
    ffn_out,
    out_biases,
    norm_gains,
    norm_shifts,
):

    def encoder_params(encoder):
        return (
            attn_in[encoder],
            attn_in_bias[encoder],
            attn_out[encoder],
            ffn_in[encoder],
            ffn_in_bias[encoder],
            ffn_out[encoder],
            out_biases[encoder],
            norm_gains[encoder],
            norm_shifts[encoder],
        )

    question_params = encoder_params(0)
    passage_params = encoder_params(1)
    question_float, question_saved = encoder_forward(
        question_tokens, question_lengths, question_params
    )
    passage_float, passage_saved = encoder_forward(passage_tokens, passage_lengths, passage_params)
    question_heads = question_float[:, 0].astype(jnp.bfloat16)
    passage_heads = passage_float[:, 0].astype(jnp.bfloat16)
    local_groups = question_heads.shape[0]
    own_start = lax.axis_index("dp") * local_groups
    all_passages = lax.all_gather(passage_heads, "dp", axis=0, tiled=True)
    own_positive = lax.dynamic_slice_in_dim(positives, own_start, local_groups)
    cross, d_class = contrastive(question_heads, all_passages, own_positive, dataset_ids)
    total = lax.psum(jnp.sum(cross), "dp")
    contrastive_loss = total / all_passages.shape[0]
    d_question_heads = jnp.einsum(
        "gj,jd->gd", d_class, all_passages.astype(jnp.float32), precision=HIGHEST
    )
    question_heads_float = question_heads.astype(jnp.float32)
    d_passage_heads = lax.psum_scatter(
        jnp.einsum("gj,gd->jd", d_class, question_heads_float, precision=HIGHEST),
        "dp",
        scatter_dimension=0,
        tiled=True,
    )
    d_question_out = question_cotangent.astype(jnp.float32).at[:, 0].add(d_question_heads)
    d_passage_out = passage_cotangent.astype(jnp.float32).at[:, 0].add(d_passage_heads)
    passage_grad, passage_weights = encoder_backward(
        d_passage_out, passage_saved, passage_lengths, passage_params
    )
    question_grad, question_weights = encoder_backward(
        d_question_out, question_saved, question_lengths, question_params
    )
    joined = (
        lax.psum_scatter(question_weights[0], "dp", scatter_dimension=0, tiled=True),
        lax.psum_scatter(question_weights[1], "dp", scatter_dimension=1, tiled=True),
        lax.psum_scatter(question_weights[2], "dp", scatter_dimension=1, tiled=True),
        lax.psum_scatter(question_weights[3], "dp", scatter_dimension=0, tiled=True),
        lax.psum_scatter(question_weights[4], "dp", scatter_dimension=0, tiled=True),
        lax.psum_scatter(question_weights[5], "dp", scatter_dimension=1, tiled=True),
        lax.psum_scatter(question_weights[6], "dp", scatter_dimension=1, tiled=True),
        lax.psum_scatter(question_weights[7], "dp", scatter_dimension=1, tiled=True),
        lax.psum_scatter(question_weights[8], "dp", scatter_dimension=1, tiled=True),
        lax.psum_scatter(passage_weights[0], "dp", scatter_dimension=0, tiled=True),
        lax.psum_scatter(passage_weights[1], "dp", scatter_dimension=1, tiled=True),
        lax.psum_scatter(passage_weights[2], "dp", scatter_dimension=1, tiled=True),
        lax.psum_scatter(passage_weights[3], "dp", scatter_dimension=0, tiled=True),
        lax.psum_scatter(passage_weights[4], "dp", scatter_dimension=0, tiled=True),
        lax.psum_scatter(passage_weights[5], "dp", scatter_dimension=1, tiled=True),
        lax.psum_scatter(passage_weights[6], "dp", scatter_dimension=1, tiled=True),
        lax.psum_scatter(passage_weights[7], "dp", scatter_dimension=1, tiled=True),
        lax.psum_scatter(passage_weights[8], "dp", scatter_dimension=1, tiled=True),
    )
    question_parts = joined[:9]
    passage_parts = joined[9:]
    stacked = [
        jnp.stack([question_piece, passage_piece])
        for question_piece, passage_piece in zip(question_parts, passage_parts)
    ]
    return (
        question_float.astype(jnp.bfloat16),
        passage_float.astype(jnp.bfloat16),
        contrastive_loss,
        question_grad,
        passage_grad,
        stacked[0],
        stacked[1],
        stacked[2],
        stacked[3],
        stacked[4],
        stacked[5],
        stacked[6],
        stacked[7],
        stacked[8],
    )


MESH_ID = pl.DeviceIdType.MESH
F32 = jnp.float32
BF16 = jnp.bfloat16
ZN = 4
ROWS_OUT = 48
JOBS = 12
COLS = 384
D1, D2, DZ, DS = 8, 8, 8, 2
LINE_FIRST = (6, 8, 9)
TOKS = (128, 512)
BLK = (128, 256)
SMALL = 24
CHUNK = 64
NORM_UNROLL = (2, 4)
UP_UNROLL = (6, 6)
DOWN_UNROLL = (3, 3)
PAIR_UNROLL = (3, 3)


def dot(a, b):
    return jnp.dot(a, b, preferred_element_type=F32)


def dot_t(a, b):
    return lax.dot_general(a, b, (((1,), (1,)), ((), ())), preferred_element_type=F32)


def t_dot(a, b):
    return lax.dot_general(a, b, (((0,), (0,)), ((), ())), preferred_element_type=F32)


def gelu_and_slope(u):
    size = jnp.abs(u)
    bell = jnp.exp(-0.5 * u * u)
    t = 1.0 / (1.0 + (0.3275911 * 0.7071067811865476) * size)
    poly = t * (
        0.127414796
        + t * (-0.142248368 + t * (0.7107068705 + t * (-0.7265760135 + t * 0.5307027145)))
    )
    tail = poly * bell
    phi = jnp.where(u >= 0.0, 1.0 - tail, tail)
    return u * phi, phi + u * bell * 0.3989422804014327


def row_mean(v):
    return jnp.sum(v, axis=-1, keepdims=True) * (1.0 / D)


def fold8(v):
    return jnp.sum(v.reshape(v.shape[0] // 8, 8, v.shape[1]), axis=0)


def rows_at(start, size, step=16):
    return pl.ds(pl.multiple_of(start, step), size)


def fused_kernel(
    xq_in, xp_in, cq_in, cp_in, qlen_in, plen_in, dsid_in, posi_in,
    win_in, bin_from, wo_in, wf_in, bfi_from, wd_in, bo_from, gain_from, shift_from,
    oq_out, op_out, gq_out, gp_out, g_in, g_out, g_fi, g_fo, sm_out,
    win, wo, wf, wd, xq, xp, cq, cp, qkvq, qkvp, prq, prp, hq, hp, n1q, n1p, n2q, n2p,
    i1q, i1p, i2q, i2p, sq, sp, obq, obp, ddq, ddp, dcq, dcp, ballq, ballp, atq, atp,
    exsq, exsp, exrq, exrp, par, pin, pfi, masks, hg, hf, dh, acc_s, acc_b, acc_f, smb, smr,
    p1s, p1r, p2r, zb, fin, fra, frb, xms, xmr, hm,
    qlen, plen, dsid, posi, bin_in, bfi_in, bo_in, gain_in, shift_in, sm,
    fin_sem, little_sem, in_sem, out_sem, exs_sem, exr_sem, hgs_sem, hgr_sem, sms_sem, smr_sem,
    p1s_sem, p1r_sem, p2s_sem, p2r_sem, zrs_sem, zrr_sem, zls_sem, zlr_sem,
    fas_sem, far_sem, fbs_sem, fbr_sem, xms_sem, xmr_sem,
    *, last,
):
    me = lax.axis_index("dp")
    core = lax.axis_index("tensor")
    z, y, x = me // 4, (me // 2) % 2, me % 2
    partner = {"dp": me, "tensor": 1 - core}
    at_x = {"dp": me + 1 - 2 * x, "tensor": core}
    at_y = {"dp": me + 2 - 4 * y, "tensor": core}

    def at_dp(index):
        return {"dp": index, "tensor": core}

    X, COT, QKV, PR, HID = (xq, xp), (cq, cp), (qkvq, qkvp), (prq, prp), (hq, hp)
    N1, N2, I1, I2, SLOPE = (n1q, n1p), (n2q, n2p), (i1q, i1p), (i2q, i2p), (sq, sp)
    OB, DD, DC, BALL, AT = (obq, obp), (ddq, ddp), (dcq, dcp), (ballq, ballp), (atq, atp)
    EXS, EXR = (exsq, exsp), (exrq, exrp)

    little = [
        (qlen_in, qlen), (plen_in, plen), (bin_from, bin_in), (bfi_from, bfi_in), (bo_from, bo_in),
        (gain_from, gain_in), (shift_from, shift_in), (dsid_in, dsid), (posi_in, posi),
    ]
    little = [pltpu.make_async_copy(s, d, little_sem.at[i]) for i, (s, d) in enumerate(little)]
    loads = [
        (xq_in, xq),
        *[(win_in.at[0, j], win.at[0, :, pl.ds(j * COLS, COLS)]) for j in range(3)],
        (xp_in, xp),
        *[(win_in.at[1, j], win.at[1, :, pl.ds(j * COLS, COLS)]) for j in range(3)],
        (wo_in.at[0], wo.at[0]),
        (wo_in.at[1], wo.at[1]),
        (wf_in.at[0], wf.at[0]),
        (wf_in.at[1], wf.at[1]),
        (wd_in.at[0], wd.at[0]),
        (wd_in.at[1], wd.at[1]),
        (cq_in, cq),
        (cp_in, cp),
    ]
    loads = [pltpu.make_async_copy(s, d, in_sem.at[i]) for i, (s, d) in enumerate(loads)]
    for copy in loads[:4]:
        copy.start()
    for copy in little:
        copy.start()
    ready = set()

    def need(*which):
        for i in which:
            if i not in ready:
                loads[i].wait()
                ready.add(i)

    barrier = pltpu.get_barrier_semaphore()
    pl.semaphore_signal(barrier, inc=1, device_id=partner, device_id_type=MESH_ID)
    for k in range(1, 16):
        pl.semaphore_signal(barrier, inc=1, device_id=at_dp(me ^ k), device_id_type=MESH_ID)

    def load(*which):
        for i in which:
            loads[i].start()

    for copy in little:
        copy.wait()
    for e in range(2):
        for i in range(2):
            par[e * 8 + i : e * 8 + i + 1, :] = bo_in[e].astype(F32)[i : i + 1]
            par[e * 8 + 2 + i : e * 8 + 3 + i, :] = gain_in[e].astype(F32)[i : i + 1]
            par[e * 8 + 4 + i : e * 8 + 5 + i, :] = shift_in[e].astype(F32)[i : i + 1]
            pin[e * 2 + i : e * 2 + i + 1, :] = bin_in[e].astype(F32)[i : i + 1]
        pfi[e : e + 1, :] = bfi_in[...].astype(F32)[e : e + 1]
    acc_s[...] = jnp.zeros_like(acc_s)
    acc_b[...] = jnp.zeros_like(acc_b)
    acc_f[...] = jnp.zeros_like(acc_f)

    r32 = lax.broadcasted_iota(jnp.int32, (32, 32), 0)
    c32 = lax.broadcasted_iota(jnp.int32, (32, 32), 1)
    own_pos = jnp.zeros((32, 32), F32)
    set_col = jnp.zeros((32, 32), F32)
    for g in range(32):
        at = (g % 2) * 16 + g // 2
        own_pos = jnp.where(r32 == at, posi[g].astype(F32), own_pos)
        set_col = jnp.where(c32 == at, dsid[g].astype(F32), set_col)
    col_group = ((c32 % 16) * 2 + c32 // 16).astype(F32)
    chosen = jnp.where(own_pos == col_group, 1.0, 0.0)
    own_set = jnp.sum(chosen * set_col, axis=1, keepdims=True)
    masks[0:32, :] = chosen
    masks[32:64, :] = jnp.where(set_col == own_set, 1.0, 0.0)

    lane_lo = lax.broadcasted_iota(jnp.int32, (1, 128), 1) < HD

    def side(v, hh):
        return jnp.where(lane_lo if hh == 0 else jnp.logical_not(lane_lo), v, jnp.zeros_like(v))

    def exchange(e, b, parity):
        slot = 0 if e == 0 else 1 + b
        rows = rows_at(b * BLK[e], BLK[e]) if not isinstance(b, int) else pl.ds(b * BLK[e], BLK[e])
        return pltpu.make_async_remote_copy(
            src_ref=EXS[e].at[rows],
            dst_ref=EXR[e].at[parity, rows],
            send_sem=exs_sem.at[slot],
            recv_sem=exr_sem.at[parity, slot],
            device_id=partner,
            device_id_type=MESH_ID,
        )

    def block_rows(e, b):
        if e == 0:
            return pl.ds(0, BLK[0])
        return rows_at(b * BLK[1], BLK[1], BLK[1])

    def blocks(e, body):
        if e == 0:
            body(0)
        else:
            pl.loop(0, 2)(body)

    def project(e, b, which):
        rows = block_rows(e, b)
        xb = X[e][rows, :]
        for j in which:
            cols = pl.ds(j * COLS, COLS)
            got = dot(xb, win[e, :, cols])
            if j == 0:
                got = (got + pin[e * 2 : e * 2 + 1, :]).astype(BF16) * jnp.asarray(HD**-0.5, BF16)
            elif j == 2:
                got = got + pin[e * 2 + 1 : e * 2 + 2, :]
            QKV[e][rows, cols] = got.astype(BF16)

    def attend(e, b):
        size = BLK[e]
        rows = block_rows(e, b)
        col = lax.broadcasted_iota(jnp.int32, (size, size), 1)
        if e == 0:
            row = lax.broadcasted_iota(jnp.int32, (size, size), 0)
            first = jnp.logical_and(row < 64, col < qlen[0])
            second = jnp.logical_and(
                row >= 64, jnp.logical_and(col >= 64, col < 64 + qlen[1])
            )
            seen = jnp.logical_or(first, second)
        else:
            seen = col < plen[b]

        @pl.loop(0, 3, unroll=PAIR_UNROLL[e])
        def _(pair):
            q2 = QKV[e][rows, rows_at(pair * 128, 128, 128)]
            k2 = QKV[e][rows, rows_at(COLS + pair * 128, 128, 128)]
            v2 = QKV[e][rows, rows_at(2 * COLS + pair * 128, 128, 128)]
            total = jnp.zeros((size, 128), F32)
            for hh in range(2):
                s = dot_t(side(q2, hh), k2)
                s = jnp.where(seen, s, NEGATIVE)
                p = jnp.exp(s - jnp.max(s, axis=-1, keepdims=True))
                p = (p * (1.0 / jnp.sum(p, axis=-1, keepdims=True))).astype(BF16)
                PR[e][b, pair * 2 + hh] = p
                total = total + dot(p, side(v2, hh))
            BALL[e][rows, rows_at(8 * COLS + pair * 128, 128, 128)] = total.astype(BF16)

        ctx = BALL[e][rows, pl.ds(8 * COLS, COLS)]
        EXS[e][rows, :] = dot(ctx, wo[e]).astype(BF16)
        exchange(e, b, 0).start()

    CH = CHUNK

    def first_norm(e, b):
        exchange(e, b, 0).wait()

        @pl.loop(0, BLK[e] // CH, unroll=NORM_UNROLL[e])
        def _(c):
            rows = rows_at(b * BLK[e] + c * CH, CH, CH)
            v = (
                X[e][rows, :].astype(F32)
                + (EXS[e][rows, :].astype(F32) + EXR[e][0, rows, :].astype(F32))
                + par[e * 8 : e * 8 + 1, :]
            )
            v = v - row_mean(v)
            inv = lax.rsqrt(row_mean(v * v) + EPSILON)
            n = v * inv
            N1[e][rows, :] = n
            I1[e][rows, :] = inv
            HID[e][rows, :] = (
                n * par[e * 8 + 2 : e * 8 + 3, :] + par[e * 8 + 4 : e * 8 + 5, :]
            ).astype(BF16)

    def feed(e, b):
        rows = block_rows(e, b)

        @pl.loop(0, 6, unroll=UP_UNROLL[e])
        def _(n):
            cols = rows_at(n * 256, 256, 256)
            u = dot(HID[e][rows, :], wf[e, :, cols]) + pfi[e : e + 1, cols]
            a, slope = gelu_and_slope(u)
            BALL[e][rows, cols] = a.astype(BF16)
            SLOPE[e][rows, cols] = slope.astype(BF16)

        @pl.loop(0, 3, unroll=DOWN_UNROLL[e])
        def _(n):
            cols = rows_at(n * 256, 256, 256)
            EXS[e][rows, cols] = dot(BALL[e][rows, pl.ds(0, FF_HERE)], wd[e, :, cols]).astype(BF16)

        exchange(e, b, 1).start()

    def second_norm(e, b):
        exchange(e, b, 1).wait()

        @pl.loop(0, BLK[e] // CH, unroll=NORM_UNROLL[e])
        def _(c):
            rows = rows_at(b * BLK[e] + c * CH, CH, CH)
            v = (
                HID[e][rows, :].astype(F32)
                + (EXS[e][rows, :].astype(F32) + EXR[e][1, rows, :].astype(F32))
                + par[e * 8 + 1 : e * 8 + 2, :]
            )
            v = v - row_mean(v)
            inv = lax.rsqrt(row_mean(v * v) + EPSILON)
            n = v * inv
            N2[e][rows, :] = n
            I2[e][rows, :] = inv
            OB[e][rows, :] = (
                n * par[e * 8 + 3 : e * 8 + 4, :] + par[e * 8 + 5 : e * 8 + 6, :]
            ).astype(BF16)

    def mini_exchange(k):
        return pltpu.make_async_remote_copy(
            src_ref=xms.at[k],
            dst_ref=xmr.at[k],
            send_sem=xms_sem.at[k],
            recv_sem=xmr_sem.at[k],
            device_id=partner,
            device_id_type=MESH_ID,
        )

    def first_rows(ref):
        rows = [ref[b * 256 : b * 256 + 16, :].astype(F32)[0:1] for b in range(2)]
        return jnp.concatenate([*rows, jnp.zeros((14, rows[0].shape[1]), F32)], axis=0)

    def mini_attend():
        xm = first_rows(xp).astype(BF16)
        q = (dot(xm, win[1, :, pl.ds(0, COLS)]) + pin[2:3, :]).astype(BF16).astype(F32) * HD**-0.5
        of_head = lax.broadcasted_iota(jnp.int32, (16, COLS), 1) // HD == lax.broadcasted_iota(
            jnp.int32, (16, COLS), 0
        )
        col = lax.broadcasted_iota(jnp.int32, (16, 256), 1)
        rows = []
        for b in range(2):
            keys = qkvp[b * 256 : (b + 1) * 256, COLS : 2 * COLS]
            vals = qkvp[b * 256 : (b + 1) * 256, 2 * COLS : 3 * COLS]
            s = dot_t(jnp.where(of_head, q[b : b + 1], 0.0).astype(BF16), keys)
            s = jnp.where(col < plen[b], s, NEGATIVE)
            p = jnp.exp(s - jnp.max(s, axis=-1, keepdims=True))
            p = (p * (1.0 / jnp.sum(p, axis=-1, keepdims=True))).astype(BF16)
            rows.append(jnp.sum(jnp.where(of_head, dot(p, vals), 0.0), axis=0, keepdims=True))
        ctx = jnp.concatenate([*rows, jnp.zeros((14, COLS), F32)], axis=0)
        xms[0] = dot(ctx.astype(BF16), wo[1]).astype(BF16)
        mini_exchange(0).start()

    def mini_norm(k, v):
        mini_exchange(k).wait()
        v = v + (xms[k].astype(F32) + xmr[k].astype(F32)) + par[8 + k : 9 + k, :]
        v = v - row_mean(v)
        n = v * lax.rsqrt(row_mean(v * v) + EPSILON)
        return (n * par[10 + k : 11 + k, :] + par[12 + k : 13 + k, :]).astype(BF16)

    def mini_feed():
        hm[...] = mini_norm(0, first_rows(xp))

        u = dot(hm[...], wf[1]) + pfi[1:2, :]
        a = gelu_and_slope(u)[0].astype(BF16)
        xms[1] = dot(a, wd[1]).astype(BF16)

        mini_exchange(1).start()

    def transpose_into(e, k, src, b):
        rows = block_rows(e, b)

        @pl.loop(0, 2)
        def _(c):
            tile = src[rows, rows_at(c * COLS, COLS, 128)].T
            AT[e][k, pl.ds(c * 2, 2), :, :, :, rows] = tile.reshape(2, 2, 2, ROWS_OUT, BLK[e])

    def left_factor(axis, k):
        return pltpu.make_async_remote_copy(
            src_ref=atq.at[k, :, :, 1 - x] if axis == 0 else atq.at[k, :, 1 - y],
            dst_ref=fra.at[axis, k],
            send_sem=fas_sem.at[axis, k],
            recv_sem=far_sem.at[axis, k],
            device_id=first_dev[axis],
            device_id_type=MESH_ID,
        )

    def right_factor(axis, pair):
        return pltpu.make_async_remote_copy(
            src_ref=ballq.at[:, pl.ds((pair * 2 + axis) * COLS, COLS)],
            dst_ref=frb.at[axis, pair],
            send_sem=fbs_sem.at[axis, pair],
            recv_sem=fbr_sem.at[axis, pair],
            device_id=first_dev[axis],
            device_id_type=MESH_ID,
        )

    first_dev, other_dev = (at_x, at_y), (at_y, at_x)
    first_at, other_at = (x, y), (y, x)

    need(0, 1, 2, 3)
    load(4, 6, 7, 8, 5, 9, 10, 12, 11, 13, 14, 15)
    project(0, 0, (0, 1, 2))
    need(8)
    pl.semaphore_wait(barrier, 16)
    attend(0, 0)
    right_factor(0, 4).start()
    need(4, 5, 6, 7, 9)
    blocks(1, lambda b: project(1, b, (1, 2)))
    mini_attend()
    first_norm(0, 0)
    need(10, 12)
    feed(0, 0)
    for axis in range(2):
        for pair in range(2):
            right_factor(axis, pair).start()
    need(11, 13)
    mini_feed()
    second_norm(0, 0)
    out_q = pltpu.make_async_copy(obq, oq_out, out_sem.at[0])
    out_p = pltpu.make_async_copy(obp, op_out, out_sem.at[1])
    out_q.start()
    mini_out = mini_norm(1, hm[...].astype(F32)).astype(F32)

    pieces = []
    rows = [obq[at : at + 16, :].astype(F32)[0:1] for at in (0, 64)]
    for head in (*rows, mini_out[0:1], mini_out[1:2]):
        pieces += [head[:, k * 256 : (k + 1) * 256] for k in range(3)]
    pieces.append(jnp.zeros((4, 256), F32))
    hg[me] = jnp.concatenate(pieces, axis=0).astype(BF16)

    def heads(k):
        return pltpu.make_async_remote_copy(
            src_ref=hg.at[me],
            dst_ref=hg.at[me],
            send_sem=hgs_sem.at[k],
            recv_sem=hgr_sem.at[k],
            device_id=at_dp(me ^ k),
            device_id_type=MESH_ID,
        )

    for k in range(1, 16):
        heads(k).start()
    need(14, 15)
    transpose_into(0, 1, hq, 0)
    for axis in range(2):
        left_factor(axis, 1).start()
    transpose_into(0, 3, xq, 0)
    for axis in range(2):
        left_factor(axis, 3).start()
    blocks(1, lambda b: project(1, b, (0,)))
    attend(1, 0)
    for k in range(1, 16):
        copy = pltpu.make_async_remote_copy(
            src_ref=hg.at[me],
            dst_ref=hg.at[me ^ k],
            send_sem=hgs_sem.at[k],
            recv_sem=hgr_sem.at[k],
            device_id=at_dp(me ^ k),
            device_id_type=MESH_ID,
        )
        copy.wait()
    gathered = hg[...].astype(F32).reshape(256, 256)
    hf[0] = gathered[:, 0:128]
    hf[1] = gathered[:, 128:256]

    def all_heads(first):
        groups = []
        for i in range(2):
            parts = [
                hf[c, pl.ds(first + i * 3 + k, 16, stride=16), :] for k in range(3) for c in range(2)
            ]
            groups.append(jnp.concatenate(parts, axis=1))
        return jnp.concatenate(groups, axis=0)

    heads_q, heads_p = all_heads(0), all_heads(6)
    gain = score_gain * D ** (-0.5)
    class_scores = dot_t(heads_q.astype(BF16), heads_p.astype(BF16)) * gain
    chosen = masks[0:32, :]
    logits = jnp.where(masks[32:64, :] > 0.5, class_scores, NEGATIVE)
    top = jnp.max(logits, axis=1, keepdims=True)
    log_total = top + jnp.log(jnp.sum(jnp.exp(logits - top), axis=1, keepdims=True))
    target = jnp.sum(chosen * class_scores, axis=1, keepdims=True)
    loss = jnp.sum(log_total - target, axis=0, keepdims=True) * (1.0 / 32)
    sm[SMALL : SMALL + 8, :] = jnp.broadcast_to(loss, (8, 128))
    d_class = (jnp.exp(logits - log_total) - chosen) * gain
    dh[0:32, :] = lax.dot_general(
        d_class, heads_p, (((1,), (0,)), ((), ())), precision=HIGHEST, preferred_element_type=F32
    )
    dh[32:64, :] = lax.dot_general(
        d_class, heads_q, (((0,), (0,)), ((), ())), precision=HIGHEST, preferred_element_type=F32
    )

    def norm_back(incoming, n, inv, scale):
        scaled = incoming * scale
        return inv * (scaled - row_mean(scaled) - n * row_mean(scaled * n))

    def second_back(e, b):
        row0 = lax.broadcasted_iota(jnp.int32, (CH, 1), 0)
        seqs = 2 if e == 0 else 1
        length = 64 if e == 0 else 256
        for i in range(seqs):
            group = i if e == 0 else b
            extra = dh[pl.ds(e * 32 + group * 16 + me, 1), :]

            @pl.loop(0, length // CH, unroll=NORM_UNROLL[e])
            def _(c):
                rows = rows_at(group * length + c * CH, CH, CH)
                add = jnp.where(row0 + c * CH == 0, extra, 0.0)
                d = COT[e][rows, :].astype(F32) + add
                n = N2[e][rows, :]
                out = norm_back(d, n, I2[e][rows, :], par[e * 8 + 3 : e * 8 + 4, :])
                N2[e][rows, :] = out
                low = out.astype(BF16)
                DD[e][rows, :] = low
                acc_s[e * 6 + 1] += fold8(d * n)
                acc_s[e * 6 + 3] += fold8(d)
                acc_s[e * 6 + 5] += fold8(low.astype(F32))

        transpose_into(e, 0, DD[e], b)

    def feed_back(e, b):
        rows = block_rows(e, b)

        @pl.loop(0, 6, unroll=UP_UNROLL[e])
        def _(n):
            cols = rows_at(n * 256, 256, 256)
            d = dot_t(DD[e][rows, :], wd[e, cols, :]) * SLOPE[e][rows, cols].astype(F32)
            d = d.astype(BF16)
            BALL[e][rows, rows_at(4 * COLS + n * 256, 256, 256)] = d
            acc_f[e, :, cols] += fold8(d.astype(F32))

        @pl.loop(0, 3, unroll=DOWN_UNROLL[e])
        def _(n):
            cols = rows_at(n * 256, 256, 256)
            EXS[e][rows, cols] = dot_t(BALL[e][rows, pl.ds(4 * COLS, FF_HERE)], wf[e, cols, :]).astype(BF16)

        exchange(e, b, 0).start()
        if e == 1:
            transpose_into(e, 1, HID[e], b)

    def first_back(e, b):
        exchange(e, b, 0).wait()

        @pl.loop(0, BLK[e] // CH, unroll=NORM_UNROLL[e])
        def _(c):
            rows = rows_at(b * BLK[e] + c * CH, CH, CH)
            d = N2[e][rows, :] + (EXS[e][rows, :].astype(F32) + EXR[e][0, rows, :].astype(F32))
            n = N1[e][rows, :]
            out = norm_back(d, n, I1[e][rows, :], par[e * 8 + 2 : e * 8 + 3, :])
            N1[e][rows, :] = out
            low = out.astype(BF16)
            DD[e][rows, :] = low
            acc_s[e * 6 + 0] += fold8(d * n)
            acc_s[e * 6 + 2] += fold8(d)
            acc_s[e * 6 + 4] += fold8(low.astype(F32))

        transpose_into(e, 2, DD[e], b)

    def attend_back(e, b):
        rows = block_rows(e, b)
        size = BLK[e]
        DC[e][rows, :] = dot_t(DD[e][rows, :], wo[e]).astype(BF16)

        @pl.loop(0, 3, unroll=PAIR_UNROLL[e])
        def _(pair):
            q2 = QKV[e][rows, rows_at(pair * 128, 128, 128)]
            k2 = QKV[e][rows, rows_at(COLS + pair * 128, 128, 128)]
            v2 = QKV[e][rows, rows_at(2 * COLS + pair * 128, 128, 128)]
            dc2 = DC[e][rows, rows_at(pair * 128, 128, 128)]
            dq = jnp.zeros((size, 128), F32)
            dk = jnp.zeros((size, 128), F32)
            dv = jnp.zeros((size, 128), F32)
            for hh in range(2):
                low = PR[e][b, pair * 2 + hh]
                p = low.astype(F32)
                dch = side(dc2, hh)
                dp = dot_t(dch, v2)
                ds = (p * (dp - jnp.sum(p * dp, axis=-1, keepdims=True))).astype(BF16)
                dv = dv + t_dot(low, dch)
                dq = dq + dot(ds, side(k2, hh))
                dk = dk + t_dot(ds, side(q2, hh))
            dq = (dq * HD**-0.5).astype(BF16)
            dv = dv.astype(BF16)
            cols = rows_at(pair * 128, 128, 128)
            BALL[e][rows, rows_at(9 * COLS + pair * 128, 128, 128)] = dq
            BALL[e][rows, rows_at(10 * COLS + pair * 128, 128, 128)] = dk.astype(BF16)
            BALL[e][rows, rows_at(11 * COLS + pair * 128, 128, 128)] = dv
            acc_b[e, :, cols] += fold8(dq.astype(F32))
            acc_b[e, :, rows_at(COLS + pair * 128, 128, 128)] += fold8(dv.astype(F32))

        if e == 1:
            transpose_into(e, 3, X[e], b)

    def token_back(e, b):
        rows = block_rows(e, b)

        @pl.loop(0, 3, unroll=DOWN_UNROLL[e])
        def _(n):
            cols = rows_at(n * 256, 256, 256)
            EXS[e][rows, cols] = dot_t(BALL[e][rows, pl.ds(9 * COLS, 3 * COLS)], win[e, cols, :]).astype(BF16)

        exchange(e, b, 1).start()

    def token_end(e, b):
        exchange(e, b, 1).wait()

        @pl.loop(0, BLK[e] // CH, unroll=NORM_UNROLL[e])
        def _(c):
            rows = rows_at(b * BLK[e] + c * CH, CH, CH)
            OB[e][rows, :] = (
                N1[e][rows, :] + (EXS[e][rows, :].astype(F32) + EXR[e][1, rows, :].astype(F32))
            ).astype(BF16)

    def job_of(j):
        return j // 6, j % 6

    def product(half, blk, sel):
        k = jnp.where(blk < 8, blk // 4, jnp.where(blk == 8, 2, 3))
        rows = atp[k, :, :, sel] if half == 0 else atp[k, :, sel]
        out = dot(rows.reshape(COLS, TOKS[1]), ballp[:, rows_at(blk * COLS, COLS, 128)])
        return out.reshape(ZN, 2, ROWS_OUT, COLS)

    def pair_product(half, pair):
        blk = pair * 2 + half
        k = blk // 4 if blk < 8 else 2 if blk == 8 else 3
        rows = atq[k, :, :, x] if half == 0 else atq[k, :, y]
        rows = jnp.concatenate([rows.reshape(COLS, TOKS[0]), fra[half, k].reshape(COLS, TOKS[0])], axis=1)
        cols = jnp.concatenate([ballq[:, blk * COLS : (blk + 1) * COLS], frb[half, pair]], axis=0)
        return dot(rows, cols).reshape(ZN, 2, ROWS_OUT, COLS)

    def p1(j, half):
        return pltpu.make_async_remote_copy(
            src_ref=p1s.at[j % DS, half],
            dst_ref=p1r.at[j % D1, half],
            send_sem=p1s_sem.at[j % DS, half],
            recv_sem=p1r_sem.at[j % D1, half],
            device_id=first_dev[half],
            device_id_type=MESH_ID,
        )

    def other(j, half, line_first):
        mine, to = p1r.at[j % D1, half], p2r.at[j % D2, half]
        return pltpu.make_async_remote_copy(
            src_ref=mine.at[z, 1 - other_at[half]] if line_first else mine.at[:, 1 - other_at[half]],
            dst_ref=to.at[0] if line_first else to,
            send_sem=p2s_sem.at[j % D2, half],
            recv_sem=p2r_sem.at[j % D2, half],
            device_id=other_dev[half],
            device_id_type=MESH_ID,
        )

    def block(j, half, d, right, line_first, at):
        slot = d if right else jnp.where(d == at, ZN, d)
        return zb.at[j % DZ, half, slot] if line_first else zb.at[j % DZ, half, slot, 0]

    def own_block(j, half, d, line_first):
        return p1r.at[j % D1, half, d] if line_first else p2r.at[j % D2, half, d]

    def along(j, half, d, right, relayed, line_first):
        send, recv = (zrs_sem, zrr_sem) if right else (zls_sem, zlr_sem)
        here = block(j, half, d, right, line_first, z)
        return pltpu.make_async_remote_copy(
            src_ref=here if relayed else own_block(j, half, d, line_first),
            dst_ref=block(j, half, d, right, line_first, z + 1 if right else z - 1),
            send_sem=send.at[j % DZ, half, d],
            recv_sem=recv.at[j % DZ, half, d],
            device_id=at_dp(me + 4 if right else me - 4),
            device_id_type=MESH_ID,
        )

    def total_of(a, b):
        return (a[...].astype(F32) + b[...].astype(F32)).astype(BF16)

    def step0(j):
        _, pair = job_of(j)
        for half in range(2):
            p1s[j % DS, half] = product(half, pair * 2 + half, 1 - first_at[half]).astype(BF16)
            p1(j, half).start()

    def step1(j):
        e_of, pair = job_of(j)

        @pl.when(e_of == 1)
        def _():
            for half in range(2):
                p1(j, half).wait()
            for half in range(2):
                own = product(half, pair * 2 + half, first_at[half])
                p1r[j % D1, half] = (own + p1r[j % D1, half].astype(F32)).astype(BF16)

        for p in range(6):

            @pl.when(jnp.logical_and(e_of == 0, pair == p))
            def _():
                for half in range(2):
                    if p in (0, 2):
                        left_factor(half, p // 2).wait()
                    elif p == 4:
                        left_factor(half, 2 + half).wait()
                    elif p == 5 and half == 0:
                        left_factor(0, 3).wait()
                    right_factor(half, p).wait()
                    p1r[j % D1, half] = pair_product(half, p).astype(BF16)

    def turn(j):
        for half in range(2):
            other(j, half, False).start()

    def turned(j):
        for half in range(2):
            other(j, half, False).wait()
            mine = p2r.at[j % D2, half]
            mine[...] = total_of(mine, p1r.at[j % D1, half, :, other_at[half]])

    def ends(j, line_first):
        @pl.when(z == 0)
        def _():
            for half in range(2):
                for d in (3, 2, 1):
                    along(j, half, d, True, False, line_first).start()

        @pl.when(z == 3)
        def _():
            for half in range(2):
                for d in (0, 1, 2):
                    along(j, half, d, False, False, line_first).start()

    def relay(j, half, d, right, line_first):
        held = block(j, half, d, right, line_first, z)
        along(j, half, d, right, True, line_first).wait_recv()
        held[...] = total_of(held, own_block(j, half, d, line_first))
        along(j, half, d, right, True, line_first).start()

    def middle1(j, line_first):
        @pl.when(z == 1)
        def _():
            for half in range(2):
                for d in (3, 2):
                    relay(j, half, d, True, line_first)

        @pl.when(z == 2)
        def _():
            for half in range(2):
                for d in (0, 1):
                    relay(j, half, d, False, line_first)

    def middle2(j, line_first):
        @pl.when(z == 2)
        def _():
            for half in range(2):
                relay(j, half, 3, True, line_first)

        @pl.when(z == 1)
        def _():
            for half in range(2):
                relay(j, half, 0, False, line_first)

    def line_end(j, line_first):
        for half in range(2):
            mine = own_block(j, half, z, line_first)

            @pl.when(z > 0)
            def _():
                along(j, half, z, True, True, line_first).wait_recv()
                mine[...] = total_of(mine, block(j, half, z, True, line_first, z))

            @pl.when(z < 3)
            def _():
                along(j, half, z, False, True, line_first).wait_recv()
                mine[...] = total_of(mine, block(j, half, z, False, line_first, z))

            for d in range(4):

                @pl.when(d > z)
                def _():
                    along(j, half, d, True, True, line_first).wait_send()

                @pl.when(d < z)
                def _():
                    along(j, half, d, False, True, line_first).wait_send()

    def pass_on(j):
        for half in range(2):
            other(j, half, True).start()

    def passed(j):
        for half in range(2):
            other(j, half, True).wait()

    def result(slot, half, to):
        return pltpu.make_async_copy(fin.at[slot, half], to, fin_sem.at[slot, half])

    def output(j, line_first):
        e_of, pair = job_of(j)
        for half in range(2):

            @pl.when(j >= 2)
            def _():
                result(j % 2, half, g_out.at[0]).wait()

            if line_first:
                total = p1r[j % D1, half, z, other_at[half]].astype(F32) + p2r[j % D2, half, 0].astype(F32)
            else:
                total = p2r[j % D2, half, z].astype(F32)
            fin[j % 2, half] = total
            for e in range(2):
                for p in range(6):

                    @pl.when(jnp.logical_and(e_of == e, pair == p))
                    def _():
                        blk = p * 2 + half
                        if blk < 4:
                            to = g_fo.at[e, :, pl.ds(blk * COLS, COLS)]
                        elif blk < 8:
                            to = g_fi.at[e, :, pl.ds((blk - 4) * COLS, COLS)]
                        elif blk == 8:
                            to = g_out.at[e]
                        else:
                            to = g_in.at[e, blk - 9]
                        result(j % 2, half, to).start()

    small_to = (at_x, at_y, at_dp(me ^ 4), at_dp(me ^ 8))

    def small(k):
        return pltpu.make_async_remote_copy(
            src_ref=smb.at[k],
            dst_ref=smr.at[k],
            send_sem=sms_sem.at[k],
            recv_sem=smr_sem.at[k],
            device_id=small_to[k],
            device_id_type=MESH_ID,
        )

    def small_first():
        smb[0] = jnp.zeros_like(smb[0])
        for e in range(2):
            for i in range(6):
                smb[0, e * 9 + i : e * 9 + i + 1, :] = jnp.sum(acc_s[e * 6 + i], axis=0, keepdims=True)
            smb[0, e * 9 + 6 : e * 9 + 7, :] = jnp.sum(acc_b[e], axis=0, keepdims=True)
            for i in range(2):
                smb[0, e * 9 + 7 + i : e * 9 + 8 + i, :] = jnp.sum(
                    acc_f[e, :, i * D : (i + 1) * D], axis=0, keepdims=True
                )
        small(0).start()

    def small_next(k):
        small(k).wait()
        if k < 3:
            smb[k + 1] = smb[k] + smr[k]
            small(k + 1).start()
        else:
            total = smb[k] + smr[k]
            sm[0:SMALL, :] = jnp.zeros((SMALL, 128), F32)
            wide = pltpu.roll(total, lax.rem(D - me * ROWS_OUT, D), 1)
            sm[0:SMALL, 0:ROWS_OUT] = wide[:, 0:ROWS_OUT]
            heads_own = pltpu.roll(total, lax.rem(D - me * 24, D), 1)
            feed_own = pltpu.roll(total, lax.rem(D - (me % 8) * 96, D), 1)
            for e in range(2):
                at = e * 9 + 6
                for i in range(2):
                    sm[at + i : at + i + 1, 0:24] = heads_own[at : at + 1, i * COLS : i * COLS + 24]
                low, high = feed_own[at + 1 : at + 2, 0:96], feed_own[at + 2 : at + 3, 0:96]
                sm[at + 2 : at + 3, 0:96] = jnp.where(me < 8, low, high)
            pltpu.make_async_copy(sm, sm_out, out_sem.at[2]).start()

    def q_second_back():
        second_back(0, 0)
        left_factor(0, 0).start()
        left_factor(1, 0).start()

    def q_feed_back():
        feed_back(0, 0)
        for axis in range(2):
            for pair in (2, 3):
                right_factor(axis, pair).start()

    def q_first_back():
        first_back(0, 0)
        left_factor(0, 2).start()

    def q_attend_back():
        attend_back(0, 0)
        right_factor(1, 4).start()
        right_factor(0, 5).start()
        right_factor(1, 5).start()

    def q_token_end():
        token_end(0, 0)
        pltpu.make_async_copy(obq, gq_out, out_sem.at[0]).start()

    def p_token_end():
        blocks(1, lambda b: token_end(1, b))
        pltpu.make_async_copy(obp, gp_out, out_sem.at[1]).start()

    def p_mid(b):
        first_norm(1, b)
        feed(1, b)

    def p_second():
        blocks(1, lambda b: second_norm(1, b))
        out_p.start()

    def passages(piece):
        return lambda: blocks(1, lambda b: piece(1, b))

    work = {
        1: [q_feed_back, lambda: attend(1, 1)],
        2: [q_first_back, lambda: p_mid(0), q_attend_back, lambda: p_mid(1)],
        3: [lambda: token_back(0, 0), p_second, out_q.wait, q_token_end, passages(second_back)],
        4: [passages(feed_back)],
        7: [passages(first_back), passages(attend_back)],
        9: [passages(token_back)],
        11: [small_first],
        12: [out_p.wait, p_token_end, lambda: small_next(0)],
        13: [lambda: small_next(1)],
        14: [lambda: small_next(2)],
        15: [lambda: small_next(3)],
    }

    def is_line_first(j):
        found = j == LINE_FIRST[0]
        for k in LINE_FIRST[1:]:
            found = jnp.logical_or(found, j == k)
        return found

    def steps(late, j):
        line_first = is_line_first(j)
        if late == 1:
            step1(j)

        @pl.when(line_first)
        def _():
            if late == 1:
                ends(j, True)
            elif late == 2:
                middle1(j, True)
            elif late == 3:
                middle2(j, True)
            elif late == 4:
                line_end(j, True)
                pass_on(j)
            else:
                passed(j)
                output(j, True)

        @pl.when(jnp.logical_not(line_first))
        def _():
            if late == 1:
                turn(j)
            elif late == 2:
                turned(j)
                ends(j, False)
            elif late == 3:
                middle1(j, False)
            elif late == 4:
                middle2(j, False)
            else:
                line_end(j, False)
                output(j, False)

    q_second_back()

    @pl.loop(0, JOBS + 5)
    def _(tick):
        for at, things in work.items():

            @pl.when(tick == at)
            def _():
                for thing in things:
                    thing()

        @pl.when(jnp.logical_and(tick >= 6, tick < JOBS))
        def _():
            step0(tick)

        for late in (1, 2, 3, 4, 5):

            @pl.when(jnp.logical_and(tick >= late, tick < JOBS + late))
            def _():
                steps(late, tick - late)

    pltpu.make_async_copy(obq, gq_out, out_sem.at[0]).wait()
    pltpu.make_async_copy(obp, gp_out, out_sem.at[1]).wait()
    pltpu.make_async_copy(sm, sm_out, out_sem.at[2]).wait()
    for slot in range(2):
        for half in range(2):
            result(slot, half, g_out.at[0]).wait()


def finish_kernel(*refs):
    oq, op, gq, gp, g_in, g_out, g_fi, g_fo, sums_in = refs[:9]
    large, (loss_to, in_bias, fi_bias, bo, gain, shift) = refs[9:17], refs[17:23]
    held, sums, in_sems, out_sems = refs[23:31], refs[31], refs[32], refs[33]
    sources = (oq, op, gq, gp, g_in, g_out, g_fi, g_fo)
    loads = [pltpu.make_async_copy(sources[i], held[i], in_sems.at[i]) for i in range(8)]
    stores = [pltpu.make_async_copy(held[i], large[i], out_sems.at[i]) for i in range(8)]
    little = pltpu.make_async_copy(sums_in, sums, in_sems.at[8])
    little.start()
    for load in loads:
        load.start()
    little.wait()
    loss_to[...] = sums[SMALL : SMALL + 1, 0:1]
    for e in range(2):
        at = e * 9
        gain[e] = sums[at : at + 2, 0:ROWS_OUT]
        shift[e] = sums[at + 2 : at + 4, 0:ROWS_OUT]
        bo[e] = sums[at + 4 : at + 6, 0:ROWS_OUT]
        in_bias[e] = sums[at + 6 : at + 8, 0:24]
        fi_bias[e : e + 1] = sums[at + 8 : at + 9, 0:96]
    for load, store in zip(loads, stores):
        load.wait()
        store.start()
    for store in stores:
        store.wait()


FF_HERE = 1536


def fused(
    question_tokens, passage_tokens, question_cotangent, passage_cotangent,
    question_lengths, passage_lengths, dataset_ids, positives,
    attn_in, attn_in_bias, attn_out, ffn_in, ffn_in_bias, ffn_out, out_biases, norm_gains, norm_shifts,
):
    any_spec = pl.BlockSpec(memory_space=pl.ANY)
    vmem = pl.BlockSpec(memory_space=pltpu.VMEM)

    def both(shape, dtype):
        return [pltpu.VMEM(shape(m), dtype) for m in TOKS]

    shape = jax.ShapeDtypeStruct
    dma = pltpu.SemaphoreType.DMA
    outs = pl.pallas_call(
        partial(fused_kernel, last=0),
        name="fused",
        in_specs=[any_spec] * 17,
        out_specs=[any_spec] * 9,
        out_shape=[
            shape((128, D), BF16),
            shape((512, D), BF16),
            shape((128, D), BF16),
            shape((512, D), BF16),
            shape((2, 3, ROWS_OUT, COLS), F32),
            shape((2, ROWS_OUT, COLS), F32),
            shape((2, ROWS_OUT, FF_HERE), F32),
            shape((2, ROWS_OUT, FF_HERE), F32),
            shape((SMALL + 8, 128), F32),
        ],
        scratch_shapes=[
            pltpu.VMEM((2, D, 3 * COLS), BF16),
            pltpu.VMEM((2, COLS, D), BF16),
            pltpu.VMEM((2, D, FF_HERE), BF16),
            pltpu.VMEM((2, FF_HERE, D), BF16),
            *both(lambda m: (m, D), BF16),
            *both(lambda m: (m, D), BF16),
            *both(lambda m: (m, 3 * COLS), BF16),
            pltpu.VMEM((1, 6, 128, 128), BF16),
            pltpu.VMEM((2, 6, 256, 256), BF16),
            *both(lambda m: (m, D), BF16),
            *both(lambda m: (m, D), F32),
            *both(lambda m: (m, D), F32),
            *both(lambda m: (m, 1), F32),
            *both(lambda m: (m, 1), F32),
            *both(lambda m: (m, FF_HERE), BF16),
            *both(lambda m: (m, D), BF16),
            *both(lambda m: (m, D), BF16),
            *both(lambda m: (m, COLS), BF16),
            *both(lambda m: (m, 12 * COLS), BF16),
            *both(lambda m: (4, ZN, 2, 2, ROWS_OUT, m), BF16),
            *both(lambda m: (m, D), BF16),
            *both(lambda m: (2, m, D), BF16),
            pltpu.VMEM((16, D), F32),
            pltpu.VMEM((8, COLS), F32),
            pltpu.VMEM((8, FF_HERE), F32),
            pltpu.VMEM((64, 32), F32),
            pltpu.VMEM((16, 16, 256), BF16),
            pltpu.VMEM((2, 256, 128), F32),
            pltpu.VMEM((64, D), F32),
            pltpu.VMEM((12, 8, D), F32),
            pltpu.VMEM((2, 8, 2 * COLS), F32),
            pltpu.VMEM((2, 8, FF_HERE), F32),
            pltpu.VMEM((4, SMALL, D), F32),
            pltpu.VMEM((4, SMALL, D), F32),
            pltpu.VMEM((DS, 2, ZN, 2, ROWS_OUT, COLS), BF16),
            pltpu.VMEM((D1, 2, ZN, 2, ROWS_OUT, COLS), BF16),
            pltpu.VMEM((D2, 2, ZN, ROWS_OUT, COLS), BF16),
            pltpu.VMEM((DZ, 2, ZN + 1, 2, ROWS_OUT, COLS), BF16),
            pltpu.VMEM((2, 2, ROWS_OUT, COLS), F32),
            pltpu.VMEM((2, 4, ZN, 2, ROWS_OUT, TOKS[0]), BF16),
            pltpu.VMEM((2, 6, TOKS[0], COLS), BF16),
            pltpu.VMEM((2, 16, D), BF16),
            pltpu.VMEM((2, 16, D), BF16),
            pltpu.VMEM((16, D), BF16),
            *[pltpu.SMEM((n,), jnp.int32) for n in (2, 2, 32, 32)],
            pltpu.VMEM((2, 2, COLS), BF16),
            pltpu.VMEM((2, FF_HERE), BF16),
            *[pltpu.VMEM((2, 2, D), BF16) for _ in range(3)],
            pltpu.VMEM((SMALL + 8, 128), F32),
            dma((2, 2)),
            dma((9,)),
            dma((16,)),
            dma((3,)),
            dma((3,)),
            dma((2, 3)),
            dma((16,)),
            dma((16,)),
            dma((4,)),
            dma((4,)),
            dma((DS, 2)),
            dma((D1, 2)),
            dma((D2, 2)),
            dma((D2, 2)),
            dma((DZ, 2, ZN)),
            dma((DZ, 2, ZN)),
            dma((DZ, 2, ZN)),
            dma((DZ, 2, ZN)),
            dma((2, 4)),
            dma((2, 4)),
            dma((2, 6)),
            dma((2, 6)),
            dma((2,)),
            dma((2,)),
        ],
        compiler_params=pltpu.CompilerParams(
            collective_id=0, has_side_effects=True, vmem_limit_bytes=VMEM_BYTES
        ),
    )(
        question_tokens.reshape(128, D),
        passage_tokens.reshape(512, D),
        question_cotangent.reshape(128, D),
        passage_cotangent.reshape(512, D),
        question_lengths, passage_lengths, dataset_ids, positives,
        attn_in.transpose(0, 2, 1, 3), attn_in_bias, attn_out, ffn_in, ffn_in_bias, ffn_out,
        out_biases, norm_gains, norm_shifts,
    )
    oq, op, gq, gp, g_in, g_out, g_fi, g_fo, sums = outs
    large = (oq, op, gq, gp, g_in, g_out, g_fi, g_fo)
    small = [(1, 1), (2, 2, 24), (2, 96), (2, 2, ROWS_OUT), (2, 2, ROWS_OUT), (2, 2, ROWS_OUT)]
    oq, op, gq, gp, g_in, g_out, g_fi, g_fo, loss, in_bias, fi_bias, bo, gain, shift = pl.pallas_call(
        finish_kernel,
        name="finish",
        in_specs=[any_spec] * 9,
        out_specs=[any_spec] * 8 + [vmem] * 6,
        out_shape=[shape(a.shape, a.dtype) for a in large] + [shape(dims, F32) for dims in small],
        scratch_shapes=[*[pltpu.VMEM(a.shape, a.dtype) for a in (*large, sums)], dma((9,)), dma((8,))],
        compiler_params=pltpu.CompilerParams(vmem_limit_bytes=VMEM_BYTES),
    )(*large, sums)
    return (
        oq.reshape(2, 64, D),
        op.reshape(2, 256, D),
        loss.reshape(()),
        gq.reshape(2, 64, D),
        gp.reshape(2, 256, D),
        g_in.transpose(0, 2, 1, 3),
        in_bias,
        g_out.transpose(0, 2, 1),
        g_fi,
        fi_bias,
        g_fo.transpose(0, 2, 1),
        bo,
        gain,
        shift,
    )


VMEM_BYTES = 62 * 1024 * 1024


def solution(mesh):
    in_specs = (
        P("dp", None, None),
        P("dp", None, None),
        P("dp", None, None),
        P("dp", None, None),
        P("dp"),
        P("dp"),
        P(),
        P(),
        P(None, None, None, "tensor"),
        P(None, None, "tensor"),
        P(None, "tensor", None),
        P(None, None, "tensor"),
        P(None, "tensor"),
        P(None, "tensor", None),
        P(),
        P(),
        P(),
    )
    out_specs = (
        P("dp", None, None),
        P("dp", None, None),
        P(),
        P("dp", None, None),
        P("dp", None, None),
        P(None, "dp", None, "tensor"),
        P(None, None, ("tensor", "dp")),
        P(None, "tensor", "dp"),
        P(None, "dp", "tensor"),
        P(None, ("tensor", "dp")),
        P(None, "tensor", "dp"),
        P(None, None, "dp"),
        P(None, None, "dp"),
        P(None, None, "dp"),
    )
    step = fused if mesh.shape["dp"] == 4 * ZN and mesh.shape["tensor"] == 2 else per_device
    return jax.shard_map(
        step, mesh=mesh, in_specs=in_specs, out_specs=out_specs, check_vma=False
    )
```

```python
from functools import partial

import jax
import jax.numpy as jnp
from jax import lax
from jax.experimental import pallas as pl
from jax.experimental.pallas import tpu as pltpu
from jax.sharding import PartitionSpec as P

D = 768
HD = 64


EPSILON = 1e-06
NEGATIVE = -1e30
HIGHEST = lax.Precision.HIGHEST
score_gain = 3.0


def norm_forward(summed, scale_row, shift_row):
    row_mean = jnp.mean(summed, axis=-1, keepdims=True)
    centred = summed - row_mean
    inv_std = lax.rsqrt(jnp.mean(centred * centred, axis=-1, keepdims=True) + EPSILON)
    normed = centred * inv_std
    return (normed * scale_row + shift_row, normed, inv_std)


def norm_backward(incoming, normed, inv_std, scale_row):
    scaled = incoming * scale_row
    outgoing = inv_std * (
        scaled
        - jnp.mean(scaled, axis=-1, keepdims=True)
        - normed * jnp.mean(scaled * normed, axis=-1, keepdims=True)
    )
    return (outgoing, jnp.sum(incoming * normed, axis=(0, 1)), jnp.sum(incoming, axis=(0, 1)))


def key_visible(lengths, length):
    positions = jnp.arange(length, dtype=jnp.int32)
    return (positions[None, :] < lengths[:, None])[:, None, None, :]


def head_scores(queries, key_rows, visible):
    raw_scores = jnp.einsum(
        "bqhe,bkhe->bhqk", queries, key_rows, preferred_element_type=jnp.float32
    ) * HD ** (-0.5)
    return jnp.where(visible, raw_scores, NEGATIVE)


def split_heads(matrix):
    return matrix.reshape(matrix.shape[0], matrix.shape[1], matrix.shape[2] // HD, HD)


def join_heads(per_head):
    return per_head.reshape(
        per_head.shape[0], per_head.shape[1], per_head.shape[2] * per_head.shape[3]
    )


def encoder_forward(tokens, lengths, params):
    (
        attn_in,
        attn_in_bias,
        attn_out,
        ffn_in,
        ffn_in_bias,
        ffn_out,
        out_biases,
        norm_gains,
        norm_shifts,
    ) = params
    projected = jnp.einsum("bld,dce->blce", tokens, attn_in, preferred_element_type=jnp.float32)
    in_bias = attn_in_bias.astype(jnp.float32)
    queries = split_heads((projected[:, :, 0] + in_bias[0]).astype(jnp.bfloat16))
    key_rows = split_heads(projected[:, :, 1].astype(jnp.bfloat16))
    values = split_heads((projected[:, :, 2] + in_bias[1]).astype(jnp.bfloat16))
    visible = key_visible(lengths, tokens.shape[1])
    scores = head_scores(queries, key_rows, visible)
    row_top = jnp.max(scores, axis=-1, keepdims=True)
    log_total = row_top + jnp.log(jnp.sum(jnp.exp(scores - row_top), axis=-1, keepdims=True))
    attn_probs = jnp.exp(scores - log_total).astype(jnp.bfloat16)
    context = join_heads(
        jnp.einsum(
            "bhqk,bkhe->bqhe", attn_probs, values, preferred_element_type=jnp.float32
        ).astype(jnp.bfloat16)
    )
    attn_part = jnp.einsum("ble,ed->bld", context, attn_out, preferred_element_type=jnp.float32)
    attn_sum = lax.psum(attn_part.astype(jnp.bfloat16), "tensor").astype(jnp.float32)
    bias_rows = out_biases.astype(jnp.float32)
    gain_rows = norm_gains.astype(jnp.float32)
    shift_rows = norm_shifts.astype(jnp.float32)
    hidden_float, normed_first, inv_first = norm_forward(
        tokens.astype(jnp.float32) + attn_sum + bias_rows[0], gain_rows[0], shift_rows[0]
    )
    hidden = hidden_float.astype(jnp.bfloat16)
    up_pre = jnp.einsum(
        "bld,df->blf", hidden, ffn_in, preferred_element_type=jnp.float32
    ) + ffn_in_bias.astype(jnp.float32)
    activated = jax.nn.gelu(up_pre, approximate=False).astype(jnp.bfloat16)
    down_part = jnp.einsum("blf,fd->bld", activated, ffn_out, preferred_element_type=jnp.float32)
    down_sum = lax.psum(down_part.astype(jnp.bfloat16), "tensor").astype(jnp.float32)
    outputs, normed_second, inv_second = norm_forward(
        hidden.astype(jnp.float32) + down_sum + bias_rows[1], gain_rows[1], shift_rows[1]
    )
    saved = (
        tokens,
        queries,
        key_rows,
        values,
        log_total,
        context,
        normed_first,
        inv_first,
        hidden,
        up_pre,
        activated,
        normed_second,
        inv_second,
    )
    return (outputs, saved)


def encoder_backward(incoming, saved, lengths, params):
    (
        attn_in,
        attn_in_bias,
        attn_out,
        ffn_in,
        ffn_in_bias,
        ffn_out,
        out_biases,
        norm_gains,
        norm_shifts,
    ) = params
    (
        tokens,
        queries,
        key_rows,
        values,
        log_total,
        context,
        normed_first,
        inv_first,
        hidden,
        up_pre,
        activated,
        normed_second,
        inv_second,
    ) = saved
    groups_here, length, model_width = tokens.shape
    gain_rows = norm_gains.astype(jnp.float32)
    d_second, gain_second, shift_second = norm_backward(
        incoming, normed_second, inv_second, gain_rows[1]
    )
    d_down = d_second.astype(jnp.bfloat16)
    grad_ffn_out = jnp.einsum("blf,bld->fd", activated, d_down, preferred_element_type=jnp.float32)
    d_activated = jnp.einsum("bld,fd->blf", d_down, ffn_out, preferred_element_type=jnp.float32)
    gelu_pull = jax.vjp(partial(jax.nn.gelu, approximate=False), up_pre)[1]
    d_up = gelu_pull(d_activated)[0].astype(jnp.bfloat16)
    grad_ffn_in = jnp.einsum("bld,blf->df", hidden, d_up, preferred_element_type=jnp.float32)
    hidden_part = jnp.einsum("blf,df->bld", d_up, ffn_in, preferred_element_type=jnp.float32)
    d_hidden = d_second + lax.psum(hidden_part.astype(jnp.bfloat16), "tensor").astype(jnp.float32)
    d_first, gain_first, shift_first = norm_backward(
        d_hidden, normed_first, inv_first, gain_rows[0]
    )
    d_attn = d_first.astype(jnp.bfloat16)
    grad_attn_out = jnp.einsum("ble,bld->ed", context, d_attn, preferred_element_type=jnp.float32)
    d_context = split_heads(
        jnp.einsum("bld,ed->ble", d_attn, attn_out, preferred_element_type=jnp.float32).astype(
            jnp.bfloat16
        )
    )
    visible = key_visible(lengths, length)
    scores = head_scores(queries, key_rows, visible)
    probs_float = jnp.exp(scores - log_total)
    d_probs = jnp.einsum("bqhe,bkhe->bhqk", d_context, values, preferred_element_type=jnp.float32)
    d_values = jnp.einsum(
        "bhqk,bqhe->bkhe",
        probs_float.astype(jnp.bfloat16),
        d_context,
        preferred_element_type=jnp.float32,
    ).astype(jnp.bfloat16)
    d_scores = (
        probs_float * (d_probs - jnp.sum(probs_float * d_probs, axis=-1, keepdims=True))
    ).astype(jnp.bfloat16)
    d_queries = (
        jnp.einsum("bhqk,bkhe->bqhe", d_scores, key_rows, preferred_element_type=jnp.float32)
        * HD ** (-0.5)
    ).astype(jnp.bfloat16)
    d_keys = (
        jnp.einsum("bhqk,bqhe->bkhe", d_scores, queries, preferred_element_type=jnp.float32)
        * HD ** (-0.5)
    ).astype(jnp.bfloat16)
    query_grad = join_heads(d_queries)
    value_grad = join_heads(d_values)
    d_projected = jnp.stack([query_grad, join_heads(d_keys), value_grad], axis=2)
    grad_attn_in = jnp.einsum(
        "bld,blce->dce", tokens, d_projected, preferred_element_type=jnp.float32
    )
    token_part = jnp.einsum(
        "blce,dce->bld", d_projected, attn_in, preferred_element_type=jnp.float32
    )
    d_tokens = (
        d_first + lax.psum(token_part.astype(jnp.bfloat16), "tensor").astype(jnp.float32)
    ).astype(jnp.bfloat16)
    grad_in_bias = jnp.stack(
        [
            jnp.sum(query_grad.astype(jnp.float32), axis=(0, 1)),
            jnp.sum(value_grad.astype(jnp.float32), axis=(0, 1)),
        ]
    )
    grad_ffn_bias = jnp.sum(d_up.astype(jnp.float32), axis=(0, 1))
    grad_out_biases = jnp.stack(
        [
            jnp.sum(d_attn.astype(jnp.float32), axis=(0, 1)),
            jnp.sum(d_down.astype(jnp.float32), axis=(0, 1)),
        ]
    )
    grad_gains = jnp.stack([gain_first, gain_second])
    grad_shifts = jnp.stack([shift_first, shift_second])
    return (
        d_tokens,
        (
            grad_attn_in,
            grad_in_bias,
            grad_attn_out,
            grad_ffn_in,
            grad_ffn_bias,
            grad_ffn_out,
            grad_out_biases,
            grad_gains,
            grad_shifts,
        ),
    )


def contrastive(question_rows, passage_rows, own_positive, dataset_ids):
    class_scores = jnp.einsum(
        "gd,jd->gj", question_rows, passage_rows, preferred_element_type=jnp.float32
    ) * (score_gain * D ** (-0.5))
    columns = jnp.arange(passage_rows.shape[0], dtype=jnp.int32)
    chosen = own_positive[:, None] == columns[None, :]
    own_set = jnp.sum(jnp.where(chosen, dataset_ids[None, :], 0), axis=1)
    logits = jnp.where(dataset_ids[None, :] == own_set[:, None], class_scores, NEGATIVE)
    row_top = jnp.max(logits, axis=1, keepdims=True)
    log_total = row_top + jnp.log(jnp.sum(jnp.exp(logits - row_top), axis=1, keepdims=True))
    target = jnp.sum(jnp.where(chosen, class_scores, 0.0), axis=1)
    d_class = (jnp.exp(logits - log_total) - chosen.astype(jnp.float32)) * (
        score_gain * D ** (-0.5)
    )
    return (log_total[:, 0] - target, d_class)


def per_device(
    question_tokens,
    passage_tokens,
    question_cotangent,
    passage_cotangent,
    question_lengths,
    passage_lengths,
    dataset_ids,
    positives,
    attn_in,
    attn_in_bias,
    attn_out,
    ffn_in,
    ffn_in_bias,
    ffn_out,
    out_biases,
    norm_gains,
    norm_shifts,
):

    def encoder_params(encoder):
        return (
            attn_in[encoder],
            attn_in_bias[encoder],
            attn_out[encoder],
            ffn_in[encoder],
            ffn_in_bias[encoder],
            ffn_out[encoder],
            out_biases[encoder],
            norm_gains[encoder],
            norm_shifts[encoder],
        )

    question_params = encoder_params(0)
    passage_params = encoder_params(1)
    question_float, question_saved = encoder_forward(
        question_tokens, question_lengths, question_params
    )
    passage_float, passage_saved = encoder_forward(passage_tokens, passage_lengths, passage_params)
    question_heads = question_float[:, 0].astype(jnp.bfloat16)
    passage_heads = passage_float[:, 0].astype(jnp.bfloat16)
    local_groups = question_heads.shape[0]
    own_start = lax.axis_index("dp") * local_groups
    all_passages = lax.all_gather(passage_heads, "dp", axis=0, tiled=True)
    own_positive = lax.dynamic_slice_in_dim(positives, own_start, local_groups)
    cross, d_class = contrastive(question_heads, all_passages, own_positive, dataset_ids)
    total = lax.psum(jnp.sum(cross), "dp")
    contrastive_loss = total / all_passages.shape[0]
    d_question_heads = jnp.einsum(
        "gj,jd->gd", d_class, all_passages.astype(jnp.float32), precision=HIGHEST
    )
    question_heads_float = question_heads.astype(jnp.float32)
    d_passage_heads = lax.psum_scatter(
        jnp.einsum("gj,gd->jd", d_class, question_heads_float, precision=HIGHEST),
        "dp",
        scatter_dimension=0,
        tiled=True,
    )
    d_question_out = question_cotangent.astype(jnp.float32).at[:, 0].add(d_question_heads)
    d_passage_out = passage_cotangent.astype(jnp.float32).at[:, 0].add(d_passage_heads)
    passage_grad, passage_weights = encoder_backward(
        d_passage_out, passage_saved, passage_lengths, passage_params
    )
    question_grad, question_weights = encoder_backward(
        d_question_out, question_saved, question_lengths, question_params
    )
    joined = (
        lax.psum_scatter(question_weights[0], "dp", scatter_dimension=0, tiled=True),
        lax.psum_scatter(question_weights[1], "dp", scatter_dimension=1, tiled=True),
        lax.psum_scatter(question_weights[2], "dp", scatter_dimension=1, tiled=True),
        lax.psum_scatter(question_weights[3], "dp", scatter_dimension=0, tiled=True),
        lax.psum_scatter(question_weights[4], "dp", scatter_dimension=0, tiled=True),
        lax.psum_scatter(question_weights[5], "dp", scatter_dimension=1, tiled=True),
        lax.psum_scatter(question_weights[6], "dp", scatter_dimension=1, tiled=True),
        lax.psum_scatter(question_weights[7], "dp", scatter_dimension=1, tiled=True),
        lax.psum_scatter(question_weights[8], "dp", scatter_dimension=1, tiled=True),
        lax.psum_scatter(passage_weights[0], "dp", scatter_dimension=0, tiled=True),
        lax.psum_scatter(passage_weights[1], "dp", scatter_dimension=1, tiled=True),
        lax.psum_scatter(passage_weights[2], "dp", scatter_dimension=1, tiled=True),
        lax.psum_scatter(passage_weights[3], "dp", scatter_dimension=0, tiled=True),
        lax.psum_scatter(passage_weights[4], "dp", scatter_dimension=0, tiled=True),
        lax.psum_scatter(passage_weights[5], "dp", scatter_dimension=1, tiled=True),
        lax.psum_scatter(passage_weights[6], "dp", scatter_dimension=1, tiled=True),
        lax.psum_scatter(passage_weights[7], "dp", scatter_dimension=1, tiled=True),
        lax.psum_scatter(passage_weights[8], "dp", scatter_dimension=1, tiled=True),
    )
    question_parts = joined[:9]
    passage_parts = joined[9:]
    stacked = [
        jnp.stack([question_piece, passage_piece])
        for question_piece, passage_piece in zip(question_parts, passage_parts)
    ]
    return (
        question_float.astype(jnp.bfloat16),
        passage_float.astype(jnp.bfloat16),
        contrastive_loss,
        question_grad,
        passage_grad,
        stacked[0],
        stacked[1],
        stacked[2],
        stacked[3],
        stacked[4],
        stacked[5],
        stacked[6],
        stacked[7],
        stacked[8],
    )


MESH_ID = pl.DeviceIdType.MESH
F32 = jnp.float32
BF16 = jnp.bfloat16
ZN = 4
ROWS_OUT = 48
JOBS = 12
COLS = 384
D1, D2, DZ, DS = 8, 8, 8, 2
LINE_FIRST = (0, 5, 8, 9)
TOKS = (128, 512)
BLK = (128, 256)
SMALL = 24
CHUNK = 64
NORM_UNROLL = (2, 4)
UP_UNROLL = (6, 6)
DOWN_UNROLL = (3, 3)
PAIR_UNROLL = (3, 3)


def dot(a, b):
    return jnp.dot(a, b, preferred_element_type=F32)


def dot_t(a, b):
    return lax.dot_general(a, b, (((1,), (1,)), ((), ())), preferred_element_type=F32)


def t_dot(a, b):
    return lax.dot_general(a, b, (((0,), (0,)), ((), ())), preferred_element_type=F32)


def gelu_and_slope(u):
    size = jnp.abs(u)
    bell = jnp.exp(-0.5 * u * u)
    t = 1.0 / (1.0 + (0.3275911 * 0.7071067811865476) * size)
    poly = t * (
        0.127414796
        + t * (-0.142248368 + t * (0.7107068705 + t * (-0.7265760135 + t * 0.5307027145)))
    )
    tail = poly * bell
    phi = jnp.where(u >= 0.0, 1.0 - tail, tail)
    return u * phi, phi + u * bell * 0.3989422804014327


def row_mean(v):
    return jnp.sum(v, axis=-1, keepdims=True) * (1.0 / D)


def fold8(v):
    return jnp.sum(v.reshape(v.shape[0] // 8, 8, v.shape[1]), axis=0)


def rows_at(start, size, step=16):
    return pl.ds(pl.multiple_of(start, step), size)


def fused_kernel(
    xq_in, xp_in, cq_in, cp_in, qlen_in, plen_in, dsid_in, posi_in,
    win_in, bin_from, wo_in, wf_in, bfi_from, wd_in, bo_from, gain_from, shift_from,
    oq_out, op_out, gq_out, gp_out, g_in, g_out, g_fi, g_fo, sm_out,
    win, wo, wf, wd, xq, xp, cq, cp, qkvq, qkvp, prq, prp, hq, hp, n1q, n1p, n2q, n2p,
    i1q, i1p, i2q, i2p, sq, sp, obq, obp, ddq, ddp, dcq, dcp, ballq, ballp, atq, atp,
    exsq, exsp, exrq, exrp, par, pin, pfi, masks, hg, hf, dh, acc_s, acc_b, acc_f, smb, smr,
    p1s, p1r, p2r, zb, fin, fra, frb, xms, xmr, hm,
    qlen, plen, dsid, posi, bin_in, bfi_in, bo_in, gain_in, shift_in, sm,
    fin_sem, little_sem, in_sem, out_sem, exs_sem, exr_sem, hgs_sem, hgr_sem, sms_sem, smr_sem,
    p1s_sem, p1r_sem, p2s_sem, p2r_sem, zrs_sem, zrr_sem, zls_sem, zlr_sem,
    fas_sem, far_sem, fbs_sem, fbr_sem, xms_sem, xmr_sem,
    *, last,
):
    me = lax.axis_index("dp")
    core = lax.axis_index("tensor")
    z, y, x = me // 4, (me // 2) % 2, me % 2
    partner = {"dp": me, "tensor": 1 - core}
    at_x = {"dp": me + 1 - 2 * x, "tensor": core}
    at_y = {"dp": me + 2 - 4 * y, "tensor": core}

    def at_dp(index):
        return {"dp": index, "tensor": core}

    X, COT, QKV, PR, HID = (xq, xp), (cq, cp), (qkvq, qkvp), (prq, prp), (hq, hp)
    N1, N2, I1, I2, SLOPE = (n1q, n1p), (n2q, n2p), (i1q, i1p), (i2q, i2p), (sq, sp)
    OB, DD, DC, BALL, AT = (obq, obp), (ddq, ddp), (dcq, dcp), (ballq, ballp), (atq, atp)
    EXS, EXR = (exsq, exsp), (exrq, exrp)

    little = [
        (qlen_in, qlen), (plen_in, plen), (bin_from, bin_in), (bfi_from, bfi_in), (bo_from, bo_in),
        (gain_from, gain_in), (shift_from, shift_in), (dsid_in, dsid), (posi_in, posi),
    ]
    little = [pltpu.make_async_copy(s, d, little_sem.at[i]) for i, (s, d) in enumerate(little)]
    loads = [
        (xq_in, xq),
        *[(win_in.at[0, j], win.at[0, :, pl.ds(j * COLS, COLS)]) for j in range(3)],
        (xp_in, xp),
        *[(win_in.at[1, j], win.at[1, :, pl.ds(j * COLS, COLS)]) for j in range(3)],
        (wo_in.at[0], wo.at[0]),
        (wo_in.at[1], wo.at[1]),
        (wf_in.at[0], wf.at[0]),
        (wf_in.at[1], wf.at[1]),
        (wd_in.at[0], wd.at[0]),
        (wd_in.at[1], wd.at[1]),
        (cq_in, cq),
        (cp_in, cp),
    ]
    loads = [pltpu.make_async_copy(s, d, in_sem.at[i]) for i, (s, d) in enumerate(loads)]
    for copy in loads[:4]:
        copy.start()
    for copy in little:
        copy.start()
    ready = set()

    def need(*which):
        for i in which:
            if i not in ready:
                loads[i].wait()
                ready.add(i)

    barrier = pltpu.get_barrier_semaphore()
    pl.semaphore_signal(barrier, inc=1, device_id=partner, device_id_type=MESH_ID)
    for k in range(1, 16):
        pl.semaphore_signal(barrier, inc=1, device_id=at_dp(me ^ k), device_id_type=MESH_ID)

    def load(*which):
        for i in which:
            loads[i].start()

    for copy in little:
        copy.wait()
    for e in range(2):
        for i in range(2):
            par[e * 8 + i : e * 8 + i + 1, :] = bo_in[e].astype(F32)[i : i + 1]
            par[e * 8 + 2 + i : e * 8 + 3 + i, :] = gain_in[e].astype(F32)[i : i + 1]
            par[e * 8 + 4 + i : e * 8 + 5 + i, :] = shift_in[e].astype(F32)[i : i + 1]
            pin[e * 2 + i : e * 2 + i + 1, :] = bin_in[e].astype(F32)[i : i + 1]
        pfi[e : e + 1, :] = bfi_in[...].astype(F32)[e : e + 1]
    acc_s[...] = jnp.zeros_like(acc_s)
    acc_b[...] = jnp.zeros_like(acc_b)
    acc_f[...] = jnp.zeros_like(acc_f)

    r32 = lax.broadcasted_iota(jnp.int32, (32, 32), 0)
    c32 = lax.broadcasted_iota(jnp.int32, (32, 32), 1)
    own_pos = jnp.zeros((32, 32), F32)
    set_col = jnp.zeros((32, 32), F32)
    for g in range(32):
        at = (g % 2) * 16 + g // 2
        own_pos = jnp.where(r32 == at, posi[g].astype(F32), own_pos)
        set_col = jnp.where(c32 == at, dsid[g].astype(F32), set_col)
    col_group = ((c32 % 16) * 2 + c32 // 16).astype(F32)
    chosen = jnp.where(own_pos == col_group, 1.0, 0.0)
    own_set = jnp.sum(chosen * set_col, axis=1, keepdims=True)
    masks[0:32, :] = chosen
    masks[32:64, :] = jnp.where(set_col == own_set, 1.0, 0.0)

    lane_lo = lax.broadcasted_iota(jnp.int32, (1, 128), 1) < HD

    def side(v, hh):
        return jnp.where(lane_lo if hh == 0 else jnp.logical_not(lane_lo), v, jnp.zeros_like(v))

    def exchange(e, b, parity):
        slot = 0 if e == 0 else 1 + b
        rows = rows_at(b * BLK[e], BLK[e]) if not isinstance(b, int) else pl.ds(b * BLK[e], BLK[e])
        return pltpu.make_async_remote_copy(
            src_ref=EXS[e].at[rows],
            dst_ref=EXR[e].at[parity, rows],
            send_sem=exs_sem.at[slot],
            recv_sem=exr_sem.at[parity, slot],
            device_id=partner,
            device_id_type=MESH_ID,
        )

    def block_rows(e, b):
        if e == 0:
            return pl.ds(0, BLK[0])
        return rows_at(b * BLK[1], BLK[1], BLK[1])

    def blocks(e, body):
        if e == 0:
            body(0)
        else:
            pl.loop(0, 2)(body)

    def project(e, b, which):
        rows = block_rows(e, b)
        xb = X[e][rows, :]
        for j in which:
            cols = pl.ds(j * COLS, COLS)
            got = dot(xb, win[e, :, cols])
            if j == 0:
                got = (got + pin[e * 2 : e * 2 + 1, :]).astype(BF16) * jnp.asarray(HD**-0.5, BF16)
            elif j == 2:
                got = got + pin[e * 2 + 1 : e * 2 + 2, :]
            QKV[e][rows, cols] = got.astype(BF16)

    def attend(e, b):
        size = BLK[e]
        rows = block_rows(e, b)
        col = lax.broadcasted_iota(jnp.int32, (size, size), 1)
        if e == 0:
            row = lax.broadcasted_iota(jnp.int32, (size, size), 0)
            first = jnp.logical_and(row < 64, col < qlen[0])
            second = jnp.logical_and(
                row >= 64, jnp.logical_and(col >= 64, col < 64 + qlen[1])
            )
            seen = jnp.logical_or(first, second)
        else:
            seen = col < plen[b]

        @pl.loop(0, 3, unroll=PAIR_UNROLL[e])
        def _(pair):
            q2 = QKV[e][rows, rows_at(pair * 128, 128, 128)]
            k2 = QKV[e][rows, rows_at(COLS + pair * 128, 128, 128)]
            v2 = QKV[e][rows, rows_at(2 * COLS + pair * 128, 128, 128)]
            total = jnp.zeros((size, 128), F32)
            for hh in range(2):
                s = dot_t(side(q2, hh), k2)
                s = jnp.where(seen, s, NEGATIVE)
                p = jnp.exp(s - jnp.max(s, axis=-1, keepdims=True))
                p = (p * (1.0 / jnp.sum(p, axis=-1, keepdims=True))).astype(BF16)
                PR[e][b, pair * 2 + hh] = p
                total = total + dot(p, side(v2, hh))
            BALL[e][rows, rows_at(8 * COLS + pair * 128, 128, 128)] = total.astype(BF16)

        ctx = BALL[e][rows, pl.ds(8 * COLS, COLS)]
        EXS[e][rows, :] = dot(ctx, wo[e]).astype(BF16)
        exchange(e, b, 0).start()

    CH = CHUNK

    def first_norm(e, b):
        exchange(e, b, 0).wait()

        @pl.loop(0, BLK[e] // CH, unroll=NORM_UNROLL[e])
        def _(c):
            rows = rows_at(b * BLK[e] + c * CH, CH, CH)
            v = (
                X[e][rows, :].astype(F32)
                + (EXS[e][rows, :].astype(F32) + EXR[e][0, rows, :].astype(F32))
                + par[e * 8 : e * 8 + 1, :]
            )
            v = v - row_mean(v)
            inv = lax.rsqrt(row_mean(v * v) + EPSILON)
            n = v * inv
            N1[e][rows, :] = n
            I1[e][rows, :] = inv
            HID[e][rows, :] = (
                n * par[e * 8 + 2 : e * 8 + 3, :] + par[e * 8 + 4 : e * 8 + 5, :]
            ).astype(BF16)

    def feed(e, b):
        rows = block_rows(e, b)

        @pl.loop(0, 6, unroll=UP_UNROLL[e])
        def _(n):
            cols = rows_at(n * 256, 256, 256)
            u = dot(HID[e][rows, :], wf[e, :, cols]) + pfi[e : e + 1, cols]
            a, slope = gelu_and_slope(u)
            BALL[e][rows, cols] = a.astype(BF16)
            SLOPE[e][rows, cols] = slope.astype(BF16)

        @pl.loop(0, 3, unroll=DOWN_UNROLL[e])
        def _(n):
            cols = rows_at(n * 256, 256, 256)
            EXS[e][rows, cols] = dot(BALL[e][rows, pl.ds(0, FF_HERE)], wd[e, :, cols]).astype(BF16)

        exchange(e, b, 1).start()

    def second_norm(e, b):
        exchange(e, b, 1).wait()

        @pl.loop(0, BLK[e] // CH, unroll=NORM_UNROLL[e])
        def _(c):
            rows = rows_at(b * BLK[e] + c * CH, CH, CH)
            v = (
                HID[e][rows, :].astype(F32)
                + (EXS[e][rows, :].astype(F32) + EXR[e][1, rows, :].astype(F32))
                + par[e * 8 + 1 : e * 8 + 2, :]
            )
            v = v - row_mean(v)
            inv = lax.rsqrt(row_mean(v * v) + EPSILON)
            n = v * inv
            N2[e][rows, :] = n
            I2[e][rows, :] = inv
            OB[e][rows, :] = (
                n * par[e * 8 + 3 : e * 8 + 4, :] + par[e * 8 + 5 : e * 8 + 6, :]
            ).astype(BF16)

    def mini_exchange(k):
        return pltpu.make_async_remote_copy(
            src_ref=xms.at[k],
            dst_ref=xmr.at[k],
            send_sem=xms_sem.at[k],
            recv_sem=xmr_sem.at[k],
            device_id=partner,
            device_id_type=MESH_ID,
        )

    def first_rows(ref):
        rows = [ref[b * 256 : b * 256 + 16, :].astype(F32)[0:1] for b in range(2)]
        return jnp.concatenate([*rows, jnp.zeros((14, rows[0].shape[1]), F32)], axis=0)

    def mini_attend():
        xm = first_rows(xp).astype(BF16)
        q = (dot(xm, win[1, :, pl.ds(0, COLS)]) + pin[2:3, :]).astype(BF16).astype(F32) * HD**-0.5
        of_head = lax.broadcasted_iota(jnp.int32, (16, COLS), 1) // HD == lax.broadcasted_iota(
            jnp.int32, (16, COLS), 0
        )
        col = lax.broadcasted_iota(jnp.int32, (16, 256), 1)
        rows = []
        for b in range(2):
            keys = qkvp[b * 256 : (b + 1) * 256, COLS : 2 * COLS]
            vals = qkvp[b * 256 : (b + 1) * 256, 2 * COLS : 3 * COLS]
            s = dot_t(jnp.where(of_head, q[b : b + 1], 0.0).astype(BF16), keys)
            s = jnp.where(col < plen[b], s, NEGATIVE)
            p = jnp.exp(s - jnp.max(s, axis=-1, keepdims=True))
            p = (p * (1.0 / jnp.sum(p, axis=-1, keepdims=True))).astype(BF16)
            rows.append(jnp.sum(jnp.where(of_head, dot(p, vals), 0.0), axis=0, keepdims=True))
        ctx = jnp.concatenate([*rows, jnp.zeros((14, COLS), F32)], axis=0)
        xms[0] = dot(ctx.astype(BF16), wo[1]).astype(BF16)
        mini_exchange(0).start()

    def mini_norm(k, v):
        mini_exchange(k).wait()
        v = v + (xms[k].astype(F32) + xmr[k].astype(F32)) + par[8 + k : 9 + k, :]
        v = v - row_mean(v)
        n = v * lax.rsqrt(row_mean(v * v) + EPSILON)
        return (n * par[10 + k : 11 + k, :] + par[12 + k : 13 + k, :]).astype(BF16)

    def mini_feed():
        hm[...] = mini_norm(0, first_rows(xp))

        u = dot(hm[...], wf[1]) + pfi[1:2, :]
        a = gelu_and_slope(u)[0].astype(BF16)
        xms[1] = dot(a, wd[1]).astype(BF16)

        mini_exchange(1).start()

    def transpose_into(e, k, src, b):
        rows = block_rows(e, b)

        @pl.loop(0, 2)
        def _(c):
            tile = src[rows, rows_at(c * COLS, COLS, 128)].T
            AT[e][k, pl.ds(c * 2, 2), :, :, :, rows] = tile.reshape(2, 2, 2, ROWS_OUT, BLK[e])

    def left_factor(axis, k):
        return pltpu.make_async_remote_copy(
            src_ref=atq.at[k, :, :, 1 - x] if axis == 0 else atq.at[k, :, 1 - y],
            dst_ref=fra.at[axis, k],
            send_sem=fas_sem.at[axis, k],
            recv_sem=far_sem.at[axis, k],
            device_id=first_dev[axis],
            device_id_type=MESH_ID,
        )

    def right_factor(axis, pair):
        return pltpu.make_async_remote_copy(
            src_ref=ballq.at[:, pl.ds((pair * 2 + axis) * COLS, COLS)],
            dst_ref=frb.at[axis, pair],
            send_sem=fbs_sem.at[axis, pair],
            recv_sem=fbr_sem.at[axis, pair],
            device_id=first_dev[axis],
            device_id_type=MESH_ID,
        )

    first_dev, other_dev = (at_x, at_y), (at_y, at_x)
    first_at, other_at = (x, y), (y, x)

    need(0, 1, 2, 3)
    load(4, 6, 7, 8, 5, 9, 10, 12, 11, 13, 14, 15)
    project(0, 0, (0, 1, 2))
    need(8)
    pl.semaphore_wait(barrier, 16)
    attend(0, 0)
    right_factor(0, 4).start()
    need(4, 5, 6, 7, 9)
    blocks(1, lambda b: project(1, b, (1, 2)))
    mini_attend()
    first_norm(0, 0)
    need(10, 12)
    feed(0, 0)
    for axis in range(2):
        for pair in range(2):
            right_factor(axis, pair).start()
    need(11, 13)
    mini_feed()
    second_norm(0, 0)
    out_q = pltpu.make_async_copy(obq, oq_out, out_sem.at[0])
    out_p = pltpu.make_async_copy(obp, op_out, out_sem.at[1])
    out_q.start()
    mini_out = mini_norm(1, hm[...].astype(F32)).astype(F32)

    pieces = []
    rows = [obq[at : at + 16, :].astype(F32)[0:1] for at in (0, 64)]
    for head in (*rows, mini_out[0:1], mini_out[1:2]):
        pieces += [head[:, k * 256 : (k + 1) * 256] for k in range(3)]
    pieces.append(jnp.zeros((4, 256), F32))
    hg[me] = jnp.concatenate(pieces, axis=0).astype(BF16)

    def heads(k):
        return pltpu.make_async_remote_copy(
            src_ref=hg.at[me],
            dst_ref=hg.at[me],
            send_sem=hgs_sem.at[k],
            recv_sem=hgr_sem.at[k],
            device_id=at_dp(me ^ k),
            device_id_type=MESH_ID,
        )

    for k in range(1, 16):
        heads(k).start()
    need(14, 15)
    transpose_into(0, 1, hq, 0)
    for axis in range(2):
        left_factor(axis, 1).start()
    transpose_into(0, 3, xq, 0)
    for axis in range(2):
        left_factor(axis, 3).start()
    blocks(1, lambda b: project(1, b, (0,)))
    attend(1, 0)
    for k in range(1, 16):
        copy = pltpu.make_async_remote_copy(
            src_ref=hg.at[me],
            dst_ref=hg.at[me ^ k],
            send_sem=hgs_sem.at[k],
            recv_sem=hgr_sem.at[k],
            device_id=at_dp(me ^ k),
            device_id_type=MESH_ID,
        )
        copy.wait()
    gathered = hg[...].astype(F32).reshape(256, 256)
    hf[0] = gathered[:, 0:128]
    hf[1] = gathered[:, 128:256]

    def all_heads(first):
        groups = []
        for i in range(2):
            parts = [
                hf[c, pl.ds(first + i * 3 + k, 16, stride=16), :] for k in range(3) for c in range(2)
            ]
            groups.append(jnp.concatenate(parts, axis=1))
        return jnp.concatenate(groups, axis=0)

    heads_q, heads_p = all_heads(0), all_heads(6)
    gain = score_gain * D ** (-0.5)
    class_scores = dot_t(heads_q.astype(BF16), heads_p.astype(BF16)) * gain
    chosen = masks[0:32, :]
    logits = jnp.where(masks[32:64, :] > 0.5, class_scores, NEGATIVE)
    top = jnp.max(logits, axis=1, keepdims=True)
    log_total = top + jnp.log(jnp.sum(jnp.exp(logits - top), axis=1, keepdims=True))
    target = jnp.sum(chosen * class_scores, axis=1, keepdims=True)
    loss = jnp.sum(log_total - target, axis=0, keepdims=True) * (1.0 / 32)
    sm[SMALL : SMALL + 8, :] = jnp.broadcast_to(loss, (8, 128))
    d_class = (jnp.exp(logits - log_total) - chosen) * gain
    dh[0:32, :] = lax.dot_general(
        d_class, heads_p, (((1,), (0,)), ((), ())), precision=HIGHEST, preferred_element_type=F32
    )
    dh[32:64, :] = lax.dot_general(
        d_class, heads_q, (((0,), (0,)), ((), ())), precision=HIGHEST, preferred_element_type=F32
    )

    def norm_back(incoming, n, inv, scale):
        scaled = incoming * scale
        return inv * (scaled - row_mean(scaled) - n * row_mean(scaled * n))

    def second_back(e, b):
        row0 = lax.broadcasted_iota(jnp.int32, (CH, 1), 0)
        seqs = 2 if e == 0 else 1
        length = 64 if e == 0 else 256
        for i in range(seqs):
            group = i if e == 0 else b
            extra = dh[pl.ds(e * 32 + group * 16 + me, 1), :]

            @pl.loop(0, length // CH, unroll=NORM_UNROLL[e])
            def _(c):
                rows = rows_at(group * length + c * CH, CH, CH)
                add = jnp.where(row0 + c * CH == 0, extra, 0.0)
                d = COT[e][rows, :].astype(F32) + add
                n = N2[e][rows, :]
                out = norm_back(d, n, I2[e][rows, :], par[e * 8 + 3 : e * 8 + 4, :])
                N2[e][rows, :] = out
                low = out.astype(BF16)
                DD[e][rows, :] = low
                acc_s[e * 6 + 1] += fold8(d * n)
                acc_s[e * 6 + 3] += fold8(d)
                acc_s[e * 6 + 5] += fold8(low.astype(F32))

        transpose_into(e, 0, DD[e], b)

    def feed_back(e, b):
        rows = block_rows(e, b)

        @pl.loop(0, 6, unroll=UP_UNROLL[e])
        def _(n):
            cols = rows_at(n * 256, 256, 256)
            d = dot_t(DD[e][rows, :], wd[e, cols, :]) * SLOPE[e][rows, cols].astype(F32)
            d = d.astype(BF16)
            BALL[e][rows, rows_at(4 * COLS + n * 256, 256, 256)] = d
            acc_f[e, :, cols] += fold8(d.astype(F32))

        @pl.loop(0, 3, unroll=DOWN_UNROLL[e])
        def _(n):
            cols = rows_at(n * 256, 256, 256)
            EXS[e][rows, cols] = dot_t(BALL[e][rows, pl.ds(4 * COLS, FF_HERE)], wf[e, cols, :]).astype(BF16)

        exchange(e, b, 0).start()
        if e == 1:
            transpose_into(e, 1, HID[e], b)

    def first_back(e, b):
        exchange(e, b, 0).wait()

        @pl.loop(0, BLK[e] // CH, unroll=NORM_UNROLL[e])
        def _(c):
            rows = rows_at(b * BLK[e] + c * CH, CH, CH)
            d = N2[e][rows, :] + (EXS[e][rows, :].astype(F32) + EXR[e][0, rows, :].astype(F32))
            n = N1[e][rows, :]
            out = norm_back(d, n, I1[e][rows, :], par[e * 8 + 2 : e * 8 + 3, :])
            N1[e][rows, :] = out
            low = out.astype(BF16)
            DD[e][rows, :] = low
            acc_s[e * 6 + 0] += fold8(d * n)
            acc_s[e * 6 + 2] += fold8(d)
            acc_s[e * 6 + 4] += fold8(low.astype(F32))

        transpose_into(e, 2, DD[e], b)

    def attend_back(e, b):
        rows = block_rows(e, b)
        size = BLK[e]
        DC[e][rows, :] = dot_t(DD[e][rows, :], wo[e]).astype(BF16)

        @pl.loop(0, 3, unroll=PAIR_UNROLL[e])
        def _(pair):
            q2 = QKV[e][rows, rows_at(pair * 128, 128, 128)]
            k2 = QKV[e][rows, rows_at(COLS + pair * 128, 128, 128)]
            v2 = QKV[e][rows, rows_at(2 * COLS + pair * 128, 128, 128)]
            dc2 = DC[e][rows, rows_at(pair * 128, 128, 128)]
            dq = jnp.zeros((size, 128), F32)
            dk = jnp.zeros((size, 128), F32)
            dv = jnp.zeros((size, 128), F32)
            for hh in range(2):
                low = PR[e][b, pair * 2 + hh]
                p = low.astype(F32)
                dch = side(dc2, hh)
                dp = dot_t(dch, v2)
                ds = (p * (dp - jnp.sum(p * dp, axis=-1, keepdims=True))).astype(BF16)
                dv = dv + t_dot(low, dch)
                dq = dq + dot(ds, side(k2, hh))
                dk = dk + t_dot(ds, side(q2, hh))
            dq = (dq * HD**-0.5).astype(BF16)
            dv = dv.astype(BF16)
            cols = rows_at(pair * 128, 128, 128)
            BALL[e][rows, rows_at(9 * COLS + pair * 128, 128, 128)] = dq
            BALL[e][rows, rows_at(10 * COLS + pair * 128, 128, 128)] = dk.astype(BF16)
            BALL[e][rows, rows_at(11 * COLS + pair * 128, 128, 128)] = dv
            acc_b[e, :, cols] += fold8(dq.astype(F32))
            acc_b[e, :, rows_at(COLS + pair * 128, 128, 128)] += fold8(dv.astype(F32))

        if e == 1:
            transpose_into(e, 3, X[e], b)

    def token_back(e, b):
        rows = block_rows(e, b)

        @pl.loop(0, 3, unroll=DOWN_UNROLL[e])
        def _(n):
            cols = rows_at(n * 256, 256, 256)
            EXS[e][rows, cols] = dot_t(BALL[e][rows, pl.ds(9 * COLS, 3 * COLS)], win[e, cols, :]).astype(BF16)

        exchange(e, b, 1).start()

    def token_end(e, b):
        exchange(e, b, 1).wait()

        @pl.loop(0, BLK[e] // CH, unroll=NORM_UNROLL[e])
        def _(c):
            rows = rows_at(b * BLK[e] + c * CH, CH, CH)
            OB[e][rows, :] = (
                N1[e][rows, :] + (EXS[e][rows, :].astype(F32) + EXR[e][1, rows, :].astype(F32))
            ).astype(BF16)

    def job_of(j):
        return j // 6, j % 6

    def product(half, blk, sel):
        k = jnp.where(blk < 8, blk // 4, jnp.where(blk == 8, 2, 3))
        rows = atp[k, :, :, sel] if half == 0 else atp[k, :, sel]
        out = dot(rows.reshape(COLS, TOKS[1]), ballp[:, rows_at(blk * COLS, COLS, 128)])
        return out.reshape(ZN, 2, ROWS_OUT, COLS)

    def pair_product(half, pair):
        blk = pair * 2 + half
        k = blk // 4 if blk < 8 else 2 if blk == 8 else 3
        rows = atq[k, :, :, x] if half == 0 else atq[k, :, y]
        rows = jnp.concatenate([rows.reshape(COLS, TOKS[0]), fra[half, k].reshape(COLS, TOKS[0])], axis=1)
        cols = jnp.concatenate([ballq[:, blk * COLS : (blk + 1) * COLS], frb[half, pair]], axis=0)
        return dot(rows, cols).reshape(ZN, 2, ROWS_OUT, COLS)

    def p1(j, half):
        return pltpu.make_async_remote_copy(
            src_ref=p1s.at[j % DS, half],
            dst_ref=p1r.at[j % D1, half],
            send_sem=p1s_sem.at[j % DS, half],
            recv_sem=p1r_sem.at[j % D1, half],
            device_id=first_dev[half],
            device_id_type=MESH_ID,
        )

    def other(j, half, line_first):
        mine, to = p1r.at[j % D1, half], p2r.at[j % D2, half]
        return pltpu.make_async_remote_copy(
            src_ref=mine.at[z, 1 - other_at[half]] if line_first else mine.at[:, 1 - other_at[half]],
            dst_ref=to.at[0] if line_first else to,
            send_sem=p2s_sem.at[j % D2, half],
            recv_sem=p2r_sem.at[j % D2, half],
            device_id=other_dev[half],
            device_id_type=MESH_ID,
        )

    def block(j, half, d, right, line_first, at):
        slot = d if right else jnp.where(d == at, ZN, d)
        return zb.at[j % DZ, half, slot] if line_first else zb.at[j % DZ, half, slot, 0]

    def own_block(j, half, d, line_first):
        return p1r.at[j % D1, half, d] if line_first else p2r.at[j % D2, half, d]

    def along(j, half, d, right, relayed, line_first):
        send, recv = (zrs_sem, zrr_sem) if right else (zls_sem, zlr_sem)
        here = block(j, half, d, right, line_first, z)
        return pltpu.make_async_remote_copy(
            src_ref=here if relayed else own_block(j, half, d, line_first),
            dst_ref=block(j, half, d, right, line_first, z + 1 if right else z - 1),
            send_sem=send.at[j % DZ, half, d],
            recv_sem=recv.at[j % DZ, half, d],
            device_id=at_dp(me + 4 if right else me - 4),
            device_id_type=MESH_ID,
        )

    def total_of(a, b):
        return (a[...].astype(F32) + b[...].astype(F32)).astype(BF16)

    def step0(j):
        _, pair = job_of(j)
        for half in range(2):
            p1s[j % DS, half] = product(half, pair * 2 + half, 1 - first_at[half]).astype(BF16)
            p1(j, half).start()

    def step1(j):
        e_of, pair = job_of(j)

        @pl.when(e_of == 1)
        def _():
            for half in range(2):
                p1(j, half).wait()
            for half in range(2):
                own = product(half, pair * 2 + half, first_at[half])
                p1r[j % D1, half] = (own + p1r[j % D1, half].astype(F32)).astype(BF16)

        for p in range(6):

            @pl.when(jnp.logical_and(e_of == 0, pair == p))
            def _():
                for half in range(2):
                    if p in (0, 2):
                        left_factor(half, p // 2).wait()
                    elif p == 4:
                        left_factor(half, 2 + half).wait()
                    elif p == 5 and half == 0:
                        left_factor(0, 3).wait()
                    right_factor(half, p).wait()
                    p1r[j % D1, half] = pair_product(half, p).astype(BF16)

    def turn(j):
        for half in range(2):
            other(j, half, False).start()

    def turned(j):
        for half in range(2):
            other(j, half, False).wait()
            mine = p2r.at[j % D2, half]
            mine[...] = total_of(mine, p1r.at[j % D1, half, :, other_at[half]])

    def ends(j, line_first):
        @pl.when(z == 0)
        def _():
            for half in range(2):
                for d in (3, 2, 1):
                    along(j, half, d, True, False, line_first).start()

        @pl.when(z == 3)
        def _():
            for half in range(2):
                for d in (0, 1, 2):
                    along(j, half, d, False, False, line_first).start()

    def relay(j, half, d, right, line_first):
        held = block(j, half, d, right, line_first, z)
        along(j, half, d, right, True, line_first).wait_recv()
        held[...] = total_of(held, own_block(j, half, d, line_first))
        along(j, half, d, right, True, line_first).start()

    def middle1(j, line_first):
        @pl.when(z == 1)
        def _():
            for half in range(2):
                for d in (3, 2):
                    relay(j, half, d, True, line_first)

        @pl.when(z == 2)
        def _():
            for half in range(2):
                for d in (0, 1):
                    relay(j, half, d, False, line_first)

    def middle2(j, line_first):
        @pl.when(z == 2)
        def _():
            for half in range(2):
                relay(j, half, 3, True, line_first)

        @pl.when(z == 1)
        def _():
            for half in range(2):
                relay(j, half, 0, False, line_first)

    def line_end(j, line_first):
        for half in range(2):
            mine = own_block(j, half, z, line_first)

            @pl.when(z > 0)
            def _():
                along(j, half, z, True, True, line_first).wait_recv()
                mine[...] = total_of(mine, block(j, half, z, True, line_first, z))

            @pl.when(z < 3)
            def _():
                along(j, half, z, False, True, line_first).wait_recv()
                mine[...] = total_of(mine, block(j, half, z, False, line_first, z))

            for d in range(4):

                @pl.when(d > z)
                def _():
                    along(j, half, d, True, True, line_first).wait_send()

                @pl.when(d < z)
                def _():
                    along(j, half, d, False, True, line_first).wait_send()

    def pass_on(j):
        for half in range(2):
            other(j, half, True).start()

    def passed(j):
        for half in range(2):
            other(j, half, True).wait()

    def result(slot, half, to):
        return pltpu.make_async_copy(fin.at[slot, half], to, fin_sem.at[slot, half])

    def output(j, line_first):
        e_of, pair = job_of(j)
        for half in range(2):

            @pl.when(j >= 2)
            def _():
                result(j % 2, half, g_out.at[0]).wait()

            if line_first:
                total = p1r[j % D1, half, z, other_at[half]].astype(F32) + p2r[j % D2, half, 0].astype(F32)
            else:
                total = p2r[j % D2, half, z].astype(F32)
            fin[j % 2, half] = total
            for e in range(2):
                for p in range(6):

                    @pl.when(jnp.logical_and(e_of == e, pair == p))
                    def _():
                        blk = p * 2 + half
                        if blk < 4:
                            to = g_fo.at[e, :, pl.ds(blk * COLS, COLS)]
                        elif blk < 8:
                            to = g_fi.at[e, :, pl.ds((blk - 4) * COLS, COLS)]
                        elif blk == 8:
                            to = g_out.at[e]
                        else:
                            to = g_in.at[e, blk - 9]
                        result(j % 2, half, to).start()

    small_to = (at_dp(me ^ 8), at_dp(me ^ 4), at_x, at_y)

    def small(k):
        return pltpu.make_async_remote_copy(
            src_ref=smb.at[k],
            dst_ref=smr.at[k],
            send_sem=sms_sem.at[k],
            recv_sem=smr_sem.at[k],
            device_id=small_to[k],
            device_id_type=MESH_ID,
        )

    def small_first():
        smb[0] = jnp.zeros_like(smb[0])
        for e in range(2):
            for i in range(6):
                smb[0, e * 9 + i : e * 9 + i + 1, :] = jnp.sum(acc_s[e * 6 + i], axis=0, keepdims=True)
            smb[0, e * 9 + 6 : e * 9 + 7, :] = jnp.sum(acc_b[e], axis=0, keepdims=True)
            for i in range(2):
                smb[0, e * 9 + 7 + i : e * 9 + 8 + i, :] = jnp.sum(
                    acc_f[e, :, i * D : (i + 1) * D], axis=0, keepdims=True
                )
        small(0).start()

    def small_next(k):
        small(k).wait()
        if k < 3:
            smb[k + 1] = smb[k] + smr[k]
            small(k + 1).start()
        else:
            total = smb[k] + smr[k]
            sm[0:SMALL, :] = jnp.zeros((SMALL, 128), F32)
            wide = pltpu.roll(total, lax.rem(D - me * ROWS_OUT, D), 1)
            sm[0:SMALL, 0:ROWS_OUT] = wide[:, 0:ROWS_OUT]
            heads_own = pltpu.roll(total, lax.rem(D - me * 24, D), 1)
            feed_own = pltpu.roll(total, lax.rem(D - (me % 8) * 96, D), 1)
            for e in range(2):
                at = e * 9 + 6
                for i in range(2):
                    sm[at + i : at + i + 1, 0:24] = heads_own[at : at + 1, i * COLS : i * COLS + 24]
                low, high = feed_own[at + 1 : at + 2, 0:96], feed_own[at + 2 : at + 3, 0:96]
                sm[at + 2 : at + 3, 0:96] = jnp.where(me < 8, low, high)
            pltpu.make_async_copy(sm, sm_out, out_sem.at[2]).start()

    def q_second_back():
        second_back(0, 0)
        left_factor(0, 0).start()
        left_factor(1, 0).start()

    def q_feed_back():
        feed_back(0, 0)
        for axis in range(2):
            for pair in (2, 3):
                right_factor(axis, pair).start()

    def q_first_back():
        first_back(0, 0)
        left_factor(0, 2).start()

    def q_attend_back():
        attend_back(0, 0)
        right_factor(1, 4).start()
        right_factor(0, 5).start()
        right_factor(1, 5).start()

    def q_token_end():
        token_end(0, 0)
        pltpu.make_async_copy(obq, gq_out, out_sem.at[0]).start()

    def p_token_end():
        blocks(1, lambda b: token_end(1, b))
        pltpu.make_async_copy(obp, gp_out, out_sem.at[1]).start()

    def p_mid(b):
        first_norm(1, b)
        feed(1, b)

    def p_second():
        blocks(1, lambda b: second_norm(1, b))
        out_p.start()

    def passages(piece):
        return lambda: blocks(1, lambda b: piece(1, b))

    work = {
        0: [q_feed_back, lambda: attend(1, 1)],
        2: [q_first_back, lambda: p_mid(0)],
        4: [q_attend_back, lambda: p_mid(1)],
        5: [lambda: token_back(0, 0), p_second, out_q.wait],
        6: [q_token_end, passages(second_back)],
        7: [passages(feed_back)],
        8: [passages(first_back)],
        9: [passages(attend_back)],
        10: [passages(token_back), small_first],
        12: [lambda: small_next(0)],
        14: [lambda: small_next(1)],
        15: [out_p.wait, p_token_end, lambda: small_next(2)],
        16: [lambda: small_next(3)],
    }

    def is_line_first(j):
        found = j == LINE_FIRST[0]
        for k in LINE_FIRST[1:]:
            found = jnp.logical_or(found, j == k)
        return found

    def steps(late, j):
        line_first = is_line_first(j)
        if late == 1:
            step1(j)

        @pl.when(line_first)
        def _():
            if late == 1:
                ends(j, True)
            elif late == 2:
                middle1(j, True)
            elif late == 3:
                middle2(j, True)
            elif late == 4:
                line_end(j, True)
                pass_on(j)
            else:
                passed(j)
                output(j, True)

        @pl.when(jnp.logical_not(line_first))
        def _():
            if late == 1:
                turn(j)
            elif late == 2:
                turned(j)
                ends(j, False)
            elif late == 3:
                middle1(j, False)
            elif late == 4:
                middle2(j, False)
            else:
                line_end(j, False)
                output(j, False)

    q_second_back()

    @pl.loop(0, JOBS + 5)
    def _(tick):
        for at, things in work.items():

            @pl.when(tick == at)
            def _():
                for thing in things:
                    thing()

        @pl.when(jnp.logical_and(tick >= 6, tick < JOBS))
        def _():
            step0(tick)

        for late in (1, 2, 3, 4, 5):

            @pl.when(jnp.logical_and(tick >= late, tick < JOBS + late))
            def _():
                steps(late, tick - late)

    pltpu.make_async_copy(obq, gq_out, out_sem.at[0]).wait()
    pltpu.make_async_copy(obp, gp_out, out_sem.at[1]).wait()
    pltpu.make_async_copy(sm, sm_out, out_sem.at[2]).wait()
    for slot in range(2):
        for half in range(2):
            result(slot, half, g_out.at[0]).wait()


def finish_kernel(*refs):
    oq, op, gq, gp, g_in, g_out, g_fi, g_fo, sums_in = refs[:9]
    large, (loss_to, in_bias, fi_bias, bo, gain, shift) = refs[9:17], refs[17:23]
    held, sums, in_sems, out_sems = refs[23:31], refs[31], refs[32], refs[33]
    sources = (oq, op, gq, gp, g_in, g_out, g_fi, g_fo)
    loads = [pltpu.make_async_copy(sources[i], held[i], in_sems.at[i]) for i in range(8)]
    stores = [pltpu.make_async_copy(held[i], large[i], out_sems.at[i]) for i in range(8)]
    little = pltpu.make_async_copy(sums_in, sums, in_sems.at[8])
    little.start()
    for load in loads:
        load.start()
    little.wait()
    loss_to[...] = sums[SMALL : SMALL + 1, 0:1]
    for e in range(2):
        at = e * 9
        gain[e] = sums[at : at + 2, 0:ROWS_OUT]
        shift[e] = sums[at + 2 : at + 4, 0:ROWS_OUT]
        bo[e] = sums[at + 4 : at + 6, 0:ROWS_OUT]
        in_bias[e] = sums[at + 6 : at + 8, 0:24]
        fi_bias[e : e + 1] = sums[at + 8 : at + 9, 0:96]
    for load, store in zip(loads, stores):
        load.wait()
        store.start()
    for store in stores:
        store.wait()


FF_HERE = 1536


def fused(
    question_tokens, passage_tokens, question_cotangent, passage_cotangent,
    question_lengths, passage_lengths, dataset_ids, positives,
    attn_in, attn_in_bias, attn_out, ffn_in, ffn_in_bias, ffn_out, out_biases, norm_gains, norm_shifts,
):
    any_spec = pl.BlockSpec(memory_space=pl.ANY)
    vmem = pl.BlockSpec(memory_space=pltpu.VMEM)

    def both(shape, dtype):
        return [pltpu.VMEM(shape(m), dtype) for m in TOKS]

    shape = jax.ShapeDtypeStruct
    dma = pltpu.SemaphoreType.DMA
    outs = pl.pallas_call(
        partial(fused_kernel, last=0),
        name="fused",
        in_specs=[any_spec] * 17,
        out_specs=[any_spec] * 9,
        out_shape=[
            shape((128, D), BF16),
            shape((512, D), BF16),
            shape((128, D), BF16),
            shape((512, D), BF16),
            shape((2, 3, ROWS_OUT, COLS), F32),
            shape((2, ROWS_OUT, COLS), F32),
            shape((2, ROWS_OUT, FF_HERE), F32),
            shape((2, ROWS_OUT, FF_HERE), F32),
            shape((SMALL + 8, 128), F32),
        ],
        scratch_shapes=[
            pltpu.VMEM((2, D, 3 * COLS), BF16),
            pltpu.VMEM((2, COLS, D), BF16),
            pltpu.VMEM((2, D, FF_HERE), BF16),
            pltpu.VMEM((2, FF_HERE, D), BF16),
            *both(lambda m: (m, D), BF16),
            *both(lambda m: (m, D), BF16),
            *both(lambda m: (m, 3 * COLS), BF16),
            pltpu.VMEM((1, 6, 128, 128), BF16),
            pltpu.VMEM((2, 6, 256, 256), BF16),
            *both(lambda m: (m, D), BF16),
            *both(lambda m: (m, D), F32),
            *both(lambda m: (m, D), F32),
            *both(lambda m: (m, 1), F32),
            *both(lambda m: (m, 1), F32),
            *both(lambda m: (m, FF_HERE), BF16),
            *both(lambda m: (m, D), BF16),
            *both(lambda m: (m, D), BF16),
            *both(lambda m: (m, COLS), BF16),
            *both(lambda m: (m, 12 * COLS), BF16),
            *both(lambda m: (4, ZN, 2, 2, ROWS_OUT, m), BF16),
            *both(lambda m: (m, D), BF16),
            *both(lambda m: (2, m, D), BF16),
            pltpu.VMEM((16, D), F32),
            pltpu.VMEM((8, COLS), F32),
            pltpu.VMEM((8, FF_HERE), F32),
            pltpu.VMEM((64, 32), F32),
            pltpu.VMEM((16, 16, 256), BF16),
            pltpu.VMEM((2, 256, 128), F32),
            pltpu.VMEM((64, D), F32),
            pltpu.VMEM((12, 8, D), F32),
            pltpu.VMEM((2, 8, 2 * COLS), F32),
            pltpu.VMEM((2, 8, FF_HERE), F32),
            pltpu.VMEM((4, SMALL, D), F32),
            pltpu.VMEM((4, SMALL, D), F32),
            pltpu.VMEM((DS, 2, ZN, 2, ROWS_OUT, COLS), BF16),
            pltpu.VMEM((D1, 2, ZN, 2, ROWS_OUT, COLS), BF16),
            pltpu.VMEM((D2, 2, ZN, ROWS_OUT, COLS), BF16),
            pltpu.VMEM((DZ, 2, ZN + 1, 2, ROWS_OUT, COLS), BF16),
            pltpu.VMEM((2, 2, ROWS_OUT, COLS), F32),
            pltpu.VMEM((2, 4, ZN, 2, ROWS_OUT, TOKS[0]), BF16),
            pltpu.VMEM((2, 6, TOKS[0], COLS), BF16),
            pltpu.VMEM((2, 16, D), BF16),
            pltpu.VMEM((2, 16, D), BF16),
            pltpu.VMEM((16, D), BF16),
            *[pltpu.SMEM((n,), jnp.int32) for n in (2, 2, 32, 32)],
            pltpu.VMEM((2, 2, COLS), BF16),
            pltpu.VMEM((2, FF_HERE), BF16),
            *[pltpu.VMEM((2, 2, D), BF16) for _ in range(3)],
            pltpu.VMEM((SMALL + 8, 128), F32),
            dma((2, 2)),
            dma((9,)),
            dma((16,)),
            dma((3,)),
            dma((3,)),
            dma((2, 3)),
            dma((16,)),
            dma((16,)),
            dma((4,)),
            dma((4,)),
            dma((DS, 2)),
            dma((D1, 2)),
            dma((D2, 2)),
            dma((D2, 2)),
            dma((DZ, 2, ZN)),
            dma((DZ, 2, ZN)),
            dma((DZ, 2, ZN)),
            dma((DZ, 2, ZN)),
            dma((2, 4)),
            dma((2, 4)),
            dma((2, 6)),
            dma((2, 6)),
            dma((2,)),
            dma((2,)),
        ],
        compiler_params=pltpu.CompilerParams(
            collective_id=0, has_side_effects=True, vmem_limit_bytes=VMEM_BYTES
        ),
    )(
        question_tokens.reshape(128, D),
        passage_tokens.reshape(512, D),
        question_cotangent.reshape(128, D),
        passage_cotangent.reshape(512, D),
        question_lengths, passage_lengths, dataset_ids, positives,
        attn_in.transpose(0, 2, 1, 3), attn_in_bias, attn_out, ffn_in, ffn_in_bias, ffn_out,
        out_biases, norm_gains, norm_shifts,
    )
    oq, op, gq, gp, g_in, g_out, g_fi, g_fo, sums = outs
    large = (oq, op, gq, gp, g_in, g_out, g_fi, g_fo)
    small = [(1, 1), (2, 2, 24), (2, 96), (2, 2, ROWS_OUT), (2, 2, ROWS_OUT), (2, 2, ROWS_OUT)]
    oq, op, gq, gp, g_in, g_out, g_fi, g_fo, loss, in_bias, fi_bias, bo, gain, shift = pl.pallas_call(
        finish_kernel,
        name="finish",
        in_specs=[any_spec] * 9,
        out_specs=[any_spec] * 8 + [vmem] * 6,
        out_shape=[shape(a.shape, a.dtype) for a in large] + [shape(dims, F32) for dims in small],
        scratch_shapes=[*[pltpu.VMEM(a.shape, a.dtype) for a in (*large, sums)], dma((9,)), dma((8,))],
        compiler_params=pltpu.CompilerParams(vmem_limit_bytes=VMEM_BYTES),
    )(*large, sums)
    return (
        oq.reshape(2, 64, D),
        op.reshape(2, 256, D),
        loss.reshape(()),
        gq.reshape(2, 64, D),
        gp.reshape(2, 256, D),
        g_in.transpose(0, 2, 1, 3),
        in_bias,
        g_out.transpose(0, 2, 1),
        g_fi,
        fi_bias,
        g_fo.transpose(0, 2, 1),
        bo,
        gain,
        shift,
    )


VMEM_BYTES = 62 * 1024 * 1024


def solution(mesh):
    in_specs = (
        P("dp", None, None),
        P("dp", None, None),
        P("dp", None, None),
        P("dp", None, None),
        P("dp"),
        P("dp"),
        P(),
        P(),
        P(None, None, None, "tensor"),
        P(None, None, "tensor"),
        P(None, "tensor", None),
        P(None, None, "tensor"),
        P(None, "tensor"),
        P(None, "tensor", None),
        P(),
        P(),
        P(),
    )
    out_specs = (
        P("dp", None, None),
        P("dp", None, None),
        P(),
        P("dp", None, None),
        P("dp", None, None),
        P(None, "dp", None, "tensor"),
        P(None, None, ("tensor", "dp")),
        P(None, "tensor", "dp"),
        P(None, "dp", "tensor"),
        P(None, ("tensor", "dp")),
        P(None, "tensor", "dp"),
        P(None, None, "dp"),
        P(None, None, "dp"),
        P(None, None, "dp"),
    )
    step = fused if mesh.shape["dp"] == 4 * ZN and mesh.shape["tensor"] == 2 else per_device
    return jax.shard_map(
        step, mesh=mesh, in_specs=in_specs, out_specs=out_specs, check_vma=False
    )
```

```python
from functools import partial

import jax
import jax.numpy as jnp
from jax import lax
from jax.experimental import pallas as pl
from jax.experimental.pallas import tpu as pltpu
from jax.sharding import PartitionSpec as P

D = 768
HD = 64


EPSILON = 1e-06
NEGATIVE = -1e30
HIGHEST = lax.Precision.HIGHEST
score_gain = 3.0


def norm_forward(summed, scale_row, shift_row):
    row_mean = jnp.mean(summed, axis=-1, keepdims=True)
    centred = summed - row_mean
    inv_std = lax.rsqrt(jnp.mean(centred * centred, axis=-1, keepdims=True) + EPSILON)
    normed = centred * inv_std
    return (normed * scale_row + shift_row, normed, inv_std)


def norm_backward(incoming, normed, inv_std, scale_row):
    scaled = incoming * scale_row
    outgoing = inv_std * (
        scaled
        - jnp.mean(scaled, axis=-1, keepdims=True)
        - normed * jnp.mean(scaled * normed, axis=-1, keepdims=True)
    )
    return (outgoing, jnp.sum(incoming * normed, axis=(0, 1)), jnp.sum(incoming, axis=(0, 1)))


def key_visible(lengths, length):
    positions = jnp.arange(length, dtype=jnp.int32)
    return (positions[None, :] < lengths[:, None])[:, None, None, :]


def head_scores(queries, key_rows, visible):
    raw_scores = jnp.einsum(
        "bqhe,bkhe->bhqk", queries, key_rows, preferred_element_type=jnp.float32
    ) * HD ** (-0.5)
    return jnp.where(visible, raw_scores, NEGATIVE)


def split_heads(matrix):
    return matrix.reshape(matrix.shape[0], matrix.shape[1], matrix.shape[2] // HD, HD)


def join_heads(per_head):
    return per_head.reshape(
        per_head.shape[0], per_head.shape[1], per_head.shape[2] * per_head.shape[3]
    )


def encoder_forward(tokens, lengths, params):
    (
        attn_in,
        attn_in_bias,
        attn_out,
        ffn_in,
        ffn_in_bias,
        ffn_out,
        out_biases,
        norm_gains,
        norm_shifts,
    ) = params
    projected = jnp.einsum("bld,dce->blce", tokens, attn_in, preferred_element_type=jnp.float32)
    in_bias = attn_in_bias.astype(jnp.float32)
    queries = split_heads((projected[:, :, 0] + in_bias[0]).astype(jnp.bfloat16))
    key_rows = split_heads(projected[:, :, 1].astype(jnp.bfloat16))
    values = split_heads((projected[:, :, 2] + in_bias[1]).astype(jnp.bfloat16))
    visible = key_visible(lengths, tokens.shape[1])
    scores = head_scores(queries, key_rows, visible)
    row_top = jnp.max(scores, axis=-1, keepdims=True)
    log_total = row_top + jnp.log(jnp.sum(jnp.exp(scores - row_top), axis=-1, keepdims=True))
    attn_probs = jnp.exp(scores - log_total).astype(jnp.bfloat16)
    context = join_heads(
        jnp.einsum(
            "bhqk,bkhe->bqhe", attn_probs, values, preferred_element_type=jnp.float32
        ).astype(jnp.bfloat16)
    )
    attn_part = jnp.einsum("ble,ed->bld", context, attn_out, preferred_element_type=jnp.float32)
    attn_sum = lax.psum(attn_part.astype(jnp.bfloat16), "tensor").astype(jnp.float32)
    bias_rows = out_biases.astype(jnp.float32)
    gain_rows = norm_gains.astype(jnp.float32)
    shift_rows = norm_shifts.astype(jnp.float32)
    hidden_float, normed_first, inv_first = norm_forward(
        tokens.astype(jnp.float32) + attn_sum + bias_rows[0], gain_rows[0], shift_rows[0]
    )
    hidden = hidden_float.astype(jnp.bfloat16)
    up_pre = jnp.einsum(
        "bld,df->blf", hidden, ffn_in, preferred_element_type=jnp.float32
    ) + ffn_in_bias.astype(jnp.float32)
    activated = jax.nn.gelu(up_pre, approximate=False).astype(jnp.bfloat16)
    down_part = jnp.einsum("blf,fd->bld", activated, ffn_out, preferred_element_type=jnp.float32)
    down_sum = lax.psum(down_part.astype(jnp.bfloat16), "tensor").astype(jnp.float32)
    outputs, normed_second, inv_second = norm_forward(
        hidden.astype(jnp.float32) + down_sum + bias_rows[1], gain_rows[1], shift_rows[1]
    )
    saved = (
        tokens,
        queries,
        key_rows,
        values,
        log_total,
        context,
        normed_first,
        inv_first,
        hidden,
        up_pre,
        activated,
        normed_second,
        inv_second,
    )
    return (outputs, saved)


def encoder_backward(incoming, saved, lengths, params):
    (
        attn_in,
        attn_in_bias,
        attn_out,
        ffn_in,
        ffn_in_bias,
        ffn_out,
        out_biases,
        norm_gains,
        norm_shifts,
    ) = params
    (
        tokens,
        queries,
        key_rows,
        values,
        log_total,
        context,
        normed_first,
        inv_first,
        hidden,
        up_pre,
        activated,
        normed_second,
        inv_second,
    ) = saved
    groups_here, length, model_width = tokens.shape
    gain_rows = norm_gains.astype(jnp.float32)
    d_second, gain_second, shift_second = norm_backward(
        incoming, normed_second, inv_second, gain_rows[1]
    )
    d_down = d_second.astype(jnp.bfloat16)
    grad_ffn_out = jnp.einsum("blf,bld->fd", activated, d_down, preferred_element_type=jnp.float32)
    d_activated = jnp.einsum("bld,fd->blf", d_down, ffn_out, preferred_element_type=jnp.float32)
    gelu_pull = jax.vjp(partial(jax.nn.gelu, approximate=False), up_pre)[1]
    d_up = gelu_pull(d_activated)[0].astype(jnp.bfloat16)
    grad_ffn_in = jnp.einsum("bld,blf->df", hidden, d_up, preferred_element_type=jnp.float32)
    hidden_part = jnp.einsum("blf,df->bld", d_up, ffn_in, preferred_element_type=jnp.float32)
    d_hidden = d_second + lax.psum(hidden_part.astype(jnp.bfloat16), "tensor").astype(jnp.float32)
    d_first, gain_first, shift_first = norm_backward(
        d_hidden, normed_first, inv_first, gain_rows[0]
    )
    d_attn = d_first.astype(jnp.bfloat16)
    grad_attn_out = jnp.einsum("ble,bld->ed", context, d_attn, preferred_element_type=jnp.float32)
    d_context = split_heads(
        jnp.einsum("bld,ed->ble", d_attn, attn_out, preferred_element_type=jnp.float32).astype(
            jnp.bfloat16
        )
    )
    visible = key_visible(lengths, length)
    scores = head_scores(queries, key_rows, visible)
    probs_float = jnp.exp(scores - log_total)
    d_probs = jnp.einsum("bqhe,bkhe->bhqk", d_context, values, preferred_element_type=jnp.float32)
    d_values = jnp.einsum(
        "bhqk,bqhe->bkhe",
        probs_float.astype(jnp.bfloat16),
        d_context,
        preferred_element_type=jnp.float32,
    ).astype(jnp.bfloat16)
    d_scores = (
        probs_float * (d_probs - jnp.sum(probs_float * d_probs, axis=-1, keepdims=True))
    ).astype(jnp.bfloat16)
    d_queries = (
        jnp.einsum("bhqk,bkhe->bqhe", d_scores, key_rows, preferred_element_type=jnp.float32)
        * HD ** (-0.5)
    ).astype(jnp.bfloat16)
    d_keys = (
        jnp.einsum("bhqk,bqhe->bkhe", d_scores, queries, preferred_element_type=jnp.float32)
        * HD ** (-0.5)
    ).astype(jnp.bfloat16)
    query_grad = join_heads(d_queries)
    value_grad = join_heads(d_values)
    d_projected = jnp.stack([query_grad, join_heads(d_keys), value_grad], axis=2)
    grad_attn_in = jnp.einsum(
        "bld,blce->dce", tokens, d_projected, preferred_element_type=jnp.float32
    )
    token_part = jnp.einsum(
        "blce,dce->bld", d_projected, attn_in, preferred_element_type=jnp.float32
    )
    d_tokens = (
        d_first + lax.psum(token_part.astype(jnp.bfloat16), "tensor").astype(jnp.float32)
    ).astype(jnp.bfloat16)
    grad_in_bias = jnp.stack(
        [
            jnp.sum(query_grad.astype(jnp.float32), axis=(0, 1)),
            jnp.sum(value_grad.astype(jnp.float32), axis=(0, 1)),
        ]
    )
    grad_ffn_bias = jnp.sum(d_up.astype(jnp.float32), axis=(0, 1))
    grad_out_biases = jnp.stack(
        [
            jnp.sum(d_attn.astype(jnp.float32), axis=(0, 1)),
            jnp.sum(d_down.astype(jnp.float32), axis=(0, 1)),
        ]
    )
    grad_gains = jnp.stack([gain_first, gain_second])
    grad_shifts = jnp.stack([shift_first, shift_second])
    return (
        d_tokens,
        (
            grad_attn_in,
            grad_in_bias,
            grad_attn_out,
            grad_ffn_in,
            grad_ffn_bias,
            grad_ffn_out,
            grad_out_biases,
            grad_gains,
            grad_shifts,
        ),
    )


def contrastive(question_rows, passage_rows, own_positive, dataset_ids):
    class_scores = jnp.einsum(
        "gd,jd->gj", question_rows, passage_rows, preferred_element_type=jnp.float32
    ) * (score_gain * D ** (-0.5))
    columns = jnp.arange(passage_rows.shape[0], dtype=jnp.int32)
    chosen = own_positive[:, None] == columns[None, :]
    own_set = jnp.sum(jnp.where(chosen, dataset_ids[None, :], 0), axis=1)
    logits = jnp.where(dataset_ids[None, :] == own_set[:, None], class_scores, NEGATIVE)
    row_top = jnp.max(logits, axis=1, keepdims=True)
    log_total = row_top + jnp.log(jnp.sum(jnp.exp(logits - row_top), axis=1, keepdims=True))
    target = jnp.sum(jnp.where(chosen, class_scores, 0.0), axis=1)
    d_class = (jnp.exp(logits - log_total) - chosen.astype(jnp.float32)) * (
        score_gain * D ** (-0.5)
    )
    return (log_total[:, 0] - target, d_class)


def per_device(
    question_tokens,
    passage_tokens,
    question_cotangent,
    passage_cotangent,
    question_lengths,
    passage_lengths,
    dataset_ids,
    positives,
    attn_in,
    attn_in_bias,
    attn_out,
    ffn_in,
    ffn_in_bias,
    ffn_out,
    out_biases,
    norm_gains,
    norm_shifts,
):

    def encoder_params(encoder):
        return (
            attn_in[encoder],
            attn_in_bias[encoder],
            attn_out[encoder],
            ffn_in[encoder],
            ffn_in_bias[encoder],
            ffn_out[encoder],
            out_biases[encoder],
            norm_gains[encoder],
            norm_shifts[encoder],
        )

    question_params = encoder_params(0)
    passage_params = encoder_params(1)
    question_float, question_saved = encoder_forward(
        question_tokens, question_lengths, question_params
    )
    passage_float, passage_saved = encoder_forward(passage_tokens, passage_lengths, passage_params)
    question_heads = question_float[:, 0].astype(jnp.bfloat16)
    passage_heads = passage_float[:, 0].astype(jnp.bfloat16)
    local_groups = question_heads.shape[0]
    own_start = lax.axis_index("dp") * local_groups
    all_passages = lax.all_gather(passage_heads, "dp", axis=0, tiled=True)
    own_positive = lax.dynamic_slice_in_dim(positives, own_start, local_groups)
    cross, d_class = contrastive(question_heads, all_passages, own_positive, dataset_ids)
    total = lax.psum(jnp.sum(cross), "dp")
    contrastive_loss = total / all_passages.shape[0]
    d_question_heads = jnp.einsum(
        "gj,jd->gd", d_class, all_passages.astype(jnp.float32), precision=HIGHEST
    )
    question_heads_float = question_heads.astype(jnp.float32)
    d_passage_heads = lax.psum_scatter(
        jnp.einsum("gj,gd->jd", d_class, question_heads_float, precision=HIGHEST),
        "dp",
        scatter_dimension=0,
        tiled=True,
    )
    d_question_out = question_cotangent.astype(jnp.float32).at[:, 0].add(d_question_heads)
    d_passage_out = passage_cotangent.astype(jnp.float32).at[:, 0].add(d_passage_heads)
    passage_grad, passage_weights = encoder_backward(
        d_passage_out, passage_saved, passage_lengths, passage_params
    )
    question_grad, question_weights = encoder_backward(
        d_question_out, question_saved, question_lengths, question_params
    )
    joined = (
        lax.psum_scatter(question_weights[0], "dp", scatter_dimension=0, tiled=True),
        lax.psum_scatter(question_weights[1], "dp", scatter_dimension=1, tiled=True),
        lax.psum_scatter(question_weights[2], "dp", scatter_dimension=1, tiled=True),
        lax.psum_scatter(question_weights[3], "dp", scatter_dimension=0, tiled=True),
        lax.psum_scatter(question_weights[4], "dp", scatter_dimension=0, tiled=True),
        lax.psum_scatter(question_weights[5], "dp", scatter_dimension=1, tiled=True),
        lax.psum_scatter(question_weights[6], "dp", scatter_dimension=1, tiled=True),
        lax.psum_scatter(question_weights[7], "dp", scatter_dimension=1, tiled=True),
        lax.psum_scatter(question_weights[8], "dp", scatter_dimension=1, tiled=True),
        lax.psum_scatter(passage_weights[0], "dp", scatter_dimension=0, tiled=True),
        lax.psum_scatter(passage_weights[1], "dp", scatter_dimension=1, tiled=True),
        lax.psum_scatter(passage_weights[2], "dp", scatter_dimension=1, tiled=True),
        lax.psum_scatter(passage_weights[3], "dp", scatter_dimension=0, tiled=True),
        lax.psum_scatter(passage_weights[4], "dp", scatter_dimension=0, tiled=True),
        lax.psum_scatter(passage_weights[5], "dp", scatter_dimension=1, tiled=True),
        lax.psum_scatter(passage_weights[6], "dp", scatter_dimension=1, tiled=True),
        lax.psum_scatter(passage_weights[7], "dp", scatter_dimension=1, tiled=True),
        lax.psum_scatter(passage_weights[8], "dp", scatter_dimension=1, tiled=True),
    )
    question_parts = joined[:9]
    passage_parts = joined[9:]
    stacked = [
        jnp.stack([question_piece, passage_piece])
        for question_piece, passage_piece in zip(question_parts, passage_parts)
    ]
    return (
        question_float.astype(jnp.bfloat16),
        passage_float.astype(jnp.bfloat16),
        contrastive_loss,
        question_grad,
        passage_grad,
        stacked[0],
        stacked[1],
        stacked[2],
        stacked[3],
        stacked[4],
        stacked[5],
        stacked[6],
        stacked[7],
        stacked[8],
    )


MESH_ID = pl.DeviceIdType.MESH
F32 = jnp.float32
BF16 = jnp.bfloat16
ZN = 4
ROWS_OUT = 48
JOBS = 12
COLS = 384
D1, D2, DZ, DS = 8, 8, 8, 2
LINE_FIRST = (0, 5, 8, 9)
TOKS = (128, 512)
BLK = (128, 256)
SMALL = 24
CHUNK = 64
NORM_UNROLL = (2, 4)
UP_UNROLL = (6, 6)
DOWN_UNROLL = (3, 3)
PAIR_UNROLL = (3, 3)


def dot(a, b):
    return jnp.dot(a, b, preferred_element_type=F32)


def dot_t(a, b):
    return lax.dot_general(a, b, (((1,), (1,)), ((), ())), preferred_element_type=F32)


def t_dot(a, b):
    return lax.dot_general(a, b, (((0,), (0,)), ((), ())), preferred_element_type=F32)


def gelu_and_slope(u):
    size = jnp.abs(u)
    bell = jnp.exp(-0.5 * u * u)
    t = 1.0 / (1.0 + (0.3275911 * 0.7071067811865476) * size)
    poly = t * (
        0.127414796
        + t * (-0.142248368 + t * (0.7107068705 + t * (-0.7265760135 + t * 0.5307027145)))
    )
    tail = poly * bell
    phi = jnp.where(u >= 0.0, 1.0 - tail, tail)
    return u * phi, phi + u * bell * 0.3989422804014327


def row_mean(v):
    return jnp.sum(v, axis=-1, keepdims=True) * (1.0 / D)


def fold8(v):
    return jnp.sum(v.reshape(v.shape[0] // 8, 8, v.shape[1]), axis=0)


def rows_at(start, size, step=16):
    return pl.ds(pl.multiple_of(start, step), size)


def fused_kernel(
    xq_in, xp_in, cq_in, cp_in, qlen_in, plen_in, dsid_in, posi_in,
    win_in, bin_from, wo_in, wf_in, bfi_from, wd_in, bo_from, gain_from, shift_from,
    oq_out, op_out, gq_out, gp_out, g_in, g_out, g_fi, g_fo, sm_out,
    win, wo, wf, wd, xq, xp, cq, cp, qkvq, qkvp, prq, prp, hq, hp, n1q, n1p, n2q, n2p,
    i1q, i1p, i2q, i2p, sq, sp, obq, obp, ddq, ddp, dcq, dcp, ballq, ballp, atq, atp,
    exsq, exsp, exrq, exrp, par, pin, pfi, masks, hg, hf, dh, acc_s, acc_b, acc_f, smb, smr,
    p1s, p1r, p2r, zb, fin, fra, frb, xms, xmr, hm,
    qlen, plen, dsid, posi, bin_in, bfi_in, bo_in, gain_in, shift_in, sm,
    fin_sem, little_sem, in_sem, out_sem, exs_sem, exr_sem, hgs_sem, hgr_sem, sms_sem, smr_sem,
    p1s_sem, p1r_sem, p2s_sem, p2r_sem, zrs_sem, zrr_sem, zls_sem, zlr_sem,
    fas_sem, far_sem, fbs_sem, fbr_sem, xms_sem, xmr_sem,
    *, last,
):
    me = lax.axis_index("dp")
    core = lax.axis_index("tensor")
    z, y, x = me // 4, (me // 2) % 2, me % 2
    partner = {"dp": me, "tensor": 1 - core}
    at_x = {"dp": me + 1 - 2 * x, "tensor": core}
    at_y = {"dp": me + 2 - 4 * y, "tensor": core}

    def at_dp(index):
        return {"dp": index, "tensor": core}

    X, COT, QKV, PR, HID = (xq, xp), (cq, cp), (qkvq, qkvp), (prq, prp), (hq, hp)
    N1, N2, I1, I2, SLOPE = (n1q, n1p), (n2q, n2p), (i1q, i1p), (i2q, i2p), (sq, sp)
    OB, DD, DC, BALL, AT = (obq, obp), (ddq, ddp), (dcq, dcp), (ballq, ballp), (atq, atp)
    EXS, EXR = (exsq, exsp), (exrq, exrp)

    little = [
        (qlen_in, qlen), (plen_in, plen), (bin_from, bin_in), (bfi_from, bfi_in), (bo_from, bo_in),
        (gain_from, gain_in), (shift_from, shift_in), (dsid_in, dsid), (posi_in, posi),
    ]
    little = [pltpu.make_async_copy(s, d, little_sem.at[i]) for i, (s, d) in enumerate(little)]
    loads = [
        (xq_in, xq),
        *[(win_in.at[0, j], win.at[0, :, pl.ds(j * COLS, COLS)]) for j in range(3)],
        (xp_in, xp),
        *[(win_in.at[1, j], win.at[1, :, pl.ds(j * COLS, COLS)]) for j in range(3)],
        (wo_in.at[0], wo.at[0]),
        (wo_in.at[1], wo.at[1]),
        (wf_in.at[0], wf.at[0]),
        (wf_in.at[1], wf.at[1]),
        (wd_in.at[0], wd.at[0]),
        (wd_in.at[1], wd.at[1]),
        (cq_in, cq),
        (cp_in, cp),
    ]
    loads = [pltpu.make_async_copy(s, d, in_sem.at[i]) for i, (s, d) in enumerate(loads)]
    for copy in loads[:4]:
        copy.start()
    for copy in little:
        copy.start()
    ready = set()

    def need(*which):
        for i in which:
            if i not in ready:
                loads[i].wait()
                ready.add(i)

    barrier = pltpu.get_barrier_semaphore()
    pl.semaphore_signal(barrier, inc=1, device_id=partner, device_id_type=MESH_ID)
    for k in range(1, 16):
        pl.semaphore_signal(barrier, inc=1, device_id=at_dp(me ^ k), device_id_type=MESH_ID)

    def load(*which):
        for i in which:
            loads[i].start()

    for copy in little:
        copy.wait()
    for e in range(2):
        for i in range(2):
            par[e * 8 + i : e * 8 + i + 1, :] = bo_in[e].astype(F32)[i : i + 1]
            par[e * 8 + 2 + i : e * 8 + 3 + i, :] = gain_in[e].astype(F32)[i : i + 1]
            par[e * 8 + 4 + i : e * 8 + 5 + i, :] = shift_in[e].astype(F32)[i : i + 1]
            pin[e * 2 + i : e * 2 + i + 1, :] = bin_in[e].astype(F32)[i : i + 1]
        pfi[e : e + 1, :] = bfi_in[...].astype(F32)[e : e + 1]
    acc_s[...] = jnp.zeros_like(acc_s)
    acc_b[...] = jnp.zeros_like(acc_b)
    acc_f[...] = jnp.zeros_like(acc_f)

    r32 = lax.broadcasted_iota(jnp.int32, (32, 32), 0)
    c32 = lax.broadcasted_iota(jnp.int32, (32, 32), 1)
    own_pos = jnp.zeros((32, 32), F32)
    set_col = jnp.zeros((32, 32), F32)
    for g in range(32):
        at = (g % 2) * 16 + g // 2
        own_pos = jnp.where(r32 == at, posi[g].astype(F32), own_pos)
        set_col = jnp.where(c32 == at, dsid[g].astype(F32), set_col)
    col_group = ((c32 % 16) * 2 + c32 // 16).astype(F32)
    chosen = jnp.where(own_pos == col_group, 1.0, 0.0)
    own_set = jnp.sum(chosen * set_col, axis=1, keepdims=True)
    masks[0:32, :] = chosen
    masks[32:64, :] = jnp.where(set_col == own_set, 1.0, 0.0)

    lane_lo = lax.broadcasted_iota(jnp.int32, (1, 128), 1) < HD

    def side(v, hh):
        return jnp.where(lane_lo if hh == 0 else jnp.logical_not(lane_lo), v, jnp.zeros_like(v))

    def exchange(e, b, parity):
        slot = 0 if e == 0 else 1 + b
        rows = rows_at(b * BLK[e], BLK[e]) if not isinstance(b, int) else pl.ds(b * BLK[e], BLK[e])
        return pltpu.make_async_remote_copy(
            src_ref=EXS[e].at[rows],
            dst_ref=EXR[e].at[parity, rows],
            send_sem=exs_sem.at[slot],
            recv_sem=exr_sem.at[parity, slot],
            device_id=partner,
            device_id_type=MESH_ID,
        )

    def block_rows(e, b):
        if e == 0:
            return pl.ds(0, BLK[0])
        return rows_at(b * BLK[1], BLK[1], BLK[1])

    def blocks(e, body):
        if e == 0:
            body(0)
        else:
            pl.loop(0, 2)(body)

    def project(e, b, which):
        rows = block_rows(e, b)
        xb = X[e][rows, :]
        for j in which:
            cols = pl.ds(j * COLS, COLS)
            got = dot(xb, win[e, :, cols])
            if j == 0:
                got = (got + pin[e * 2 : e * 2 + 1, :]).astype(BF16) * jnp.asarray(HD**-0.5, BF16)
            elif j == 2:
                got = got + pin[e * 2 + 1 : e * 2 + 2, :]
            QKV[e][rows, cols] = got.astype(BF16)

    def attend(e, b):
        size = BLK[e]
        rows = block_rows(e, b)
        col = lax.broadcasted_iota(jnp.int32, (size, size), 1)
        if e == 0:
            row = lax.broadcasted_iota(jnp.int32, (size, size), 0)
            first = jnp.logical_and(row < 64, col < qlen[0])
            second = jnp.logical_and(
                row >= 64, jnp.logical_and(col >= 64, col < 64 + qlen[1])
            )
            seen = jnp.logical_or(first, second)
        else:
            seen = col < plen[b]

        @pl.loop(0, 3, unroll=PAIR_UNROLL[e])
        def _(pair):
            q2 = QKV[e][rows, rows_at(pair * 128, 128, 128)]
            k2 = QKV[e][rows, rows_at(COLS + pair * 128, 128, 128)]
            v2 = QKV[e][rows, rows_at(2 * COLS + pair * 128, 128, 128)]
            total = jnp.zeros((size, 128), F32)
            for hh in range(2):
                s = dot_t(side(q2, hh), k2)
                s = jnp.where(seen, s, NEGATIVE)
                p = jnp.exp(s - jnp.max(s, axis=-1, keepdims=True))
                p = (p * (1.0 / jnp.sum(p, axis=-1, keepdims=True))).astype(BF16)
                PR[e][b, pair * 2 + hh] = p
                total = total + dot(p, side(v2, hh))
            BALL[e][rows, rows_at(8 * COLS + pair * 128, 128, 128)] = total.astype(BF16)

        ctx = BALL[e][rows, pl.ds(8 * COLS, COLS)]
        EXS[e][rows, :] = dot(ctx, wo[e]).astype(BF16)
        exchange(e, b, 0).start()

    CH = CHUNK

    def first_norm(e, b):
        exchange(e, b, 0).wait()

        @pl.loop(0, BLK[e] // CH, unroll=NORM_UNROLL[e])
        def _(c):
            rows = rows_at(b * BLK[e] + c * CH, CH, CH)
            v = (
                X[e][rows, :].astype(F32)
                + (EXS[e][rows, :].astype(F32) + EXR[e][0, rows, :].astype(F32))
                + par[e * 8 : e * 8 + 1, :]
            )
            v = v - row_mean(v)
            inv = lax.rsqrt(row_mean(v * v) + EPSILON)
            n = v * inv
            N1[e][rows, :] = n
            I1[e][rows, :] = inv
            HID[e][rows, :] = (
                n * par[e * 8 + 2 : e * 8 + 3, :] + par[e * 8 + 4 : e * 8 + 5, :]
            ).astype(BF16)

    def feed(e, b):
        rows = block_rows(e, b)

        @pl.loop(0, 6, unroll=UP_UNROLL[e])
        def _(n):
            cols = rows_at(n * 256, 256, 256)
            u = dot(HID[e][rows, :], wf[e, :, cols]) + pfi[e : e + 1, cols]
            a, slope = gelu_and_slope(u)
            BALL[e][rows, cols] = a.astype(BF16)
            SLOPE[e][rows, cols] = slope.astype(BF16)

        @pl.loop(0, 3, unroll=DOWN_UNROLL[e])
        def _(n):
            cols = rows_at(n * 256, 256, 256)
            EXS[e][rows, cols] = dot(BALL[e][rows, pl.ds(0, FF_HERE)], wd[e, :, cols]).astype(BF16)

        exchange(e, b, 1).start()

    def second_norm(e, b):
        exchange(e, b, 1).wait()

        @pl.loop(0, BLK[e] // CH, unroll=NORM_UNROLL[e])
        def _(c):
            rows = rows_at(b * BLK[e] + c * CH, CH, CH)
            v = (
                HID[e][rows, :].astype(F32)
                + (EXS[e][rows, :].astype(F32) + EXR[e][1, rows, :].astype(F32))
                + par[e * 8 + 1 : e * 8 + 2, :]
            )
            v = v - row_mean(v)
            inv = lax.rsqrt(row_mean(v * v) + EPSILON)
            n = v * inv
            N2[e][rows, :] = n
            I2[e][rows, :] = inv
            OB[e][rows, :] = (
                n * par[e * 8 + 3 : e * 8 + 4, :] + par[e * 8 + 5 : e * 8 + 6, :]
            ).astype(BF16)

    def mini_exchange(k):
        return pltpu.make_async_remote_copy(
            src_ref=xms.at[k],
            dst_ref=xmr.at[k],
            send_sem=xms_sem.at[k],
            recv_sem=xmr_sem.at[k],
            device_id=partner,
            device_id_type=MESH_ID,
        )

    def first_rows(ref):
        rows = [ref[b * 256 : b * 256 + 16, :].astype(F32)[0:1] for b in range(2)]
        return jnp.concatenate([*rows, jnp.zeros((14, rows[0].shape[1]), F32)], axis=0)

    def mini_attend():
        xm = first_rows(xp).astype(BF16)
        q = (dot(xm, win[1, :, pl.ds(0, COLS)]) + pin[2:3, :]).astype(BF16).astype(F32) * HD**-0.5
        of_head = lax.broadcasted_iota(jnp.int32, (16, COLS), 1) // HD == lax.broadcasted_iota(
            jnp.int32, (16, COLS), 0
        )
        col = lax.broadcasted_iota(jnp.int32, (16, 256), 1)
        rows = []
        for b in range(2):
            keys = qkvp[b * 256 : (b + 1) * 256, COLS : 2 * COLS]
            vals = qkvp[b * 256 : (b + 1) * 256, 2 * COLS : 3 * COLS]
            s = dot_t(jnp.where(of_head, q[b : b + 1], 0.0).astype(BF16), keys)
            s = jnp.where(col < plen[b], s, NEGATIVE)
            p = jnp.exp(s - jnp.max(s, axis=-1, keepdims=True))
            p = (p * (1.0 / jnp.sum(p, axis=-1, keepdims=True))).astype(BF16)
            rows.append(jnp.sum(jnp.where(of_head, dot(p, vals), 0.0), axis=0, keepdims=True))
        ctx = jnp.concatenate([*rows, jnp.zeros((14, COLS), F32)], axis=0)
        xms[0] = dot(ctx.astype(BF16), wo[1]).astype(BF16)
        mini_exchange(0).start()

    def mini_norm(k, v):
        mini_exchange(k).wait()
        v = v + (xms[k].astype(F32) + xmr[k].astype(F32)) + par[8 + k : 9 + k, :]
        v = v - row_mean(v)
        n = v * lax.rsqrt(row_mean(v * v) + EPSILON)
        return (n * par[10 + k : 11 + k, :] + par[12 + k : 13 + k, :]).astype(BF16)

    def mini_feed():
        hm[...] = mini_norm(0, first_rows(xp))

        u = dot(hm[...], wf[1]) + pfi[1:2, :]
        a = gelu_and_slope(u)[0].astype(BF16)
        xms[1] = dot(a, wd[1]).astype(BF16)

        mini_exchange(1).start()

    def transpose_into(e, k, src, b):
        rows = block_rows(e, b)

        @pl.loop(0, 2)
        def _(c):
            tile = src[rows, rows_at(c * COLS, COLS, 128)].T
            AT[e][k, pl.ds(c * 2, 2), :, :, :, rows] = tile.reshape(2, 2, 2, ROWS_OUT, BLK[e])

    def left_factor(axis, k):
        return pltpu.make_async_remote_copy(
            src_ref=atq.at[k, :, :, 1 - x] if axis == 0 else atq.at[k, :, 1 - y],
            dst_ref=fra.at[axis, k],
            send_sem=fas_sem.at[axis, k],
            recv_sem=far_sem.at[axis, k],
            device_id=first_dev[axis],
            device_id_type=MESH_ID,
        )

    def right_factor(axis, pair):
        return pltpu.make_async_remote_copy(
            src_ref=ballq.at[:, pl.ds((pair * 2 + axis) * COLS, COLS)],
            dst_ref=frb.at[axis, pair],
            send_sem=fbs_sem.at[axis, pair],
            recv_sem=fbr_sem.at[axis, pair],
            device_id=first_dev[axis],
            device_id_type=MESH_ID,
        )

    first_dev, other_dev = (at_x, at_y), (at_y, at_x)
    first_at, other_at = (x, y), (y, x)

    need(0, 1, 2, 3)
    load(4, 6, 7, 8, 5, 9, 10, 12, 11, 13, 14, 15)
    project(0, 0, (0, 1, 2))
    need(8)
    pl.semaphore_wait(barrier, 16)
    attend(0, 0)
    right_factor(0, 4).start()
    need(4, 5, 6, 7, 9)
    blocks(1, lambda b: project(1, b, (1, 2)))
    mini_attend()
    first_norm(0, 0)
    need(10, 12)
    feed(0, 0)
    for axis in range(2):
        for pair in range(2):
            right_factor(axis, pair).start()
    need(11, 13)
    mini_feed()
    second_norm(0, 0)
    out_q = pltpu.make_async_copy(obq, oq_out, out_sem.at[0])
    out_p = pltpu.make_async_copy(obp, op_out, out_sem.at[1])
    out_q.start()
    mini_out = mini_norm(1, hm[...].astype(F32)).astype(F32)

    pieces = []
    rows = [obq[at : at + 16, :].astype(F32)[0:1] for at in (0, 64)]
    for head in (*rows, mini_out[0:1], mini_out[1:2]):
        pieces += [head[:, k * 256 : (k + 1) * 256] for k in range(3)]
    pieces.append(jnp.zeros((4, 256), F32))
    hg[me] = jnp.concatenate(pieces, axis=0).astype(BF16)

    def heads(k):
        return pltpu.make_async_remote_copy(
            src_ref=hg.at[me],
            dst_ref=hg.at[me],
            send_sem=hgs_sem.at[k],
            recv_sem=hgr_sem.at[k],
            device_id=at_dp(me ^ k),
            device_id_type=MESH_ID,
        )

    for k in range(1, 16):
        heads(k).start()
    need(14, 15)
    transpose_into(0, 1, hq, 0)
    for axis in range(2):
        left_factor(axis, 1).start()
    transpose_into(0, 3, xq, 0)
    for axis in range(2):
        left_factor(axis, 3).start()
    blocks(1, lambda b: project(1, b, (0,)))
    attend(1, 0)
    for k in range(1, 16):
        copy = pltpu.make_async_remote_copy(
            src_ref=hg.at[me],
            dst_ref=hg.at[me ^ k],
            send_sem=hgs_sem.at[k],
            recv_sem=hgr_sem.at[k],
            device_id=at_dp(me ^ k),
            device_id_type=MESH_ID,
        )
        copy.wait()
    gathered = hg[...].astype(F32).reshape(256, 256)
    hf[0] = gathered[:, 0:128]
    hf[1] = gathered[:, 128:256]

    def all_heads(first):
        groups = []
        for i in range(2):
            parts = [
                hf[c, pl.ds(first + i * 3 + k, 16, stride=16), :] for k in range(3) for c in range(2)
            ]
            groups.append(jnp.concatenate(parts, axis=1))
        return jnp.concatenate(groups, axis=0)

    heads_q, heads_p = all_heads(0), all_heads(6)
    gain = score_gain * D ** (-0.5)
    class_scores = dot_t(heads_q.astype(BF16), heads_p.astype(BF16)) * gain
    chosen = masks[0:32, :]
    logits = jnp.where(masks[32:64, :] > 0.5, class_scores, NEGATIVE)
    top = jnp.max(logits, axis=1, keepdims=True)
    log_total = top + jnp.log(jnp.sum(jnp.exp(logits - top), axis=1, keepdims=True))
    target = jnp.sum(chosen * class_scores, axis=1, keepdims=True)
    loss = jnp.sum(log_total - target, axis=0, keepdims=True) * (1.0 / 32)
    sm[SMALL : SMALL + 8, :] = jnp.broadcast_to(loss, (8, 128))
    d_class = (jnp.exp(logits - log_total) - chosen) * gain
    dh[0:32, :] = lax.dot_general(
        d_class, heads_p, (((1,), (0,)), ((), ())), precision=HIGHEST, preferred_element_type=F32
    )
    dh[32:64, :] = lax.dot_general(
        d_class, heads_q, (((0,), (0,)), ((), ())), precision=HIGHEST, preferred_element_type=F32
    )

    def norm_back(incoming, n, inv, scale):
        scaled = incoming * scale
        return inv * (scaled - row_mean(scaled) - n * row_mean(scaled * n))

    def second_back(e, b):
        row0 = lax.broadcasted_iota(jnp.int32, (CH, 1), 0)
        seqs = 2 if e == 0 else 1
        length = 64 if e == 0 else 256
        for i in range(seqs):
            group = i if e == 0 else b
            extra = dh[pl.ds(e * 32 + group * 16 + me, 1), :]

            @pl.loop(0, length // CH, unroll=NORM_UNROLL[e])
            def _(c):
                rows = rows_at(group * length + c * CH, CH, CH)
                add = jnp.where(row0 + c * CH == 0, extra, 0.0)
                d = COT[e][rows, :].astype(F32) + add
                n = N2[e][rows, :]
                out = norm_back(d, n, I2[e][rows, :], par[e * 8 + 3 : e * 8 + 4, :])
                N2[e][rows, :] = out
                low = out.astype(BF16)
                DD[e][rows, :] = low
                acc_s[e * 6 + 1] += fold8(d * n)
                acc_s[e * 6 + 3] += fold8(d)
                acc_s[e * 6 + 5] += fold8(low.astype(F32))

        transpose_into(e, 0, DD[e], b)

    def feed_back(e, b):
        rows = block_rows(e, b)

        @pl.loop(0, 6, unroll=UP_UNROLL[e])
        def _(n):
            cols = rows_at(n * 256, 256, 256)
            d = dot_t(DD[e][rows, :], wd[e, cols, :]) * SLOPE[e][rows, cols].astype(F32)
            d = d.astype(BF16)
            BALL[e][rows, rows_at(4 * COLS + n * 256, 256, 256)] = d
            acc_f[e, :, cols] += fold8(d.astype(F32))

        @pl.loop(0, 3, unroll=DOWN_UNROLL[e])
        def _(n):
            cols = rows_at(n * 256, 256, 256)
            EXS[e][rows, cols] = dot_t(BALL[e][rows, pl.ds(4 * COLS, FF_HERE)], wf[e, cols, :]).astype(BF16)

        exchange(e, b, 0).start()
        if e == 1:
            transpose_into(e, 1, HID[e], b)

    def first_back(e, b):
        exchange(e, b, 0).wait()

        @pl.loop(0, BLK[e] // CH, unroll=NORM_UNROLL[e])
        def _(c):
            rows = rows_at(b * BLK[e] + c * CH, CH, CH)
            d = N2[e][rows, :] + (EXS[e][rows, :].astype(F32) + EXR[e][0, rows, :].astype(F32))
            n = N1[e][rows, :]
            out = norm_back(d, n, I1[e][rows, :], par[e * 8 + 2 : e * 8 + 3, :])
            N1[e][rows, :] = out
            low = out.astype(BF16)
            DD[e][rows, :] = low
            acc_s[e * 6 + 0] += fold8(d * n)
            acc_s[e * 6 + 2] += fold8(d)
            acc_s[e * 6 + 4] += fold8(low.astype(F32))

        transpose_into(e, 2, DD[e], b)

    def attend_back(e, b):
        rows = block_rows(e, b)
        size = BLK[e]
        DC[e][rows, :] = dot_t(DD[e][rows, :], wo[e]).astype(BF16)

        @pl.loop(0, 3, unroll=PAIR_UNROLL[e])
        def _(pair):
            q2 = QKV[e][rows, rows_at(pair * 128, 128, 128)]
            k2 = QKV[e][rows, rows_at(COLS + pair * 128, 128, 128)]
            v2 = QKV[e][rows, rows_at(2 * COLS + pair * 128, 128, 128)]
            dc2 = DC[e][rows, rows_at(pair * 128, 128, 128)]
            dq = jnp.zeros((size, 128), F32)
            dk = jnp.zeros((size, 128), F32)
            dv = jnp.zeros((size, 128), F32)
            for hh in range(2):
                low = PR[e][b, pair * 2 + hh]
                p = low.astype(F32)
                dch = side(dc2, hh)
                dp = dot_t(dch, v2)
                ds = (p * (dp - jnp.sum(p * dp, axis=-1, keepdims=True))).astype(BF16)
                dv = dv + t_dot(low, dch)
                dq = dq + dot(ds, side(k2, hh))
                dk = dk + t_dot(ds, side(q2, hh))
            dq = (dq * HD**-0.5).astype(BF16)
            dv = dv.astype(BF16)
            cols = rows_at(pair * 128, 128, 128)
            BALL[e][rows, rows_at(9 * COLS + pair * 128, 128, 128)] = dq
            BALL[e][rows, rows_at(10 * COLS + pair * 128, 128, 128)] = dk.astype(BF16)
            BALL[e][rows, rows_at(11 * COLS + pair * 128, 128, 128)] = dv
            acc_b[e, :, cols] += fold8(dq.astype(F32))
            acc_b[e, :, rows_at(COLS + pair * 128, 128, 128)] += fold8(dv.astype(F32))

        if e == 1:
            transpose_into(e, 3, X[e], b)

    def token_back(e, b):
        rows = block_rows(e, b)

        @pl.loop(0, 3, unroll=DOWN_UNROLL[e])
        def _(n):
            cols = rows_at(n * 256, 256, 256)
            EXS[e][rows, cols] = dot_t(BALL[e][rows, pl.ds(9 * COLS, 3 * COLS)], win[e, cols, :]).astype(BF16)

        exchange(e, b, 1).start()

    def token_end(e, b):
        exchange(e, b, 1).wait()

        @pl.loop(0, BLK[e] // CH, unroll=NORM_UNROLL[e])
        def _(c):
            rows = rows_at(b * BLK[e] + c * CH, CH, CH)
            OB[e][rows, :] = (
                N1[e][rows, :] + (EXS[e][rows, :].astype(F32) + EXR[e][1, rows, :].astype(F32))
            ).astype(BF16)

    def job_of(j):
        return j // 6, j % 6

    def product(half, blk, sel):
        k = jnp.where(blk < 8, blk // 4, jnp.where(blk == 8, 2, 3))
        rows = atp[k, :, :, sel] if half == 0 else atp[k, :, sel]
        out = dot(rows.reshape(COLS, TOKS[1]), ballp[:, rows_at(blk * COLS, COLS, 128)])
        return out.reshape(ZN, 2, ROWS_OUT, COLS)

    def pair_product(half, pair):
        blk = pair * 2 + half
        k = blk // 4 if blk < 8 else 2 if blk == 8 else 3
        rows = atq[k, :, :, x] if half == 0 else atq[k, :, y]
        rows = jnp.concatenate([rows.reshape(COLS, TOKS[0]), fra[half, k].reshape(COLS, TOKS[0])], axis=1)
        cols = jnp.concatenate([ballq[:, blk * COLS : (blk + 1) * COLS], frb[half, pair]], axis=0)
        return dot(rows, cols).reshape(ZN, 2, ROWS_OUT, COLS)

    def p1(j, half):
        return pltpu.make_async_remote_copy(
            src_ref=p1s.at[j % DS, half],
            dst_ref=p1r.at[j % D1, half],
            send_sem=p1s_sem.at[j % DS, half],
            recv_sem=p1r_sem.at[j % D1, half],
            device_id=first_dev[half],
            device_id_type=MESH_ID,
        )

    def other(j, half, line_first):
        mine, to = p1r.at[j % D1, half], p2r.at[j % D2, half]
        return pltpu.make_async_remote_copy(
            src_ref=mine.at[z, 1 - other_at[half]] if line_first else mine.at[:, 1 - other_at[half]],
            dst_ref=to.at[0] if line_first else to,
            send_sem=p2s_sem.at[j % D2, half],
            recv_sem=p2r_sem.at[j % D2, half],
            device_id=other_dev[half],
            device_id_type=MESH_ID,
        )

    def block(j, half, d, right, line_first, at):
        slot = d if right else jnp.where(d == at, ZN, d)
        return zb.at[j % DZ, half, slot] if line_first else zb.at[j % DZ, half, slot, 0]

    def own_block(j, half, d, line_first):
        return p1r.at[j % D1, half, d] if line_first else p2r.at[j % D2, half, d]

    def along(j, half, d, right, relayed, line_first):
        send, recv = (zrs_sem, zrr_sem) if right else (zls_sem, zlr_sem)
        here = block(j, half, d, right, line_first, z)
        return pltpu.make_async_remote_copy(
            src_ref=here if relayed else own_block(j, half, d, line_first),
            dst_ref=block(j, half, d, right, line_first, z + 1 if right else z - 1),
            send_sem=send.at[j % DZ, half, d],
            recv_sem=recv.at[j % DZ, half, d],
            device_id=at_dp(me + 4 if right else me - 4),
            device_id_type=MESH_ID,
        )

    def total_of(a, b):
        return (a[...].astype(F32) + b[...].astype(F32)).astype(BF16)

    def step0(j):
        _, pair = job_of(j)
        for half in range(2):
            p1s[j % DS, half] = product(half, pair * 2 + half, 1 - first_at[half]).astype(BF16)
            p1(j, half).start()

    def step1(j, send):
        e_of, pair = job_of(j)

        @pl.when(e_of == 1)
        def _():
            own = [product(half, pair * 2 + half, first_at[half]) for half in range(2)]
            for half in range(2):
                p1(j, half).wait()
                p1r[j % D1, half] = (own[half] + p1r[j % D1, half].astype(F32)).astype(BF16)
                send(half)

        for p in range(6):

            @pl.when(jnp.logical_and(e_of == 0, pair == p))
            def _():
                for half in range(2):
                    if p in (0, 2):
                        left_factor(half, p // 2).wait()
                    elif p == 4:
                        left_factor(half, 2 + half).wait()
                    elif p == 5 and half == 0:
                        left_factor(0, 3).wait()
                    right_factor(half, p).wait()
                    p1r[j % D1, half] = pair_product(half, p).astype(BF16)
                    send(half)

    def turned(j, half):
        other(j, half, False).wait()
        mine = p2r.at[j % D2, half]
        mine[...] = total_of(mine, p1r.at[j % D1, half, :, other_at[half]])

    def ends(j, half, line_first):
        @pl.when(z == 0)
        def _():
            for d in (3, 2, 1):
                along(j, half, d, True, False, line_first).start()

        @pl.when(z == 3)
        def _():
            for d in (0, 1, 2):
                along(j, half, d, False, False, line_first).start()

    def relay(j, half, d, right, line_first):
        held = block(j, half, d, right, line_first, z)
        along(j, half, d, right, True, line_first).wait_recv()
        held[...] = total_of(held, own_block(j, half, d, line_first))
        along(j, half, d, right, True, line_first).start()

    def middle1(j, line_first):
        @pl.when(z == 1)
        def _():
            for half in range(2):
                for d in (3, 2):
                    relay(j, half, d, True, line_first)

        @pl.when(z == 2)
        def _():
            for half in range(2):
                for d in (0, 1):
                    relay(j, half, d, False, line_first)

    def middle2(j, line_first):
        @pl.when(z == 2)
        def _():
            for half in range(2):
                relay(j, half, 3, True, line_first)

        @pl.when(z == 1)
        def _():
            for half in range(2):
                relay(j, half, 0, False, line_first)

    def line_end(j, line_first):
        for half in range(2):
            mine = own_block(j, half, z, line_first)

            @pl.when(z > 0)
            def _():
                along(j, half, z, True, True, line_first).wait_recv()
                mine[...] = total_of(mine, block(j, half, z, True, line_first, z))

            @pl.when(z < 3)
            def _():
                along(j, half, z, False, True, line_first).wait_recv()
                mine[...] = total_of(mine, block(j, half, z, False, line_first, z))

            for d in range(4):

                @pl.when(d > z)
                def _():
                    along(j, half, d, True, True, line_first).wait_send()

                @pl.when(d < z)
                def _():
                    along(j, half, d, False, True, line_first).wait_send()

    def pass_on(j):
        for half in range(2):
            other(j, half, True).start()

    def passed(j):
        for half in range(2):
            other(j, half, True).wait()

    def result(slot, half, to):
        return pltpu.make_async_copy(fin.at[slot, half], to, fin_sem.at[slot, half])

    def output(j, line_first):
        e_of, pair = job_of(j)
        for half in range(2):

            @pl.when(j >= 2)
            def _():
                result(j % 2, half, g_out.at[0]).wait()

            if line_first:
                total = p1r[j % D1, half, z, other_at[half]].astype(F32) + p2r[j % D2, half, 0].astype(F32)
            else:
                total = p2r[j % D2, half, z].astype(F32)
            fin[j % 2, half] = total
            for e in range(2):
                for p in range(6):

                    @pl.when(jnp.logical_and(e_of == e, pair == p))
                    def _():
                        blk = p * 2 + half
                        if blk < 4:
                            to = g_fo.at[e, :, pl.ds(blk * COLS, COLS)]
                        elif blk < 8:
                            to = g_fi.at[e, :, pl.ds((blk - 4) * COLS, COLS)]
                        elif blk == 8:
                            to = g_out.at[e]
                        else:
                            to = g_in.at[e, blk - 9]
                        result(j % 2, half, to).start()

    small_to = (at_dp(me ^ 8), at_dp(me ^ 4), at_x, at_y)

    def small(k):
        return pltpu.make_async_remote_copy(
            src_ref=smb.at[k],
            dst_ref=smr.at[k],
            send_sem=sms_sem.at[k],
            recv_sem=smr_sem.at[k],
            device_id=small_to[k],
            device_id_type=MESH_ID,
        )

    def small_first():
        smb[0] = jnp.zeros_like(smb[0])
        for e in range(2):
            for i in range(6):
                smb[0, e * 9 + i : e * 9 + i + 1, :] = jnp.sum(acc_s[e * 6 + i], axis=0, keepdims=True)
            smb[0, e * 9 + 6 : e * 9 + 7, :] = jnp.sum(acc_b[e], axis=0, keepdims=True)
            for i in range(2):
                smb[0, e * 9 + 7 + i : e * 9 + 8 + i, :] = jnp.sum(
                    acc_f[e, :, i * D : (i + 1) * D], axis=0, keepdims=True
                )
        small(0).start()

    def small_next(k):
        small(k).wait()
        if k < 3:
            smb[k + 1] = smb[k] + smr[k]
            small(k + 1).start()
        else:
            total = smb[k] + smr[k]
            sm[0:SMALL, :] = jnp.zeros((SMALL, 128), F32)
            wide = pltpu.roll(total, lax.rem(D - me * ROWS_OUT, D), 1)
            sm[0:SMALL, 0:ROWS_OUT] = wide[:, 0:ROWS_OUT]
            heads_own = pltpu.roll(total, lax.rem(D - me * 24, D), 1)
            feed_own = pltpu.roll(total, lax.rem(D - (me % 8) * 96, D), 1)
            for e in range(2):
                at = e * 9 + 6
                for i in range(2):
                    sm[at + i : at + i + 1, 0:24] = heads_own[at : at + 1, i * COLS : i * COLS + 24]
                low, high = feed_own[at + 1 : at + 2, 0:96], feed_own[at + 2 : at + 3, 0:96]
                sm[at + 2 : at + 3, 0:96] = jnp.where(me < 8, low, high)
            pltpu.make_async_copy(sm, sm_out, out_sem.at[2]).start()

    def q_second_back():
        second_back(0, 0)
        left_factor(0, 0).start()
        left_factor(1, 0).start()

    def q_feed_back():
        feed_back(0, 0)
        for axis in range(2):
            for pair in (2, 3):
                right_factor(axis, pair).start()

    def q_first_back():
        first_back(0, 0)
        left_factor(0, 2).start()

    def q_attend_back():
        attend_back(0, 0)
        right_factor(1, 4).start()
        right_factor(0, 5).start()
        right_factor(1, 5).start()

    def q_token_end():
        token_end(0, 0)
        pltpu.make_async_copy(obq, gq_out, out_sem.at[0]).start()

    def p_token_end():
        blocks(1, lambda b: token_end(1, b))
        pltpu.make_async_copy(obp, gp_out, out_sem.at[1]).start()

    def p_mid(b):
        first_norm(1, b)
        feed(1, b)

    def p_second():
        blocks(1, lambda b: second_norm(1, b))
        out_p.start()

    def passages(piece):
        return lambda: blocks(1, lambda b: piece(1, b))

    work = {
        0: [q_feed_back, lambda: attend(1, 1)],
        2: [q_first_back, lambda: p_mid(0)],
        4: [q_attend_back, lambda: p_mid(1)],
        5: [lambda: token_back(0, 0), p_second, out_q.wait],
        6: [q_token_end, lambda: second_back(1, 1)],
        7: [lambda: feed_back(1, 1)],
        8: [lambda: first_back(1, 1)],
        9: [lambda: attend_back(1, 1)],
        10: [lambda: token_back(1, 1), small_first],
        12: [lambda: small_next(0)],
        14: [lambda: small_next(1)],
        15: [out_p.wait, p_token_end, lambda: small_next(2)],
        16: [lambda: small_next(3)],
    }
    between = {
        5: [lambda: second_back(1, 0)],
        6: [lambda: feed_back(1, 0)],
        7: [lambda: first_back(1, 0)],
        8: [lambda: attend_back(1, 0)],
        9: [lambda: token_back(1, 0)],
    }

    def is_line_first(j):
        found = j == LINE_FIRST[0]
        for k in LINE_FIRST[1:]:
            found = jnp.logical_or(found, j == k)
        return found

    def steps(late, j):
        line_first = is_line_first(j)
        if late == 1:

            def send(half):
                @pl.when(line_first)
                def _():
                    ends(j, half, True)

                @pl.when(jnp.logical_not(line_first))
                def _():
                    other(j, half, False).start()

            step1(j, send)
            return

        @pl.when(line_first)
        def _():
            if late == 2:
                middle1(j, True)
            elif late == 3:
                middle2(j, True)
            elif late == 4:
                line_end(j, True)
                pass_on(j)
            else:
                passed(j)
                output(j, True)

        @pl.when(jnp.logical_not(line_first))
        def _():
            if late == 2:
                for half in range(2):
                    turned(j, half)
                    ends(j, half, False)
            elif late == 3:
                middle1(j, False)
            elif late == 4:
                middle2(j, False)
            else:
                line_end(j, False)
                output(j, False)

    q_second_back()

    @pl.loop(0, JOBS + 5)
    def _(tick):
        for at, things in work.items():

            @pl.when(tick == at)
            def _():
                for thing in things:
                    thing()

        @pl.when(jnp.logical_and(tick >= 6, tick < JOBS))
        def _():
            step0(tick)

        for late in (1, 2, 3, 4, 5):

            @pl.when(jnp.logical_and(tick >= late, tick < JOBS + late))
            def _():
                steps(late, tick - late)

            if late == 2:
                for at, things in between.items():

                    @pl.when(tick == at)
                    def _():
                        for thing in things:
                            thing()

    pltpu.make_async_copy(obq, gq_out, out_sem.at[0]).wait()
    pltpu.make_async_copy(obp, gp_out, out_sem.at[1]).wait()
    pltpu.make_async_copy(sm, sm_out, out_sem.at[2]).wait()
    for slot in range(2):
        for half in range(2):
            result(slot, half, g_out.at[0]).wait()


def finish_kernel(*refs):
    oq, op, gq, gp, g_in, g_out, g_fi, g_fo, sums_in = refs[:9]
    large, (loss_to, in_bias, fi_bias, bo, gain, shift) = refs[9:17], refs[17:23]
    held, sums, in_sems, out_sems = refs[23:31], refs[31], refs[32], refs[33]
    sources = (oq, op, gq, gp, g_in, g_out, g_fi, g_fo)
    loads = [pltpu.make_async_copy(sources[i], held[i], in_sems.at[i]) for i in range(8)]
    stores = [pltpu.make_async_copy(held[i], large[i], out_sems.at[i]) for i in range(8)]
    little = pltpu.make_async_copy(sums_in, sums, in_sems.at[8])
    little.start()
    for load in loads:
        load.start()
    little.wait()
    loss_to[...] = sums[SMALL : SMALL + 1, 0:1]
    for e in range(2):
        at = e * 9
        gain[e] = sums[at : at + 2, 0:ROWS_OUT]
        shift[e] = sums[at + 2 : at + 4, 0:ROWS_OUT]
        bo[e] = sums[at + 4 : at + 6, 0:ROWS_OUT]
        in_bias[e] = sums[at + 6 : at + 8, 0:24]
        fi_bias[e : e + 1] = sums[at + 8 : at + 9, 0:96]
    for load, store in zip(loads, stores):
        load.wait()
        store.start()
    for store in stores:
        store.wait()


FF_HERE = 1536


def fused(
    question_tokens, passage_tokens, question_cotangent, passage_cotangent,
    question_lengths, passage_lengths, dataset_ids, positives,
    attn_in, attn_in_bias, attn_out, ffn_in, ffn_in_bias, ffn_out, out_biases, norm_gains, norm_shifts,
):
    any_spec = pl.BlockSpec(memory_space=pl.ANY)
    vmem = pl.BlockSpec(memory_space=pltpu.VMEM)

    def both(shape, dtype):
        return [pltpu.VMEM(shape(m), dtype) for m in TOKS]

    shape = jax.ShapeDtypeStruct
    dma = pltpu.SemaphoreType.DMA
    outs = pl.pallas_call(
        partial(fused_kernel, last=0),
        name="fused",
        in_specs=[any_spec] * 17,
        out_specs=[any_spec] * 9,
        out_shape=[
            shape((128, D), BF16),
            shape((512, D), BF16),
            shape((128, D), BF16),
            shape((512, D), BF16),
            shape((2, 3, ROWS_OUT, COLS), F32),
            shape((2, ROWS_OUT, COLS), F32),
            shape((2, ROWS_OUT, FF_HERE), F32),
            shape((2, ROWS_OUT, FF_HERE), F32),
            shape((SMALL + 8, 128), F32),
        ],
        scratch_shapes=[
            pltpu.VMEM((2, D, 3 * COLS), BF16),
            pltpu.VMEM((2, COLS, D), BF16),
            pltpu.VMEM((2, D, FF_HERE), BF16),
            pltpu.VMEM((2, FF_HERE, D), BF16),
            *both(lambda m: (m, D), BF16),
            *both(lambda m: (m, D), BF16),
            *both(lambda m: (m, 3 * COLS), BF16),
            pltpu.VMEM((1, 6, 128, 128), BF16),
            pltpu.VMEM((2, 6, 256, 256), BF16),
            *both(lambda m: (m, D), BF16),
            *both(lambda m: (m, D), F32),
            *both(lambda m: (m, D), F32),
            *both(lambda m: (m, 1), F32),
            *both(lambda m: (m, 1), F32),
            *both(lambda m: (m, FF_HERE), BF16),
            *both(lambda m: (m, D), BF16),
            *both(lambda m: (m, D), BF16),
            *both(lambda m: (m, COLS), BF16),
            *both(lambda m: (m, 12 * COLS), BF16),
            *both(lambda m: (4, ZN, 2, 2, ROWS_OUT, m), BF16),
            *both(lambda m: (m, D), BF16),
            *both(lambda m: (2, m, D), BF16),
            pltpu.VMEM((16, D), F32),
            pltpu.VMEM((8, COLS), F32),
            pltpu.VMEM((8, FF_HERE), F32),
            pltpu.VMEM((64, 32), F32),
            pltpu.VMEM((16, 16, 256), BF16),
            pltpu.VMEM((2, 256, 128), F32),
            pltpu.VMEM((64, D), F32),
            pltpu.VMEM((12, 8, D), F32),
            pltpu.VMEM((2, 8, 2 * COLS), F32),
            pltpu.VMEM((2, 8, FF_HERE), F32),
            pltpu.VMEM((4, SMALL, D), F32),
            pltpu.VMEM((4, SMALL, D), F32),
            pltpu.VMEM((DS, 2, ZN, 2, ROWS_OUT, COLS), BF16),
            pltpu.VMEM((D1, 2, ZN, 2, ROWS_OUT, COLS), BF16),
            pltpu.VMEM((D2, 2, ZN, ROWS_OUT, COLS), BF16),
            pltpu.VMEM((DZ, 2, ZN + 1, 2, ROWS_OUT, COLS), BF16),
            pltpu.VMEM((2, 2, ROWS_OUT, COLS), F32),
            pltpu.VMEM((2, 4, ZN, 2, ROWS_OUT, TOKS[0]), BF16),
            pltpu.VMEM((2, 6, TOKS[0], COLS), BF16),
            pltpu.VMEM((2, 16, D), BF16),
            pltpu.VMEM((2, 16, D), BF16),
            pltpu.VMEM((16, D), BF16),
            *[pltpu.SMEM((n,), jnp.int32) for n in (2, 2, 32, 32)],
            pltpu.VMEM((2, 2, COLS), BF16),
            pltpu.VMEM((2, FF_HERE), BF16),
            *[pltpu.VMEM((2, 2, D), BF16) for _ in range(3)],
            pltpu.VMEM((SMALL + 8, 128), F32),
            dma((2, 2)),
            dma((9,)),
            dma((16,)),
            dma((3,)),
            dma((3,)),
            dma((2, 3)),
            dma((16,)),
            dma((16,)),
            dma((4,)),
            dma((4,)),
            dma((DS, 2)),
            dma((D1, 2)),
            dma((D2, 2)),
            dma((D2, 2)),
            dma((DZ, 2, ZN)),
            dma((DZ, 2, ZN)),
            dma((DZ, 2, ZN)),
            dma((DZ, 2, ZN)),
            dma((2, 4)),
            dma((2, 4)),
            dma((2, 6)),
            dma((2, 6)),
            dma((2,)),
            dma((2,)),
        ],
        compiler_params=pltpu.CompilerParams(
            collective_id=0, has_side_effects=True, vmem_limit_bytes=VMEM_BYTES
        ),
    )(
        question_tokens.reshape(128, D),
        passage_tokens.reshape(512, D),
        question_cotangent.reshape(128, D),
        passage_cotangent.reshape(512, D),
        question_lengths, passage_lengths, dataset_ids, positives,
        attn_in.transpose(0, 2, 1, 3), attn_in_bias, attn_out, ffn_in, ffn_in_bias, ffn_out,
        out_biases, norm_gains, norm_shifts,
    )
    oq, op, gq, gp, g_in, g_out, g_fi, g_fo, sums = outs
    large = (oq, op, gq, gp, g_in, g_out, g_fi, g_fo)
    small = [(1, 1), (2, 2, 24), (2, 96), (2, 2, ROWS_OUT), (2, 2, ROWS_OUT), (2, 2, ROWS_OUT)]
    oq, op, gq, gp, g_in, g_out, g_fi, g_fo, loss, in_bias, fi_bias, bo, gain, shift = pl.pallas_call(
        finish_kernel,
        name="finish",
        in_specs=[any_spec] * 9,
        out_specs=[any_spec] * 8 + [vmem] * 6,
        out_shape=[shape(a.shape, a.dtype) for a in large] + [shape(dims, F32) for dims in small],
        scratch_shapes=[*[pltpu.VMEM(a.shape, a.dtype) for a in (*large, sums)], dma((9,)), dma((8,))],
        compiler_params=pltpu.CompilerParams(vmem_limit_bytes=VMEM_BYTES),
    )(*large, sums)
    return (
        oq.reshape(2, 64, D),
        op.reshape(2, 256, D),
        loss.reshape(()),
        gq.reshape(2, 64, D),
        gp.reshape(2, 256, D),
        g_in.transpose(0, 2, 1, 3),
        in_bias,
        g_out.transpose(0, 2, 1),
        g_fi,
        fi_bias,
        g_fo.transpose(0, 2, 1),
        bo,
        gain,
        shift,
    )


VMEM_BYTES = 62 * 1024 * 1024


def solution(mesh):
    in_specs = (
        P("dp", None, None),
        P("dp", None, None),
        P("dp", None, None),
        P("dp", None, None),
        P("dp"),
        P("dp"),
        P(),
        P(),
        P(None, None, None, "tensor"),
        P(None, None, "tensor"),
        P(None, "tensor", None),
        P(None, None, "tensor"),
        P(None, "tensor"),
        P(None, "tensor", None),
        P(),
        P(),
        P(),
    )
    out_specs = (
        P("dp", None, None),
        P("dp", None, None),
        P(),
        P("dp", None, None),
        P("dp", None, None),
        P(None, "dp", None, "tensor"),
        P(None, None, ("tensor", "dp")),
        P(None, "tensor", "dp"),
        P(None, "dp", "tensor"),
        P(None, ("tensor", "dp")),
        P(None, "tensor", "dp"),
        P(None, None, "dp"),
        P(None, None, "dp"),
        P(None, None, "dp"),
    )
    step = fused if mesh.shape["dp"] == 4 * ZN and mesh.shape["tensor"] == 2 else per_device
    return jax.shard_map(
        step, mesh=mesh, in_specs=in_specs, out_specs=out_specs, check_vma=False
    )
```

```python
from functools import partial

import jax
import jax.numpy as jnp
from jax import lax
from jax.experimental import pallas as pl
from jax.experimental.pallas import tpu as pltpu
from jax.sharding import PartitionSpec as P

D = 768
HD = 64


EPSILON = 1e-06
NEGATIVE = -1e30
HIGHEST = lax.Precision.HIGHEST
score_gain = 3.0


def norm_forward(summed, scale_row, shift_row):
    row_mean = jnp.mean(summed, axis=-1, keepdims=True)
    centred = summed - row_mean
    inv_std = lax.rsqrt(jnp.mean(centred * centred, axis=-1, keepdims=True) + EPSILON)
    normed = centred * inv_std
    return (normed * scale_row + shift_row, normed, inv_std)


def norm_backward(incoming, normed, inv_std, scale_row):
    scaled = incoming * scale_row
    outgoing = inv_std * (
        scaled
        - jnp.mean(scaled, axis=-1, keepdims=True)
        - normed * jnp.mean(scaled * normed, axis=-1, keepdims=True)
    )
    return (outgoing, jnp.sum(incoming * normed, axis=(0, 1)), jnp.sum(incoming, axis=(0, 1)))


def key_visible(lengths, length):
    positions = jnp.arange(length, dtype=jnp.int32)
    return (positions[None, :] < lengths[:, None])[:, None, None, :]


def head_scores(queries, key_rows, visible):
    raw_scores = jnp.einsum(
        "bqhe,bkhe->bhqk", queries, key_rows, preferred_element_type=jnp.float32
    ) * HD ** (-0.5)
    return jnp.where(visible, raw_scores, NEGATIVE)


def split_heads(matrix):
    return matrix.reshape(matrix.shape[0], matrix.shape[1], matrix.shape[2] // HD, HD)


def join_heads(per_head):
    return per_head.reshape(
        per_head.shape[0], per_head.shape[1], per_head.shape[2] * per_head.shape[3]
    )


def encoder_forward(tokens, lengths, params):
    (
        attn_in,
        attn_in_bias,
        attn_out,
        ffn_in,
        ffn_in_bias,
        ffn_out,
        out_biases,
        norm_gains,
        norm_shifts,
    ) = params
    projected = jnp.einsum("bld,dce->blce", tokens, attn_in, preferred_element_type=jnp.float32)
    in_bias = attn_in_bias.astype(jnp.float32)
    queries = split_heads((projected[:, :, 0] + in_bias[0]).astype(jnp.bfloat16))
    key_rows = split_heads(projected[:, :, 1].astype(jnp.bfloat16))
    values = split_heads((projected[:, :, 2] + in_bias[1]).astype(jnp.bfloat16))
    visible = key_visible(lengths, tokens.shape[1])
    scores = head_scores(queries, key_rows, visible)
    row_top = jnp.max(scores, axis=-1, keepdims=True)
    log_total = row_top + jnp.log(jnp.sum(jnp.exp(scores - row_top), axis=-1, keepdims=True))
    attn_probs = jnp.exp(scores - log_total).astype(jnp.bfloat16)
    context = join_heads(
        jnp.einsum(
            "bhqk,bkhe->bqhe", attn_probs, values, preferred_element_type=jnp.float32
        ).astype(jnp.bfloat16)
    )
    attn_part = jnp.einsum("ble,ed->bld", context, attn_out, preferred_element_type=jnp.float32)
    attn_sum = lax.psum(attn_part.astype(jnp.bfloat16), "tensor").astype(jnp.float32)
    bias_rows = out_biases.astype(jnp.float32)
    gain_rows = norm_gains.astype(jnp.float32)
    shift_rows = norm_shifts.astype(jnp.float32)
    hidden_float, normed_first, inv_first = norm_forward(
        tokens.astype(jnp.float32) + attn_sum + bias_rows[0], gain_rows[0], shift_rows[0]
    )
    hidden = hidden_float.astype(jnp.bfloat16)
    up_pre = jnp.einsum(
        "bld,df->blf", hidden, ffn_in, preferred_element_type=jnp.float32
    ) + ffn_in_bias.astype(jnp.float32)
    activated = jax.nn.gelu(up_pre, approximate=False).astype(jnp.bfloat16)
    down_part = jnp.einsum("blf,fd->bld", activated, ffn_out, preferred_element_type=jnp.float32)
    down_sum = lax.psum(down_part.astype(jnp.bfloat16), "tensor").astype(jnp.float32)
    outputs, normed_second, inv_second = norm_forward(
        hidden.astype(jnp.float32) + down_sum + bias_rows[1], gain_rows[1], shift_rows[1]
    )
    saved = (
        tokens,
        queries,
        key_rows,
        values,
        log_total,
        context,
        normed_first,
        inv_first,
        hidden,
        up_pre,
        activated,
        normed_second,
        inv_second,
    )
    return (outputs, saved)


def encoder_backward(incoming, saved, lengths, params):
    (
        attn_in,
        attn_in_bias,
        attn_out,
        ffn_in,
        ffn_in_bias,
        ffn_out,
        out_biases,
        norm_gains,
        norm_shifts,
    ) = params
    (
        tokens,
        queries,
        key_rows,
        values,
        log_total,
        context,
        normed_first,
        inv_first,
        hidden,
        up_pre,
        activated,
        normed_second,
        inv_second,
    ) = saved
    groups_here, length, model_width = tokens.shape
    gain_rows = norm_gains.astype(jnp.float32)
    d_second, gain_second, shift_second = norm_backward(
        incoming, normed_second, inv_second, gain_rows[1]
    )
    d_down = d_second.astype(jnp.bfloat16)
    grad_ffn_out = jnp.einsum("blf,bld->fd", activated, d_down, preferred_element_type=jnp.float32)
    d_activated = jnp.einsum("bld,fd->blf", d_down, ffn_out, preferred_element_type=jnp.float32)
    gelu_pull = jax.vjp(partial(jax.nn.gelu, approximate=False), up_pre)[1]
    d_up = gelu_pull(d_activated)[0].astype(jnp.bfloat16)
    grad_ffn_in = jnp.einsum("bld,blf->df", hidden, d_up, preferred_element_type=jnp.float32)
    hidden_part = jnp.einsum("blf,df->bld", d_up, ffn_in, preferred_element_type=jnp.float32)
    d_hidden = d_second + lax.psum(hidden_part.astype(jnp.bfloat16), "tensor").astype(jnp.float32)
    d_first, gain_first, shift_first = norm_backward(
        d_hidden, normed_first, inv_first, gain_rows[0]
    )
    d_attn = d_first.astype(jnp.bfloat16)
    grad_attn_out = jnp.einsum("ble,bld->ed", context, d_attn, preferred_element_type=jnp.float32)
    d_context = split_heads(
        jnp.einsum("bld,ed->ble", d_attn, attn_out, preferred_element_type=jnp.float32).astype(
            jnp.bfloat16
        )
    )
    visible = key_visible(lengths, length)
    scores = head_scores(queries, key_rows, visible)
    probs_float = jnp.exp(scores - log_total)
    d_probs = jnp.einsum("bqhe,bkhe->bhqk", d_context, values, preferred_element_type=jnp.float32)
    d_values = jnp.einsum(
        "bhqk,bqhe->bkhe",
        probs_float.astype(jnp.bfloat16),
        d_context,
        preferred_element_type=jnp.float32,
    ).astype(jnp.bfloat16)
    d_scores = (
        probs_float * (d_probs - jnp.sum(probs_float * d_probs, axis=-1, keepdims=True))
    ).astype(jnp.bfloat16)
    d_queries = (
        jnp.einsum("bhqk,bkhe->bqhe", d_scores, key_rows, preferred_element_type=jnp.float32)
        * HD ** (-0.5)
    ).astype(jnp.bfloat16)
    d_keys = (
        jnp.einsum("bhqk,bqhe->bkhe", d_scores, queries, preferred_element_type=jnp.float32)
        * HD ** (-0.5)
    ).astype(jnp.bfloat16)
    query_grad = join_heads(d_queries)
    value_grad = join_heads(d_values)
    d_projected = jnp.stack([query_grad, join_heads(d_keys), value_grad], axis=2)
    grad_attn_in = jnp.einsum(
        "bld,blce->dce", tokens, d_projected, preferred_element_type=jnp.float32
    )
    token_part = jnp.einsum(
        "blce,dce->bld", d_projected, attn_in, preferred_element_type=jnp.float32
    )
    d_tokens = (
        d_first + lax.psum(token_part.astype(jnp.bfloat16), "tensor").astype(jnp.float32)
    ).astype(jnp.bfloat16)
    grad_in_bias = jnp.stack(
        [
            jnp.sum(query_grad.astype(jnp.float32), axis=(0, 1)),
            jnp.sum(value_grad.astype(jnp.float32), axis=(0, 1)),
        ]
    )
    grad_ffn_bias = jnp.sum(d_up.astype(jnp.float32), axis=(0, 1))
    grad_out_biases = jnp.stack(
        [
            jnp.sum(d_attn.astype(jnp.float32), axis=(0, 1)),
            jnp.sum(d_down.astype(jnp.float32), axis=(0, 1)),
        ]
    )
    grad_gains = jnp.stack([gain_first, gain_second])
    grad_shifts = jnp.stack([shift_first, shift_second])
    return (
        d_tokens,
        (
            grad_attn_in,
            grad_in_bias,
            grad_attn_out,
            grad_ffn_in,
            grad_ffn_bias,
            grad_ffn_out,
            grad_out_biases,
            grad_gains,
            grad_shifts,
        ),
    )


def contrastive(question_rows, passage_rows, own_positive, dataset_ids):
    class_scores = jnp.einsum(
        "gd,jd->gj", question_rows, passage_rows, preferred_element_type=jnp.float32
    ) * (score_gain * D ** (-0.5))
    columns = jnp.arange(passage_rows.shape[0], dtype=jnp.int32)
    chosen = own_positive[:, None] == columns[None, :]
    own_set = jnp.sum(jnp.where(chosen, dataset_ids[None, :], 0), axis=1)
    logits = jnp.where(dataset_ids[None, :] == own_set[:, None], class_scores, NEGATIVE)
    row_top = jnp.max(logits, axis=1, keepdims=True)
    log_total = row_top + jnp.log(jnp.sum(jnp.exp(logits - row_top), axis=1, keepdims=True))
    target = jnp.sum(jnp.where(chosen, class_scores, 0.0), axis=1)
    d_class = (jnp.exp(logits - log_total) - chosen.astype(jnp.float32)) * (
        score_gain * D ** (-0.5)
    )
    return (log_total[:, 0] - target, d_class)


def per_device(
    question_tokens,
    passage_tokens,
    question_cotangent,
    passage_cotangent,
    question_lengths,
    passage_lengths,
    dataset_ids,
    positives,
    attn_in,
    attn_in_bias,
    attn_out,
    ffn_in,
    ffn_in_bias,
    ffn_out,
    out_biases,
    norm_gains,
    norm_shifts,
):

    def encoder_params(encoder):
        return (
            attn_in[encoder],
            attn_in_bias[encoder],
            attn_out[encoder],
            ffn_in[encoder],
            ffn_in_bias[encoder],
            ffn_out[encoder],
            out_biases[encoder],
            norm_gains[encoder],
            norm_shifts[encoder],
        )

    question_params = encoder_params(0)
    passage_params = encoder_params(1)
    question_float, question_saved = encoder_forward(
        question_tokens, question_lengths, question_params
    )
    passage_float, passage_saved = encoder_forward(passage_tokens, passage_lengths, passage_params)
    question_heads = question_float[:, 0].astype(jnp.bfloat16)
    passage_heads = passage_float[:, 0].astype(jnp.bfloat16)
    local_groups = question_heads.shape[0]
    own_start = lax.axis_index("dp") * local_groups
    all_passages = lax.all_gather(passage_heads, "dp", axis=0, tiled=True)
    own_positive = lax.dynamic_slice_in_dim(positives, own_start, local_groups)
    cross, d_class = contrastive(question_heads, all_passages, own_positive, dataset_ids)
    total = lax.psum(jnp.sum(cross), "dp")
    contrastive_loss = total / all_passages.shape[0]
    d_question_heads = jnp.einsum(
        "gj,jd->gd", d_class, all_passages.astype(jnp.float32), precision=HIGHEST
    )
    question_heads_float = question_heads.astype(jnp.float32)
    d_passage_heads = lax.psum_scatter(
        jnp.einsum("gj,gd->jd", d_class, question_heads_float, precision=HIGHEST),
        "dp",
        scatter_dimension=0,
        tiled=True,
    )
    d_question_out = question_cotangent.astype(jnp.float32).at[:, 0].add(d_question_heads)
    d_passage_out = passage_cotangent.astype(jnp.float32).at[:, 0].add(d_passage_heads)
    passage_grad, passage_weights = encoder_backward(
        d_passage_out, passage_saved, passage_lengths, passage_params
    )
    question_grad, question_weights = encoder_backward(
        d_question_out, question_saved, question_lengths, question_params
    )
    joined = (
        lax.psum_scatter(question_weights[0], "dp", scatter_dimension=0, tiled=True),
        lax.psum_scatter(question_weights[1], "dp", scatter_dimension=1, tiled=True),
        lax.psum_scatter(question_weights[2], "dp", scatter_dimension=1, tiled=True),
        lax.psum_scatter(question_weights[3], "dp", scatter_dimension=0, tiled=True),
        lax.psum_scatter(question_weights[4], "dp", scatter_dimension=0, tiled=True),
        lax.psum_scatter(question_weights[5], "dp", scatter_dimension=1, tiled=True),
        lax.psum_scatter(question_weights[6], "dp", scatter_dimension=1, tiled=True),
        lax.psum_scatter(question_weights[7], "dp", scatter_dimension=1, tiled=True),
        lax.psum_scatter(question_weights[8], "dp", scatter_dimension=1, tiled=True),
        lax.psum_scatter(passage_weights[0], "dp", scatter_dimension=0, tiled=True),
        lax.psum_scatter(passage_weights[1], "dp", scatter_dimension=1, tiled=True),
        lax.psum_scatter(passage_weights[2], "dp", scatter_dimension=1, tiled=True),
        lax.psum_scatter(passage_weights[3], "dp", scatter_dimension=0, tiled=True),
        lax.psum_scatter(passage_weights[4], "dp", scatter_dimension=0, tiled=True),
        lax.psum_scatter(passage_weights[5], "dp", scatter_dimension=1, tiled=True),
        lax.psum_scatter(passage_weights[6], "dp", scatter_dimension=1, tiled=True),
        lax.psum_scatter(passage_weights[7], "dp", scatter_dimension=1, tiled=True),
        lax.psum_scatter(passage_weights[8], "dp", scatter_dimension=1, tiled=True),
    )
    question_parts = joined[:9]
    passage_parts = joined[9:]
    stacked = [
        jnp.stack([question_piece, passage_piece])
        for question_piece, passage_piece in zip(question_parts, passage_parts)
    ]
    return (
        question_float.astype(jnp.bfloat16),
        passage_float.astype(jnp.bfloat16),
        contrastive_loss,
        question_grad,
        passage_grad,
        stacked[0],
        stacked[1],
        stacked[2],
        stacked[3],
        stacked[4],
        stacked[5],
        stacked[6],
        stacked[7],
        stacked[8],
    )


MESH_ID = pl.DeviceIdType.MESH
F32 = jnp.float32
BF16 = jnp.bfloat16
ZN = 4
ROWS_OUT = 48
JOBS = 12
COLS = 384
D1, D2, DZ, DS = 8, 8, 8, 2
LINE_FIRST = (0, 5, 8, 9)
TOKS = (128, 512)
BLK = (128, 256)
SMALL = 24
CHUNK = 64
NORM_UNROLL = (2, 4)
UP_UNROLL = (6, 6)
DOWN_UNROLL = (3, 3)
PAIR_UNROLL = (3, 3)


def dot(a, b):
    return jnp.dot(a, b, preferred_element_type=F32)


def dot_t(a, b):
    return lax.dot_general(a, b, (((1,), (1,)), ((), ())), preferred_element_type=F32)


def t_dot(a, b):
    return lax.dot_general(a, b, (((0,), (0,)), ((), ())), preferred_element_type=F32)


def gelu_and_slope(u):
    size = jnp.abs(u)
    bell = jnp.exp(-0.5 * u * u)
    t = 1.0 / (1.0 + (0.3275911 * 0.7071067811865476) * size)
    poly = t * (
        0.127414796
        + t * (-0.142248368 + t * (0.7107068705 + t * (-0.7265760135 + t * 0.5307027145)))
    )
    tail = poly * bell
    phi = jnp.where(u >= 0.0, 1.0 - tail, tail)
    return u * phi, phi + u * bell * 0.3989422804014327


def row_mean(v):
    return jnp.sum(v, axis=-1, keepdims=True) * (1.0 / D)


def fold8(v):
    return jnp.sum(v.reshape(v.shape[0] // 8, 8, v.shape[1]), axis=0)


def rows_at(start, size, step=16):
    return pl.ds(pl.multiple_of(start, step), size)


def fused_kernel(
    xq_in, xp_in, cq_in, cp_in, qlen_in, plen_in, dsid_in, posi_in,
    win_in, bin_from, wo_in, wf_in, bfi_from, wd_in, bo_from, gain_from, shift_from,
    oq_out, op_out, gq_out, gp_out, g_in, g_out, g_fi, g_fo, sm_out,
    win, wo, wf, wd, xq, xp, cq, cp, qkvq, qkvp, prq, prp, hq, hp, n1q, n1p, n2q, n2p,
    i1q, i1p, i2q, i2p, sq, sp, obq, obp, ddq, ddp, dcq, dcp, ballq, ballp, atq, atp,
    exsq, exsp, exrq, exrp, par, pin, pfi, masks, hg, hf, dh, acc_s, acc_b, acc_f, smb, smr,
    p1s, p1r, p2r, zb, fin, fra, frb, xms, xmr, hm,
    qlen, plen, dsid, posi, bin_in, bfi_in, bo_in, gain_in, shift_in, sm,
    fin_sem, little_sem, in_sem, out_sem, exs_sem, exr_sem, hgs_sem, hgr_sem, sms_sem, smr_sem,
    p1s_sem, p1r_sem, p2s_sem, p2r_sem, zrs_sem, zrr_sem, zls_sem, zlr_sem,
    fas_sem, far_sem, fbs_sem, fbr_sem, xms_sem, xmr_sem,
    *, last,
):
    me = lax.axis_index("dp")
    core = lax.axis_index("tensor")
    z, y, x = me // 4, (me // 2) % 2, me % 2
    partner = {"dp": me, "tensor": 1 - core}
    at_x = {"dp": me + 1 - 2 * x, "tensor": core}
    at_y = {"dp": me + 2 - 4 * y, "tensor": core}

    def at_dp(index):
        return {"dp": index, "tensor": core}

    X, COT, QKV, PR, HID = (xq, xp), (cq, cp), (qkvq, qkvp), (prq, prp), (hq, hp)
    N1, N2, I1, I2, SLOPE = (n1q, n1p), (n2q, n2p), (i1q, i1p), (i2q, i2p), (sq, sp)
    OB, DD, DC, BALL, AT = (obq, obp), (ddq, ddp), (dcq, dcp), (ballq, ballp), (atq, atp)
    EXS, EXR = (exsq, exsp), (exrq, exrp)

    little = [
        (qlen_in, qlen), (plen_in, plen), (bin_from, bin_in), (bfi_from, bfi_in), (bo_from, bo_in),
        (gain_from, gain_in), (shift_from, shift_in), (dsid_in, dsid), (posi_in, posi),
    ]
    little = [pltpu.make_async_copy(s, d, little_sem.at[i]) for i, (s, d) in enumerate(little)]
    loads = [
        (xq_in, xq),
        *[(win_in.at[0, j], win.at[0, :, pl.ds(j * COLS, COLS)]) for j in range(3)],
        (xp_in, xp),
        *[(win_in.at[1, j], win.at[1, :, pl.ds(j * COLS, COLS)]) for j in range(3)],
        (wo_in.at[0], wo.at[0]),
        (wo_in.at[1], wo.at[1]),
        (wf_in.at[0], wf.at[0]),
        (wf_in.at[1], wf.at[1]),
        (wd_in.at[0], wd.at[0]),
        (wd_in.at[1], wd.at[1]),
        (cq_in, cq),
        (cp_in, cp),
    ]
    loads = [pltpu.make_async_copy(s, d, in_sem.at[i]) for i, (s, d) in enumerate(loads)]
    for copy in loads[:4]:
        copy.start()
    for copy in little:
        copy.start()
    ready = set()

    def need(*which):
        for i in which:
            if i not in ready:
                loads[i].wait()
                ready.add(i)

    barrier = pltpu.get_barrier_semaphore()
    pl.semaphore_signal(barrier, inc=1, device_id=partner, device_id_type=MESH_ID)
    for k in range(1, 16):
        pl.semaphore_signal(barrier, inc=1, device_id=at_dp(me ^ k), device_id_type=MESH_ID)

    def load(*which):
        for i in which:
            loads[i].start()

    for copy in little:
        copy.wait()
    for e in range(2):
        for i in range(2):
            par[e * 8 + i : e * 8 + i + 1, :] = bo_in[e].astype(F32)[i : i + 1]
            par[e * 8 + 2 + i : e * 8 + 3 + i, :] = gain_in[e].astype(F32)[i : i + 1]
            par[e * 8 + 4 + i : e * 8 + 5 + i, :] = shift_in[e].astype(F32)[i : i + 1]
            pin[e * 2 + i : e * 2 + i + 1, :] = bin_in[e].astype(F32)[i : i + 1]
        pfi[e : e + 1, :] = bfi_in[...].astype(F32)[e : e + 1]
    acc_s[...] = jnp.zeros_like(acc_s)
    acc_b[...] = jnp.zeros_like(acc_b)
    acc_f[...] = jnp.zeros_like(acc_f)

    r32 = lax.broadcasted_iota(jnp.int32, (32, 32), 0)
    c32 = lax.broadcasted_iota(jnp.int32, (32, 32), 1)
    own_pos = jnp.zeros((32, 32), F32)
    set_col = jnp.zeros((32, 32), F32)
    for g in range(32):
        at = (g % 2) * 16 + g // 2
        own_pos = jnp.where(r32 == at, posi[g].astype(F32), own_pos)
        set_col = jnp.where(c32 == at, dsid[g].astype(F32), set_col)
    col_group = ((c32 % 16) * 2 + c32 // 16).astype(F32)
    chosen = jnp.where(own_pos == col_group, 1.0, 0.0)
    own_set = jnp.sum(chosen * set_col, axis=1, keepdims=True)
    masks[0:32, :] = chosen
    masks[32:64, :] = jnp.where(set_col == own_set, 1.0, 0.0)

    lane_lo = lax.broadcasted_iota(jnp.int32, (1, 128), 1) < HD

    def side(v, hh):
        return jnp.where(lane_lo if hh == 0 else jnp.logical_not(lane_lo), v, jnp.zeros_like(v))

    def exchange(e, b, parity):
        slot = 0 if e == 0 else 1 + b
        rows = rows_at(b * BLK[e], BLK[e]) if not isinstance(b, int) else pl.ds(b * BLK[e], BLK[e])
        return pltpu.make_async_remote_copy(
            src_ref=EXS[e].at[rows],
            dst_ref=EXR[e].at[parity, rows],
            send_sem=exs_sem.at[slot],
            recv_sem=exr_sem.at[parity, slot],
            device_id=partner,
            device_id_type=MESH_ID,
        )

    def block_rows(e, b):
        if e == 0:
            return pl.ds(0, BLK[0])
        return rows_at(b * BLK[1], BLK[1], BLK[1])

    def blocks(e, body):
        if e == 0:
            body(0)
        else:
            pl.loop(0, 2)(body)

    def project(e, b, which):
        rows = block_rows(e, b)
        xb = X[e][rows, :]
        for j in which:
            cols = pl.ds(j * COLS, COLS)
            got = dot(xb, win[e, :, cols])
            if j == 0:
                got = (got + pin[e * 2 : e * 2 + 1, :]).astype(BF16) * jnp.asarray(HD**-0.5, BF16)
            elif j == 2:
                got = got + pin[e * 2 + 1 : e * 2 + 2, :]
            QKV[e][rows, cols] = got.astype(BF16)

    def attend(e, b):
        size = BLK[e]
        rows = block_rows(e, b)
        col = lax.broadcasted_iota(jnp.int32, (size, size), 1)
        if e == 0:
            row = lax.broadcasted_iota(jnp.int32, (size, size), 0)
            first = jnp.logical_and(row < 64, col < qlen[0])
            second = jnp.logical_and(
                row >= 64, jnp.logical_and(col >= 64, col < 64 + qlen[1])
            )
            seen = jnp.logical_or(first, second)
        else:
            seen = col < plen[b]

        @pl.loop(0, 3, unroll=PAIR_UNROLL[e])
        def _(pair):
            q2 = QKV[e][rows, rows_at(pair * 128, 128, 128)]
            k2 = QKV[e][rows, rows_at(COLS + pair * 128, 128, 128)]
            v2 = QKV[e][rows, rows_at(2 * COLS + pair * 128, 128, 128)]
            total = jnp.zeros((size, 128), F32)
            for hh in range(2):
                s = dot_t(side(q2, hh), k2)
                s = jnp.where(seen, s, NEGATIVE)
                p = jnp.exp(s - jnp.max(s, axis=-1, keepdims=True))
                p = (p * (1.0 / jnp.sum(p, axis=-1, keepdims=True))).astype(BF16)
                PR[e][b, pair * 2 + hh] = p
                total = total + dot(p, side(v2, hh))
            BALL[e][rows, rows_at(8 * COLS + pair * 128, 128, 128)] = total.astype(BF16)

        ctx = BALL[e][rows, pl.ds(8 * COLS, COLS)]
        EXS[e][rows, :] = dot(ctx, wo[e]).astype(BF16)
        exchange(e, b, 0).start()

    CH = CHUNK

    def first_norm(e, b):
        exchange(e, b, 0).wait()

        @pl.loop(0, BLK[e] // CH, unroll=NORM_UNROLL[e])
        def _(c):
            rows = rows_at(b * BLK[e] + c * CH, CH, CH)
            v = (
                X[e][rows, :].astype(F32)
                + (EXS[e][rows, :].astype(F32) + EXR[e][0, rows, :].astype(F32))
                + par[e * 8 : e * 8 + 1, :]
            )
            v = v - row_mean(v)
            inv = lax.rsqrt(row_mean(v * v) + EPSILON)
            n = v * inv
            N1[e][rows, :] = n
            I1[e][rows, :] = inv
            HID[e][rows, :] = (
                n * par[e * 8 + 2 : e * 8 + 3, :] + par[e * 8 + 4 : e * 8 + 5, :]
            ).astype(BF16)

    def feed(e, b):
        rows = block_rows(e, b)

        @pl.loop(0, 6, unroll=UP_UNROLL[e])
        def _(n):
            cols = rows_at(n * 256, 256, 256)
            u = dot(HID[e][rows, :], wf[e, :, cols]) + pfi[e : e + 1, cols]
            a, slope = gelu_and_slope(u)
            BALL[e][rows, cols] = a.astype(BF16)
            SLOPE[e][rows, cols] = slope.astype(BF16)

        @pl.loop(0, 3, unroll=DOWN_UNROLL[e])
        def _(n):
            cols = rows_at(n * 256, 256, 256)
            EXS[e][rows, cols] = dot(BALL[e][rows, pl.ds(0, FF_HERE)], wd[e, :, cols]).astype(BF16)

        exchange(e, b, 1).start()

    def second_norm(e, b):
        exchange(e, b, 1).wait()

        @pl.loop(0, BLK[e] // CH, unroll=NORM_UNROLL[e])
        def _(c):
            rows = rows_at(b * BLK[e] + c * CH, CH, CH)
            v = (
                HID[e][rows, :].astype(F32)
                + (EXS[e][rows, :].astype(F32) + EXR[e][1, rows, :].astype(F32))
                + par[e * 8 + 1 : e * 8 + 2, :]
            )
            v = v - row_mean(v)
            inv = lax.rsqrt(row_mean(v * v) + EPSILON)
            n = v * inv
            N2[e][rows, :] = n
            I2[e][rows, :] = inv
            OB[e][rows, :] = (
                n * par[e * 8 + 3 : e * 8 + 4, :] + par[e * 8 + 5 : e * 8 + 6, :]
            ).astype(BF16)

    def mini_exchange(k):
        return pltpu.make_async_remote_copy(
            src_ref=xms.at[k],
            dst_ref=xmr.at[k],
            send_sem=xms_sem.at[k],
            recv_sem=xmr_sem.at[k],
            device_id=partner,
            device_id_type=MESH_ID,
        )

    def first_rows(ref):
        rows = [ref[b * 256 : b * 256 + 16, :].astype(F32)[0:1] for b in range(2)]
        return jnp.concatenate([*rows, jnp.zeros((14, rows[0].shape[1]), F32)], axis=0)

    def mini_attend():
        xm = first_rows(xp).astype(BF16)
        q = (dot(xm, win[1, :, pl.ds(0, COLS)]) + pin[2:3, :]).astype(BF16).astype(F32) * HD**-0.5
        of_head = lax.broadcasted_iota(jnp.int32, (16, COLS), 1) // HD == lax.broadcasted_iota(
            jnp.int32, (16, COLS), 0
        )
        col = lax.broadcasted_iota(jnp.int32, (16, 256), 1)
        rows = []
        for b in range(2):
            keys = qkvp[b * 256 : (b + 1) * 256, COLS : 2 * COLS]
            vals = qkvp[b * 256 : (b + 1) * 256, 2 * COLS : 3 * COLS]
            s = dot_t(jnp.where(of_head, q[b : b + 1], 0.0).astype(BF16), keys)
            s = jnp.where(col < plen[b], s, NEGATIVE)
            p = jnp.exp(s - jnp.max(s, axis=-1, keepdims=True))
            p = (p * (1.0 / jnp.sum(p, axis=-1, keepdims=True))).astype(BF16)
            rows.append(jnp.sum(jnp.where(of_head, dot(p, vals), 0.0), axis=0, keepdims=True))
        ctx = jnp.concatenate([*rows, jnp.zeros((14, COLS), F32)], axis=0)
        xms[0] = dot(ctx.astype(BF16), wo[1]).astype(BF16)
        mini_exchange(0).start()

    def mini_norm(k, v):
        mini_exchange(k).wait()
        v = v + (xms[k].astype(F32) + xmr[k].astype(F32)) + par[8 + k : 9 + k, :]
        v = v - row_mean(v)
        n = v * lax.rsqrt(row_mean(v * v) + EPSILON)
        return (n * par[10 + k : 11 + k, :] + par[12 + k : 13 + k, :]).astype(BF16)

    def mini_feed():
        hm[...] = mini_norm(0, first_rows(xp))

        u = dot(hm[...], wf[1]) + pfi[1:2, :]
        a = gelu_and_slope(u)[0].astype(BF16)
        xms[1] = dot(a, wd[1]).astype(BF16)

        mini_exchange(1).start()

    def transpose_into(e, k, src, b):
        rows = block_rows(e, b)

        @pl.loop(0, 2)
        def _(c):
            tile = src[rows, rows_at(c * COLS, COLS, 128)].T
            AT[e][k, pl.ds(c * 2, 2), :, :, :, rows] = tile.reshape(2, 2, 2, ROWS_OUT, BLK[e])

    def left_factor(axis, k):
        return pltpu.make_async_remote_copy(
            src_ref=atq.at[k, :, :, 1 - x] if axis == 0 else atq.at[k, :, 1 - y],
            dst_ref=fra.at[axis, k],
            send_sem=fas_sem.at[axis, k],
            recv_sem=far_sem.at[axis, k],
            device_id=first_dev[axis],
            device_id_type=MESH_ID,
        )

    def right_factor(axis, pair):
        return pltpu.make_async_remote_copy(
            src_ref=ballq.at[:, pl.ds((pair * 2 + axis) * COLS, COLS)],
            dst_ref=frb.at[axis, pair],
            send_sem=fbs_sem.at[axis, pair],
            recv_sem=fbr_sem.at[axis, pair],
            device_id=first_dev[axis],
            device_id_type=MESH_ID,
        )

    first_dev, other_dev = (at_x, at_y), (at_y, at_x)
    first_at, other_at = (x, y), (y, x)

    need(0, 1, 2, 3)
    load(4, 6, 7, 8, 5, 9, 10, 12, 11, 13, 14, 15)
    project(0, 0, (0, 1, 2))
    need(8)
    pl.semaphore_wait(barrier, 16)
    attend(0, 0)
    right_factor(0, 4).start()
    need(4, 5, 6, 7, 9)
    blocks(1, lambda b: project(1, b, (1, 2)))
    mini_attend()
    first_norm(0, 0)
    need(10, 12)
    feed(0, 0)
    for axis in range(2):
        for pair in range(2):
            right_factor(axis, pair).start()
    need(11, 13)
    mini_feed()
    second_norm(0, 0)
    out_q = pltpu.make_async_copy(obq, oq_out, out_sem.at[0])
    out_p = pltpu.make_async_copy(obp, op_out, out_sem.at[1])
    out_q.start()
    mini_out = mini_norm(1, hm[...].astype(F32)).astype(F32)

    pieces = []
    rows = [obq[at : at + 16, :].astype(F32)[0:1] for at in (0, 64)]
    for head in (*rows, mini_out[0:1], mini_out[1:2]):
        pieces += [head[:, k * 256 : (k + 1) * 256] for k in range(3)]
    pieces.append(jnp.zeros((4, 256), F32))
    hg[me] = jnp.concatenate(pieces, axis=0).astype(BF16)

    def heads(k):
        return pltpu.make_async_remote_copy(
            src_ref=hg.at[me],
            dst_ref=hg.at[me],
            send_sem=hgs_sem.at[k],
            recv_sem=hgr_sem.at[k],
            device_id=at_dp(me ^ k),
            device_id_type=MESH_ID,
        )

    for k in range(1, 16):
        heads(k).start()
    need(14, 15)
    transpose_into(0, 1, hq, 0)
    for axis in range(2):
        left_factor(axis, 1).start()
    transpose_into(0, 3, xq, 0)
    for axis in range(2):
        left_factor(axis, 3).start()
    blocks(1, lambda b: project(1, b, (0,)))
    attend(1, 0)
    for k in range(1, 16):
        copy = pltpu.make_async_remote_copy(
            src_ref=hg.at[me],
            dst_ref=hg.at[me ^ k],
            send_sem=hgs_sem.at[k],
            recv_sem=hgr_sem.at[k],
            device_id=at_dp(me ^ k),
            device_id_type=MESH_ID,
        )
        copy.wait()
    gathered = hg[...].astype(F32).reshape(256, 256)
    hf[0] = gathered[:, 0:128]
    hf[1] = gathered[:, 128:256]

    def all_heads(first):
        groups = []
        for i in range(2):
            parts = [
                hf[c, pl.ds(first + i * 3 + k, 16, stride=16), :] for k in range(3) for c in range(2)
            ]
            groups.append(jnp.concatenate(parts, axis=1))
        return jnp.concatenate(groups, axis=0)

    heads_q, heads_p = all_heads(0), all_heads(6)
    gain = score_gain * D ** (-0.5)
    class_scores = dot_t(heads_q.astype(BF16), heads_p.astype(BF16)) * gain
    chosen = masks[0:32, :]
    logits = jnp.where(masks[32:64, :] > 0.5, class_scores, NEGATIVE)
    top = jnp.max(logits, axis=1, keepdims=True)
    log_total = top + jnp.log(jnp.sum(jnp.exp(logits - top), axis=1, keepdims=True))
    target = jnp.sum(chosen * class_scores, axis=1, keepdims=True)
    loss = jnp.sum(log_total - target, axis=0, keepdims=True) * (1.0 / 32)
    sm[SMALL : SMALL + 8, :] = jnp.broadcast_to(loss, (8, 128))
    d_class = (jnp.exp(logits - log_total) - chosen) * gain
    dh[0:32, :] = lax.dot_general(
        d_class, heads_p, (((1,), (0,)), ((), ())), precision=HIGHEST, preferred_element_type=F32
    )
    dh[32:64, :] = lax.dot_general(
        d_class, heads_q, (((0,), (0,)), ((), ())), precision=HIGHEST, preferred_element_type=F32
    )

    def norm_back(incoming, n, inv, scale):
        scaled = incoming * scale
        return inv * (scaled - row_mean(scaled) - n * row_mean(scaled * n))

    def second_back(e, b):
        row0 = lax.broadcasted_iota(jnp.int32, (CH, 1), 0)
        seqs = 2 if e == 0 else 1
        length = 64 if e == 0 else 256
        for i in range(seqs):
            group = i if e == 0 else b
            extra = dh[pl.ds(e * 32 + group * 16 + me, 1), :]

            @pl.loop(0, length // CH, unroll=NORM_UNROLL[e])
            def _(c):
                rows = rows_at(group * length + c * CH, CH, CH)
                add = jnp.where(row0 + c * CH == 0, extra, 0.0)
                d = COT[e][rows, :].astype(F32) + add
                n = N2[e][rows, :]
                out = norm_back(d, n, I2[e][rows, :], par[e * 8 + 3 : e * 8 + 4, :])
                N2[e][rows, :] = out
                low = out.astype(BF16)
                DD[e][rows, :] = low
                acc_s[e * 6 + 1] += fold8(d * n)
                acc_s[e * 6 + 3] += fold8(d)
                acc_s[e * 6 + 5] += fold8(low.astype(F32))

        transpose_into(e, 0, DD[e], b)

    def feed_back(e, b):
        rows = block_rows(e, b)

        @pl.loop(0, 6, unroll=UP_UNROLL[e])
        def _(n):
            cols = rows_at(n * 256, 256, 256)
            d = dot_t(DD[e][rows, :], wd[e, cols, :]) * SLOPE[e][rows, cols].astype(F32)
            d = d.astype(BF16)
            BALL[e][rows, rows_at(4 * COLS + n * 256, 256, 256)] = d
            acc_f[e, :, cols] += fold8(d.astype(F32))

        @pl.loop(0, 3, unroll=DOWN_UNROLL[e])
        def _(n):
            cols = rows_at(n * 256, 256, 256)
            EXS[e][rows, cols] = dot_t(BALL[e][rows, pl.ds(4 * COLS, FF_HERE)], wf[e, cols, :]).astype(BF16)

        exchange(e, b, 0).start()
        if e == 1:
            transpose_into(e, 1, HID[e], b)

    def first_back(e, b):
        exchange(e, b, 0).wait()

        @pl.loop(0, BLK[e] // CH, unroll=NORM_UNROLL[e])
        def _(c):
            rows = rows_at(b * BLK[e] + c * CH, CH, CH)
            d = N2[e][rows, :] + (EXS[e][rows, :].astype(F32) + EXR[e][0, rows, :].astype(F32))
            n = N1[e][rows, :]
            out = norm_back(d, n, I1[e][rows, :], par[e * 8 + 2 : e * 8 + 3, :])
            N1[e][rows, :] = out
            low = out.astype(BF16)
            DD[e][rows, :] = low
            acc_s[e * 6 + 0] += fold8(d * n)
            acc_s[e * 6 + 2] += fold8(d)
            acc_s[e * 6 + 4] += fold8(low.astype(F32))

        transpose_into(e, 2, DD[e], b)

    def attend_back(e, b):
        rows = block_rows(e, b)
        size = BLK[e]
        DC[e][rows, :] = dot_t(DD[e][rows, :], wo[e]).astype(BF16)

        @pl.loop(0, 3, unroll=PAIR_UNROLL[e])
        def _(pair):
            q2 = QKV[e][rows, rows_at(pair * 128, 128, 128)]
            k2 = QKV[e][rows, rows_at(COLS + pair * 128, 128, 128)]
            v2 = QKV[e][rows, rows_at(2 * COLS + pair * 128, 128, 128)]
            dc2 = DC[e][rows, rows_at(pair * 128, 128, 128)]
            dq = jnp.zeros((size, 128), F32)
            dk = jnp.zeros((size, 128), F32)
            dv = jnp.zeros((size, 128), F32)
            for hh in range(2):
                low = PR[e][b, pair * 2 + hh]
                p = low.astype(F32)
                dch = side(dc2, hh)
                dp = dot_t(dch, v2)
                ds = (p * (dp - jnp.sum(p * dp, axis=-1, keepdims=True))).astype(BF16)
                dv = dv + t_dot(low, dch)
                dq = dq + dot(ds, side(k2, hh))
                dk = dk + t_dot(ds, side(q2, hh))
            dq = (dq * HD**-0.5).astype(BF16)
            dv = dv.astype(BF16)
            cols = rows_at(pair * 128, 128, 128)
            BALL[e][rows, rows_at(9 * COLS + pair * 128, 128, 128)] = dq
            BALL[e][rows, rows_at(10 * COLS + pair * 128, 128, 128)] = dk.astype(BF16)
            BALL[e][rows, rows_at(11 * COLS + pair * 128, 128, 128)] = dv
            acc_b[e, :, cols] += fold8(dq.astype(F32))
            acc_b[e, :, rows_at(COLS + pair * 128, 128, 128)] += fold8(dv.astype(F32))

        if e == 1:
            transpose_into(e, 3, X[e], b)

    def token_back(e, b):
        rows = block_rows(e, b)

        @pl.loop(0, 3, unroll=DOWN_UNROLL[e])
        def _(n):
            cols = rows_at(n * 256, 256, 256)
            EXS[e][rows, cols] = dot_t(BALL[e][rows, pl.ds(9 * COLS, 3 * COLS)], win[e, cols, :]).astype(BF16)

        exchange(e, b, 1).start()

    def token_end(e, b):
        exchange(e, b, 1).wait()

        @pl.loop(0, BLK[e] // CH, unroll=NORM_UNROLL[e])
        def _(c):
            rows = rows_at(b * BLK[e] + c * CH, CH, CH)
            OB[e][rows, :] = (
                N1[e][rows, :] + (EXS[e][rows, :].astype(F32) + EXR[e][1, rows, :].astype(F32))
            ).astype(BF16)

    def job_of(j):
        return j // 6, j % 6

    def product(half, blk, sel):
        k = jnp.where(blk < 8, blk // 4, jnp.where(blk == 8, 2, 3))
        rows = atp[k, :, :, sel] if half == 0 else atp[k, :, sel]
        out = dot(rows.reshape(COLS, TOKS[1]), ballp[:, rows_at(blk * COLS, COLS, 128)])
        return out.reshape(ZN, 2, ROWS_OUT, COLS)

    def pair_product(half, pair):
        blk = pair * 2 + half
        k = blk // 4 if blk < 8 else 2 if blk == 8 else 3
        rows = atq[k, :, :, x] if half == 0 else atq[k, :, y]
        rows = jnp.concatenate([rows.reshape(COLS, TOKS[0]), fra[half, k].reshape(COLS, TOKS[0])], axis=1)
        cols = jnp.concatenate([ballq[:, blk * COLS : (blk + 1) * COLS], frb[half, pair]], axis=0)
        return dot(rows, cols).reshape(ZN, 2, ROWS_OUT, COLS)

    def p1(j, half):
        return pltpu.make_async_remote_copy(
            src_ref=p1s.at[j % DS, half],
            dst_ref=p1r.at[j % D1, half],
            send_sem=p1s_sem.at[j % DS, half],
            recv_sem=p1r_sem.at[j % D1, half],
            device_id=first_dev[half],
            device_id_type=MESH_ID,
        )

    def other(j, half, line_first):
        mine, to = p1r.at[j % D1, half], p2r.at[j % D2, half]
        return pltpu.make_async_remote_copy(
            src_ref=mine.at[z, 1 - other_at[half]] if line_first else mine.at[:, 1 - other_at[half]],
            dst_ref=to.at[0] if line_first else to,
            send_sem=p2s_sem.at[j % D2, half],
            recv_sem=p2r_sem.at[j % D2, half],
            device_id=other_dev[half],
            device_id_type=MESH_ID,
        )

    def block(j, half, d, right, line_first, at):
        slot = d if right else jnp.where(d == at, ZN, d)
        return zb.at[j % DZ, half, slot] if line_first else zb.at[j % DZ, half, slot, 0]

    def own_block(j, half, d, line_first):
        return p1r.at[j % D1, half, d] if line_first else p2r.at[j % D2, half, d]

    def along(j, half, d, right, relayed, line_first):
        send, recv = (zrs_sem, zrr_sem) if right else (zls_sem, zlr_sem)
        here = block(j, half, d, right, line_first, z)
        return pltpu.make_async_remote_copy(
            src_ref=here if relayed else own_block(j, half, d, line_first),
            dst_ref=block(j, half, d, right, line_first, z + 1 if right else z - 1),
            send_sem=send.at[j % DZ, half, d],
            recv_sem=recv.at[j % DZ, half, d],
            device_id=at_dp((me + 4 if right else me + 12) % 16),
            device_id_type=MESH_ID,
        )

    def total_of(a, b):
        return (a[...].astype(F32) + b[...].astype(F32)).astype(BF16)

    def step0(j):
        _, pair = job_of(j)
        for half in range(2):
            p1s[j % DS, half] = product(half, pair * 2 + half, 1 - first_at[half]).astype(BF16)
            p1(j, half).start()

    def step1(j, send):
        e_of, pair = job_of(j)

        @pl.when(e_of == 1)
        def _():
            own = [product(half, pair * 2 + half, first_at[half]) for half in range(2)]
            for half in range(2):
                p1(j, half).wait()
                p1r[j % D1, half] = (own[half] + p1r[j % D1, half].astype(F32)).astype(BF16)
                send(half)

        for p in range(6):

            @pl.when(jnp.logical_and(e_of == 0, pair == p))
            def _():
                for half in range(2):
                    if p in (0, 2):
                        left_factor(half, p // 2).wait()
                    elif p == 4:
                        left_factor(half, 2 + half).wait()
                    elif p == 5 and half == 0:
                        left_factor(0, 3).wait()
                    right_factor(half, p).wait()
                    p1r[j % D1, half] = pair_product(half, p).astype(BF16)
                    send(half)

    def turned(j, half):
        other(j, half, False).wait()
        mine = p2r.at[j % D2, half]
        mine[...] = total_of(mine, p1r.at[j % D1, half, :, other_at[half]])

    def ends(j, half, line_first):
        @pl.when(z == 0)
        def _():
            for d in (3, 2, 1):
                along(j, half, d, True, False, line_first).start()

        @pl.when(z == 3)
        def _():
            for d in (0, 1, 2):
                along(j, half, d, False, False, line_first).start()

    def relay(j, half, d, right, line_first):
        held = block(j, half, d, right, line_first, z)
        along(j, half, d, right, True, line_first).wait_recv()
        held[...] = total_of(held, own_block(j, half, d, line_first))
        along(j, half, d, right, True, line_first).start()

    def middle1(j, line_first):
        @pl.when(z == 1)
        def _():
            for half in range(2):
                for d in (3, 2):
                    relay(j, half, d, True, line_first)

        @pl.when(z == 2)
        def _():
            for half in range(2):
                for d in (0, 1):
                    relay(j, half, d, False, line_first)

    def middle2(j, line_first):
        @pl.when(z == 2)
        def _():
            for half in range(2):
                relay(j, half, 3, True, line_first)

        @pl.when(z == 1)
        def _():
            for half in range(2):
                relay(j, half, 0, False, line_first)

    def line_end(j, line_first):
        for half in range(2):
            mine = own_block(j, half, z, line_first)

            @pl.when(z > 0)
            def _():
                along(j, half, z, True, True, line_first).wait_recv()
                mine[...] = total_of(mine, block(j, half, z, True, line_first, z))

            @pl.when(z < 3)
            def _():
                along(j, half, z, False, True, line_first).wait_recv()
                mine[...] = total_of(mine, block(j, half, z, False, line_first, z))

            for d in range(4):

                @pl.when(d > z)
                def _():
                    along(j, half, d, True, True, line_first).wait_send()

                @pl.when(d < z)
                def _():
                    along(j, half, d, False, True, line_first).wait_send()

    def pass_on(j):
        for half in range(2):
            other(j, half, True).start()

    def passed(j):
        for half in range(2):
            other(j, half, True).wait()

    def result(slot, half, to):
        return pltpu.make_async_copy(fin.at[slot, half], to, fin_sem.at[slot, half])

    def output(j, line_first):
        e_of, pair = job_of(j)
        for half in range(2):

            @pl.when(j >= 2)
            def _():
                result(j % 2, half, g_out.at[0]).wait()

            if line_first:
                total = p1r[j % D1, half, z, other_at[half]].astype(F32) + p2r[j % D2, half, 0].astype(F32)
            else:
                total = p2r[j % D2, half, z].astype(F32)
            fin[j % 2, half] = total
            for e in range(2):
                for p in range(6):

                    @pl.when(jnp.logical_and(e_of == e, pair == p))
                    def _():
                        blk = p * 2 + half
                        if blk < 4:
                            to = g_fo.at[e, :, pl.ds(blk * COLS, COLS)]
                        elif blk < 8:
                            to = g_fi.at[e, :, pl.ds((blk - 4) * COLS, COLS)]
                        elif blk == 8:
                            to = g_out.at[e]
                        else:
                            to = g_in.at[e, blk - 9]
                        result(j % 2, half, to).start()

    small_to = (at_dp(me ^ 8), at_dp(me ^ 4), at_x, at_y)

    def small(k):
        return pltpu.make_async_remote_copy(
            src_ref=smb.at[k],
            dst_ref=smr.at[k],
            send_sem=sms_sem.at[k],
            recv_sem=smr_sem.at[k],
            device_id=small_to[k],
            device_id_type=MESH_ID,
        )

    def small_first():
        smb[0] = jnp.zeros_like(smb[0])
        for e in range(2):
            for i in range(6):
                smb[0, e * 9 + i : e * 9 + i + 1, :] = jnp.sum(acc_s[e * 6 + i], axis=0, keepdims=True)
            smb[0, e * 9 + 6 : e * 9 + 7, :] = jnp.sum(acc_b[e], axis=0, keepdims=True)
            for i in range(2):
                smb[0, e * 9 + 7 + i : e * 9 + 8 + i, :] = jnp.sum(
                    acc_f[e, :, i * D : (i + 1) * D], axis=0, keepdims=True
                )
        small(0).start()

    def small_next(k):
        small(k).wait()
        if k < 3:
            smb[k + 1] = smb[k] + smr[k]
            small(k + 1).start()
        else:
            total = smb[k] + smr[k]
            sm[0:SMALL, :] = jnp.zeros((SMALL, 128), F32)
            wide = pltpu.roll(total, lax.rem(D - me * ROWS_OUT, D), 1)
            sm[0:SMALL, 0:ROWS_OUT] = wide[:, 0:ROWS_OUT]
            heads_own = pltpu.roll(total, lax.rem(D - me * 24, D), 1)
            feed_own = pltpu.roll(total, lax.rem(D - (me % 8) * 96, D), 1)
            for e in range(2):
                at = e * 9 + 6
                for i in range(2):
                    sm[at + i : at + i + 1, 0:24] = heads_own[at : at + 1, i * COLS : i * COLS + 24]
                low, high = feed_own[at + 1 : at + 2, 0:96], feed_own[at + 2 : at + 3, 0:96]
                sm[at + 2 : at + 3, 0:96] = jnp.where(me < 8, low, high)
            pltpu.make_async_copy(sm, sm_out, out_sem.at[2]).start()

    def q_second_back():
        second_back(0, 0)
        left_factor(0, 0).start()
        left_factor(1, 0).start()

    def q_feed_back():
        feed_back(0, 0)
        for axis in range(2):
            for pair in (2, 3):
                right_factor(axis, pair).start()

    def q_first_back():
        first_back(0, 0)
        left_factor(0, 2).start()

    def q_attend_back():
        attend_back(0, 0)
        right_factor(1, 4).start()
        right_factor(0, 5).start()
        right_factor(1, 5).start()

    def q_token_end():
        token_end(0, 0)
        pltpu.make_async_copy(obq, gq_out, out_sem.at[0]).start()

    def p_token_end():
        blocks(1, lambda b: token_end(1, b))
        pltpu.make_async_copy(obp, gp_out, out_sem.at[1]).start()

    def p_mid(b):
        first_norm(1, b)
        feed(1, b)

    def p_second():
        blocks(1, lambda b: second_norm(1, b))
        out_p.start()

    def passages(piece):
        return lambda: blocks(1, lambda b: piece(1, b))

    work = {
        0: [q_feed_back, lambda: attend(1, 1)],
        2: [q_first_back, lambda: p_mid(0)],
        4: [q_attend_back, lambda: p_mid(1)],
        5: [lambda: token_back(0, 0), p_second, out_q.wait],
        6: [q_token_end, lambda: second_back(1, 1)],
        7: [lambda: feed_back(1, 1)],
        8: [lambda: first_back(1, 1)],
        9: [lambda: attend_back(1, 1)],
        10: [lambda: token_back(1, 1), small_first],
        12: [lambda: small_next(0)],
        14: [lambda: small_next(1)],
        15: [out_p.wait, p_token_end, lambda: small_next(2)],
        16: [lambda: small_next(3)],
    }
    between = {
        5: [lambda: second_back(1, 0)],
        6: [lambda: feed_back(1, 0)],
        7: [lambda: first_back(1, 0)],
        8: [lambda: attend_back(1, 0)],
        9: [lambda: token_back(1, 0)],
    }

    def is_line_first(j):
        found = j == LINE_FIRST[0]
        for k in LINE_FIRST[1:]:
            found = jnp.logical_or(found, j == k)
        return found

    def steps(late, j):
        line_first = is_line_first(j)
        if late == 1:

            def send(half):
                @pl.when(line_first)
                def _():
                    ends(j, half, True)

                @pl.when(jnp.logical_not(line_first))
                def _():
                    other(j, half, False).start()

            step1(j, send)
            return

        @pl.when(line_first)
        def _():
            if late == 2:
                middle1(j, True)
            elif late == 3:
                middle2(j, True)
            elif late == 4:
                line_end(j, True)
                pass_on(j)
            else:
                passed(j)
                output(j, True)

        @pl.when(jnp.logical_not(line_first))
        def _():
            if late == 2:
                for half in range(2):
                    turned(j, half)
                    ends(j, half, False)
            elif late == 3:
                middle1(j, False)
            elif late == 4:
                middle2(j, False)
            else:
                line_end(j, False)
                output(j, False)

    q_second_back()

    @pl.loop(0, JOBS + 5)
    def _(tick):
        for at, things in work.items():

            @pl.when(tick == at)
            def _():
                for thing in things:
                    thing()

        @pl.when(jnp.logical_and(tick >= 6, tick < JOBS))
        def _():
            step0(tick)

        for late in (1, 2, 3, 4, 5):

            @pl.when(jnp.logical_and(tick >= late, tick < JOBS + late))
            def _():
                steps(late, tick - late)

            if late == 2:
                for at, things in between.items():

                    @pl.when(tick == at)
                    def _():
                        for thing in things:
                            thing()

    pltpu.make_async_copy(obq, gq_out, out_sem.at[0]).wait()
    pltpu.make_async_copy(obp, gp_out, out_sem.at[1]).wait()
    pltpu.make_async_copy(sm, sm_out, out_sem.at[2]).wait()
    for slot in range(2):
        for half in range(2):
            result(slot, half, g_out.at[0]).wait()


def finish_kernel(*refs):
    oq, op, gq, gp, g_in, g_out, g_fi, g_fo, sums_in = refs[:9]
    large, (loss_to, in_bias, fi_bias, bo, gain, shift) = refs[9:17], refs[17:23]
    held, sums, in_sems, out_sems = refs[23:31], refs[31], refs[32], refs[33]
    sources = (oq, op, gq, gp, g_in, g_out, g_fi, g_fo)
    loads = [pltpu.make_async_copy(sources[i], held[i], in_sems.at[i]) for i in range(8)]
    stores = [pltpu.make_async_copy(held[i], large[i], out_sems.at[i]) for i in range(8)]
    little = pltpu.make_async_copy(sums_in, sums, in_sems.at[8])
    little.start()
    for load in loads:
        load.start()
    little.wait()
    loss_to[...] = sums[SMALL : SMALL + 1, 0:1]
    for e in range(2):
        at = e * 9
        gain[e] = sums[at : at + 2, 0:ROWS_OUT]
        shift[e] = sums[at + 2 : at + 4, 0:ROWS_OUT]
        bo[e] = sums[at + 4 : at + 6, 0:ROWS_OUT]
        in_bias[e] = sums[at + 6 : at + 8, 0:24]
        fi_bias[e : e + 1] = sums[at + 8 : at + 9, 0:96]
    for load, store in zip(loads, stores):
        load.wait()
        store.start()
    for store in stores:
        store.wait()


FF_HERE = 1536


def fused(
    question_tokens, passage_tokens, question_cotangent, passage_cotangent,
    question_lengths, passage_lengths, dataset_ids, positives,
    attn_in, attn_in_bias, attn_out, ffn_in, ffn_in_bias, ffn_out, out_biases, norm_gains, norm_shifts,
):
    any_spec = pl.BlockSpec(memory_space=pl.ANY)
    vmem = pl.BlockSpec(memory_space=pltpu.VMEM)

    def both(shape, dtype):
        return [pltpu.VMEM(shape(m), dtype) for m in TOKS]

    shape = jax.ShapeDtypeStruct
    dma = pltpu.SemaphoreType.DMA
    outs = pl.pallas_call(
        partial(fused_kernel, last=0),
        name="fused",
        in_specs=[any_spec] * 17,
        out_specs=[any_spec] * 9,
        out_shape=[
            shape((128, D), BF16),
            shape((512, D), BF16),
            shape((128, D), BF16),
            shape((512, D), BF16),
            shape((2, 3, ROWS_OUT, COLS), F32),
            shape((2, ROWS_OUT, COLS), F32),
            shape((2, ROWS_OUT, FF_HERE), F32),
            shape((2, ROWS_OUT, FF_HERE), F32),
            shape((SMALL + 8, 128), F32),
        ],
        scratch_shapes=[
            pltpu.VMEM((2, D, 3 * COLS), BF16),
            pltpu.VMEM((2, COLS, D), BF16),
            pltpu.VMEM((2, D, FF_HERE), BF16),
            pltpu.VMEM((2, FF_HERE, D), BF16),
            *both(lambda m: (m, D), BF16),
            *both(lambda m: (m, D), BF16),
            *both(lambda m: (m, 3 * COLS), BF16),
            pltpu.VMEM((1, 6, 128, 128), BF16),
            pltpu.VMEM((2, 6, 256, 256), BF16),
            *both(lambda m: (m, D), BF16),
            *both(lambda m: (m, D), F32),
            *both(lambda m: (m, D), F32),
            *both(lambda m: (m, 1), F32),
            *both(lambda m: (m, 1), F32),
            *both(lambda m: (m, FF_HERE), BF16),
            *both(lambda m: (m, D), BF16),
            *both(lambda m: (m, D), BF16),
            *both(lambda m: (m, COLS), BF16),
            *both(lambda m: (m, 12 * COLS), BF16),
            *both(lambda m: (4, ZN, 2, 2, ROWS_OUT, m), BF16),
            *both(lambda m: (m, D), BF16),
            *both(lambda m: (2, m, D), BF16),
            pltpu.VMEM((16, D), F32),
            pltpu.VMEM((8, COLS), F32),
            pltpu.VMEM((8, FF_HERE), F32),
            pltpu.VMEM((64, 32), F32),
            pltpu.VMEM((16, 16, 256), BF16),
            pltpu.VMEM((2, 256, 128), F32),
            pltpu.VMEM((64, D), F32),
            pltpu.VMEM((12, 8, D), F32),
            pltpu.VMEM((2, 8, 2 * COLS), F32),
            pltpu.VMEM((2, 8, FF_HERE), F32),
            pltpu.VMEM((4, SMALL, D), F32),
            pltpu.VMEM((4, SMALL, D), F32),
            pltpu.VMEM((DS, 2, ZN, 2, ROWS_OUT, COLS), BF16),
            pltpu.VMEM((D1, 2, ZN, 2, ROWS_OUT, COLS), BF16),
            pltpu.VMEM((D2, 2, ZN, ROWS_OUT, COLS), BF16),
            pltpu.VMEM((DZ, 2, ZN + 1, 2, ROWS_OUT, COLS), BF16),
            pltpu.VMEM((2, 2, ROWS_OUT, COLS), F32),
            pltpu.VMEM((2, 4, ZN, 2, ROWS_OUT, TOKS[0]), BF16),
            pltpu.VMEM((2, 6, TOKS[0], COLS), BF16),
            pltpu.VMEM((2, 16, D), BF16),
            pltpu.VMEM((2, 16, D), BF16),
            pltpu.VMEM((16, D), BF16),
            *[pltpu.SMEM((n,), jnp.int32) for n in (2, 2, 32, 32)],
            pltpu.VMEM((2, 2, COLS), BF16),
            pltpu.VMEM((2, FF_HERE), BF16),
            *[pltpu.VMEM((2, 2, D), BF16) for _ in range(3)],
            pltpu.VMEM((SMALL + 8, 128), F32),
            dma((2, 2)),
            dma((9,)),
            dma((16,)),
            dma((3,)),
            dma((3,)),
            dma((2, 3)),
            dma((16,)),
            dma((16,)),
            dma((4,)),
            dma((4,)),
            dma((DS, 2)),
            dma((D1, 2)),
            dma((D2, 2)),
            dma((D2, 2)),
            dma((DZ, 2, ZN)),
            dma((DZ, 2, ZN)),
            dma((DZ, 2, ZN)),
            dma((DZ, 2, ZN)),
            dma((2, 4)),
            dma((2, 4)),
            dma((2, 6)),
            dma((2, 6)),
            dma((2,)),
            dma((2,)),
        ],
        compiler_params=pltpu.CompilerParams(
            collective_id=0, has_side_effects=True, vmem_limit_bytes=VMEM_BYTES
        ),
    )(
        question_tokens.reshape(128, D),
        passage_tokens.reshape(512, D),
        question_cotangent.reshape(128, D),
        passage_cotangent.reshape(512, D),
        question_lengths, passage_lengths, dataset_ids, positives,
        attn_in.transpose(0, 2, 1, 3), attn_in_bias, attn_out, ffn_in, ffn_in_bias, ffn_out,
        out_biases, norm_gains, norm_shifts,
    )
    oq, op, gq, gp, g_in, g_out, g_fi, g_fo, sums = outs
    large = (oq, op, gq, gp, g_in, g_out, g_fi, g_fo)
    small = [(1, 1), (2, 2, 24), (2, 96), (2, 2, ROWS_OUT), (2, 2, ROWS_OUT), (2, 2, ROWS_OUT)]
    oq, op, gq, gp, g_in, g_out, g_fi, g_fo, loss, in_bias, fi_bias, bo, gain, shift = pl.pallas_call(
        finish_kernel,
        name="finish",
        in_specs=[any_spec] * 9,
        out_specs=[any_spec] * 8 + [vmem] * 6,
        out_shape=[shape(a.shape, a.dtype) for a in large] + [shape(dims, F32) for dims in small],
        scratch_shapes=[*[pltpu.VMEM(a.shape, a.dtype) for a in (*large, sums)], dma((9,)), dma((8,))],
        compiler_params=pltpu.CompilerParams(vmem_limit_bytes=VMEM_BYTES),
    )(*large, sums)
    return (
        oq.reshape(2, 64, D),
        op.reshape(2, 256, D),
        loss.reshape(()),
        gq.reshape(2, 64, D),
        gp.reshape(2, 256, D),
        g_in.transpose(0, 2, 1, 3),
        in_bias,
        g_out.transpose(0, 2, 1),
        g_fi,
        fi_bias,
        g_fo.transpose(0, 2, 1),
        bo,
        gain,
        shift,
    )


VMEM_BYTES = 62 * 1024 * 1024


def solution(mesh):
    in_specs = (
        P("dp", None, None),
        P("dp", None, None),
        P("dp", None, None),
        P("dp", None, None),
        P("dp"),
        P("dp"),
        P(),
        P(),
        P(None, None, None, "tensor"),
        P(None, None, "tensor"),
        P(None, "tensor", None),
        P(None, None, "tensor"),
        P(None, "tensor"),
        P(None, "tensor", None),
        P(),
        P(),
        P(),
    )
    out_specs = (
        P("dp", None, None),
        P("dp", None, None),
        P(),
        P("dp", None, None),
        P("dp", None, None),
        P(None, "dp", None, "tensor"),
        P(None, None, ("tensor", "dp")),
        P(None, "tensor", "dp"),
        P(None, "dp", "tensor"),
        P(None, ("tensor", "dp")),
        P(None, "tensor", "dp"),
        P(None, None, "dp"),
        P(None, None, "dp"),
        P(None, None, "dp"),
    )
    step = fused if mesh.shape["dp"] == 4 * ZN and mesh.shape["tensor"] == 2 else per_device
    return jax.shard_map(
        step, mesh=mesh, in_specs=in_specs, out_specs=out_specs, check_vma=False
    )
```
